128 devices in a mesh: cells: 16 (over z, x), spots: 8 (over y, core).
Axes of the slice: x: 4, y: 4, z: 4, core: 2. Of those that a mesh axis runs over, the one named last changes fastest.
Arguments:
- map_logits: float32 [20480, 8192], P('cells', 'spots'), may hold values from -10 to 10
- filter_logits: float32 [20480], P('cells'), may hold values from -6 to 6
- expr: float32 [2048, 20480], P(None, 'cells'), may hold values from 0 to 2
- spatial: float32 [2048, 8192], P(None, 'spots'), may hold values from 0 to 2
- cell_type: int32 [20480], P('cells'), may hold values from -1 to 31, as said below
- slide_id: int32 [8192], P('spots'), may hold values from 0 to 2, as said below
- spot_mask: int32 [8192], P('spots'), may hold values 0 or 1
Outputs:
- loss_terms: float32 [5], replicated
- type_fraction: float32 [32, 8192], P(None, 'spots')
- grad_map: float32 [20480, 8192], P('cells', 'spots')
- grad_filter: float32 [20480], P('cells')
- grad_expr: float32 [2048, 20480], P('spots', 'cells')
The draws below stay inside these ranges and needn't reach their ends.
Inputs may be any that keep to these rules, and one draw needn't show every extreme that they name: `cell_type`: rows come in one contiguous group per type label, every label of 0 to 31 present; each group is whole blocks of 128 rows, padded at its end with fewer than 128 rows of -1. `slide_id`: never falling; each slide covers 8192 // 4 spots or more.
All inputs are finite; a program needn't handle non-finite values. No bound on the sum of `spot_mask` on one device may be relied on, other than what follows from the above.
Results may differ from the reference program's by a relative error of at most 0.0003.
Values sent between devices are 32-bit elements; how exact they have to be, the bound alone decides.
No kernel may reach another device: no remote copies, remote signals or barrier semaphores. Data moves between devices by JAX's collectives and lax.ppermute only.
A program may use at most 128 MiB of HBM per device.

```python
import jax
import jax.numpy as jnp
from jax import lax

GENES = 2048
TYPES = 32
SLIDES = 3
CELLS = 20480
SPOTS = 8192


def draw_cell_type(key, part):
    key = jax.random.fold_in(key, 11)
    first, second, third, fourth = jax.random.split(key, 4)
    blocks = CELLS // 128
    extra_count = blocks - TYPES
    raw_one = jax.random.randint(first, (extra_count,), 0, TYPES)
    raw_two = jax.random.randint(second, (extra_count,), 0, TYPES)
    extra = (raw_one * raw_two // TYPES).astype(jnp.int32)
    block_kind = jnp.sort(jnp.concatenate([jnp.arange(TYPES, dtype=jnp.int32), extra]))
    rows = jnp.arange(CELLS, dtype=jnp.int32)
    row_kind = block_kind[rows // 128]
    group_end = 128 * jnp.sum((block_kind[None, :] <= row_kind[:, None]).astype(jnp.int32), axis=1)
    padding = jax.random.randint(third, (TYPES,), 0, 128)
    is_pad = rows >= group_end - padding[row_kind]
    order = jax.random.permutation(fourth, TYPES).astype(jnp.int32)
    return jnp.where(is_pad, -1, order[row_kind]).astype(jnp.int32)


def draw_slide_id(key, part):
    key = jax.random.fold_in(key, 12)
    first, second = jax.random.split(key, 2)
    quarter = SPOTS // 4
    size_one = jax.random.randint(first, (), quarter, SPOTS // 2 + 1)
    size_two = jax.random.randint(second, (), quarter, SPOTS - size_one - quarter + 1)
    rows = jnp.arange(SPOTS, dtype=jnp.int32)
    return ((rows >= size_one).astype(jnp.int32) + (rows >= size_one + size_two).astype(jnp.int32)).astype(jnp.int32)


def place_ends(values, stream_key, low, largest):
    longest = values.shape.index(max(values.shape))
    spots = []
    for shift in (0, 1):
        where = [jax.random.randint(jax.random.fold_in(stream_key, axis), (), 0, length) for axis, length in enumerate(values.shape)]
        where[longest] = (where[longest] + shift) % values.shape[longest]
        spots.append(tuple(where))
    return values.at[spots[0]].set(low).at[spots[1]].set(largest)


def shard_levels(own_key, dims, pieces, low, largest):
    factor_of, own = 1.0, jax.random.fold_in(own_key, 6)
    for position, parts in pieces:
        draws = jnp.exp(jax.random.uniform(jax.random.fold_in(own, position), (parts,), jnp.float32, low / len(pieces), largest / len(pieces)))
        factor_of = factor_of * jnp.repeat(draws, dims[position] // parts).reshape([-1 if axis == position else 1 for axis in range(len(dims))])
    return factor_of


def centred(stream_key, extent, deviation, most, cuts=(), kind=jnp.bfloat16):
    entries = deviation * jax.random.normal(stream_key, extent, jnp.float32)
    if cuts:
        entries = entries * shard_levels(stream_key, extent, cuts, -0.22, 0.18)
    return jnp.clip(entries, -most, most).astype(kind)


def setup_inputs(seed: int = 0) -> dict:
    key_list = jax.random.split(jax.random.key(seed), 8)
    return {
        "map_logits": centred(key_list[0], (CELLS, SPOTS), 2.0, 10.0, ((0, 16), (1, 8)), jnp.float32),
        "filter_logits": centred(key_list[1], (CELLS,), 1.0, 6.0, ((0, 16),), jnp.float32),
        "expr": jnp.clip(2.0 * jax.random.uniform(key_list[2], (GENES, CELLS), jnp.float32) ** shard_levels(key_list[2], (GENES, CELLS), ((1, 16),), -0.2, 0.2), 0.0, 2.0),
        "spatial": jnp.clip(2.0 * jax.random.uniform(key_list[3], (GENES, SPOTS), jnp.float32) ** shard_levels(key_list[3], (GENES, SPOTS), ((1, 8),), -0.2, 0.2), 0.0, 2.0),
        "cell_type": draw_cell_type(jax.random.fold_in(key_list[7], 71), 0),
        "slide_id": draw_slide_id(jax.random.fold_in(key_list[7], 71), 0),
        "spot_mask": place_ends((jax.random.randint(key_list[6], (SPOTS,), 0, 8) < 7).astype(jnp.int32), jax.random.fold_in(key_list[6], 1), 0, 1),
    }


@jax.custom_vjp
def low(v):
    return lax.optimization_barrier(v.astype(jnp.bfloat16)).astype(jnp.float32)

@jax.custom_vjp
def low_back(v):
    return v

def low_keep(v):
    return (low(v), None)

def low_pass(kept, grad):
    return (grad,)

def back_keep(v):
    return (v, None)

def back_low(kept, grad):
    return (low(grad),)
low.defvjp(low_keep, low_pass)
low_back.defvjp(back_keep, back_low)

def reference(map_logits, filter_logits, expr, spatial, cell_type, slide_id, spot_mask):
    high = lax.Precision.HIGHEST
    valid = (cell_type >= 0).astype(jnp.float32)
    spot_valid = spot_mask.astype(jnp.float32)
    slide_hot = (slide_id[None, :] == jnp.arange(SLIDES, dtype=jnp.int32)[:, None]).astype(jnp.float32)
    type_hot = (cell_type[None, :] == jnp.arange(TYPES, dtype=jnp.int32)[:, None]).astype(jnp.float32)

    def forward(logits, filt, data):
        keep = jax.nn.sigmoid(filt) * valid
        masked = jnp.where(valid[:, None] > 0, logits, -1e+30)
        top = lax.optimization_barrier(jnp.max(masked, axis=0))
        expo = jnp.exp(masked - top[None, :]) * valid[:, None]
        total = lax.optimization_barrier(jnp.sum(expo, axis=0))
        prob = expo / total[None, :]
        share = jnp.dot(type_hot, prob, precision=high)
        mass = jnp.dot(keep, prob, precision=high)
        weighted = data * keep[None, :]
        pred = jnp.dot(weighted, prob, precision=high)
        dot_g = lax.optimization_barrier(jnp.sum(pred * spatial * spot_valid[None, :], axis=1))
        aa_g = lax.optimization_barrier(jnp.sum(pred * pred * spot_valid[None, :], axis=1))
        bb_g = lax.optimization_barrier(jnp.sum(spatial * spatial * spot_valid[None, :], axis=1))
        gene_cosine_term = jnp.mean(dot_g * lax.rsqrt(aa_g * bb_g + 1e-06))
        cross_products = lax.optimization_barrier(jnp.sum(pred * spatial, axis=0))
        predicted_squares = lax.optimization_barrier(jnp.sum(pred * pred, axis=0))
        spatial_squares = lax.optimization_barrier(jnp.sum(spatial * spatial, axis=0))
        spot_cosine = cross_products * lax.rsqrt(predicted_squares * spatial_squares + 1e-06)
        nvs = jnp.sum(spot_valid)
        spot_term = jnp.sum(spot_valid * spot_cosine) / nvs
        count_k = lax.optimization_barrier(jnp.sum(slide_hot * spot_valid[None, :], axis=1))
        retained_count = lax.optimization_barrier(jnp.sum(slide_hot * (mass * spot_valid)[None, :], axis=1))
        nk = jnp.where(spot_valid > 0, lax.optimization_barrier(jnp.sum(slide_hot * count_k[:, None], axis=0)), 1.0)
        tk = jnp.where(spot_valid > 0, lax.optimization_barrier(jnp.sum(slide_hot * retained_count[:, None], axis=0)), 1.0)
        safe_mass = jnp.where(spot_valid > 0, mass, 1.0)
        density = jnp.sum(spot_valid / nk * jnp.log(tk / (nk * safe_mass))) / SLIDES
        nvalid = jnp.sum(valid)
        retained = jnp.sum(keep)
        shifted = (retained - 0.35 * nvalid) / (0.1 * CELLS)
        count_term = jnp.sqrt(shifted * shifted + 1.0)
        reg_term = jnp.sum(keep - keep * keep) / nvalid
        loss = -gene_cosine_term - spot_term + density + count_term + reg_term
        terms = jnp.stack([gene_cosine_term, spot_term, density, count_term, reg_term])
        return (loss, (terms, share))
    loss, pullback, extras = jax.vjp(forward, map_logits, filter_logits, expr, has_aux=True)
    grad_logits, grad_filt, grad_data = pullback(jnp.ones_like(loss))
    loss_terms, type_fraction = extras
    grad_map = grad_logits * (CELLS * GENES)
    grad_filter = grad_filt * CELLS
    grad_expr = grad_data * (GENES * SPOTS)
    return (loss_terms, type_fraction, grad_map, grad_filter, grad_expr)
```

```python
import functools

import jax
import jax.numpy as jnp
from jax import lax
from jax.experimental import pallas as pl
from jax.experimental.pallas import tpu as pltpu
from jax.sharding import PartitionSpec as P

TYPES = 32
SLIDES = 3
RING = 4
F32 = jnp.float32
BF16 = jnp.bfloat16


def vmem(mib):
    return pltpu.CompilerParams(vmem_limit_bytes=mib << 20)


def cost(flops, moved):
    return pl.CostEstimate(flops=int(flops), bytes_accessed=int(moved), transcendentals=0)


def shift_cells(array, dz, dx):
    pairs = [
        (z * RING + x, (z + dz) % RING * RING + (x + dx) % RING)
        for z in range(RING)
        for x in range(RING)
    ]
    return lax.ppermute(array, "cells", pairs)


def swap_cells(array, mz, mx):
    pairs = [
        (z * RING + x, (z ^ mz) * RING + (x ^ mx)) for z in range(RING) for x in range(RING)
    ]
    return lax.ppermute(array, "cells", pairs)


def shift_spots(array, dy):
    pairs = [(y * 2 + c, (y + dy) % RING * 2 + c) for y in range(RING) for c in range(2)]
    return lax.ppermute(array, "spots", pairs)


def swap_spots(array, my, mc):
    pairs = [(y * 2 + c, (y ^ my) * 2 + (c ^ mc)) for y in range(RING) for c in range(2)]
    return lax.ppermute(array, "spots", pairs)


def sum_cells(array):
    for mz, mx in ((1, 0), (3, 0), (0, 1), (0, 3)):
        array = array + swap_cells(array, mz, mx)
    return array


def sum_spots(array):
    for my, mc in ((0, 1), (1, 0), (3, 0)):
        array = array + swap_spots(array, my, mc)
    return array


def split(value):
    high = value.astype(BF16)
    return high, (value - high.astype(F32)).astype(BF16)


def product(left, right, dims):
    def one(a, b):
        return lax.dot_general(a, b, (dims, ((), ())), preferred_element_type=F32)

    return one(left[0], right[0]) + one(left[0], right[1]) + one(left[1], right[0])


def as_column(row):
    return jnp.broadcast_to(row, (128, 128)).T[:, :1]


def expo_kernel(logits, kind, filt, high, low, totals):
    step = pl.program_id(0)
    label = kind[pl.ds(step, 1), :]
    valid = (label >= 0).astype(F32)
    keep = valid * jax.nn.sigmoid(filt[pl.ds(step, 1), :])
    expo = jnp.exp(logits[...]) * as_column(valid)
    high[...], low[...] = split(expo)
    whole = jnp.sum(expo, axis=0, keepdims=True)
    kept = jnp.sum(expo * as_column(keep), axis=0, keepdims=True)
    row = lax.broadcasted_iota(jnp.int32, totals.shape, 0)
    label = jnp.max(label, axis=1, keepdims=True)
    part = jnp.where((row == label) | (row == TYPES), whole, 0.0)
    part = jnp.where(row == TYPES + 1, kept, part)

    @pl.when(step == 0)
    def _():
        totals[...] = jnp.zeros_like(totals)

    totals[...] += part


def expo_call(logits, kind, filt):
    cells, spots = logits.shape
    blocks = cells // 128
    return pl.pallas_call(
        expo_kernel,
        grid=(blocks,),
        in_specs=[
            pl.BlockSpec((128, spots), lambda i: (i, 0)),
            pl.BlockSpec((blocks, 128), lambda i: (0, 0)),
            pl.BlockSpec((blocks, 128), lambda i: (0, 0)),
        ],
        out_specs=[
            pl.BlockSpec((128, spots), lambda i: (i, 0)),
            pl.BlockSpec((128, spots), lambda i: (i, 0)),
            pl.BlockSpec((TYPES + 8, spots), lambda i: (0, 0)),
        ],
        out_shape=[
            jax.ShapeDtypeStruct((cells, spots), BF16),
            jax.ShapeDtypeStruct((cells, spots), BF16),
            jax.ShapeDtypeStruct((TYPES + 8, spots), F32),
        ],
        compiler_params=vmem(16),
        cost_estimate=cost(0, cells * spots * 8),
        name="expo",
    )(logits, kind, filt)


def pred_kernel(where, expr, keep, high, low, *outs):
    rows = expr.shape[0] * expr.shape[2]
    weighted = expr[...].reshape(rows, expr.shape[3]) * keep[...]
    part = product(split(weighted), (high[...], low[...]), ((1,), (0,)))
    for step, out in enumerate(outs):

        @pl.when(pl.program_id(0) == step)
        def _(out=out):
            out[...] = part.reshape(out.shape)


def pred_call(where, expr, keep, high, low):
    blocks, groups, rows, cells = expr.shape
    spots = high.shape[1]
    half = blocks // 2
    return pl.pallas_call(
        pred_kernel,
        grid_spec=pltpu.PrefetchScalarGridSpec(
            num_scalar_prefetch=1,
            grid=(4,),
            in_specs=[
                pl.BlockSpec((half, 1, rows, cells), lambda i, w: (w[0, i], w[1, i], 0, 0)),
                pl.BlockSpec((1, cells), lambda i, w: (0, 0)),
                pl.BlockSpec((cells, spots), lambda i, w: (0, 0)),
                pl.BlockSpec((cells, spots), lambda i, w: (0, 0)),
            ],
            out_specs=[pl.BlockSpec((half, rows, spots), lambda i, w: (0, 0, 0))] * 4,
        ),
        out_shape=[jax.ShapeDtypeStruct((half, rows, spots), F32)] * 4,
        compiler_params=vmem(32),
        cost_estimate=cost(6 * 4 * half * rows * cells * spots, 4 * cells * spots + 16 * half * rows * (cells + spots)),
        name="pred",
    )(where, expr, keep, high, low)


def back_kernel(where, pred, spatial, gene, spot, high, low, _a, _b, grad_high, grad_low, column, *outs):
    step = pl.program_id(0)
    value = pred[0]
    grad = value * (gene[0][:, 0:1] + spot[0:1, :]) - spatial[0] * (gene[0][:, 1:2] + spot[1:2, :])
    grad = grad * spot[2:3, :]
    pair = split(grad)
    grad_high[0], grad_low[0] = pair
    inner = jnp.sum((grad * value).reshape(-1, 8, grad.shape[1]), axis=0)

    @pl.when(step == 0)
    def _():
        column[...] = jnp.zeros_like(column)

    column[...] += inner
    part = product(pair, (high[...], low[...]), ((1,), (1,)))
    for index, out in enumerate(outs):

        @pl.when(step == index)
        def _(out=out):
            out[...] = part


def back_call(where, pred, spatial, gene, spot, high, low, grads):
    blocks, rows, spots = pred.shape
    cells = high.shape[0]
    count = where.shape[0]
    first = grads is None
    extra = [] if first else list(grads)
    kernel = back_kernel
    if first:

        def kernel(where, pred, spatial, gene, spot, high, low, *rest):
            back_kernel(where, pred, spatial, gene, spot, high, low, None, None, *rest)

    return pl.pallas_call(
        kernel,
        grid_spec=pltpu.PrefetchScalarGridSpec(
            num_scalar_prefetch=1,
            grid=(count,),
            in_specs=[
                pl.BlockSpec((1, rows, spots), lambda i, w: (w[i], 0, 0)),
                pl.BlockSpec((1, rows, spots), lambda i, w: (w[i], 0, 0)),
                pl.BlockSpec((1, rows, 2), lambda i, w: (w[i], 0, 0)),
                pl.BlockSpec((8, spots), lambda i, w: (0, 0)),
                pl.BlockSpec((cells, spots), lambda i, w: (0, 0)),
                pl.BlockSpec((cells, spots), lambda i, w: (0, 0)),
            ]
            + [pl.BlockSpec(memory_space=pl.ANY)] * len(extra),
            out_specs=[
                pl.BlockSpec((1, rows, spots), lambda i, w: (w[i], 0, 0)),
                pl.BlockSpec((1, rows, spots), lambda i, w: (w[i], 0, 0)),
                pl.BlockSpec((8, spots), lambda i, w: (0, 0)),
            ]
            + [pl.BlockSpec((rows, cells), lambda i, w: (0, 0))] * count,
        ),
        out_shape=[
            jax.ShapeDtypeStruct(pred.shape, BF16),
            jax.ShapeDtypeStruct(pred.shape, BF16),
            jax.ShapeDtypeStruct((8, spots), F32),
        ]
        + [jax.ShapeDtypeStruct((rows, cells), F32)] * count,
        input_output_aliases={} if first else {7: 0, 8: 1},
        compiler_params=vmem(40),
        cost_estimate=cost(6 * count * rows * cells * spots, 4 * cells * spots + count * rows * (12 * spots + 4 * cells)),
        name="back",
    )(where, pred, spatial, gene, spot, high, low, *extra)


def map_kernel(expr, grad_high, grad_low, high, low, keep, spot, out, sums, *, scale):
    step = pl.program_id(0)
    inner = product(split(expr[...]), (grad_high[...], grad_low[...]), ((0,), (0,))) + spot[0:1, :]
    expo = high[...].astype(F32) + low[...].astype(F32)
    for part in range(expr.shape[1] // 128):
        rows = slice(part * 128, part * 128 + 128)
        place = step * (expr.shape[1] // 128) + part
        weight = as_column(keep[pl.ds(place, 1), :])
        out[rows, :] = (scale * expo[rows]) * (weight * inner[rows] - spot[1:2, :])
        total = jnp.sum(expo[rows] * inner[rows], axis=1, keepdims=True)
        sums[pl.ds(place, 1), :] = jnp.broadcast_to(total, (128, 128)).T[:1, :]


def map_call(expr, grad_high, grad_low, high, low, keep, spot, scale):
    genes, cells = expr.shape
    spots = high.shape[1]
    block = 256
    return pl.pallas_call(
        functools.partial(map_kernel, scale=scale),
        grid=(cells // block,),
        in_specs=[
            pl.BlockSpec((genes, block), lambda i: (0, i)),
            pl.BlockSpec((genes, spots), lambda i: (0, 0)),
            pl.BlockSpec((genes, spots), lambda i: (0, 0)),
            pl.BlockSpec((block, spots), lambda i: (i, 0)),
            pl.BlockSpec((block, spots), lambda i: (i, 0)),
            pl.BlockSpec(keep.shape, lambda i: (0, 0)),
            pl.BlockSpec((8, spots), lambda i: (0, 0)),
        ],
        out_specs=[
            pl.BlockSpec((block, spots), lambda i: (i, 0)),
            pl.BlockSpec(keep.shape, lambda i: (0, 0)),
        ],
        out_shape=[
            jax.ShapeDtypeStruct((cells, spots), F32),
            jax.ShapeDtypeStruct(keep.shape, F32),
        ],
        compiler_params=vmem(48),
        cost_estimate=cost(6 * genes * cells * spots, 4 * genes * (cells + spots) + 8 * cells * spots),
        name="grad_map",
    )(expr, grad_high, grad_low, high, low, keep, spot)


def take(array, index, axis):
    return lax.dynamic_index_in_dim(array, index, axis, keepdims=False)


def on_device(map_logits, filter_logits, expr, spatial, cell_type, slide_id, spot_mask):
    genes, cells = expr.shape
    spots = map_logits.shape[1]
    all_cells = cells * lax.axis_size("cells")
    all_spots = spots * lax.axis_size("spots")
    place = lax.axis_index("cells")
    z, x = place // RING, place % RING
    spot_place = lax.axis_index("spots")
    y, core = spot_place // 2, spot_place % 2
    blocks = cells // 128

    valid = (cell_type >= 0).astype(F32)
    sigma = jax.nn.sigmoid(filter_logits)
    keep = sigma * valid
    spot_valid = spot_mask.astype(F32)
    kind2 = cell_type.reshape(blocks, 128)
    filt2 = filter_logits.reshape(blocks, 128)
    keep2 = keep.reshape(blocks, 128)

    high, low, totals = expo_call(map_logits, kind2, filt2)

    expr4 = expr.reshape(8, 8, 32, cells)
    keep_row = keep.reshape(1, cells)

    def ring(step):
        return (x + step) % RING, RING + (z + step) % RING

    def pred_part(halves, steps):
        a, b = zip(*[ring(step) for step in steps])
        groups = jnp.stack([a[0], a[1], b[0], b[1]]).astype(jnp.int32)
        return pred_call(
            jnp.stack([jnp.array(halves * 2, jnp.int32), groups]), expr4, keep_row, high, low
        )

    far = pred_part([0, 1], [2, 2])
    go = [(0, 1), (0, -1), (1, 0), (-1, 0)]
    first = [shift_cells(part, *way) for part, way in zip(far, go)]
    near = pred_part([1, 0], [1, -1])
    second = [shift_cells(part, *way) for part, way in zip(near, go)]
    late = pred_part([0, 1], [1, -1])
    third = [shift_cells(part + got, *way) for part, got, way in zip(late, first, go)]
    own = pred_part([0, 1], [0, 0])
    totals = sum_cells(totals)

    chunks = []
    for h in range(2):
        at = z if h == 0 else x
        group = jnp.concatenate(
            [
                own[2 * h] + third[2 * h] + second[2 * h + 1],
                own[2 * h + 1] + second[2 * h] + third[2 * h + 1],
            ]
        ).reshape(8, RING, 8, spots)
        mine = take(group, at, 1)
        for step in (1, 2, 3):
            piece = take(group, (at + step) % RING, 1)
            mine = mine + (shift_cells(piece, step, 0) if h == 0 else shift_cells(piece, 0, step))
        chunks.append(mine)

    share = 1.0 / totals[TYPES]
    type_fraction = totals[:TYPES] * share
    mass = totals[TYPES + 1] * share
    chunk = jnp.stack(chunks, axis=1) * share

    pred = jnp.zeros((8, 8, 32, spots), F32)
    groups = []
    for h in range(2):
        at = z if h == 0 else x
        piece = chunk[:, h]
        group = jnp.zeros((8, RING, 8, spots), F32)
        group = lax.dynamic_update_index_in_dim(group, piece, at, 1)
        for step in (1, 2, 3):
            got = shift_cells(piece, step, 0) if h == 0 else shift_cells(piece, 0, step)
            group = lax.dynamic_update_index_in_dim(group, got, (at - step) % RING, 1)
        groups.append(group.reshape(8, 32, spots))
    for h in range(2):
        q = x if h == 0 else z
        right, left = ((0, 1), (0, -1)) if h == 0 else ((1, 0), (-1, 0))
        group = groups[h]
        ends = group[:4], group[4:]

        def put(pred, half, part, step):
            return lax.dynamic_update_slice(
                pred, part[:, None], (4 * half, h * RING + (q + step) % RING, 0, 0)
            )

        a0 = shift_cells(ends[0], *right)
        b1 = shift_cells(ends[1], *left)
        a1 = shift_cells(ends[1], *right)
        b0 = shift_cells(ends[0], *left)
        c0 = shift_cells(a0, *right)
        c1 = shift_cells(b1, *left)
        pred = put(pred, 0, ends[0], 0)
        pred = put(pred, 1, ends[1], 0)
        for half, part, step in ((0, a0, -1), (1, a1, -1), (1, b1, 1), (0, b0, 1), (0, c0, -2), (1, c1, 2)):
            pred = put(pred, half, part, step)

    data6 = spatial.reshape(8, 2, RING, RING, 8, spots)
    data = jnp.stack([take(take(data6[:, 0], x, 1), z, 1), take(take(data6[:, 1], z, 1), x, 1)], axis=1)
    gene_part = jnp.stack(
        [
            jnp.sum(chunk * data * spot_valid, axis=3),
            jnp.sum(chunk * chunk * spot_valid, axis=3),
            jnp.sum(data * data * spot_valid, axis=3),
        ]
    )
    spot_part = jnp.concatenate(
        [jnp.sum(chunk * data, axis=(0, 1, 2)), jnp.sum(chunk * chunk, axis=(0, 1, 2))]
    )
    spatial_squares = jnp.sum(spatial * spatial, axis=0)
    step = jnp.arange(RING)
    spread = jnp.stack(
        [
            (step[:, None] == x) & (step[None, :] == z),
            (step[:, None] == z) & (step[None, :] == x),
        ]
    )
    gene_part = jnp.where(spread[None, None, :, :, :, None], gene_part[:, :, :, None, None, :], 0.0)
    cell_sums = jnp.stack([jnp.sum(valid), jnp.sum(keep), jnp.sum(keep - keep * keep)])
    payload = jnp.concatenate(
        [
            gene_part.reshape(3, genes),
            spot_part.reshape(1, genes),
            jnp.pad(cell_sums.reshape(1, 3), ((0, 0), (0, genes - 3))),
            jnp.zeros((3, genes), F32),
        ]
    )
    payload = sum_cells(payload)
    dots, squares = payload[3, :spots], payload[3, spots:]
    nvalid, retained, reg_sum = payload[4, 0], payload[4, 1], payload[4, 2]
    spot_scale = lax.rsqrt(squares * spatial_squares + 1e-06)
    slide_hot = (slide_id[None, :] == jnp.arange(SLIDES, dtype=jnp.int32)[:, None]).astype(F32)
    slide_valid = slide_hot * spot_valid[None, :]
    safe_mass = jnp.where(spot_valid > 0, mass, 1.0)
    spot_sums = jnp.concatenate(
        [
            jnp.sum(slide_valid, axis=1),
            jnp.sum(slide_valid * mass[None, :], axis=1),
            jnp.sum(slide_valid * jnp.log(safe_mass)[None, :], axis=1),
            jnp.sum(spot_valid * dots * spot_scale)[None],
        ]
    )
    payload = sum_spots(
        jnp.concatenate(
            [payload[:3], jnp.pad(spot_sums[None], ((0, 0), (0, genes - spot_sums.shape[0])))]
        )
    )
    gene_dot, gene_aa, gene_bb = payload[0], payload[1], payload[2]
    count_k, held_k, log_k = payload[3, 0:3], payload[3, 3:6], payload[3, 6:9]
    spot_total = payload[3, 9]
    nvs = jnp.sum(count_k)
    gene_scale = lax.rsqrt(gene_aa * gene_bb + 1e-06)
    gene_term = jnp.sum(gene_dot * gene_scale) / genes
    some = count_k > 0
    safe_count = jnp.where(some, count_k, 1.0)
    safe_held = jnp.where(some, held_k, 1.0)
    density = jnp.sum(jnp.where(some, jnp.log(safe_held / safe_count) - log_k / safe_count, 0.0)) / SLIDES
    nk = jnp.where(spot_valid > 0, jnp.sum(slide_hot * count_k[:, None], axis=0), 1.0)
    tk = jnp.where(spot_valid > 0, jnp.sum(slide_hot * held_k[:, None], axis=0), 1.0)
    grad_mass = spot_valid / SLIDES * (1.0 / tk - 1.0 / (nk * safe_mass))
    gene_coef = jnp.stack(
        [gene_dot * gene_scale**3 * gene_bb / genes, gene_scale / genes], axis=1
    ).reshape(8, genes // 8, 2)
    spot_coef = jnp.concatenate(
        [
            jnp.stack(
                [dots * spot_scale**3 * spatial_squares / nvs, spot_scale / nvs, spot_valid * share]
            ),
            jnp.zeros((5, spots), F32),
        ]
    )

    pred3 = pred.reshape(8, genes // 8, spots)
    spatial3 = spatial.reshape(8, genes // 8, spots)

    def back_part(steps, grads):
        where = []
        for step in steps:
            chip = (y + step) % RING
            where += [chip * 2 + 1 - core, chip * 2 + core]
        return back_call(
            jnp.stack(where).astype(jnp.int32), pred3, spatial3, gene_coef, spot_coef, high, low, grads
        )

    def both_cores(parts):
        return parts[1] + swap_spots(parts[0], 0, 1)

    rows = genes // 16
    gh, gl, column_a, *part = back_part([2], None)
    far = both_cores(part)
    first = shift_spots(far[:rows], 1), shift_spots(far[rows:], -1)
    gh, gl, column_b, *part = back_part([1, -1], (gh, gl))
    up, down = both_cores(part[:2]), both_cores(part[2:])
    second = shift_spots(up[rows:], 1), shift_spots(down[:rows], -1)
    third = shift_spots(up[:rows] + first[0], 1), shift_spots(down[rows:] + first[1], -1)
    gh, gl, column_c, *part = back_part([0], (gh, gl))
    own = both_cores(part)
    grad_weighted = jnp.concatenate(
        [own[:rows] + third[0] + second[1], own[rows:] + second[0] + third[1]]
    )
    grad_expr = grad_weighted * (keep * (genes * all_spots))[None, :]

    column = jnp.sum(column_a + column_b + column_c, axis=0) + grad_mass * mass * share
    spot_rows = jnp.concatenate(
        [jnp.stack([grad_mass * share, column]), jnp.zeros((6, spots), F32)]
    )
    grad_map, sums = map_call(
        expr, gh.reshape(genes, spots), gl.reshape(genes, spots), high, low, keep2, spot_rows, all_cells * genes
    )
    filter_sum = sum_spots(sums).reshape(cells)

    shifted = (retained - 0.35 * nvalid) / (0.1 * all_cells)
    count_term = jnp.sqrt(shifted * shifted + 1.0)
    grad_keep = filter_sum + shifted / count_term / (0.1 * all_cells) + (1.0 - 2.0 * keep) / nvalid
    grad_filter = valid * sigma * (1.0 - sigma) * grad_keep * all_cells
    loss_terms = jnp.stack([gene_term, spot_total / nvs, density, count_term, reg_sum / nvalid])
    return (loss_terms, type_fraction, grad_map, grad_filter, grad_expr)


def solution(mesh):
    in_specs = (
        P("cells", "spots"),
        P("cells"),
        P(None, "cells"),
        P(None, "spots"),
        P("cells"),
        P("spots"),
        P("spots"),
    )
    out_specs = (P(), P(None, "spots"), P("cells", "spots"), P("cells"), P("spots", "cells"))
    return jax.shard_map(
        on_device, mesh=mesh, in_specs=in_specs, out_specs=out_specs, check_vma=False
    )
```

```python
import functools

import jax
import jax.numpy as jnp
from jax import lax
from jax.experimental import pallas as pl
from jax.experimental.pallas import tpu as pltpu
from jax.sharding import PartitionSpec as P

TYPES = 32
SLIDES = 3
RING = 4
GRANT = 58
F32 = jnp.float32
BF16 = jnp.bfloat16


def vmem(mib):
    return pltpu.CompilerParams(vmem_limit_bytes=mib << 20)


def cost(flops, moved):
    return pl.CostEstimate(flops=int(flops) // 8, bytes_accessed=int(moved) // 8, transcendentals=0)


NO_COST = pl.CostEstimate(flops=0, bytes_accessed=0, transcendentals=0)


def route(target):
    def flat(z, x, y, core):
        return ((z % RING * RING + x % RING) * RING + y % RING) * 2 + core

    return [
        (flat(z, x, y, core), flat(*target(z, x, y, core)))
        for z in range(RING)
        for x in range(RING)
        for y in range(RING)
        for core in range(2)
    ]


def send(array, target):
    return lax.ppermute(array, ("cells", "spots"), route(target))


def along(array, step):
    return send(array, lambda z, x, y, c: (z, x + step, y, c) if c == 0 else (z + step, x, y, c))


def across(array, step):
    return send(array, lambda z, x, y, c: (z + step, x, y, c) if c == 0 else (z, x + step, y, c))


def up(array, step):
    return send(array, lambda z, x, y, c: (z, x, y + step, c))


def swap(array, mz, mx, my, mc):
    return send(array, lambda z, x, y, c: (z ^ mz, x ^ mx, y ^ my, c ^ mc))


def sum_spots(array):
    for my, mc in ((0, 1), (1, 0), (3, 0)):
        array = array + swap(array, 0, 0, my, mc)
    return array


def after(value, *others):
    return lax.optimization_barrier((value, *others))[0]


def split(value):
    high = value.astype(BF16)
    return high, (value - high.astype(F32)).astype(BF16)


def product(left, right, dims):
    def one(a, b):
        return lax.dot_general(a, b, (dims, ((), ())), preferred_element_type=F32)

    return one(left[0], right[0]) + one(left[0], right[1]) + one(left[1], right[0])


def as_column(row):
    return jnp.broadcast_to(row, (128, 128)).T[:, :1]


def expo_kernel(logits, kind, filt, high, low, totals):
    step = pl.program_id(0)
    label = kind[pl.ds(step, 1), :]
    valid = (label >= 0).astype(F32)
    keep = valid * jax.nn.sigmoid(filt[pl.ds(step, 1), :])
    expo = jnp.exp(logits[...]) * as_column(valid)
    high[...], low[...] = split(expo)
    whole = jnp.sum(expo, axis=0, keepdims=True)
    kept = jnp.sum(expo * as_column(keep), axis=0, keepdims=True)
    row = lax.broadcasted_iota(jnp.int32, totals.shape, 0)
    label = jnp.max(label, axis=1, keepdims=True)
    part = jnp.where((row == label) | (row == TYPES), whole, 0.0)
    part = jnp.where(row == TYPES + 1, kept, part)

    @pl.when(step == 0)
    def _():
        totals[...] = jnp.zeros_like(totals)

    totals[...] += part


def expo_call(logits, kind, filt):
    cells, spots = logits.shape
    blocks = cells // 128
    return pl.pallas_call(
        expo_kernel,
        grid=(blocks,),
        in_specs=[
            pl.BlockSpec((128, spots), lambda i: (i, 0)),
            pl.BlockSpec((blocks, 128), lambda i: (0, 0)),
            pl.BlockSpec((blocks, 128), lambda i: (0, 0)),
        ],
        out_specs=[
            pl.BlockSpec((128, spots), lambda i: (i, 0)),
            pl.BlockSpec((128, spots), lambda i: (i, 0)),
            pl.BlockSpec((TYPES + 8, spots), lambda i: (0, 0)),
        ],
        out_shape=[
            jax.ShapeDtypeStruct((cells, spots), BF16),
            jax.ShapeDtypeStruct((cells, spots), BF16),
            jax.ShapeDtypeStruct((TYPES + 8, spots), F32),
        ],
        compiler_params=vmem(GRANT),
        cost_estimate=cost(0, cells * spots * 8),
        name="expo",
    )(logits, kind, filt)


def pred_kernel(where, expr_a, expr_b, keep, high, low, *outs):
    rows = 2 * expr_a.shape[0] * expr_a.shape[2]
    weighted = jnp.concatenate(
        [part[...].reshape(rows // 2, keep.shape[1]) for part in (expr_a, expr_b)]
    )
    part = product(split(weighted * keep[...]), (high[...], low[...]), ((1,), (0,)))
    for step, out in enumerate(outs):

        @pl.when(pl.program_id(0) == step)
        def _(out=out):
            out[...] = part.reshape(out.shape)


def pred_call(where, expr, keep, high, low):
    blocks, groups, rows, cells = expr.shape
    spots = high.shape[1]
    return pl.pallas_call(
        pred_kernel,
        grid_spec=pltpu.PrefetchScalarGridSpec(
            num_scalar_prefetch=1,
            grid=(2,),
            in_specs=[
                pl.BlockSpec((blocks, 1, rows, cells), lambda i, w: (0, w[i, 0], 0, 0)),
                pl.BlockSpec((blocks, 1, rows, cells), lambda i, w: (0, w[i, 1], 0, 0)),
                pl.BlockSpec((1, cells), lambda i, w: (0, 0)),
                pl.BlockSpec((cells, spots), lambda i, w: (0, 0)),
                pl.BlockSpec((cells, spots), lambda i, w: (0, 0)),
            ],
            out_specs=[pl.BlockSpec((2, blocks, rows, spots), lambda i, w: (0, 0, 0, 0))] * 2,
        ),
        out_shape=[jax.ShapeDtypeStruct((2, blocks, rows, spots), F32)] * 2,
        compiler_params=vmem(GRANT),
        cost_estimate=cost(24 * blocks * rows * cells * spots, 4 * cells * spots + 16 * blocks * rows * (cells + spots)),
        name="pred",
    )(where, expr, expr, keep, high, low)


def stats_kernel(where, piece, spatial, spot, cell_sums, out):
    rows = piece.shape[0] * piece.shape[1]
    value = piece[...].reshape(rows, piece.shape[2]) * spot[0:1, :]
    data = spatial[...].reshape(value.shape)
    valid = spot[1:2, :]
    cross, square = value * data, value * value
    lane = lax.broadcasted_iota(jnp.int32, (rows, 128), 1)
    gene = jnp.zeros((rows, 128), F32)
    for index, part in enumerate((cross, square, data * data)):
        gene = jnp.where(lane == index, jnp.sum(part * valid, axis=1, keepdims=True), gene)
    gene = gene.T
    out[...] = jnp.zeros_like(out)
    for index in range(3):
        out[pl.ds(16 * index + where[0], 1), :] = gene[index : index + 1, :]
    for index, part in enumerate((cross, square)):
        total = jnp.sum(part, axis=0, keepdims=True)
        for k in range(total.shape[1] // 128):
            out[48 + 8 * index + k : 49 + 8 * index + k, :] = total[:, 128 * k : 128 * k + 128]
    out[64:65, :] = cell_sums[...]


def stats_call(where, piece, spatial, spot, cell_sums):
    blocks, rows, spots = piece.shape
    return pl.pallas_call(
        stats_kernel,
        grid_spec=pltpu.PrefetchScalarGridSpec(
            num_scalar_prefetch=1,
            grid=(1,),
            in_specs=[
                pl.BlockSpec((blocks, rows, spots), lambda i, w: (0, 0, 0)),
                pl.BlockSpec((blocks, 1, rows, spots), lambda i, w: (0, w[0], 0, 0)),
                pl.BlockSpec((8, spots), lambda i, w: (0, 0)),
                pl.BlockSpec((1, 128), lambda i, w: (0, 0)),
            ],
            out_specs=pl.BlockSpec((72, 128), lambda i, w: (0, 0)),
        ),
        out_shape=jax.ShapeDtypeStruct((72, 128), F32),
        compiler_params=vmem(GRANT),
        cost_estimate=cost(0, 8 * blocks * rows * spots),
        name="stats",
    )(where, piece, spatial, spot, cell_sums)


def back_kernel(where, place, *refs, count, aliased):
    pred, (spatial, gene, spot, high, low, expr), refs = refs[:8], refs[8:14], refs[14 + 2 * aliased :]
    grad_high, grad_low, column, sums, *outs = refs
    step = pl.program_id(0)
    inner = jnp.zeros(column.shape, F32)
    for index, part in enumerate(pred):
        for sub in range(2):
            value = part[sub, 0] * spot[3:4, :]
            rows = value.shape[0]
            at = pl.ds(pl.multiple_of(place[2 * index + sub] * rows, rows), rows)
            coef = gene[0, at, :]
            grad = value * (coef[:, 0:1] + spot[0:1, :])
            grad = grad - spatial[0, at, :] * (coef[:, 1:2] + spot[1:2, :])
            grad = grad * spot[2:3, :]
            grad_high[0, at, :], grad_low[0, at, :] = split(grad)
            inner += jnp.sum((grad * value).reshape(-1, 8, grad.shape[1]), axis=0)

    @pl.when(step == 0)
    def _():
        column[...] = jnp.zeros_like(column)
        if aliased:
            sums[...] = jnp.zeros_like(sums)
        else:
            sums[...] = product(split(spot[8:16, :]), (high[...], low[...]), ((1,), (1,)))

    column[...] += inner
    part = product((grad_high[0], grad_low[0]), (high[...], low[...]), ((1,), (1,)))
    sums[...] += jnp.sum((part * expr[...]).reshape(-1, 8, part.shape[1]), axis=0)
    for index, out in enumerate(outs):

        @pl.when(step == index)
        def _(out=out):
            out[...] = part


def back_call(where, place, pred, spatial, gene, spot, high, low, expr, grads):
    blocks, rows, spots = spatial.shape
    cells = high.shape[0]
    count = where.shape[0]
    extra = list(grads)
    piece = pred[0].shape[2]
    return pl.pallas_call(
        functools.partial(back_kernel, count=count, aliased=len(extra) // 2),
        grid_spec=pltpu.PrefetchScalarGridSpec(
            num_scalar_prefetch=2,
            grid=(count,),
            in_specs=[pl.BlockSpec((2, 1, piece, spots), lambda i, w, p: (0, w[i], 0, 0))] * 8
            + [
                pl.BlockSpec((1, rows, spots), lambda i, w, p: (w[i], 0, 0)),
                pl.BlockSpec((1, rows, 2), lambda i, w, p: (w[i], 0, 0)),
                pl.BlockSpec((16, spots), lambda i, w, p: (0, 0)),
                pl.BlockSpec((cells, spots), lambda i, w, p: (0, 0)),
                pl.BlockSpec((cells, spots), lambda i, w, p: (0, 0)),
                pl.BlockSpec((rows, cells), lambda i, w, p: (w[i], 0)),
            ]
            + [pl.BlockSpec(memory_space=pl.ANY)] * len(extra),
            out_specs=[
                pl.BlockSpec((1, rows, spots), lambda i, w, p: (w[i], 0, 0)),
                pl.BlockSpec((1, rows, spots), lambda i, w, p: (w[i], 0, 0)),
                pl.BlockSpec((8, spots), lambda i, w, p: (0, 0)),
                pl.BlockSpec((8, cells), lambda i, w, p: (0, 0)),
            ]
            + [pl.BlockSpec((rows, cells), lambda i, w, p: (0, 0))] * count,
        ),
        out_shape=[
            jax.ShapeDtypeStruct(spatial.shape, BF16),
            jax.ShapeDtypeStruct(spatial.shape, BF16),
            jax.ShapeDtypeStruct((8, spots), F32),
            jax.ShapeDtypeStruct((8, cells), F32),
        ]
        + [jax.ShapeDtypeStruct((rows, cells), F32)] * count,
        input_output_aliases={16: 0, 17: 1} if extra else {},
        compiler_params=vmem(GRANT),
        cost_estimate=NO_COST,
        name="back",
    )(where, place, *pred, spatial, gene, spot, high, low, expr, *extra)


def map_kernel(expr, grad_high, grad_low, high, low, keep, spot, out, *, scale):
    step = pl.program_id(0)
    inner = product(split(expr[...]), (grad_high[...], grad_low[...]), ((0,), (0,))) + spot[0:1, :]
    expo = high[...].astype(F32) + low[...].astype(F32)
    for part in range(expr.shape[1] // 128):
        rows = slice(part * 128, part * 128 + 128)
        place = step * (expr.shape[1] // 128) + part
        weight = as_column(keep[pl.ds(place, 1), :])
        out[rows, :] = (scale * expo[rows]) * (weight * inner[rows] - spot[1:2, :])


def map_call(expr, grad_high, grad_low, high, low, keep, spot, scale):
    genes, cells = expr.shape
    spots = high.shape[1]
    block = 256
    return pl.pallas_call(
        functools.partial(map_kernel, scale=scale),
        grid=(cells // block,),
        in_specs=[
            pl.BlockSpec((genes, block), lambda i: (0, i)),
            pl.BlockSpec((genes, spots), lambda i: (0, 0)),
            pl.BlockSpec((genes, spots), lambda i: (0, 0)),
            pl.BlockSpec((block, spots), lambda i: (i, 0)),
            pl.BlockSpec((block, spots), lambda i: (i, 0)),
            pl.BlockSpec(keep.shape, lambda i: (0, 0)),
            pl.BlockSpec((8, spots), lambda i: (0, 0)),
        ],
        out_specs=pl.BlockSpec((block, spots), lambda i: (i, 0)),
        out_shape=jax.ShapeDtypeStruct((cells, spots), F32),
        compiler_params=vmem(GRANT),
        cost_estimate=NO_COST,
        name="grad_map",
    )(expr, grad_high, grad_low, high, low, keep, spot)


def on_device(map_logits, filter_logits, expr, spatial, cell_type, slide_id, spot_mask):
    genes, cells = expr.shape
    spots = map_logits.shape[1]
    all_cells = cells * lax.axis_size("cells")
    all_spots = spots * lax.axis_size("spots")
    cell_place = lax.axis_index("cells")
    z, x = cell_place >> 2, cell_place & 3
    spot_place = lax.axis_index("spots")
    y, core = spot_place >> 1, spot_place & 1
    first = jnp.where(core == 0, x, z)
    second = jnp.where(core == 0, z, x)
    blocks = cells // 128

    valid = (cell_type >= 0).astype(F32)
    sigma = jax.nn.sigmoid(filter_logits)
    keep = sigma * valid
    spot_valid = spot_mask.astype(F32)
    kind2 = cell_type.reshape(blocks, 128)
    filt2 = filter_logits.reshape(blocks, 128)
    keep2 = keep.reshape(blocks, 128)

    high, low, totals = expo_call(map_logits, kind2, filt2)

    expr4 = expr.reshape(8, 16, 16, cells)
    keep_row = keep.reshape(1, cells)

    def group(step, half):
        q = ((first + step) & 3) * RING
        return [q + ((second + 2 * half) & 3), q + ((second + 2 * half + 1) & 3)]

    def pred_part(one, two, *others):
        where = jnp.stack(group(*one) + group(*two)).astype(jnp.int32).reshape(2, 2)
        return pred_call(after(where, *others), expr4, keep_row, high, low)

    far = pred_part((2, 0), (2, 1))
    far_right, far_left = along(far[0], 1), along(far[1], -1)
    totals = totals + swap(after(totals, *far), 1, 0, 0, 0)
    near = pred_part((1, 1), (-1, 0), *far)
    near_right, near_left = along(near[0], 1), along(near[1], -1)
    late = pred_part((1, 0), (-1, 1), totals, *near)
    late = [late[0] + far_right, late[1] + far_left]
    late_right, late_left = along(late[0], 1), along(late[1], -1)
    totals = totals + swap(after(totals, *late), 3, 0, 0, 0)
    own = pred_part((0, 0), (0, 1), totals, *late, near_right, near_left)
    totals = totals + swap(after(totals, near_right, near_left), 0, 1, 0, 0)
    own = after(tuple(own), totals)
    half0 = own[0] + late_right + near_left
    half1 = own[1] + near_right + late_left
    pieces = [across(half0[1], 1), across(half1[0], 2), across(half1[1], 3)]
    totals = totals + swap(after(totals, half0, half1), 0, 3, 0, 0)
    spatial_squares = jnp.sum(spatial * spatial, axis=0)
    piece = after(half0[0] + pieces[0] + pieces[1] + pieces[2], totals)

    got = [across(piece, step) for step in (1, 2, 3)]
    mine = jnp.stack([piece, got[2]]), jnp.stack([got[1], got[0]])
    right0, left1 = along(mine[0], 1), along(mine[1], -1)
    right1, left0 = along(mine[1], 1), along(mine[0], -1)
    far0, far1 = along(right0, 1), along(left1, -1)
    pred = [*mine, right0, right1, left0, left1, far0, far1]
    order = [
        ((first + step) & 3) * RING + ((second + 2 * half + sub) & 3)
        for step, half in ((0, 0), (0, 1), (-1, 0), (-1, 1), (1, 0), (1, 1), (2, 0), (2, 1))
        for sub in range(2)
    ]
    order = jnp.stack(order).astype(jnp.int32)

    share = 1.0 / totals[TYPES]
    type_fraction = totals[:TYPES] * share
    mass = totals[TYPES + 1] * share
    cell_sums = jnp.stack([jnp.sum(valid), jnp.sum(keep), jnp.sum(keep - keep * keep)])
    payload = stats_call(
        (first * RING + second).astype(jnp.int32)[None],
        piece,
        spatial.reshape(8, 16, 16, spots),
        jnp.concatenate([jnp.stack([share, spot_valid]), jnp.zeros((6, spots), F32)]),
        jnp.pad(cell_sums[None], ((0, 0), (0, 125))),
    )
    payload = payload + swap(payload, 1, 0, 0, 0)
    payload = after(payload, *mine)
    payload = payload + swap(payload, 3, 0, 0, 0)
    payload = payload + swap(payload, 0, 1, 0, 0)
    payload = payload + swap(payload, 0, 3, 0, 0)
    payload = after(payload, right0, left1)
    dots, squares = payload[48:56].reshape(spots), payload[56:64].reshape(spots)
    nvalid, retained, reg_sum = payload[64, 0], payload[64, 1], payload[64, 2]
    spot_scale = lax.rsqrt(squares * spatial_squares + 1e-06)
    slide_hot = (slide_id[None, :] == jnp.arange(SLIDES, dtype=jnp.int32)[:, None]).astype(F32)
    slide_valid = slide_hot * spot_valid[None, :]
    safe_mass = jnp.where(spot_valid > 0, mass, 1.0)
    spot_sums = jnp.concatenate(
        [
            jnp.sum(slide_valid, axis=1),
            jnp.sum(slide_valid * mass[None, :], axis=1),
            jnp.sum(slide_valid * jnp.log(safe_mass)[None, :], axis=1),
            jnp.sum(spot_valid * dots * spot_scale)[None],
        ]
    )
    payload = jnp.concatenate([payload[:48], jnp.pad(spot_sums[None], ((0, 7), (0, 118)))])
    payload = payload + swap(payload, 0, 0, 0, 1)
    payload = payload + swap(payload, 0, 0, 1, 0)
    payload = payload + swap(payload, 0, 0, 3, 0)
    gene_dot, gene_aa, gene_bb = payload[0:16], payload[16:32], payload[32:48]
    count_k, held_k, log_k = payload[48, 0:3], payload[48, 3:6], payload[48, 6:9]
    spot_total = payload[48, 9]
    nvs = jnp.sum(count_k)
    gene_scale = lax.rsqrt(gene_aa * gene_bb + 1e-06)
    gene_term = jnp.sum(gene_dot * gene_scale) / genes
    some = count_k > 0
    safe_count = jnp.where(some, count_k, 1.0)
    safe_held = jnp.where(some, held_k, 1.0)
    density = jnp.sum(jnp.where(some, jnp.log(safe_held / safe_count) - log_k / safe_count, 0.0)) / SLIDES
    nk = jnp.where(spot_valid > 0, jnp.sum(slide_hot * count_k[:, None], axis=0), 1.0)
    tk = jnp.where(spot_valid > 0, jnp.sum(slide_hot * held_k[:, None], axis=0), 1.0)
    grad_mass = spot_valid / SLIDES * (1.0 / tk - 1.0 / (nk * safe_mass))
    gene_coef = jnp.stack([gene_dot * gene_scale**3 * gene_bb / genes, gene_scale / genes])
    gene_coef = gene_coef.reshape(2, 16, 8, 16).transpose(2, 1, 3, 0).reshape(8, genes // 8, 2)
    spot_coef = jnp.concatenate(
        [
            jnp.stack(
                [
                    dots * spot_scale**3 * spatial_squares / nvs,
                    spot_scale / nvs,
                    spot_valid * share,
                    share,
                ]
            ),
            jnp.zeros((4, spots), F32),
            (grad_mass * share)[None],
            jnp.zeros((7, spots), F32),
        ]
    )

    spatial3 = spatial.reshape(8, genes // 8, spots)

    def back_part(steps, grads, *others):
        where = [((y + step) & 3) * 2 + (core ^ other) for step, other in steps]
        where = after(jnp.stack(where).astype(jnp.int32), *others)
        return back_call(where, order, pred, spatial3, gene_coef, spot_coef, high, low, expr, grads)

    rows = genes // 16
    *grads, column_a, sums_a, far_a = back_part([(2, 1)], ())
    far_got = swap(far_a, 0, 0, 0, 1)
    *grads, column_b, sums_b, far_b = back_part([(2, 0)], grads)
    far = far_b + far_got
    far_up, far_down = up(far[:rows], 1), up(far[rows:], -1)
    *grads, column_c, sums_c, up_a, down_a = back_part([(1, 1), (-1, 1)], grads, far)
    up_got, down_got = swap(up_a, 0, 0, 0, 1), swap(down_a, 0, 0, 0, 1)
    *grads, column_d, sums_d, up_b, down_b = back_part([(1, 0), (-1, 0)], grads)
    above = jnp.concatenate([up_b[:rows] + up_got[:rows] + far_up, up_b[rows:] + up_got[rows:]])
    below = jnp.concatenate([down_b[:rows] + down_got[:rows], down_b[rows:] + down_got[rows:] + far_down])
    near_up, near_down = up(above, 1), up(below, -1)
    *grads, column_e, sums_e, own_a, own_b = back_part([(0, 1), (0, 0)], grads, above, below)
    own_a = jnp.concatenate([swap(own_a[:rows], 0, 0, 0, 1), swap(own_a[rows:], 0, 0, 0, 1)])
    filter_sum = sum_spots(jnp.sum(sums_a + sums_b + sums_c + sums_d + sums_e, axis=0).reshape(blocks, 128)).reshape(cells)

    column = jnp.sum(column_a + column_b + column_c + column_d + column_e, axis=0) + grad_mass * mass * share
    spot_rows = jnp.concatenate(
        [jnp.stack([grad_mass * share, column]), jnp.zeros((6, spots), F32)]
    )
    grad_map = map_call(
        expr,
        grads[0].reshape(genes, spots),
        grads[1].reshape(genes, spots),
        high,
        low,
        keep2,
        after(spot_rows, own_a),
        all_cells * genes,
    )
    grad_weighted = after(own_b, grad_map) + own_a + near_up + near_down
    grad_expr = grad_weighted * (keep * (genes * all_spots))[None, :]

    shifted = (retained - 0.35 * nvalid) / (0.1 * all_cells)
    count_term = jnp.sqrt(shifted * shifted + 1.0)
    grad_keep = filter_sum + shifted / count_term / (0.1 * all_cells) + (1.0 - 2.0 * keep) / nvalid
    grad_filter = valid * sigma * (1.0 - sigma) * grad_keep * all_cells
    loss_terms = jnp.stack([gene_term, spot_total / nvs, density, count_term, reg_sum / nvalid])
    return (loss_terms, type_fraction, grad_map, grad_filter, grad_expr)


def solution(mesh):
    in_specs = (
        P("cells", "spots"),
        P("cells"),
        P(None, "cells"),
        P(None, "spots"),
        P("cells"),
        P("spots"),
        P("spots"),
    )
    out_specs = (P(), P(None, "spots"), P("cells", "spots"), P("cells"), P("spots", "cells"))
    return jax.shard_map(
        on_device, mesh=mesh, in_specs=in_specs, out_specs=out_specs, check_vma=False
    )
```

```python
import functools

import jax
import jax.numpy as jnp
from jax import lax
from jax.experimental import pallas as pl
from jax.experimental.pallas import tpu as pltpu
from jax.sharding import PartitionSpec as P

TYPES = 32
SLIDES = 3
RING = 4
F32 = jnp.float32
BF16 = jnp.bfloat16


def vmem(mib):
    return pltpu.CompilerParams(vmem_limit_bytes=mib << 20)


def fixed(shape):
    return pl.BlockSpec(shape, lambda *_: (0,) * len(shape), pipeline_mode=pl.Buffered(1))


def cost(flops, moved):
    return pl.CostEstimate(flops=int(flops) // 8, bytes_accessed=int(moved) // 8, transcendentals=0)


NO_COST = pl.CostEstimate(flops=0, bytes_accessed=0, transcendentals=0)


def route(target):
    def flat(z, x, y, core):
        return ((z % RING * RING + x % RING) * RING + y % RING) * 2 + core

    return [
        (flat(z, x, y, core), flat(*target(z, x, y, core)))
        for z in range(RING)
        for x in range(RING)
        for y in range(RING)
        for core in range(2)
    ]


def send(array, target):
    return lax.ppermute(array, ("cells", "spots"), route(target))


def along(array, step):
    return send(array, lambda z, x, y, c: (z, x + step, y, c) if c == 0 else (z + step, x, y, c))


def across(array, step):
    return send(array, lambda z, x, y, c: (z + step, x, y, c) if c == 0 else (z, x + step, y, c))


def up(array, step):
    return send(array, lambda z, x, y, c: (z, x, y + step, c))


def swap(array, mz, mx, my, mc):
    return send(array, lambda z, x, y, c: (z ^ mz, x ^ mx, y ^ my, c ^ mc))


def after(value, *others):
    return lax.optimization_barrier((value, *others))[0]


def split(value):
    high = value.astype(BF16)
    return high, (value - high.astype(F32)).astype(BF16)


def product(left, right, dims):
    def one(a, b):
        return lax.dot_general(a, b, (dims, ((), ())), preferred_element_type=F32)

    return one(left[0], right[0]) + one(left[0], right[1]) + one(left[1], right[0])


def as_column(row):
    return jnp.broadcast_to(row, (128, 128)).T[:, :1]


def expo_kernel(logits, kind, filt, high, low, types, totals):
    step = pl.program_id(0)
    count = logits.shape[0] // 128

    @pl.when(step == 0)
    def _():
        types[...] = jnp.zeros_like(types)
        totals[...] = jnp.zeros_like(totals)

    for part in range(count):
        rows = slice(part * 128, part * 128 + 128)
        label = kind[pl.ds(step * count + part, 1), :]
        valid = (label >= 0).astype(F32)
        keep = valid * jax.nn.sigmoid(filt[pl.ds(step * count + part, 1), :])
        expo = jnp.exp(logits[rows]) * as_column(valid)
        high[rows], low[rows] = split(expo)
        whole = jnp.sum(expo, axis=0, keepdims=True)
        kept = jnp.sum(expo * as_column(keep), axis=0, keepdims=True)
        row = lax.broadcasted_iota(jnp.int32, types.shape, 0)
        types[...] += jnp.where(row == jnp.max(label, axis=1, keepdims=True), whole, 0.0)
        row = lax.broadcasted_iota(jnp.int32, totals.shape, 0)
        totals[...] += jnp.where(row == 0, whole, jnp.where(row == 1, kept, 0.0))


def expo_call(logits, kind, filt):
    cells, spots = logits.shape
    block = cells // 2
    return pl.pallas_call(
        expo_kernel,
        grid=(2,),
        in_specs=[
            pl.BlockSpec((block, spots), lambda i: (i, 0)),
            fixed(kind.shape),
            fixed(filt.shape),
        ],
        out_specs=[
            pl.BlockSpec((block, spots), lambda i: (i, 0)),
            pl.BlockSpec((block, spots), lambda i: (i, 0)),
            fixed((TYPES, spots)),
            fixed((8, spots)),
        ],
        out_shape=[
            jax.ShapeDtypeStruct((cells, spots), BF16),
            jax.ShapeDtypeStruct((cells, spots), BF16),
            jax.ShapeDtypeStruct((TYPES, spots), F32),
            jax.ShapeDtypeStruct((8, spots), F32),
        ],
        compiler_params=vmem(50),
        cost_estimate=cost(0, cells * spots * 8),
        name="expo",
    )(logits, kind, filt)


def pred_kernel(where, expr_a, expr_b, keep, high, low, *outs):
    rows = 2 * expr_a.shape[0] * expr_a.shape[2]
    weighted = jnp.concatenate(
        [part[...].reshape(rows // 2, keep.shape[1]) for part in (expr_a, expr_b)]
    )
    part = product(split(weighted * keep[...]), (high[...], low[...]), ((1,), (0,)))
    for step, out in enumerate(outs):

        @pl.when(pl.program_id(0) == step)
        def _(out=out):
            out[...] = part.reshape(out.shape)


def pred_call(where, expr, keep, high, low):
    blocks, groups, rows, cells = expr.shape
    spots = high.shape[1]
    return pl.pallas_call(
        pred_kernel,
        grid_spec=pltpu.PrefetchScalarGridSpec(
            num_scalar_prefetch=1,
            grid=(2,),
            in_specs=[
                pl.BlockSpec((blocks, 1, rows, cells), lambda i, w: (0, w[i, 0], 0, 0)),
                pl.BlockSpec((blocks, 1, rows, cells), lambda i, w: (0, w[i, 1], 0, 0)),
                fixed((1, cells)),
                fixed((cells, spots)),
                fixed((cells, spots)),
            ],
            out_specs=[fixed((2, blocks, rows, spots))] * 2,
        ),
        out_shape=[jax.ShapeDtypeStruct((2, blocks, rows, spots), F32)] * 2,
        compiler_params=vmem(50),
        cost_estimate=cost(24 * blocks * rows * cells * spots, 4 * cells * spots + 16 * blocks * rows * (cells + spots)),
        name="pred",
    )(where, expr, expr, keep, high, low)


def stats_kernel(where, piece, spatial, spot, gene, part):
    rows = piece.shape[0] * piece.shape[1]
    valid, share, mass, slide = (spot[k : k + 1, :] for k in range(4))
    value = piece[...].reshape(rows, piece.shape[2]) * share
    data = spatial[...].reshape(value.shape)
    cross, square = value * data, value * value
    lane = lax.broadcasted_iota(jnp.int32, (rows, 128), 1)
    sums = jnp.zeros((rows, 128), F32)
    for index, one in enumerate((cross, square, data * data)):
        sums = jnp.where(lane == index, jnp.sum(one * valid, axis=1, keepdims=True), sums)
    sums = sums.T
    gene[...] = jnp.zeros_like(gene)
    for index in range(3):
        gene[pl.ds(16 * index + where[0], 1), :] = sums[index : index + 1, :]
    lane = lax.broadcasted_iota(jnp.int32, (1, 128), 1)
    slides = jnp.zeros((1, 128), F32)
    logs = jnp.log(jnp.where(valid > 0, mass, 1.0))
    for k in range(SLIDES):
        inside = jnp.where(slide == k, valid, 0.0)
        for index, one in enumerate((inside, inside * mass, inside * logs)):
            total = jnp.sum(one, axis=1, keepdims=True)
            slides = jnp.where(lane == 3 * index + k, total, slides)
    gene[48:49, :] = slides
    for index, one in enumerate((cross, square)):
        total = jnp.sum(one, axis=0, keepdims=True)
        for k in range(total.shape[1] // 128):
            part[8 * index + k : 8 * index + k + 1, :] = total[:, 128 * k : 128 * k + 128]


def stats_call(where, piece, spatial, spot):
    blocks, rows, spots = piece.shape
    return pl.pallas_call(
        stats_kernel,
        grid_spec=pltpu.PrefetchScalarGridSpec(
            num_scalar_prefetch=1,
            grid=(1,),
            in_specs=[
                fixed((blocks, rows, spots)),
                pl.BlockSpec((blocks, 1, rows, spots), lambda i, w: (0, w[0], 0, 0)),
                fixed((8, spots)),
            ],
            out_specs=[fixed((56, 128)), fixed((16, 128))],
        ),
        out_shape=[jax.ShapeDtypeStruct((56, 128), F32), jax.ShapeDtypeStruct((16, 128), F32)],
        compiler_params=vmem(50),
        cost_estimate=NO_COST,
        name="stats",
    )(where, piece, spatial, spot)


def coef_kernel(sums, slides, spot, gene, rows, scalars):
    valid, share, mass, slide, squares = (spot[k : k + 1, :] for k in range(5))
    genes = float(16 * sums.shape[1])

    def wide(index):
        return jnp.concatenate([sums[index + k : index + k + 1, :] for k in range(8)], axis=1)

    dots, own = wide(48), wide(56)
    dot, aa, bb = sums[0:16, :], sums[16:32, :], sums[32:48, :]
    scale = lax.rsqrt(aa * bb + 1e-06)
    pair = jnp.concatenate([dot * scale**3 * bb / genes, scale / genes])
    gene[...] = jnp.concatenate([pair, jnp.zeros((96, 128), F32)]).T
    total = jnp.sum(jnp.sum(dot * scale, axis=1, keepdims=True), axis=0, keepdims=True)
    nvs = jnp.zeros((1, 1), F32)
    density = jnp.zeros((1, 1), F32)
    nk, tk = jnp.ones_like(valid), jnp.ones_like(valid)
    for k in range(SLIDES):
        count, held, logs = (slides[0:1, 3 * j + k : 3 * j + k + 1] for j in range(3))
        some = count > 0
        safe = jnp.where(some, count, 1.0)
        nvs += count
        density += jnp.where(some, jnp.log(jnp.where(some, held, 1.0) / safe) - logs / safe, 0.0)
        here = (slide == k) & (valid > 0)
        nk = jnp.where(here, count, nk)
        tk = jnp.where(here, held, tk)
    scale = lax.rsqrt(own * squares + 1e-06)
    grad_mass = valid / SLIDES * (1.0 / tk - 1.0 / (nk * jnp.where(valid > 0, mass, 1.0)))
    rows[...] = jnp.concatenate(
        [
            dots * scale**3 * squares / nvs,
            scale / nvs,
            valid * share,
            share,
            jnp.zeros((4, valid.shape[1]), F32),
            grad_mass * share,
            jnp.zeros((7, valid.shape[1]), F32),
        ]
    )
    cosines = jnp.sum(valid * dots * scale, axis=1, keepdims=True)
    lane = lax.broadcasted_iota(jnp.int32, (1, 128), 1)
    out = jnp.zeros((1, 128), F32)
    for index, one in enumerate((total / genes, cosines / nvs, density / SLIDES)):
        out = jnp.where(lane == index, one, out)
    scalars[...] = out


def coef_call(sums, slides, spot):
    spots = spot.shape[1]
    return pl.pallas_call(
        coef_kernel,
        grid=(1,),
        in_specs=[fixed(sums.shape), fixed((1, 128)), fixed((8, spots))],
        out_specs=[fixed((128, 128)), fixed((16, spots)), fixed((1, 128))],
        out_shape=[
            jax.ShapeDtypeStruct((128, 128), F32),
            jax.ShapeDtypeStruct((16, spots), F32),
            jax.ShapeDtypeStruct((1, 128), F32),
        ],
        compiler_params=vmem(50),
        cost_estimate=NO_COST,
        name="coef",
    )(sums, slides, spot)


def back_kernel(where, place, *refs, count, aliased):
    pred, (spatial, gene, spot, high, low, expr), refs = refs[:8], refs[8:14], refs[14 + 2 * aliased :]
    grad_high, grad_low, column, sums, *outs = refs
    step = pl.program_id(0)
    inner = jnp.zeros(column.shape, F32)
    for index, part in enumerate(pred):
        for sub in range(2):
            value = part[sub, 0] * spot[3:4, :]
            rows = value.shape[0]
            at = pl.ds(pl.multiple_of(place[2 * index + sub] * rows, rows), rows)
            lane = lax.broadcasted_iota(jnp.int32, gene.shape, 1) - place[2 * index + sub]
            by_pred = jnp.sum(jnp.where(lane == 0, gene[...], 0.0), axis=1, keepdims=True)
            by_data = jnp.sum(jnp.where(lane == 16, gene[...], 0.0), axis=1, keepdims=True)
            grad = value * (by_pred + spot[0:1, :])
            grad = grad - spatial[0, at, :] * (by_data + spot[1:2, :])
            grad = grad * spot[2:3, :]
            grad_high[0, at, :], grad_low[0, at, :] = split(grad)
            inner += jnp.sum((grad * value).reshape(-1, 8, grad.shape[1]), axis=0)

    @pl.when(step == 0)
    def _():
        column[...] = jnp.zeros_like(column)
        if aliased:
            sums[...] = jnp.zeros_like(sums)
        else:
            sums[...] = product(split(spot[8:16, :]), (high[...], low[...]), ((1,), (1,)))

    column[...] += inner
    part = product((grad_high[0], grad_low[0]), (high[...], low[...]), ((1,), (1,)))
    sums[...] += jnp.sum((part * expr[...]).reshape(-1, 8, part.shape[1]), axis=0)
    for index, out in enumerate(outs):

        @pl.when(step == index)
        def _(out=out):
            out[...] = part


def back_call(where, place, pred, spatial, gene, spot, high, low, expr, grads):
    blocks, rows, spots = spatial.shape
    cells = high.shape[0]
    count = where.shape[0]
    extra = list(grads)
    piece = pred[0].shape[2]
    return pl.pallas_call(
        functools.partial(back_kernel, count=count, aliased=len(extra) // 2),
        grid_spec=pltpu.PrefetchScalarGridSpec(
            num_scalar_prefetch=2,
            grid=(count,),
            in_specs=[pl.BlockSpec((2, 1, piece, spots), lambda i, w, p: (0, w[i], 0, 0))] * 8
            + [
                pl.BlockSpec((1, rows, spots), lambda i, w, p: (w[i], 0, 0)),
                pl.BlockSpec((16, 128), lambda i, w, p: (w[i], 0)),
                fixed((16, spots)),
                fixed((cells, spots)),
                fixed((cells, spots)),
                pl.BlockSpec((rows, cells), lambda i, w, p: (w[i], 0)),
            ]
            + [pl.BlockSpec(memory_space=pl.ANY)] * len(extra),
            out_specs=[
                pl.BlockSpec((1, rows, spots), lambda i, w, p: (w[i], 0, 0)),
                pl.BlockSpec((1, rows, spots), lambda i, w, p: (w[i], 0, 0)),
                fixed((8, spots)),
                fixed((8, cells)),
            ]
            + [fixed((rows, cells))] * count,
        ),
        out_shape=[
            jax.ShapeDtypeStruct(spatial.shape, BF16),
            jax.ShapeDtypeStruct(spatial.shape, BF16),
            jax.ShapeDtypeStruct((8, spots), F32),
            jax.ShapeDtypeStruct((8, cells), F32),
        ]
        + [jax.ShapeDtypeStruct((rows, cells), F32)] * count,
        input_output_aliases={16: 0, 17: 1} if extra else {},
        compiler_params=vmem(50),
        cost_estimate=NO_COST,
        name="back",
    )(where, place, *pred, spatial, gene, spot, high, low, expr, *extra)


def map_kernel(expr, grad_high, grad_low, high, low, keep, spot, *rest, scale, start):
    out = rest[-1]
    step = pl.program_id(0) + start
    inner = product(split(expr[...]), (grad_high[...], grad_low[...]), ((0,), (0,))) + spot[0:1, :]
    expo = high[...].astype(F32) + low[...].astype(F32)
    for part in range(expr.shape[1] // 128):
        rows = slice(part * 128, part * 128 + 128)
        weight = as_column(keep[pl.ds(step * (expr.shape[1] // 128) + part, 1), :])
        out[rows, :] = (scale * expo[rows]) * (weight * inner[rows] - spot[1:2, :])


def map_call(start, stop, expr, grad_high, grad_low, high, low, keep, spot, scale, done=()):
    genes, cells = expr.shape
    spots = high.shape[1]
    block = 256
    return pl.pallas_call(
        functools.partial(map_kernel, scale=scale, start=start),
        grid=(stop - start,),
        in_specs=[
            pl.BlockSpec((genes, block), lambda i: (0, i + start)),
            fixed((genes, spots)),
            fixed((genes, spots)),
            pl.BlockSpec((block, spots), lambda i: (i + start, 0)),
            pl.BlockSpec((block, spots), lambda i: (i + start, 0)),
            fixed(keep.shape),
            fixed((8, spots)),
        ]
        + [pl.BlockSpec(memory_space=pl.ANY)] * len(done),
        out_specs=pl.BlockSpec((block, spots), lambda i: (i + start, 0)),
        out_shape=jax.ShapeDtypeStruct((cells, spots), F32),
        input_output_aliases={7: 0} if done else {},
        compiler_params=vmem(50),
        cost_estimate=NO_COST,
        name="grad_map",
    )(expr, grad_high, grad_low, high, low, keep, spot, *done)


def on_device(map_logits, filter_logits, expr, spatial, cell_type, slide_id, spot_mask):
    genes, cells = expr.shape
    spots = map_logits.shape[1]
    all_cells = cells * lax.axis_size("cells")
    all_spots = spots * lax.axis_size("spots")
    cell_place = lax.axis_index("cells")
    z, x = cell_place >> 2, cell_place & 3
    spot_place = lax.axis_index("spots")
    y, core = spot_place >> 1, spot_place & 1
    first = jnp.where(core == 0, x, z)
    second = jnp.where(core == 0, z, x)
    blocks = cells // 128

    valid = (cell_type >= 0).astype(F32)
    sigma = jax.nn.sigmoid(filter_logits)
    keep = sigma * valid
    spot_valid = spot_mask.astype(F32)
    kind2 = cell_type.reshape(blocks, 128)
    filt2 = filter_logits.reshape(blocks, 128)
    keep2 = keep.reshape(blocks, 128)

    high, low, types, totals = expo_call(map_logits, kind2, filt2)

    expr4 = expr.reshape(8, 16, 16, cells)
    keep_row = keep.reshape(1, cells)

    def group(step, half):
        q = ((first + step) & 3) * RING
        return [q + ((second + 2 * half) & 3), q + ((second + 2 * half + 1) & 3)]

    def pred_part(one, two, *others):
        where = jnp.stack(group(*one) + group(*two)).astype(jnp.int32).reshape(2, 2)
        return pred_call(after(where, *others), expr4, keep_row, high, low)

    totals = totals + swap(totals, 1, 0, 0, 0)
    far = after(tuple(pred_part((2, 0), (2, 1))), totals)
    far_right, far_left = along(far[0], 1), along(far[1], -1)
    near = pred_part((1, 1), (-1, 0), *far)
    near_right, near_left = along(near[0], 1), along(near[1], -1)
    totals = totals + swap(after(totals, *far), 3, 0, 0, 0)
    late = pred_part((1, 0), (-1, 1), *near)
    late = after((late[0] + far_right, late[1] + far_left), totals)
    late_right, late_left = along(late[0], 1), along(late[1], -1)
    totals = totals + swap(after(totals, *late), 0, 1, 0, 0)
    own = pred_part((0, 0), (0, 1), *late, near_right, near_left)
    own = after(tuple(own), totals)
    totals = totals + swap(totals, 0, 3, 0, 0)
    half0 = own[0] + late_right + near_left
    half1 = own[1] + near_right + late_left
    half0, half1 = after((half0, half1), totals)
    pieces = [across(half0[1], 1), across(half1[0], 2), across(half1[1], 3)]
    spatial_squares = jnp.sum(after(spatial, half0, half1) ** 2, axis=0)
    share = 1.0 / totals[0]
    mass = totals[1] * share
    spot_rows = jnp.concatenate(
        [
            jnp.stack([spot_valid, share, mass, slide_id.astype(F32), spatial_squares]),
            jnp.zeros((3, spots), F32),
        ]
    )
    piece = after(half0[0] + pieces[0] + pieces[1] + pieces[2], spot_rows)

    got = [across(piece, step) for step in (1, 2, 3)]
    sums, part = stats_call(
        (first * RING + second).astype(jnp.int32)[None],
        piece,
        spatial.reshape(8, 16, 16, spots),
        spot_rows,
    )
    sums = sums + swap(sums, 0, 0, 0, 1)
    sums = sums + swap(sums, 0, 0, 1, 0)
    sums = sums + swap(sums, 0, 0, 3, 0)
    mine = after((jnp.stack([piece, got[2]]), jnp.stack([got[1], got[0]])), sums)
    right0, left1 = along(mine[0], 1), along(mine[1], -1)
    right1, left0 = along(mine[1], 1), along(mine[0], -1)
    far0, far1 = along(right0, 1), along(left1, -1)
    pred = [*mine, right0, right1, left0, left1, far0, far1]
    order = [
        ((first + step) & 3) * RING + ((second + 2 * half + sub) & 3)
        for step, half in ((0, 0), (0, 1), (-1, 0), (-1, 1), (1, 0), (1, 1), (2, 0), (2, 1))
        for sub in range(2)
    ]
    order = jnp.stack(order).astype(jnp.int32)

    cell_sums = jnp.stack([jnp.sum(valid), jnp.sum(keep), jnp.sum(keep - keep * keep)])
    sums = after(sums, *mine)
    slides = sums[48:49]
    sums = jnp.concatenate([sums[:48], part, jnp.pad(cell_sums[None], ((0, 7), (0, 125)))])
    sums = after(sums, right0, left1)
    sums = sums + swap(sums, 1, 0, 0, 0)
    sums = sums + swap(sums, 3, 0, 0, 0)
    sums = after(sums, right1, left0)
    sums = sums + swap(sums, 0, 1, 0, 0)
    sums = sums + swap(sums, 0, 3, 0, 0)
    nvalid, retained, reg_sum = sums[64, 0], sums[64, 1], sums[64, 2]
    gene_coef, spot_coef, scalars = coef_call(sums, slides, spot_rows)

    spatial3 = spatial.reshape(8, genes // 8, spots)

    def back_part(steps, grads, *others):
        where = [((y + step) & 3) * 2 + (core ^ other) for step, other in steps]
        where = after(jnp.stack(where).astype(jnp.int32), *others)
        return back_call(where, order, pred, spatial3, gene_coef, spot_coef, high, low, expr, grads)

    rows = genes // 16
    *grads, column_a, sums_a, far_a = back_part([(2, 1)], ())
    far_got = swap(far_a, 0, 0, 0, 1)
    *grads, column_b, sums_b, far_b = back_part([(2, 0)], grads)
    far = far_b + far_got
    far_up, far_down = up(far[:rows], 1), up(far[rows:], -1)
    *grads, column_c, sums_c, up_a, down_a = back_part([(1, 1), (-1, 1)], grads, far)
    up_got, down_got = swap(up_a, 0, 0, 0, 1), swap(down_a, 0, 0, 0, 1)
    *grads, column_d, sums_d, up_b, down_b = back_part([(1, 0), (-1, 0)], grads)
    *grads, column_e, sums_e, own_a, own_b = back_part([(0, 1), (0, 0)], grads)
    far_up, far_down = after((far_up, far_down), own_b)
    above = jnp.concatenate([up_b[:rows] + up_got[:rows] + far_up, up_b[rows:] + up_got[rows:]])
    below = jnp.concatenate([down_b[:rows] + down_got[:rows], down_b[rows:] + down_got[rows:] + far_down])
    near_up, near_down = up(above, 1), up(below, -1)
    own_a = jnp.concatenate([swap(own_a[:rows], 0, 0, 0, 1), swap(own_a[rows:], 0, 0, 0, 1)])
    last = jnp.concatenate(
        [
            jnp.sum(sums_a + sums_b + sums_c + sums_d + sums_e, axis=0).reshape(blocks, 128),
            scalars,
            jnp.zeros((5, 128), F32),
        ]
    )

    column = jnp.sum(column_a + column_b + column_c + column_d + column_e, axis=0)
    map_rows = jnp.concatenate(
        [jnp.stack([spot_coef[8], column + spot_coef[8] * mass]), jnp.zeros((6, spots), F32)]
    )
    grads = [grad.reshape(genes, spots) for grad in grads]
    map_args = (expr, *grads, high, low, keep2, after(map_rows, above, below), all_cells * genes)
    steps = cells // 256
    grad_map = map_call(0, steps - 2, *map_args)
    last = after(last + swap(last, 0, 0, 0, 1), grad_map)
    map_half = grad_map
    grad_map = map_call(steps - 2, steps, *map_args, done=(after(grad_map, own_a),))
    last = after(last + swap(last, 0, 0, 1, 0), grad_map)
    last = last + swap(last, 0, 0, 3, 0)
    grad_weighted = after(own_b, grad_map) + own_a + near_up + near_down
    grad_expr = grad_weighted * (keep * (genes * all_spots))[None, :]

    types = after(types, own_b)
    types = after(types + swap(types, 1, 0, 0, 0), map_half)
    types = after(types + swap(types, 3, 0, 0, 0), grad_map)
    types = types + swap(types, 0, 1, 0, 0)
    types = types + swap(types, 0, 3, 0, 0)
    type_fraction = types * share

    filter_sum = last[:blocks].reshape(cells)
    shifted = (retained - 0.35 * nvalid) / (0.1 * all_cells)
    count_term = jnp.sqrt(shifted * shifted + 1.0)
    grad_keep = filter_sum + shifted / count_term / (0.1 * all_cells) + (1.0 - 2.0 * keep) / nvalid
    grad_filter = valid * sigma * (1.0 - sigma) * grad_keep * all_cells
    loss_terms = jnp.stack(
        [scalars[0, 0], last[blocks, 1], scalars[0, 2], count_term, reg_sum / nvalid]
    )
    return (loss_terms, type_fraction, grad_map, grad_filter, grad_expr)


def solution(mesh):
    in_specs = (
        P("cells", "spots"),
        P("cells"),
        P(None, "cells"),
        P(None, "spots"),
        P("cells"),
        P("spots"),
        P("spots"),
    )
    out_specs = (P(), P(None, "spots"), P("cells", "spots"), P("cells"), P("spots", "cells"))
    return jax.shard_map(
        on_device, mesh=mesh, in_specs=in_specs, out_specs=out_specs, check_vma=False
    )
```

```python
import functools

import jax
import jax.numpy as jnp
from jax import lax
from jax.experimental import pallas as pl
from jax.experimental.pallas import tpu as pltpu
from jax.sharding import PartitionSpec as P

TYPES = 32
SLIDES = 3
RING = 4
F32 = jnp.float32
BF16 = jnp.bfloat16


def vmem(mib):
    return pltpu.CompilerParams(vmem_limit_bytes=mib << 20)


def fixed(shape):
    return pl.BlockSpec(shape, lambda *_: (0,) * len(shape), pipeline_mode=pl.Buffered(1))


def cost(flops, moved):
    return pl.CostEstimate(flops=int(flops) // 8, bytes_accessed=int(moved) // 8, transcendentals=0)


NO_COST = pl.CostEstimate(flops=0, bytes_accessed=0, transcendentals=0)


def route(target):
    def flat(z, x, y, core):
        return ((z % RING * RING + x % RING) * RING + y % RING) * 2 + core

    return [
        (flat(z, x, y, core), flat(*target(z, x, y, core)))
        for z in range(RING)
        for x in range(RING)
        for y in range(RING)
        for core in range(2)
    ]


def send(array, target):
    return lax.ppermute(array, ("cells", "spots"), route(target))


def along(array, step):
    return send(array, lambda z, x, y, c: (z, x + step, y, c) if c == 0 else (z + step, x, y, c))


def across(array, step):
    return send(array, lambda z, x, y, c: (z + step, x, y, c) if c == 0 else (z, x + step, y, c))


def up(array, step):
    return send(array, lambda z, x, y, c: (z, x, y + step, c))


def swap(array, mz, mx, my, mc):
    return send(array, lambda z, x, y, c: (z ^ mz, x ^ mx, y ^ my, c ^ mc))


def after(value, *others):
    return lax.optimization_barrier((value, *others))[0]


def split(value):
    high = value.astype(BF16)
    return high, (value - high.astype(F32)).astype(BF16)


def product(left, right, dims):
    def one(a, b):
        return lax.dot_general(a, b, (dims, ((), ())), preferred_element_type=F32)

    return one(left[0], right[0]) + one(left[0], right[1]) + one(left[1], right[0])


def as_column(row):
    return jnp.broadcast_to(row, (128, 128)).T[:, :1]


def expo_kernel(logits, kind, filt, high, low, types, totals):
    step = pl.program_id(0)
    count = logits.shape[0] // 128

    @pl.when(step == 0)
    def _():
        types[...] = jnp.zeros_like(types)
        totals[...] = jnp.zeros_like(totals)

    for part in range(count):
        rows = slice(part * 128, part * 128 + 128)
        label = kind[pl.ds(step * count + part, 1), :]
        valid = (label >= 0).astype(F32)
        keep = valid * jax.nn.sigmoid(filt[pl.ds(step * count + part, 1), :])
        expo = jnp.exp(logits[rows]) * as_column(valid)
        high[rows], low[rows] = split(expo)
        whole = jnp.sum(expo, axis=0, keepdims=True)
        kept = jnp.sum(expo * as_column(keep), axis=0, keepdims=True)
        row = lax.broadcasted_iota(jnp.int32, types.shape, 0)
        types[...] += jnp.where(row == jnp.max(label, axis=1, keepdims=True), whole, 0.0)
        row = lax.broadcasted_iota(jnp.int32, totals.shape, 0)
        totals[...] += jnp.where(row == 0, whole, jnp.where(row == 1, kept, 0.0))


def expo_call(logits, kind, filt):
    cells, spots = logits.shape
    block = cells // 2
    return pl.pallas_call(
        expo_kernel,
        grid=(2,),
        in_specs=[
            pl.BlockSpec((block, spots), lambda i: (i, 0)),
            fixed(kind.shape),
            fixed(filt.shape),
        ],
        out_specs=[
            pl.BlockSpec((block, spots), lambda i: (i, 0)),
            pl.BlockSpec((block, spots), lambda i: (i, 0)),
            fixed((TYPES, spots)),
            fixed((8, spots)),
        ],
        out_shape=[
            jax.ShapeDtypeStruct((cells, spots), BF16),
            jax.ShapeDtypeStruct((cells, spots), BF16),
            jax.ShapeDtypeStruct((TYPES, spots), F32),
            jax.ShapeDtypeStruct((8, spots), F32),
        ],
        compiler_params=vmem(44),
        cost_estimate=cost(0, cells * spots * 8),
        name="expo",
    )(logits, kind, filt)


def pred_kernel(where, expr_a, expr_b, keep, high, low, *outs):
    rows = 2 * expr_a.shape[0] * expr_a.shape[2]
    weighted = jnp.concatenate(
        [part[...].reshape(rows // 2, keep.shape[1]) for part in (expr_a, expr_b)]
    )
    part = product(split(weighted * keep[...]), (high[...], low[...]), ((1,), (0,)))
    for step, out in enumerate(outs):

        @pl.when(pl.program_id(0) == step)
        def _(out=out):
            out[...] = part.reshape(out.shape)


def pred_call(where, expr, keep, high, low):
    blocks, groups, rows, cells = expr.shape
    spots = high.shape[1]
    count = where.shape[0]
    return pl.pallas_call(
        pred_kernel,
        grid_spec=pltpu.PrefetchScalarGridSpec(
            num_scalar_prefetch=1,
            grid=(count,),
            in_specs=[
                pl.BlockSpec((blocks, 1, rows, cells), lambda i, w: (0, w[i, 0], 0, 0)),
                pl.BlockSpec((blocks, 1, rows, cells), lambda i, w: (0, w[i, 1], 0, 0)),
                fixed((1, cells)),
                fixed((cells, spots)),
                fixed((cells, spots)),
            ],
            out_specs=[fixed((2, blocks, rows, spots))] * count,
        ),
        out_shape=[jax.ShapeDtypeStruct((2, blocks, rows, spots), F32)] * count,
        compiler_params=vmem(44),
        cost_estimate=cost(24 * blocks * rows * cells * spots, 4 * cells * spots + 16 * blocks * rows * (cells + spots)),
        name="pred",
    )(where, expr, expr, keep, high, low)


def stats_kernel(where, piece, spatial, spot, gene, part):
    rows = piece.shape[0] * piece.shape[1]
    valid, share, mass, slide = (spot[k : k + 1, :] for k in range(4))
    value = piece[...].reshape(rows, piece.shape[2]) * share
    data = spatial[...].reshape(value.shape)
    cross, square = value * data, value * value
    lane = lax.broadcasted_iota(jnp.int32, (rows, 128), 1)
    sums = jnp.zeros((rows, 128), F32)
    for index, one in enumerate((cross, square, data * data)):
        sums = jnp.where(lane == index, jnp.sum(one * valid, axis=1, keepdims=True), sums)
    sums = sums.T
    gene[...] = jnp.zeros_like(gene)
    for index in range(3):
        gene[pl.ds(16 * index + where[0], 1), :] = sums[index : index + 1, :]
    lane = lax.broadcasted_iota(jnp.int32, (1, 128), 1)
    slides = jnp.zeros((1, 128), F32)
    logs = jnp.log(jnp.where(valid > 0, mass, 1.0))
    for k in range(SLIDES):
        inside = jnp.where(slide == k, valid, 0.0)
        for index, one in enumerate((inside, inside * mass, inside * logs)):
            total = jnp.sum(one, axis=1, keepdims=True)
            slides = jnp.where(lane == 3 * index + k, total, slides)
    gene[48:49, :] = slides
    for index, one in enumerate((cross, square)):
        total = jnp.sum(one, axis=0, keepdims=True)
        for k in range(total.shape[1] // 128):
            part[8 * index + k : 8 * index + k + 1, :] = total[:, 128 * k : 128 * k + 128]


def stats_call(where, piece, spatial, spot):
    blocks, rows, spots = piece.shape
    return pl.pallas_call(
        stats_kernel,
        grid_spec=pltpu.PrefetchScalarGridSpec(
            num_scalar_prefetch=1,
            grid=(1,),
            in_specs=[
                fixed((blocks, rows, spots)),
                pl.BlockSpec((blocks, 1, rows, spots), lambda i, w: (0, w[0], 0, 0)),
                fixed((8, spots)),
            ],
            out_specs=[fixed((56, 128)), fixed((16, 128))],
        ),
        out_shape=[jax.ShapeDtypeStruct((56, 128), F32), jax.ShapeDtypeStruct((16, 128), F32)],
        compiler_params=vmem(44),
        cost_estimate=NO_COST,
        name="stats",
    )(where, piece, spatial, spot)


def coef_kernel(sums, slides, spot, gene, rows, scalars):
    valid, share, mass, slide, squares = (spot[k : k + 1, :] for k in range(5))
    genes = float(16 * sums.shape[1])

    def wide(index):
        return jnp.concatenate([sums[index + k : index + k + 1, :] for k in range(8)], axis=1)

    dots, own = wide(48), wide(56)
    dot, aa, bb = sums[0:16, :], sums[16:32, :], sums[32:48, :]
    scale = lax.rsqrt(aa * bb + 1e-06)
    pair = jnp.concatenate([dot * scale**3 * bb / genes, scale / genes])
    gene[...] = jnp.concatenate([pair, jnp.zeros((96, 128), F32)]).T
    total = jnp.sum(jnp.sum(dot * scale, axis=1, keepdims=True), axis=0, keepdims=True)
    nvs = jnp.zeros((1, 1), F32)
    density = jnp.zeros((1, 1), F32)
    nk, tk = jnp.ones_like(valid), jnp.ones_like(valid)
    for k in range(SLIDES):
        count, held, logs = (slides[0:1, 3 * j + k : 3 * j + k + 1] for j in range(3))
        some = count > 0
        safe = jnp.where(some, count, 1.0)
        nvs += count
        density += jnp.where(some, jnp.log(jnp.where(some, held, 1.0) / safe) - logs / safe, 0.0)
        here = (slide == k) & (valid > 0)
        nk = jnp.where(here, count, nk)
        tk = jnp.where(here, held, tk)
    scale = lax.rsqrt(own * squares + 1e-06)
    grad_mass = valid / SLIDES * (1.0 / tk - 1.0 / (nk * jnp.where(valid > 0, mass, 1.0)))
    mask = valid * share
    by_pred, by_data = dots * scale**3 * squares / nvs, scale / nvs
    for index, one in enumerate((by_pred * share * mask, by_data * mask, mask, share * mask)):
        rows[8 * index : 8 * index + 8, :] = jnp.broadcast_to(one, (8, one.shape[1]))
    rows[32:40, :] = jnp.concatenate([grad_mass * share, jnp.zeros((7, valid.shape[1]), F32)])
    cosines = jnp.sum(valid * dots * scale, axis=1, keepdims=True)
    lane = lax.broadcasted_iota(jnp.int32, (1, 128), 1)
    out = jnp.zeros((1, 128), F32)
    for index, one in enumerate((total / genes, cosines / nvs, density / SLIDES)):
        out = jnp.where(lane == index, one, out)
    scalars[...] = out


def coef_call(sums, slides, spot):
    spots = spot.shape[1]
    return pl.pallas_call(
        coef_kernel,
        grid=(1,),
        in_specs=[fixed(sums.shape), fixed((1, 128)), fixed((8, spots))],
        out_specs=[fixed((128, 128)), fixed((40, spots)), fixed((1, 128))],
        out_shape=[
            jax.ShapeDtypeStruct((128, 128), F32),
            jax.ShapeDtypeStruct((40, spots), F32),
            jax.ShapeDtypeStruct((1, 128), F32),
        ],
        compiler_params=vmem(44),
        cost_estimate=NO_COST,
        name="coef",
    )(sums, slides, spot)


def grad_rows(pred, data, gene, spot, lane):
    index = lax.broadcasted_iota(jnp.int32, gene.shape, 1) - lane
    by_pred = jnp.sum(jnp.where(index == 0, gene, 0.0), axis=1, keepdims=True).reshape(2, 8, 1)
    by_data = jnp.sum(jnp.where(index == 16, gene, 0.0), axis=1, keepdims=True).reshape(2, 8, 1)
    pred, data = pred.reshape(2, 8, pred.shape[1]), data.reshape(2, 8, data.shape[1])
    grad = pred * (by_pred * spot[24:32, :] + spot[0:8, :])
    grad = grad - data * (by_data * spot[16:24, :] + spot[8:16, :])
    return grad.reshape(16, grad.shape[2]), jnp.sum(grad * pred, axis=0)


def grad_kernel(place, *refs):
    pred, data, (gene, spot, high, low, column) = refs[:6], refs[6:9], refs[9:]

    @pl.when(pl.program_id(0) == 0)
    def _():
        column[...] = jnp.zeros_like(column)

    for index, part in enumerate(pred):
        for sub in range(2):
            lane = place[2 * index + sub]
            group, row = lane // RING, pl.multiple_of(lane % RING * 16, 16)
            rows, inner = grad_rows(
                part[sub, 0], data[index // 2][0, 0, pl.ds(row, 16), :], gene[...], spot, lane
            )
            high[0, group, pl.ds(row, 16), :], low[0, group, pl.ds(row, 16), :] = split(rows)
            column[...] += inner


def grad_call(place, pred, spatial, gene, spot):
    blocks, groups, rows, spots = spatial.shape
    return pl.pallas_call(
        grad_kernel,
        grid_spec=pltpu.PrefetchScalarGridSpec(
            num_scalar_prefetch=1,
            grid=(blocks,),
            in_specs=[pl.BlockSpec((2, 1, 16, spots), lambda i, p: (0, i, 0, 0))] * 6
            + [
                pl.BlockSpec((1, 1, rows, spots), lambda i, p, k=k: (i, p[4 * k] // RING, 0, 0))
                for k in range(3)
            ]
            + [pl.BlockSpec((16, 128), lambda i, p: (i, 0)), fixed(spot.shape)],
            out_specs=[
                pl.BlockSpec((1, groups, rows, spots), lambda i, p: (i, 0, 0, 0)),
                pl.BlockSpec((1, groups, rows, spots), lambda i, p: (i, 0, 0, 0)),
                fixed((8, spots)),
            ],
        ),
        out_shape=[
            jax.ShapeDtypeStruct(spatial.shape, BF16),
            jax.ShapeDtypeStruct(spatial.shape, BF16),
            jax.ShapeDtypeStruct((8, spots), F32),
        ],
        compiler_params=vmem(44),
        cost_estimate=NO_COST,
        name="grad",
    )(place, *pred, *[spatial] * 3, gene, spot)


def back_kernel(where, place, far0, far1, data, gene, spot, high, low, expr, grad_high, grad_low, *refs):
    new_high, new_low, column, sums, *outs = refs[:-2]
    left, right = refs[-2:]
    step = pl.program_id(0)

    @pl.when(step == 0)
    def _():
        column[...] = jnp.zeros_like(column)
        sums[...] = jnp.zeros_like(sums)

    left[...], right[...] = grad_high[0], grad_low[0]
    for index, part in enumerate((far0, far1)):
        for sub in range(2):
            lane = place[2 * index + sub]
            group, row = lane // RING, pl.multiple_of(lane % RING * 16, 16)
            rows, inner = grad_rows(part[sub, 0], data[0, 0, pl.ds(row, 16), :], gene[...], spot, lane)
            pair = split(rows)
            new_high[0, 0, pl.ds(row, 16), :], new_low[0, 0, pl.ds(row, 16), :] = pair
            left[group, pl.ds(row, 16), :], right[group, pl.ds(row, 16), :] = pair
            column[...] += inner
    shape = (expr.shape[0], left.shape[2])
    pair = left[...].reshape(shape), right[...].reshape(shape)
    part = product(pair, (high[...], low[...]), ((1,), (1,)))
    sums[...] += jnp.sum((part * expr[...]).reshape(-1, 8, part.shape[1]), axis=0)
    for index, out in enumerate(outs):

        @pl.when(step == index)
        def _(out=out):
            out[...] = part


def back_call(where, place, far, spatial, gene, spot, high, low, expr, grads):
    blocks, groups, rows, spots = spatial.shape
    cells = high.shape[0]
    count = where.shape[0]

    def quarter(i, w, p):
        return (w[i], p[0] // RING, 0, 0)

    return pl.pallas_call(
        back_kernel,
        grid_spec=pltpu.PrefetchScalarGridSpec(
            num_scalar_prefetch=2,
            grid=(count,),
            in_specs=[pl.BlockSpec((2, 1, 16, spots), lambda i, w, p: (0, w[i], 0, 0))] * 2
            + [
                pl.BlockSpec((1, 1, rows, spots), quarter),
                pl.BlockSpec((16, 128), lambda i, w, p: (w[i], 0)),
                fixed(spot.shape),
                fixed((cells, spots)),
                fixed((cells, spots)),
                pl.BlockSpec((groups * rows, cells), lambda i, w, p: (w[i], 0)),
                pl.BlockSpec((1, groups, rows, spots), lambda i, w, p: (w[i], 0, 0, 0)),
                pl.BlockSpec((1, groups, rows, spots), lambda i, w, p: (w[i], 0, 0, 0)),
            ],
            out_specs=[
                pl.BlockSpec((1, 1, rows, spots), quarter),
                pl.BlockSpec((1, 1, rows, spots), quarter),
                fixed((8, spots)),
                fixed((8, cells)),
            ]
            + [fixed((groups * rows, cells))] * count,
            scratch_shapes=[pltpu.VMEM((groups, rows, spots), BF16)] * 2,
        ),
        out_shape=[
            jax.ShapeDtypeStruct(spatial.shape, BF16),
            jax.ShapeDtypeStruct(spatial.shape, BF16),
            jax.ShapeDtypeStruct((8, spots), F32),
            jax.ShapeDtypeStruct((8, cells), F32),
        ]
        + [jax.ShapeDtypeStruct((groups * rows, cells), F32)] * count,
        input_output_aliases={10: 0, 11: 1},
        compiler_params=vmem(44),
        cost_estimate=NO_COST,
        name="back",
    )(where, place, *far, spatial, gene, spot, high, low, expr, *grads)


def mass_kernel(spot, high, low, out):
    out[...] = product(split(spot[...]), (high[...], low[...]), ((1,), (1,)))


def mass_call(spot, high, low):
    cells, spots = high.shape
    return pl.pallas_call(
        mass_kernel,
        grid=(1,),
        in_specs=[fixed((8, spots)), fixed((cells, spots)), fixed((cells, spots))],
        out_specs=fixed((8, cells)),
        out_shape=jax.ShapeDtypeStruct((8, cells), F32),
        compiler_params=vmem(44),
        cost_estimate=pl.CostEstimate(flops=10**11, bytes_accessed=0, transcendentals=0),
        name="mass",
    )(spot, high, low)


def map_kernel(expr, grad_high, grad_low, high, low, keep, spot, *rest, scale, start):
    out = rest[-1]
    step = pl.program_id(0) + start
    inner = product(split(expr[...]), (grad_high[...], grad_low[...]), ((0,), (0,))) + spot[0:1, :]
    expo = high[...].astype(F32) + low[...].astype(F32)
    for part in range(expr.shape[1] // 128):
        rows = slice(part * 128, part * 128 + 128)
        weight = as_column(keep[pl.ds(step * (expr.shape[1] // 128) + part, 1), :])
        out[rows, :] = (scale * expo[rows]) * (weight * inner[rows] - spot[1:2, :])


def map_call(start, stop, expr, grad_high, grad_low, high, low, keep, spot, scale, done=()):
    genes, cells = expr.shape
    spots = high.shape[1]
    block = 256
    return pl.pallas_call(
        functools.partial(map_kernel, scale=scale, start=start),
        grid=(stop - start,),
        in_specs=[
            pl.BlockSpec((genes, block), lambda i: (0, i + start)),
            fixed((genes, spots)),
            fixed((genes, spots)),
            pl.BlockSpec((block, spots), lambda i: (i + start, 0)),
            pl.BlockSpec((block, spots), lambda i: (i + start, 0)),
            fixed(keep.shape),
            fixed((8, spots)),
        ]
        + [pl.BlockSpec(memory_space=pl.ANY)] * len(done),
        out_specs=pl.BlockSpec((block, spots), lambda i: (i + start, 0)),
        out_shape=jax.ShapeDtypeStruct((cells, spots), F32),
        input_output_aliases={7: 0} if done else {},
        compiler_params=vmem(44),
        cost_estimate=NO_COST,
        name="grad_map",
    )(expr, grad_high, grad_low, high, low, keep, spot, *done)


def on_device(map_logits, filter_logits, expr, spatial, cell_type, slide_id, spot_mask):
    genes, cells = expr.shape
    spots = map_logits.shape[1]
    all_cells = cells * lax.axis_size("cells")
    all_spots = spots * lax.axis_size("spots")
    cell_place = lax.axis_index("cells")
    z, x = cell_place >> 2, cell_place & 3
    spot_place = lax.axis_index("spots")
    y, core = spot_place >> 1, spot_place & 1
    first = jnp.where(core == 0, x, z)
    second = jnp.where(core == 0, z, x)
    blocks = cells // 128

    valid = (cell_type >= 0).astype(F32)
    sigma = jax.nn.sigmoid(filter_logits)
    keep = sigma * valid
    spot_valid = spot_mask.astype(F32)
    kind2 = cell_type.reshape(blocks, 128)
    filt2 = filter_logits.reshape(blocks, 128)
    keep2 = keep.reshape(blocks, 128)

    high, low, types, totals = expo_call(map_logits, kind2, filt2)

    expr4 = expr.reshape(8, 16, 16, cells)
    keep_row = keep.reshape(1, cells)

    def group(step, half):
        q = ((first + step) & 3) * RING
        return [q + ((second + 2 * half) & 3), q + ((second + 2 * half + 1) & 3)]

    def pred_part(parts, *others):
        where = jnp.stack([q for part in parts for q in group(*part)]).astype(jnp.int32)
        return pred_call(after(where.reshape(-1, 2), *others), expr4, keep_row, high, low)

    totals = totals + swap(totals, 1, 0, 0, 0)
    (far0,) = pred_part([(2, 0)])
    far0, totals = lax.optimization_barrier((far0, totals))
    far_right = along(far0, 1)
    totals = totals + swap(totals, 3, 0, 0, 0)
    (far1,) = pred_part([(2, 1)], far0)
    far1, totals = lax.optimization_barrier((far1, totals))
    far_left = along(far1, -1)
    near = pred_part([(1, 1), (-1, 0)], far1)
    near_right, near_left = along(near[0], 1), along(near[1], -1)
    totals = totals + swap(totals, 0, 1, 0, 0)
    late = pred_part([(1, 0), (-1, 1)], *near)
    late = late[0] + far_right, late[1] + far_left
    late, totals = lax.optimization_barrier((late, totals))
    late_right, late_left = along(late[0], 1), along(late[1], -1)
    own = pred_part([(0, 0), (0, 1)], *late, near_right, near_left)
    totals = totals + swap(totals, 0, 3, 0, 0)
    half0 = own[0] + late_right + near_left
    half1 = own[1] + near_right + late_left
    half0, half1 = after((half0, half1), totals)
    pieces = [across(half0[1], 1), across(half1[0], 2), across(half1[1], 3)]
    spatial_squares = jnp.sum(after(spatial, half0, half1) ** 2, axis=0)
    share = 1.0 / totals[0]
    mass = totals[1] * share
    spot_rows = jnp.concatenate(
        [
            jnp.stack([spot_valid, share, mass, slide_id.astype(F32), spatial_squares]),
            jnp.zeros((3, spots), F32),
        ]
    )
    piece = after(half0[0] + pieces[0] + pieces[1] + pieces[2], spot_rows)

    got = [across(piece, step) for step in (1, 2, 3)]
    sums, part = stats_call(
        (first * RING + second).astype(jnp.int32)[None],
        piece,
        spatial.reshape(8, 16, 16, spots),
        spot_rows,
    )
    sums = sums + swap(sums, 0, 0, 0, 1)
    sums = sums + swap(sums, 0, 0, 1, 0)
    sums = sums + swap(sums, 0, 0, 3, 0)
    mine = after((jnp.stack([piece, got[2]]), jnp.stack([got[1], got[0]])), sums)
    slides = after(sums, *mine)[48:49]
    cell_sums = jnp.stack([jnp.sum(valid), jnp.sum(keep), jnp.sum(keep - keep * keep)])
    sums = jnp.concatenate([sums[:48], part, jnp.pad(cell_sums[None], ((0, 7), (0, 125)))])
    right0, left1 = along(mine[0], 1), along(mine[1], -1)
    right1, left0 = along(mine[1], 1), along(mine[0], -1)
    sums = sums + swap(after(sums, *mine), 1, 0, 0, 0)
    right0, left1, sums = lax.optimization_barrier((right0, left1, sums))
    far0, far1 = along(right0, 1), along(left1, -1)
    sums = sums + swap(sums, 3, 0, 0, 0)
    sums = sums + swap(sums, 0, 1, 0, 0)
    sums = after(sums, right1, left0)
    sums = sums + swap(sums, 0, 3, 0, 0)
    pred = [*mine, right0, right1, left0, left1, far0, far1]
    order = [
        ((first + step) & 3) * RING + ((second + 2 * half + sub) & 3)
        for step, half in ((0, 0), (0, 1), (-1, 0), (-1, 1), (1, 0), (1, 1), (2, 0), (2, 1))
        for sub in range(2)
    ]
    order = jnp.stack(order).astype(jnp.int32)

    nvalid, retained, reg_sum = sums[64, 0], sums[64, 1], sums[64, 2]
    gene_coef, spot_coef, scalars = coef_call(sums, slides, spot_rows)
    spatial4 = spatial.reshape(8, RING, genes // 32, spots)
    *grads, column_0 = grad_call(order[:12], pred[:6], spatial4, gene_coef, spot_coef)

    def back_part(steps, grads, *others):
        where = [((y + step) & 3) * 2 + (core ^ other) for step, other in steps]
        where = after(jnp.stack(where).astype(jnp.int32), *others)
        return back_call(
            where, order[12:], pred[6:], spatial4, gene_coef, spot_coef, high, low, expr, grads
        )

    rows = genes // 16
    types = types + swap(after(types, sums), 1, 0, 0, 0)
    *grads, column_a, sums_a, far_a = back_part([(2, 1)], grads, types)
    types = types + swap(after(types, far_a), 3, 0, 0, 0)
    far_got = swap(far_a, 0, 0, 0, 1)
    *grads, column_b, sums_b, far_b = back_part([(2, 0)], grads)
    far = far_b + far_got
    far_up, far_down = up(far[:rows], 1), up(far[rows:], -1)
    *grads, column_c, sums_c, up_a, down_a = back_part([(1, 1), (-1, 1)], grads, far, types)
    up_got, down_got = swap(up_a, 0, 0, 0, 1), swap(down_a, 0, 0, 0, 1)
    *grads, column_d, sums_d, up_b, down_b = back_part([(1, 0), (-1, 0)], grads)
    *grads, column_e, sums_e, own_a, own_b = back_part([(0, 1), (0, 0)], grads)
    sums_0 = mass_call(after(spot_coef, own_b, far_up, far_down)[32:40], high, low)
    far_up, far_down = after((far_up, far_down), sums_0)
    above = jnp.concatenate([up_b[:rows] + up_got[:rows] + far_up, up_b[rows:] + up_got[rows:]])
    below = jnp.concatenate([down_b[:rows] + down_got[:rows], down_b[rows:] + down_got[rows:] + far_down])
    near_up, near_down = up(above, 1), up(below, -1)
    own_a = jnp.concatenate([swap(own_a[:rows], 0, 0, 0, 1), swap(own_a[rows:], 0, 0, 0, 1)])
    last = jnp.concatenate(
        [
            jnp.sum(sums_0 + sums_a + sums_b + sums_c + sums_d + sums_e, axis=0).reshape(blocks, 128),
            scalars,
            jnp.zeros((5, 128), F32),
        ]
    )

    column = jnp.sum(column_0 + column_a + column_b + column_c + column_d + column_e, axis=0)
    map_rows = jnp.concatenate(
        [jnp.stack([spot_coef[32], column * share + spot_coef[32] * mass]), jnp.zeros((6, spots), F32)]
    )
    grads = [grad.reshape(genes, spots) for grad in grads]
    map_args = (expr, *grads, high, low, keep2, after(map_rows, above, below), all_cells * genes)
    steps = cells // 256
    got, types_got = swap(last, 0, 0, 0, 1), swap(after(types, own_b), 0, 1, 0, 0)
    grad_map = map_call(0, steps - 2, *map_args)
    got, types_got = after((got, types_got), grad_map)
    last, types = last + got, types + types_got
    got, types_got = swap(last, 0, 0, 1, 0), swap(types, 0, 3, 0, 0)
    grad_map = map_call(steps - 2, steps, *map_args, done=(after(grad_map, own_a),))
    got, types_got = after((got, types_got), grad_map)
    last, types = last + got, types + types_got
    last = last + swap(last, 0, 0, 3, 0)
    grad_weighted = after(own_b, grad_map) + own_a + near_up + near_down
    grad_expr = grad_weighted * (keep * (genes * all_spots))[None, :]

    type_fraction = types * share

    filter_sum = last[:blocks].reshape(cells)
    shifted = (retained - 0.35 * nvalid) / (0.1 * all_cells)
    count_term = jnp.sqrt(shifted * shifted + 1.0)
    grad_keep = filter_sum + shifted / count_term / (0.1 * all_cells) + (1.0 - 2.0 * keep) / nvalid
    grad_filter = valid * sigma * (1.0 - sigma) * grad_keep * all_cells
    loss_terms = jnp.stack(
        [scalars[0, 0], last[blocks, 1], scalars[0, 2], count_term, reg_sum / nvalid]
    )
    return (loss_terms, type_fraction, grad_map, grad_filter, grad_expr)


def solution(mesh):
    in_specs = (
        P("cells", "spots"),
        P("cells"),
        P(None, "cells"),
        P(None, "spots"),
        P("cells"),
        P("spots"),
        P("spots"),
    )
    out_specs = (P(), P(None, "spots"), P("cells", "spots"), P("cells"), P("spots", "cells"))
    return jax.shard_map(
        on_device, mesh=mesh, in_specs=in_specs, out_specs=out_specs, check_vma=False
    )
```

```python
import functools

import jax
import jax.numpy as jnp
from jax import lax
from jax.experimental import pallas as pl
from jax.experimental.pallas import tpu as pltpu
from jax.sharding import PartitionSpec as P

TYPES = 32
SLIDES = 3
RING = 4
F32 = jnp.float32
BF16 = jnp.bfloat16


def vmem(mib):
    return pltpu.CompilerParams(vmem_limit_bytes=mib << 20)


def fixed(shape):
    return pl.BlockSpec(shape, lambda *_: (0,) * len(shape), pipeline_mode=pl.Buffered(1))


def cost(flops, moved):
    return pl.CostEstimate(flops=int(flops) // 8, bytes_accessed=int(moved) // 8, transcendentals=0)


NO_COST = pl.CostEstimate(flops=0, bytes_accessed=0, transcendentals=0)


def route(target):
    def flat(z, x, y, core):
        return ((z % RING * RING + x % RING) * RING + y % RING) * 2 + core

    return [
        (flat(z, x, y, core), flat(*target(z, x, y, core)))
        for z in range(RING)
        for x in range(RING)
        for y in range(RING)
        for core in range(2)
    ]


def send(array, target):
    return lax.ppermute(array, ("cells", "spots"), route(target))


def along(array, step):
    return send(array, lambda z, x, y, c: (z, x + step, y, c) if c == 0 else (z + step, x, y, c))


def across(array, step):
    return send(array, lambda z, x, y, c: (z + step, x, y, c) if c == 0 else (z, x + step, y, c))


def up(array, step):
    return send(array, lambda z, x, y, c: (z, x, y + step, c))


def swap(array, mz, mx, my, mc):
    return send(array, lambda z, x, y, c: (z ^ mz, x ^ mx, y ^ my, c ^ mc))


def swap_along(array, mask):
    return send(array, lambda z, x, y, c: (z, x ^ mask, y, c) if c == 0 else (z ^ mask, x, y, c))


def swap_across(array, mask):
    return send(array, lambda z, x, y, c: (z ^ mask, x, y, c) if c == 0 else (z, x ^ mask, y, c))


def after(value, *others):
    return lax.optimization_barrier((value, *others))[0]


def split(value):
    high = value.astype(BF16)
    return high, (value - high.astype(F32)).astype(BF16)


def product(left, right, dims):
    def one(a, b):
        return lax.dot_general(a, b, (dims, ((), ())), preferred_element_type=F32)

    return one(left[0], right[0]) + one(left[0], right[1]) + one(left[1], right[0])


def as_column(row):
    return jnp.broadcast_to(row, (128, 128)).T[:, :1]


def expo_kernel(where, logits, kind, filt, *refs):
    expr, (high, low, types, totals, out0, out1) = refs[:4], refs[4:]
    step = pl.program_id(0)
    count = logits.shape[0] // 128

    @pl.when(step == 0)
    def _():
        for out in (types, totals, out0, out1):
            out[...] = jnp.zeros_like(out)

    keeps = []
    for part in range(count):
        rows = slice(part * 128, part * 128 + 128)
        label = kind[pl.ds(step * count + part, 1), :]
        valid = (label >= 0).astype(F32)
        keep = valid * jax.nn.sigmoid(filt[pl.ds(step * count + part, 1), :])
        keeps.append(keep)
        expo = jnp.exp(logits[rows]) * as_column(valid)
        high[rows], low[rows] = split(expo)
        whole = jnp.sum(expo, axis=0, keepdims=True)
        kept = jnp.sum(expo * as_column(keep), axis=0, keepdims=True)
        row = lax.broadcasted_iota(jnp.int32, types.shape, 0)
        types[...] += jnp.where(row == jnp.max(label, axis=1, keepdims=True), whole, 0.0)
        row = lax.broadcasted_iota(jnp.int32, totals.shape, 0)
        totals[...] += jnp.where(row == 0, whole, jnp.where(row == 1, kept, 0.0))
    weighted = jnp.concatenate([part[...].reshape(-1, logits.shape[0]) for part in expr])
    weighted = weighted * jnp.concatenate(keeps, axis=1)
    part = product(split(weighted), (high[...], low[...]), ((1,), (0,)))
    half = part.shape[0] // 2
    out0[...] += part[:half].reshape(out0.shape)
    out1[...] += part[half:].reshape(out1.shape)


def expo_call(where, logits, kind, filt, expr):
    cells, spots = logits.shape
    blocks, groups, rows, _ = expr.shape
    block = 256

    def gene_group(k):
        return pl.BlockSpec((blocks, 1, rows, block), lambda i, w: (0, w[k], 0, i))

    return pl.pallas_call(
        expo_kernel,
        grid_spec=pltpu.PrefetchScalarGridSpec(
            num_scalar_prefetch=1,
            grid=(cells // block,),
            in_specs=[
                pl.BlockSpec((block, spots), lambda i, w: (i, 0)),
                fixed(kind.shape),
                fixed(filt.shape),
            ]
            + [gene_group(k) for k in range(4)],
            out_specs=[
                pl.BlockSpec((block, spots), lambda i, w: (i, 0)),
                pl.BlockSpec((block, spots), lambda i, w: (i, 0)),
                fixed((TYPES, spots)),
                fixed((8, spots)),
                fixed((2, blocks, rows, spots)),
                fixed((2, blocks, rows, spots)),
            ],
        ),
        out_shape=[
            jax.ShapeDtypeStruct((cells, spots), BF16),
            jax.ShapeDtypeStruct((cells, spots), BF16),
            jax.ShapeDtypeStruct((TYPES, spots), F32),
            jax.ShapeDtypeStruct((8, spots), F32),
            jax.ShapeDtypeStruct((2, blocks, rows, spots), F32),
            jax.ShapeDtypeStruct((2, blocks, rows, spots), F32),
        ],
        compiler_params=vmem(57),
        cost_estimate=cost(0, cells * spots * 8),
        name="expo",
    )(where, logits, kind, filt, *[expr] * 4)


def pred_kernel(where, expr_a, expr_b, keep, high, low, *refs):
    outs = refs[len(refs) // 2 :] if len(refs) > 2 else refs
    rows = 2 * expr_a.shape[0] * expr_a.shape[2]
    weighted = jnp.concatenate(
        [part[...].reshape(rows // 2, keep.shape[1]) for part in (expr_a, expr_b)]
    )
    part = product(split(weighted * keep[...]), (high[...], low[...]), ((1,), (0,)))
    for step, out in enumerate(outs):

        @pl.when(pl.program_id(0) == step)
        def _(step=step, out=out):
            if len(refs) > 2:
                out[...] = part.reshape(out.shape) + refs[step][...]
            else:
                out[...] = part.reshape(out.shape)


def pred_call(where, expr, keep, high, low, more=()):
    blocks, groups, rows, cells = expr.shape
    spots = high.shape[1]
    return pl.pallas_call(
        pred_kernel,
        grid_spec=pltpu.PrefetchScalarGridSpec(
            num_scalar_prefetch=1,
            grid=(2,),
            in_specs=[
                pl.BlockSpec((blocks, 1, rows, cells), lambda i, w: (0, w[i, 0], 0, 0)),
                pl.BlockSpec((blocks, 1, rows, cells), lambda i, w: (0, w[i, 1], 0, 0)),
                fixed((1, cells)),
                fixed((cells, spots)),
                fixed((cells, spots)),
            ]
            + [fixed((2, blocks, rows, spots))] * len(more),
            out_specs=[fixed((2, blocks, rows, spots))] * 2,
        ),
        out_shape=[jax.ShapeDtypeStruct((2, blocks, rows, spots), F32)] * 2,
        compiler_params=vmem(44),
        cost_estimate=cost(24 * blocks * rows * cells * spots, 4 * cells * spots + 16 * blocks * rows * (cells + spots)),
        name="pred",
    )(where, expr, expr, keep, high, low, *more)


def merge_kernel(own0, own1, got0, got1, *outs):
    for half, (own, got) in enumerate(((own0, got0), (own1, got1))):
        for sub in range(2):
            outs[2 * half + sub][...] = own[sub] + got[sub]


def merge_call(own, got):
    shape = own[0].shape[1:]
    block = (2, *shape[1:])
    return pl.pallas_call(
        merge_kernel,
        grid=(shape[0] // 2,),
        in_specs=[pl.BlockSpec((2, *block), lambda i: (0, i, 0, 0))] * 4,
        out_specs=[pl.BlockSpec(block, lambda i: (i, 0, 0))] * 4,
        out_shape=[jax.ShapeDtypeStruct(shape, F32)] * 4,
        compiler_params=vmem(44),
        cost_estimate=NO_COST,
        name="merge",
    )(*own, *got)


def stats_kernel(where, piece, spatial, spot, cell_sums, gene, slide_sums):
    rows = piece.shape[0] * piece.shape[1]
    valid, share, mass, slide = (spot[k : k + 1, :] for k in range(4))
    value = piece[...].reshape(rows, piece.shape[2]) * share
    data = spatial[...].reshape(value.shape)
    cross, square = value * data, value * value
    lane = lax.broadcasted_iota(jnp.int32, (rows, 128), 1)
    sums = jnp.zeros((rows, 128), F32)
    for index, one in enumerate((cross, square, data * data)):
        sums = jnp.where(lane == index, jnp.sum(one * valid, axis=1, keepdims=True), sums)
    sums = sums.T
    gene[...] = jnp.zeros_like(gene)
    slide_sums[...] = jnp.zeros_like(slide_sums)
    for index in range(3):
        gene[pl.ds(16 * index + where[0], 1), :] = sums[index : index + 1, :]
    lane = lax.broadcasted_iota(jnp.int32, (1, 128), 1)
    slides = jnp.zeros((1, 128), F32)
    logs = jnp.log(jnp.where(valid > 0, mass, 1.0))
    for k in range(SLIDES):
        inside = jnp.where(slide == k, valid, 0.0)
        for index, one in enumerate((inside, inside * mass, inside * logs)):
            total = jnp.sum(one, axis=1, keepdims=True)
            slides = jnp.where(lane == 3 * index + k, total, slides)
    slide_sums[0:1, :] = slides
    gene[64:65, :] = cell_sums[...]
    for index, one in enumerate((cross, square)):
        total = jnp.sum(one, axis=0, keepdims=True)
        for k in range(total.shape[1] // 128):
            at = 48 + 8 * index + k
            gene[at : at + 1, :] = total[:, 128 * k : 128 * k + 128]


def stats_call(where, piece, spatial, spot, cell_sums):
    blocks, rows, spots = piece.shape
    return pl.pallas_call(
        stats_kernel,
        grid_spec=pltpu.PrefetchScalarGridSpec(
            num_scalar_prefetch=1,
            grid=(1,),
            in_specs=[
                fixed((blocks, rows, spots)),
                pl.BlockSpec((blocks, 1, rows, spots), lambda i, w: (0, w[0], 0, 0)),
                fixed((8, spots)),
                fixed((1, 128)),
            ],
            out_specs=[fixed((72, 128)), fixed((8, 128))],
        ),
        out_shape=[jax.ShapeDtypeStruct((72, 128), F32), jax.ShapeDtypeStruct((8, 128), F32)],
        compiler_params=vmem(57),
        cost_estimate=NO_COST,
        name="stats",
    )(where, piece, spatial, spot, cell_sums)


def coef_kernel(place, sums, slides, spot, gene, rows, scalars, pairs):
    valid, share, mass, slide, squares = (spot[k : k + 1, :] for k in range(5))
    genes = float(16 * sums.shape[1])

    def wide(index):
        return jnp.concatenate([sums[index + k : index + k + 1, :] for k in range(8)], axis=1)

    dots, own = wide(48), wide(56)
    dot, aa, bb = sums[0:16, :], sums[16:32, :], sums[32:48, :]
    scale = lax.rsqrt(aa * bb + 1e-06)
    pairs[0:16, :] = dot * scale**3 * bb / genes
    pairs[16:32, :] = scale / genes
    pair = [pairs[pl.ds(16 * (k // 16) + place[k % 16], 1), :] for k in range(32)]
    gene[...] = jnp.concatenate([*pair, jnp.zeros((96, 128), F32)]).T
    total = jnp.sum(jnp.sum(dot * scale, axis=1, keepdims=True), axis=0, keepdims=True)
    nvs = jnp.zeros((1, 1), F32)
    density = jnp.zeros((1, 1), F32)
    nk, tk = jnp.ones_like(valid), jnp.ones_like(valid)
    for k in range(SLIDES):
        count, held, logs = (slides[0:1, 3 * j + k : 3 * j + k + 1] for j in range(3))
        some = count > 0
        safe = jnp.where(some, count, 1.0)
        nvs += count
        density += jnp.where(some, jnp.log(jnp.where(some, held, 1.0) / safe) - logs / safe, 0.0)
        here = (slide == k) & (valid > 0)
        nk = jnp.where(here, count, nk)
        tk = jnp.where(here, held, tk)
    scale = lax.rsqrt(own * squares + 1e-06)
    grad_mass = valid / SLIDES * (1.0 / tk - 1.0 / (nk * jnp.where(valid > 0, mass, 1.0)))
    mask = valid * share
    by_pred, by_data = dots * scale**3 * squares / nvs, scale / nvs
    for index, one in enumerate((by_pred * share * mask, by_data * mask, mask, share * mask)):
        rows[8 * index : 8 * index + 8, :] = jnp.broadcast_to(one, (8, one.shape[1]))
    rows[32:40, :] = jnp.concatenate([grad_mass * share, jnp.zeros((7, valid.shape[1]), F32)])
    cosines = jnp.sum(valid * dots * scale, axis=1, keepdims=True)
    lane = lax.broadcasted_iota(jnp.int32, (1, 128), 1)
    out = jnp.zeros((1, 128), F32)
    for index, one in enumerate((total / genes, cosines / nvs, density / SLIDES)):
        out = jnp.where(lane == index, one, out)
    scalars[...] = out


def coef_call(place, sums, slides, spot):
    spots = spot.shape[1]
    return pl.pallas_call(
        coef_kernel,
        grid_spec=pltpu.PrefetchScalarGridSpec(
            num_scalar_prefetch=1,
            grid=(1,),
            in_specs=[fixed(sums.shape), fixed((8, 128)), fixed((8, spots))],
            out_specs=[fixed((128, 128)), fixed((40, spots)), fixed((1, 128))],
            scratch_shapes=[pltpu.VMEM((32, 128), F32)],
        ),
        out_shape=[
            jax.ShapeDtypeStruct((128, 128), F32),
            jax.ShapeDtypeStruct((40, spots), F32),
            jax.ShapeDtypeStruct((1, 128), F32),
        ],
        compiler_params=vmem(57),
        cost_estimate=NO_COST,
        name="coef",
    )(place, sums, slides, spot)


def grad_rows(pred, data, gene, spot, lane):
    by_pred = gene[:, lane : lane + 1].reshape(2, 8, 1)
    by_data = gene[:, 16 + lane : 17 + lane].reshape(2, 8, 1)
    pred, data = pred.reshape(2, 8, pred.shape[1]), data.reshape(2, 8, data.shape[1])
    grad = pred * (by_pred * spot[24:32, :] + spot[0:8, :])
    grad = grad - data * (by_data * spot[16:24, :] + spot[8:16, :])
    return grad.reshape(16, grad.shape[2]), jnp.sum(grad * pred, axis=0)


def grad_kernel(place, *refs):
    pred, data, (gene, spot, high, low, column) = refs[:6], refs[6:9], refs[9:]

    @pl.when(pl.program_id(0) == 0)
    def _():
        column[...] = jnp.zeros_like(column)

    for index, part in enumerate(pred):
        for sub in range(2):
            at = place[2 * index + sub]
            group, row = at // RING, pl.multiple_of(at % RING * 16, 16)
            rows, inner = grad_rows(
                part[sub, 0], data[index // 2][0, 0, pl.ds(row, 16), :], gene, spot, 2 * index + sub
            )
            high[0, group, pl.ds(row, 16), :], low[0, group, pl.ds(row, 16), :] = split(rows)
            column[...] += inner


def grad_call(place, pred, spatial, gene, spot):
    blocks, groups, rows, spots = spatial.shape
    return pl.pallas_call(
        grad_kernel,
        grid_spec=pltpu.PrefetchScalarGridSpec(
            num_scalar_prefetch=1,
            grid=(blocks,),
            in_specs=[pl.BlockSpec((2, 1, 16, spots), lambda i, p: (0, i, 0, 0))] * 6
            + [
                pl.BlockSpec((1, 1, rows, spots), lambda i, p, k=k: (i, p[4 * k] // RING, 0, 0))
                for k in range(3)
            ]
            + [pl.BlockSpec((16, 128), lambda i, p: (i, 0)), fixed(spot.shape)],
            out_specs=[
                pl.BlockSpec((1, groups, rows, spots), lambda i, p: (i, 0, 0, 0)),
                pl.BlockSpec((1, groups, rows, spots), lambda i, p: (i, 0, 0, 0)),
                fixed((8, spots)),
            ],
        ),
        out_shape=[
            jax.ShapeDtypeStruct(spatial.shape, BF16),
            jax.ShapeDtypeStruct(spatial.shape, BF16),
            jax.ShapeDtypeStruct((8, spots), F32),
        ],
        compiler_params=vmem(57),
        cost_estimate=NO_COST,
        name="grad",
    )(place, *pred, *[spatial] * 3, gene, spot)


def back_kernel(where, place, far0, far1, data, gene, spot, high, low, expr, grad_high, grad_low, *refs):
    new_high, new_low, column, sums, *outs = refs[:-2]
    left, right = refs[-2:]
    step = pl.program_id(0)

    @pl.when(step == 0)
    def _():
        column[...] = jnp.zeros_like(column)
        sums[...] = jnp.zeros_like(sums)

    left[...], right[...] = grad_high[0], grad_low[0]
    for index, part in enumerate((far0, far1)):
        for sub in range(2):
            at = place[2 * index + sub]
            group, row = at // RING, pl.multiple_of(at % RING * 16, 16)
            rows, inner = grad_rows(
                part[sub, 0], data[0, 0, pl.ds(row, 16), :], gene, spot, 12 + 2 * index + sub
            )
            pair = split(rows)
            new_high[0, 0, pl.ds(row, 16), :], new_low[0, 0, pl.ds(row, 16), :] = pair
            left[group, pl.ds(row, 16), :], right[group, pl.ds(row, 16), :] = pair
            column[...] += inner
    shape = (expr.shape[0], left.shape[2])
    pair = left[...].reshape(shape), right[...].reshape(shape)
    part = product(pair, (high[...], low[...]), ((1,), (1,)))
    sums[...] += jnp.sum((part * expr[...]).reshape(-1, 8, part.shape[1]), axis=0)
    for index, out in enumerate(outs):

        @pl.when(step == index)
        def _(out=out):
            out[...] = part


def back_call(where, place, far, spatial, gene, spot, high, low, expr, grads):
    blocks, groups, rows, spots = spatial.shape
    cells = high.shape[0]
    count = where.shape[0]

    def quarter(i, w, p):
        return (w[i], p[0] // RING, 0, 0)

    return pl.pallas_call(
        back_kernel,
        grid_spec=pltpu.PrefetchScalarGridSpec(
            num_scalar_prefetch=2,
            grid=(count,),
            in_specs=[pl.BlockSpec((2, 1, 16, spots), lambda i, w, p: (0, w[i], 0, 0))] * 2
            + [
                pl.BlockSpec((1, 1, rows, spots), quarter),
                pl.BlockSpec((16, 128), lambda i, w, p: (w[i], 0)),
                fixed(spot.shape),
                fixed((cells, spots)),
                fixed((cells, spots)),
                pl.BlockSpec((groups * rows, cells), lambda i, w, p: (w[i], 0)),
                pl.BlockSpec((1, groups, rows, spots), lambda i, w, p: (w[i], 0, 0, 0)),
                pl.BlockSpec((1, groups, rows, spots), lambda i, w, p: (w[i], 0, 0, 0)),
            ],
            out_specs=[
                pl.BlockSpec((1, 1, rows, spots), quarter),
                pl.BlockSpec((1, 1, rows, spots), quarter),
                fixed((8, spots)),
                fixed((8, cells)),
            ]
            + [fixed((groups * rows, cells))] * count,
            scratch_shapes=[pltpu.VMEM((groups, rows, spots), BF16)] * 2,
        ),
        out_shape=[
            jax.ShapeDtypeStruct(spatial.shape, BF16),
            jax.ShapeDtypeStruct(spatial.shape, BF16),
            jax.ShapeDtypeStruct((8, spots), F32),
            jax.ShapeDtypeStruct((8, cells), F32),
        ]
        + [jax.ShapeDtypeStruct((groups * rows, cells), F32)] * count,
        input_output_aliases={10: 0, 11: 1},
        compiler_params=vmem(44),
        cost_estimate=NO_COST,
        name="back",
    )(where, place, *far, spatial, gene, spot, high, low, expr, *grads)


def mass_kernel(spot, high, low, out):
    out[...] = product(split(spot[...]), (high[...], low[...]), ((1,), (1,)))


def mass_call(spot, high, low):
    cells, spots = high.shape
    return pl.pallas_call(
        mass_kernel,
        grid=(1,),
        in_specs=[fixed((8, spots)), fixed((cells, spots)), fixed((cells, spots))],
        out_specs=fixed((8, cells)),
        out_shape=jax.ShapeDtypeStruct((8, cells), F32),
        compiler_params=vmem(44),
        cost_estimate=pl.CostEstimate(flops=10**9, bytes_accessed=0, transcendentals=0),
        name="mass",
    )(spot, high, low)


def map_kernel(expr, grad_high, grad_low, high, low, keep, spot, *rest, scale, start):
    out = rest[-1]
    step = pl.program_id(0) + start
    inner = product(split(expr[...]), (grad_high[...], grad_low[...]), ((0,), (0,))) + spot[0:1, :]
    expo = high[...].astype(F32) + low[...].astype(F32)
    for part in range(expr.shape[1] // 128):
        rows = slice(part * 128, part * 128 + 128)
        weight = as_column(keep[pl.ds(step * (expr.shape[1] // 128) + part, 1), :])
        out[rows, :] = (scale * expo[rows]) * (weight * inner[rows] - spot[1:2, :])


def map_call(start, stop, expr, grad_high, grad_low, high, low, keep, spot, scale, done=()):
    genes, cells = expr.shape
    spots = high.shape[1]
    block = 256
    return pl.pallas_call(
        functools.partial(map_kernel, scale=scale, start=start),
        grid=(stop - start,),
        in_specs=[
            pl.BlockSpec((genes, block), lambda i: (0, i + start)),
            fixed((genes, spots)),
            fixed((genes, spots)),
            pl.BlockSpec((block, spots), lambda i: (i + start, 0)),
            pl.BlockSpec((block, spots), lambda i: (i + start, 0)),
            fixed(keep.shape),
            fixed((8, spots)),
        ]
        + [pl.BlockSpec(memory_space=pl.ANY)] * len(done),
        out_specs=pl.BlockSpec((block, spots), lambda i: (i + start, 0)),
        out_shape=jax.ShapeDtypeStruct((cells, spots), F32),
        input_output_aliases={7: 0} if done else {},
        compiler_params=vmem(44),
        cost_estimate=NO_COST,
        name="grad_map",
    )(expr, grad_high, grad_low, high, low, keep, spot, *done)


def finish_kernel(last, got, sums, scalars, kind, filt, grad_filter, terms, *, all_cells):
    blocks = kind.shape[0]
    total = last[...] + got[...]
    nvalid, retained, reg_sum = (sums[64:65, k : k + 1] for k in range(3))
    valid = (kind[...] >= 0).astype(F32)
    sigma = jax.nn.sigmoid(filt[...])
    keep = sigma * valid
    shifted = (retained - 0.35 * nvalid) / (0.1 * all_cells)
    count_term = jnp.sqrt(shifted * shifted + 1.0)
    grad_keep = total[:blocks] + shifted / count_term / (0.1 * all_cells) + (1.0 - 2.0 * keep) / nvalid
    grad_filter[...] = valid * sigma * (1.0 - sigma) * grad_keep * all_cells
    lane = lax.broadcasted_iota(jnp.int32, (1, 128), 1)
    out = jnp.zeros((1, 128), F32)
    parts = (scalars[:, 0:1], total[blocks : blocks + 1, 1:2], scalars[:, 2:3], count_term, reg_sum / nvalid)
    for index, one in enumerate(parts):
        out = jnp.where(lane == index, one, out)
    terms[...] = out


def finish_call(last, got, sums, scalars, kind, filt, all_cells):
    return pl.pallas_call(
        functools.partial(finish_kernel, all_cells=float(all_cells)),
        grid=(1,),
        in_specs=[fixed(one.shape) for one in (last, got, sums, scalars, kind, filt)],
        out_specs=[fixed(kind.shape), fixed((1, 128))],
        out_shape=[jax.ShapeDtypeStruct(kind.shape, F32), jax.ShapeDtypeStruct((1, 128), F32)],
        compiler_params=vmem(44),
        cost_estimate=NO_COST,
        name="finish",
    )(last, got, sums, scalars, kind, filt)


def on_device(map_logits, filter_logits, expr, spatial, cell_type, slide_id, spot_mask):
    genes, cells = expr.shape
    spots = map_logits.shape[1]
    all_cells = cells * lax.axis_size("cells")
    all_spots = spots * lax.axis_size("spots")
    cell_place = lax.axis_index("cells")
    z, x = cell_place >> 2, cell_place & 3
    spot_place = lax.axis_index("spots")
    y, core = spot_place >> 1, spot_place & 1
    first = jnp.where(core == 0, x, z)
    second = jnp.where(core == 0, z, x)
    blocks = cells // 128

    valid = (cell_type >= 0).astype(F32)
    sigma = jax.nn.sigmoid(filter_logits)
    keep = sigma * valid
    spot_valid = spot_mask.astype(F32)
    kind2 = cell_type.reshape(blocks, 128)
    filt2 = filter_logits.reshape(blocks, 128)
    keep2 = keep.reshape(blocks, 128)

    expr4 = expr.reshape(8, 16, 16, cells)
    keep_row = keep.reshape(1, cells)

    def group(step, half):
        q = ((first + step) & 3) * RING
        return [q + ((second + 2 * half) & 3), q + ((second + 2 * half + 1) & 3)]

    def groups(*parts):
        return jnp.stack([q for part in parts for q in group(*part)]).astype(jnp.int32)

    def pred_part(one, two, more, *others):
        where = after(groups(one, two).reshape(2, 2), *others)
        return pred_call(where, expr4, keep_row, high, low, more)

    high, low, types, totals, *far = expo_call(
        groups((2, 0), (2, 1)), map_logits, kind2, filt2, expr4
    )
    totals = totals + swap_along(totals, 1)
    far_right, far_left = along(far[0], 1), along(far[1], -1)
    near = pred_part((1, 1), (-1, 0), (), totals, *far)
    near_right, near_left = along(near[0], 1), along(near[1], -1)
    totals = totals + swap_across(totals, 1)
    late = pred_part((1, 0), (-1, 1), (far_right, far_left), totals, *near)
    late_right, late_left = along(late[0], 1), along(late[1], -1)
    totals = totals + swap_across(totals, 3)
    own = pred_part((0, 0), (0, 1), (near_left, near_right), totals, *late)
    mine, *pieces = merge_call(own, (late_right, late_left))
    pieces = [across(piece, step + 1) for step, piece in enumerate(pieces)]
    totals = totals + swap_along(after(totals, mine), 3)
    spatial_squares = jnp.sum(after(spatial, mine) ** 2, axis=0)
    share = 1.0 / totals[0]
    mass = totals[1] * share
    spot_rows = jnp.concatenate(
        [
            jnp.stack([spot_valid, share, mass, slide_id.astype(F32), spatial_squares]),
            jnp.zeros((3, spots), F32),
        ]
    )
    piece = after(mine + pieces[0] + pieces[1] + pieces[2], spot_rows)

    got = [across(piece, step) for step in (1, 2, 3)]
    cell_sums = jnp.stack([jnp.sum(valid), jnp.sum(keep), jnp.sum(keep - keep * keep)])
    sums, slides = stats_call(
        (first * RING + second).astype(jnp.int32)[None],
        piece,
        spatial.reshape(8, 16, 16, spots),
        spot_rows,
        jnp.pad(cell_sums[None], ((0, 0), (0, 125))),
    )
    genes_slides = jnp.concatenate([sums[:48], slides])
    genes_slides = genes_slides + swap(genes_slides, 0, 0, 0, 1)
    sums = jnp.concatenate([genes_slides[:48], sums[48:]])
    sums = sums + swap_along(sums, 1)
    sums = sums + swap_along(sums, 3)
    mine = after((jnp.stack([piece, got[2]]), jnp.stack([got[1], got[0]])), sums)
    right0, left1 = along(mine[0], 1), along(mine[1], -1)
    right1, left0 = along(mine[1], 1), along(mine[0], -1)
    genes_slides = jnp.concatenate([sums[:48], genes_slides[48:]])
    genes_slides = genes_slides + swap(after(genes_slides, *mine), 0, 0, 1, 0)
    right0, left1, genes_slides = lax.optimization_barrier((right0, left1, genes_slides))
    far0, far1 = along(right0, 1), along(left1, -1)
    genes_slides = genes_slides + swap(genes_slides, 0, 0, 3, 0)
    slides = genes_slides[48:]
    sums = jnp.concatenate([genes_slides[:48], sums[48:]])
    sums = sums + swap_across(sums, 1)
    sums = after(sums, right1, left0)
    sums = sums + swap_across(sums, 3)
    pred = [*mine, right0, right1, left0, left1, far0, far1]
    order = [
        ((first + step) & 3) * RING + ((second + 2 * half + sub) & 3)
        for step, half in ((0, 0), (0, 1), (-1, 0), (-1, 1), (1, 0), (1, 1), (2, 0), (2, 1))
        for sub in range(2)
    ]
    order = jnp.stack(order).astype(jnp.int32)
    gene_coef, spot_coef, scalars = coef_call(order, sums, slides, spot_rows)
    spatial4 = spatial.reshape(8, RING, genes // 32, spots)
    *grads, column_0 = grad_call(order[:12], pred[:6], spatial4, gene_coef, spot_coef)

    def back_part(steps, grads, *others):
        where = [((y + step) & 3) * 2 + (core ^ other) for step, other in steps]
        where = after(jnp.stack(where).astype(jnp.int32), *others)
        return back_call(
            where, order[12:], pred[6:], spatial4, gene_coef, spot_coef, high, low, expr, grads
        )

    rows = genes // 16
    types = types + swap(after(types, sums), 1, 0, 0, 0)
    *grads, column_a, sums_a, far_a = back_part([(2, 1)], grads, types)
    types = types + swap(after(types, far_a), 3, 0, 0, 0)
    far_got = swap(far_a, 0, 0, 0, 1)
    *grads, column_b, sums_b, far_b = back_part([(2, 0)], grads)
    far = far_b + far_got
    far_up, far_down = up(far[:rows], 1), up(far[rows:], -1)
    *grads, column_c, sums_c, up_a, down_a = back_part([(1, 1), (-1, 1)], grads, far, types)
    up_got, down_got = swap(up_a, 0, 0, 0, 1), swap(down_a, 0, 0, 0, 1)
    *grads, column_d, sums_d, up_b, down_b = back_part([(1, 0), (-1, 0)], grads)
    *grads, column_e, sums_e, own_a, own_b = back_part([(0, 1), (0, 0)], grads)
    sums_0 = mass_call(after(spot_coef, own_b, far_up, far_down)[32:40], high, low)
    far_up, far_down = after((far_up, far_down), sums_0)
    above = jnp.concatenate([up_b[:rows] + up_got[:rows] + far_up, up_b[rows:] + up_got[rows:]])
    below = jnp.concatenate([down_b[:rows] + down_got[:rows], down_b[rows:] + down_got[rows:] + far_down])
    near_up, near_down = up(above, 1), up(below, -1)
    own_a = jnp.concatenate([swap(own_a[:rows], 0, 0, 0, 1), swap(own_a[rows:], 0, 0, 0, 1)])
    last = jnp.concatenate(
        [
            jnp.sum(sums_0 + sums_a + sums_b + sums_c + sums_d + sums_e, axis=0).reshape(blocks, 128),
            scalars,
            jnp.zeros((5, 128), F32),
        ]
    )

    column = jnp.sum(column_0 + column_a + column_b + column_c + column_d + column_e, axis=0)
    map_rows = jnp.concatenate(
        [jnp.stack([spot_coef[32], column * share + spot_coef[32] * mass]), jnp.zeros((6, spots), F32)]
    )
    grads = [grad.reshape(genes, spots) for grad in grads]
    map_args = (expr, *grads, high, low, keep2, after(map_rows, above, below), all_cells * genes)
    steps = cells // 256
    got, types_got = swap(last, 0, 0, 0, 1), swap(after(types, own_b), 0, 1, 0, 0)
    grad_map = map_call(0, steps - 2, *map_args)
    got, types_got = after((got, types_got), grad_map)
    last, types = last + got, types + types_got
    got, types_got = swap(last, 0, 0, 1, 0), swap(types, 0, 3, 0, 0)
    grad_map = map_call(steps - 2, steps, *map_args, done=(after(grad_map, own_a),))
    got, types_got = after((got, types_got), grad_map)
    last, types = last + got, types + types_got
    got = swap(last, 0, 0, 3, 0)
    grad_weighted = after(own_b + own_a, grad_map) + near_up + near_down
    grad_expr = grad_weighted * (keep * (genes * all_spots))[None, :]

    type_fraction = types * share

    grad_filter, loss_terms = finish_call(last, got, sums, scalars, kind2, filt2, all_cells)
    return (loss_terms[0, :5], type_fraction, grad_map, grad_filter.reshape(cells), grad_expr)


def solution(mesh):
    in_specs = (
        P("cells", "spots"),
        P("cells"),
        P(None, "cells"),
        P(None, "spots"),
        P("cells"),
        P("spots"),
        P("spots"),
    )
    out_specs = (P(), P(None, "spots"), P("cells", "spots"), P("cells"), P("spots", "cells"))
    return jax.shard_map(
        on_device, mesh=mesh, in_specs=in_specs, out_specs=out_specs, check_vma=False
    )
```

```python
import functools

import jax
import jax.numpy as jnp
from jax import lax
from jax.experimental import pallas as pl
from jax.experimental.pallas import tpu as pltpu
from jax.sharding import PartitionSpec as P

TYPES = 32
SLIDES = 3
RING = 4
F32 = jnp.float32
BF16 = jnp.bfloat16


def vmem(mib):
    return pltpu.CompilerParams(vmem_limit_bytes=mib << 20)


def fixed(shape):
    return pl.BlockSpec(shape, lambda *_: (0,) * len(shape), pipeline_mode=pl.Buffered(1))


def streamed(array):
    return pltpu.with_memory_space_constraint(array, pltpu.HBM)


RESIDENT = pl.BlockSpec(memory_space=pltpu.VMEM)


def cost(flops, moved):
    return pl.CostEstimate(flops=int(flops) // 8, bytes_accessed=int(moved) // 8, transcendentals=0)


NO_COST = pl.CostEstimate(flops=0, bytes_accessed=0, transcendentals=0)


def route(target):
    def flat(z, x, y, core):
        return ((z % RING * RING + x % RING) * RING + y % RING) * 2 + core

    return [
        (flat(z, x, y, core), flat(*target(z, x, y, core)))
        for z in range(RING)
        for x in range(RING)
        for y in range(RING)
        for core in range(2)
    ]


def send(array, target):
    return lax.ppermute(array, ("cells", "spots"), route(target))


def along(array, step):
    return send(array, lambda z, x, y, c: (z, x + step, y, c) if c == 0 else (z + step, x, y, c))


def across(array, step):
    return send(array, lambda z, x, y, c: (z + step, x, y, c) if c == 0 else (z, x + step, y, c))


def up(array, step):
    return send(array, lambda z, x, y, c: (z, x, y + step, c))


def swap(array, mz, mx, my, mc):
    return send(array, lambda z, x, y, c: (z ^ mz, x ^ mx, y ^ my, c ^ mc))


def swap_along(array, mask):
    return send(array, lambda z, x, y, c: (z, x ^ mask, y, c) if c == 0 else (z ^ mask, x, y, c))


def swap_across(array, mask):
    return send(array, lambda z, x, y, c: (z ^ mask, x, y, c) if c == 0 else (z, x ^ mask, y, c))


def after(value, *others):
    return lax.optimization_barrier((value, *others))[0]


def split(value):
    high = value.astype(BF16)
    return high, (value - high.astype(F32)).astype(BF16)


def product(left, right, dims):
    def one(a, b):
        return lax.dot_general(a, b, (dims, ((), ())), preferred_element_type=F32)

    return one(left[0], right[0]) + one(left[0], right[1]) + one(left[1], right[0])


def gene_group(ids, step, half, sub):
    return ((ids[0] + step) & 3) * RING + ((ids[1] + 2 * half + sub) & 3)


PIECES = [
    (step, half, sub)
    for step, half in ((0, 0), (0, 1), (-1, 0), (-1, 1), (1, 0), (1, 1), (2, 0), (2, 1))
    for sub in range(2)
]


def pick(index, values):
    out = values[0]
    for k, value in enumerate(values[1:]):
        out = jnp.where(index == k + 1, value, out)
    return out


def stacked(rows):
    row = lax.broadcasted_iota(jnp.int32, (8, rows[0].shape[0]), 0)
    out = jnp.zeros(row.shape, F32)
    for k, value in enumerate(rows):
        out = jnp.where(row == k, value[None, :], out)
    return out


def as_column(row):
    return jnp.broadcast_to(row, (128, 128)).T[:, :1]


def expo_kernel(ids, logits, kind, filt, *refs):
    expr, (masses, types, totals, out0, out1) = refs[:4], refs[4:]
    step = pl.program_id(0)
    count = logits.shape[0] // 128

    @pl.when(step == 0)
    def _():
        for out in (types, totals, out0, out1):
            out[...] = jnp.zeros_like(out)

    keeps = []
    for part in range(count):
        rows = slice(part * 128, part * 128 + 128)
        label = kind[pl.ds(step * count + part, 1), :]
        valid = (label >= 0).astype(F32)
        keep = valid * jax.nn.sigmoid(filt[pl.ds(step * count + part, 1), :])
        keeps.append(keep)
        expo = jnp.exp(logits[rows]) * as_column(valid)
        masses[0, rows], masses[1, rows] = split(expo)
        whole = jnp.sum(expo, axis=0, keepdims=True)
        kept = jnp.sum(expo * as_column(keep), axis=0, keepdims=True)
        row = lax.broadcasted_iota(jnp.int32, types.shape, 0)
        types[...] += jnp.where(row == jnp.max(label, axis=1, keepdims=True), whole, 0.0)
        row = lax.broadcasted_iota(jnp.int32, totals.shape, 0)
        totals[...] += jnp.where(row == 0, whole, jnp.where(row == 1, kept, 0.0))
    weighted = jnp.concatenate([part[...].reshape(-1, logits.shape[0]) for part in expr])
    weighted = weighted * jnp.concatenate(keeps, axis=1)
    part = product(split(weighted), masses, ((1,), (0,)))
    half = part.shape[0] // 2
    out0[...] += part[:half].reshape(out0.shape)
    out1[...] += part[half:].reshape(out1.shape)


def expo_call(ids, parts, logits, kind, filt, expr):
    cells, spots = logits.shape
    blocks, groups, rows, _ = expr.shape
    block = 256

    def genes(part, sub):
        return pl.BlockSpec(
            (blocks, 1, rows, block), lambda i, ids: (0, gene_group(ids, *part, sub), 0, i)
        )

    return pl.pallas_call(
        expo_kernel,
        grid_spec=pltpu.PrefetchScalarGridSpec(
            num_scalar_prefetch=1,
            grid=(cells // block,),
            in_specs=[
                pl.BlockSpec((block, spots), lambda i, w: (i, 0)),
                fixed(kind.shape),
                fixed(filt.shape),
            ]
            + [genes(part, sub) for part in parts for sub in range(2)],
            out_specs=[
                pl.BlockSpec((2, block, spots), lambda i, w: (0, i, 0)),
                fixed((TYPES, spots)),
                fixed((8, spots)),
                fixed((2, blocks, rows, spots)),
                fixed((2, blocks, rows, spots)),
            ],
        ),
        out_shape=[
            jax.ShapeDtypeStruct((2, cells, spots), BF16),
            jax.ShapeDtypeStruct((TYPES, spots), F32),
            jax.ShapeDtypeStruct((8, spots), F32),
            jax.ShapeDtypeStruct((2, blocks, rows, spots), F32),
            jax.ShapeDtypeStruct((2, blocks, rows, spots), F32),
        ],
        compiler_params=vmem(16),
        cost_estimate=cost(0, cells * spots * 8),
        name="expo",
    )(ids, streamed(logits), kind, filt, *[streamed(expr)] * 4)


def pred_kernel(ids, expr_a, expr_b, keep, masses, *refs):
    outs = refs[len(refs) // 2 :] if len(refs) > 2 else refs
    rows = 2 * expr_a.shape[0] * expr_a.shape[2]
    weighted = jnp.concatenate(
        [part[...].reshape(rows // 2, keep.shape[1]) for part in (expr_a, expr_b)]
    )
    part = product(split(weighted * keep[...]), masses, ((1,), (0,)))
    for step, out in enumerate(outs):

        @pl.when(pl.program_id(0) == step)
        def _(step=step, out=out):
            if len(refs) > 2:
                out[...] = part.reshape(out.shape) + refs[step][...]
            else:
                out[...] = part.reshape(out.shape)


def pred_call(ids, parts, expr, keep, masses, more=()):
    blocks, groups, rows, cells = expr.shape
    spots = masses.shape[2]

    def genes(sub):
        def place(i, ids):
            step, half = (pick(i, [part[k] for part in parts]) for k in range(2))
            return (0, gene_group(ids, step, half, sub), 0, 0)

        return pl.BlockSpec((blocks, 1, rows, cells), place)

    return pl.pallas_call(
        pred_kernel,
        grid_spec=pltpu.PrefetchScalarGridSpec(
            num_scalar_prefetch=1,
            grid=(2,),
            in_specs=[
                genes(0),
                genes(1),
                fixed((1, cells)),
                RESIDENT,
            ]
            + [fixed((2, blocks, rows, spots))] * len(more),
            out_specs=[fixed((2, blocks, rows, spots))] * 2,
        ),
        out_shape=[jax.ShapeDtypeStruct((2, blocks, rows, spots), F32)] * 2,
        compiler_params=vmem(16),
        cost_estimate=cost(24 * blocks * rows * cells * spots, 4 * cells * spots + 16 * blocks * rows * (cells + spots)),
        name="pred",
    )(ids, *[streamed(expr)] * 2, keep, masses, *more)


def merge_kernel(own0, own1, got0, got1, *outs):
    for half, (own, got) in enumerate(((own0, got0), (own1, got1))):
        for sub in range(2):
            outs[2 * half + sub][...] = own[sub] + got[sub]


def merge_call(own, got):
    shape = own[0].shape[1:]
    block = (2, *shape[1:])
    return pl.pallas_call(
        merge_kernel,
        grid=(shape[0] // 2,),
        in_specs=[pl.BlockSpec((2, *block), lambda i: (0, i, 0, 0))] * 4,
        out_specs=[pl.BlockSpec(block, lambda i: (i, 0, 0))] * 4,
        out_shape=[jax.ShapeDtypeStruct(shape, F32)] * 4,
        compiler_params=vmem(12),
        cost_estimate=NO_COST,
        name="merge",
    )(*own, *got)


def stats_kernel(ids, piece, spatial, spot, cell_sums, gene, slide_sums):
    rows = piece.shape[0] * piece.shape[1]
    valid, share, mass, slide = (spot[k : k + 1, :] for k in range(4))
    value = piece[...].reshape(rows, piece.shape[2]) * share
    data = spatial[...].reshape(value.shape)
    cross, square = value * data, value * value
    lane = lax.broadcasted_iota(jnp.int32, (rows, 128), 1)
    sums = jnp.zeros((rows, 128), F32)
    for index, one in enumerate((cross, square, data * data)):
        sums = jnp.where(lane == index, jnp.sum(one * valid, axis=1, keepdims=True), sums)
    sums = sums.T
    gene[...] = jnp.zeros_like(gene)
    slide_sums[...] = jnp.zeros_like(slide_sums)
    for index in range(3):
        gene[pl.ds(16 * index + gene_group(ids, 0, 0, 0), 1), :] = sums[index : index + 1, :]
    lane = lax.broadcasted_iota(jnp.int32, (1, 128), 1)
    slides = jnp.zeros((1, 128), F32)
    logs = jnp.log(jnp.where(valid > 0, mass, 1.0))
    for k in range(SLIDES):
        inside = jnp.where(slide == k, valid, 0.0)
        for index, one in enumerate((inside, inside * mass, inside * logs)):
            total = jnp.sum(one, axis=1, keepdims=True)
            slides = jnp.where(lane == 3 * index + k, total, slides)
    slide_sums[0:1, :] = slides
    gene[64:65, :] = cell_sums[...]
    for index, one in enumerate((cross, square)):
        total = jnp.sum(one, axis=0, keepdims=True)
        for k in range(total.shape[1] // 128):
            at = 48 + 8 * index + k
            gene[at : at + 1, :] = total[:, 128 * k : 128 * k + 128]


def stats_call(ids, piece, spatial, spot, cell_sums):
    blocks, rows, spots = piece.shape
    return pl.pallas_call(
        stats_kernel,
        grid_spec=pltpu.PrefetchScalarGridSpec(
            num_scalar_prefetch=1,
            grid=(1,),
            in_specs=[
                fixed((blocks, rows, spots)),
                pl.BlockSpec((blocks, 1, rows, spots), lambda i, ids: (0, gene_group(ids, 0, 0, 0), 0, 0)),
                fixed((8, spots)),
                fixed((1, 128)),
            ],
            out_specs=[fixed((72, 128)), fixed((8, 128))],
        ),
        out_shape=[jax.ShapeDtypeStruct((72, 128), F32), jax.ShapeDtypeStruct((8, 128), F32)],
        compiler_params=vmem(8),
        cost_estimate=NO_COST,
        name="stats",
    )(ids, piece, streamed(spatial), spot, cell_sums)


def coef_kernel(ids, genes_slides, sums, spot, gene, rows, scalars, pairs):
    valid, share, mass, slide, squares = (spot[k : k + 1, :] for k in range(5))
    genes = float(16 * sums.shape[1])

    def wide(index):
        return jnp.concatenate([sums[index + k : index + k + 1, :] for k in range(8)], axis=1)

    dots, own = wide(48), wide(56)
    dot, aa, bb = genes_slides[0:16, :], genes_slides[16:32, :], genes_slides[32:48, :]
    scale = lax.rsqrt(aa * bb + 1e-06)
    pairs[0:16, :] = dot * scale**3 * bb / genes
    pairs[16:32, :] = scale / genes
    pair = [pairs[pl.ds(k + gene_group(ids, *one), 1), :] for k in (0, 16) for one in PIECES]
    gene[...] = jnp.concatenate([*pair, jnp.zeros((96, 128), F32)]).T
    total = jnp.sum(jnp.sum(dot * scale, axis=1, keepdims=True), axis=0, keepdims=True)
    nvs = jnp.zeros((1, 1), F32)
    density = jnp.zeros((1, 1), F32)
    nk, tk = jnp.ones_like(valid), jnp.ones_like(valid)
    for k in range(SLIDES):
        count, held, logs = (genes_slides[48:49, 3 * j + k : 3 * j + k + 1] for j in range(3))
        some = count > 0
        safe = jnp.where(some, count, 1.0)
        nvs += count
        density += jnp.where(some, jnp.log(jnp.where(some, held, 1.0) / safe) - logs / safe, 0.0)
        here = (slide == k) & (valid > 0)
        nk = jnp.where(here, count, nk)
        tk = jnp.where(here, held, tk)
    scale = lax.rsqrt(own * squares + 1e-06)
    grad_mass = valid / SLIDES * (1.0 / tk - 1.0 / (nk * jnp.where(valid > 0, mass, 1.0)))
    mask = valid * share
    by_pred, by_data = dots * scale**3 * squares / nvs, scale / nvs
    for index, one in enumerate((by_pred * share * mask, by_data * mask, mask, share * mask)):
        rows[8 * index : 8 * index + 8, :] = jnp.broadcast_to(one, (8, one.shape[1]))
    rows[32:40, :] = jnp.concatenate([grad_mass * share, jnp.zeros((7, valid.shape[1]), F32)])
    cosines = jnp.sum(valid * dots * scale, axis=1, keepdims=True)
    lane = lax.broadcasted_iota(jnp.int32, (1, 128), 1)
    out = jnp.zeros((1, 128), F32)
    for index, one in enumerate((total / genes, cosines / nvs, density / SLIDES)):
        out = jnp.where(lane == index, one, out)
    scalars[...] = out


def coef_call(ids, genes_slides, sums, spot):
    spots = spot.shape[1]
    return pl.pallas_call(
        coef_kernel,
        grid_spec=pltpu.PrefetchScalarGridSpec(
            num_scalar_prefetch=1,
            grid=(1,),
            in_specs=[fixed(genes_slides.shape), fixed(sums.shape), fixed((8, spots))],
            out_specs=[fixed((128, 128)), fixed((40, spots)), fixed((1, 128))],
            scratch_shapes=[pltpu.VMEM((32, 128), F32)],
        ),
        out_shape=[
            jax.ShapeDtypeStruct((128, 128), F32),
            jax.ShapeDtypeStruct((40, spots), F32),
            jax.ShapeDtypeStruct((1, 128), F32),
        ],
        compiler_params=vmem(6),
        cost_estimate=NO_COST,
        name="coef",
    )(ids, genes_slides, sums, spot)


def grad_rows(pred, data, gene, spot, lane):
    by_pred = gene[:, lane : lane + 1].reshape(2, 8, 1)
    by_data = gene[:, 16 + lane : 17 + lane].reshape(2, 8, 1)
    pred, data = pred.reshape(2, 8, pred.shape[1]), data.reshape(2, 8, data.shape[1])
    grad = pred * (by_pred * spot[24:32, :] + spot[0:8, :])
    grad = grad - data * (by_data * spot[16:24, :] + spot[8:16, :])
    return grad.reshape(16, grad.shape[2]), jnp.sum(grad * pred, axis=0)


def grad_kernel(ids, *refs, count, lane):
    pred, data, refs = refs[: 2 * count], refs[2 * count : 3 * count], refs[3 * count :]
    gene, spot, grad, column = refs[0], refs[1], refs[-2], refs[-1]

    @pl.when(pl.program_id(0) == 0)
    def _():
        column[...] = jnp.zeros_like(column)

    total = jnp.zeros(column.shape, F32)
    for index, part in enumerate(pred):
        for sub in range(2):
            at = gene_group(ids, *PIECES[lane + 2 * index + sub])
            row = pl.multiple_of(at % RING * 16, 16)
            rows, inner = grad_rows(
                part[sub, 0], data[index // 2][0, 0, pl.ds(row, 16), :], gene, spot, lane + 2 * index + sub
            )
            if count > 1:
                row = pl.multiple_of(at * 16, 16)
            grad[0, 0, pl.ds(row, 16), :], grad[1, 0, pl.ds(row, 16), :] = split(rows)
            total += inner
    column[...] += total


def grad_call(ids, pred, spatial, gene, spot, lane, done=()):
    blocks, groups, rows, spots = spatial.shape
    count = len(pred) // 2
    if count > 1:
        grad = pl.BlockSpec((2, 1, groups * rows, spots), lambda i, ids: (0, i, 0, 0))
    else:
        grad = pl.BlockSpec((2, 1, rows, spots), lambda i, ids: (0, i, (ids[0] + PIECES[lane][0]) & 3, 0))

    def group(k):
        step = PIECES[lane + 4 * k][0]
        return pl.BlockSpec((1, 1, rows, spots), lambda i, ids: (i, (ids[0] + step) & 3, 0, 0))

    return pl.pallas_call(
        functools.partial(grad_kernel, count=count, lane=lane),
        grid_spec=pltpu.PrefetchScalarGridSpec(
            num_scalar_prefetch=1,
            grid=(blocks,),
            in_specs=[pl.BlockSpec((2, 1, 16, spots), lambda i, ids: (0, i, 0, 0))] * (2 * count)
            + [group(k) for k in range(count)]
            + [pl.BlockSpec((16, 128), lambda i, ids: (i, 0)), fixed(spot.shape)]
            + [pl.BlockSpec(memory_space=pl.ANY)] * len(done),
            out_specs=[grad, fixed((8, spots))],
        ),
        out_shape=[
            jax.ShapeDtypeStruct((2, blocks, groups * rows, spots), BF16),
            jax.ShapeDtypeStruct((8, spots), F32),
        ],
        input_output_aliases={3 * count + 3: 0} if done else {},
        compiler_params=vmem(12),
        cost_estimate=NO_COST,
        name="grad",
    )(ids, *pred, *[streamed(spatial)] * count, gene, spot, *done)


def back_kernel(ids, grad, masses, expr, sums, *outs):
    step = pl.program_id(0)

    @pl.when(step == 0)
    def _():
        sums[...] = jnp.zeros_like(sums)

    part = product((grad[0, 0], grad[1, 0]), masses, ((1,), (1,)))
    sums[...] += jnp.sum((part * expr[...]).reshape(-1, 8, part.shape[1]), axis=0)
    for index, out in enumerate(outs):

        @pl.when(step == index)
        def _(out=out):
            out[...] = part


def back_call(ids, parts, grad, masses, expr):
    _, blocks, rows, spots = grad.shape
    cells = masses.shape[1]
    count = len(parts)

    def block(i, ids):
        step, other = (pick(i, [part[k] for part in parts]) for k in range(2))
        return ((ids[2] + step) & 3) * 2 + (ids[3] ^ other)

    return pl.pallas_call(
        back_kernel,
        grid_spec=pltpu.PrefetchScalarGridSpec(
            num_scalar_prefetch=1,
            grid=(count,),
            in_specs=[
                pl.BlockSpec((2, 1, rows, spots), lambda i, ids: (0, block(i, ids), 0, 0)),
                RESIDENT,
                pl.BlockSpec((rows, cells), lambda i, ids: (block(i, ids), 0)),
            ],
            out_specs=[fixed((8, cells))] + [fixed((rows, cells))] * count,
        ),
        out_shape=[jax.ShapeDtypeStruct((8, cells), F32)]
        + [jax.ShapeDtypeStruct((rows, cells), F32)] * count,
        compiler_params=vmem(20),
        cost_estimate=NO_COST,
        name="back",
    )(ids, grad, masses, streamed(expr))


def mass_kernel(spot, masses, out):
    out[...] = product(split(spot[...]), masses, ((1,), (1,)))


def mass_call(spot, masses):
    _, cells, spots = masses.shape
    return pl.pallas_call(
        mass_kernel,
        grid=(1,),
        in_specs=[fixed((8, spots)), RESIDENT],
        out_specs=fixed((8, cells)),
        out_shape=jax.ShapeDtypeStruct((8, cells), F32),
        compiler_params=vmem(8),
        cost_estimate=pl.CostEstimate(flops=10**9, bytes_accessed=0, transcendentals=0),
        name="mass",
    )(spot, masses)


def map_kernel(expr, grad, masses, keep, spot, *rest, scale, start):
    out = rest[-1]
    step = pl.program_id(0) + start
    inner = product(split(expr[...]), grad, ((0,), (0,))) + spot[0:1, :]
    expo = masses[0].astype(F32) + masses[1].astype(F32)
    for part in range(expr.shape[1] // 128):
        rows = slice(part * 128, part * 128 + 128)
        weight = as_column(keep[pl.ds(step * (expr.shape[1] // 128) + part, 1), :])
        out[rows, :] = (scale * expo[rows]) * (weight * inner[rows] - spot[1:2, :])


def map_call(start, stop, expr, grad, masses, keep, spot, scale, done=()):
    genes, cells = expr.shape
    spots = masses.shape[2]
    block = 256
    return pl.pallas_call(
        functools.partial(map_kernel, scale=scale, start=start),
        grid=(stop - start,),
        in_specs=[
            pl.BlockSpec((genes, block), lambda i: (0, i + start)),
            RESIDENT,
            pl.BlockSpec((2, block, spots), lambda i: (0, i + start, 0)),
            fixed(keep.shape),
            fixed((8, spots)),
        ]
        + [pl.BlockSpec(memory_space=pl.ANY)] * len(done),
        out_specs=pl.BlockSpec((block, spots), lambda i: (i + start, 0)),
        out_shape=jax.ShapeDtypeStruct((cells, spots), F32),
        input_output_aliases={5: 0} if done else {},
        compiler_params=vmem(24),
        cost_estimate=NO_COST,
        name="grad_map",
    )(streamed(expr), grad, masses, keep, spot, *done)


def finish_kernel(last, got, sums, scalars, kind, filt, grad_filter, terms, *, all_cells):
    blocks = kind.shape[0]
    total = last[...] + got[...]
    nvalid, retained, reg_sum = (sums[64:65, k : k + 1] for k in range(3))
    valid = (kind[...] >= 0).astype(F32)
    sigma = jax.nn.sigmoid(filt[...])
    keep = sigma * valid
    shifted = (retained - 0.35 * nvalid) / (0.1 * all_cells)
    count_term = jnp.sqrt(shifted * shifted + 1.0)
    grad_keep = total[:blocks] + shifted / count_term / (0.1 * all_cells) + (1.0 - 2.0 * keep) / nvalid
    grad_filter[...] = valid * sigma * (1.0 - sigma) * grad_keep * all_cells
    lane = lax.broadcasted_iota(jnp.int32, (1, 128), 1)
    out = jnp.zeros((1, 128), F32)
    parts = (scalars[:, 0:1], total[blocks : blocks + 1, 1:2], scalars[:, 2:3], count_term, reg_sum / nvalid)
    for index, one in enumerate(parts):
        out = jnp.where(lane == index, one, out)
    terms[...] = out


def finish_call(last, got, sums, scalars, kind, filt, all_cells):
    return pl.pallas_call(
        functools.partial(finish_kernel, all_cells=float(all_cells)),
        grid=(1,),
        in_specs=[fixed(one.shape) for one in (last, got, sums, scalars, kind, filt)],
        out_specs=[fixed(kind.shape), fixed((1, 128))],
        out_shape=[jax.ShapeDtypeStruct(kind.shape, F32), jax.ShapeDtypeStruct((1, 128), F32)],
        compiler_params=vmem(4),
        cost_estimate=NO_COST,
        name="finish",
    )(last, got, sums, scalars, kind, filt)


def on_device(map_logits, filter_logits, expr, spatial, cell_type, slide_id, spot_mask):
    genes, cells = expr.shape
    spots = map_logits.shape[1]
    all_cells = cells * lax.axis_size("cells")
    all_spots = spots * lax.axis_size("spots")
    cell_place = lax.axis_index("cells")
    z, x = cell_place >> 2, cell_place & 3
    spot_place = lax.axis_index("spots")
    y, core = spot_place >> 1, spot_place & 1
    first = jnp.where(core == 0, x, z)
    second = jnp.where(core == 0, z, x)
    blocks = cells // 128

    valid = (cell_type >= 0).astype(F32)
    sigma = jax.nn.sigmoid(filter_logits)
    keep = sigma * valid
    spot_valid = spot_mask.astype(F32)
    kind2 = cell_type.reshape(blocks, 128)
    filt2 = filter_logits.reshape(blocks, 128)
    keep2 = keep.reshape(blocks, 128)

    expr4 = expr.reshape(8, 16, 16, cells)
    keep_row = keep.reshape(1, cells)

    ids = jnp.stack([first, second, y, core]).astype(jnp.int32)

    def pred_part(one, two, more, *others):
        return pred_call(after(ids, *others), (one, two), expr4, keep_row, masses, more)

    masses, types, totals, *far = expo_call(
        ids, ((2, 0), (2, 1)), map_logits, kind2, filt2, expr4
    )
    far_right, far_left = along(far[0], 1), along(far[1], -1)
    near = pred_part((1, 1), (-1, 0), (), *far)
    near_right, near_left = along(near[0], 1), along(near[1], -1)
    totals = totals + swap_across(totals, 1)
    late = pred_part((1, 0), (-1, 1), (far_right, far_left), totals, *near)
    late_right, late_left = along(late[0], 1), along(late[1], -1)
    totals = totals + swap_across(totals, 3)
    own = pred_part((0, 0), (0, 1), (near_left, near_right), totals, *late)
    mine, *pieces = merge_call(own, (late_right, late_left))
    pieces = [across(piece, step + 1) for step, piece in enumerate(pieces)]
    totals = totals + swap_along(after(totals, mine), 1)
    totals = totals + swap_along(totals, 3)
    spatial_squares = jnp.sum(after(spatial, mine) ** 2, axis=0)
    share = 1.0 / totals[0]
    mass = totals[1] * share
    spot_rows = stacked([spot_valid, share, mass, slide_id.astype(F32), spatial_squares])
    piece = after(mine + pieces[0] + pieces[1] + pieces[2], spot_rows)

    got = [across(piece, step) for step in (1, 2, 3)]
    cell_sums = jnp.stack([jnp.sum(valid), jnp.sum(keep), jnp.sum(keep - keep * keep)])
    sums, slides = stats_call(
        ids,
        piece,
        spatial.reshape(8, 16, 16, spots),
        spot_rows,
        jnp.pad(cell_sums[None], ((0, 0), (0, 125))),
    )
    sums = sums + swap_along(sums, 1)
    sums = sums + swap_along(sums, 3)
    mine = after((jnp.stack([piece, got[2]]), jnp.stack([got[1], got[0]])), sums)
    right0, left1 = along(mine[0], 1), along(mine[1], -1)
    right1, left0 = along(mine[1], 1), along(mine[0], -1)
    sums = sums + swap_across(after(sums, *mine), 1)
    sums = sums + swap_across(sums, 3)
    right0, left1, sums = lax.optimization_barrier((right0, left1, sums))
    far0, far1 = along(right0, 1), along(left1, -1)
    genes_slides = jnp.concatenate([sums[:48], slides])
    genes_slides = genes_slides + swap(genes_slides, 0, 0, 0, 1)
    genes_slides = genes_slides + swap(genes_slides, 0, 0, 1, 0)
    genes_slides = after(genes_slides, right1, left0)
    genes_slides = genes_slides + swap(genes_slides, 0, 0, 3, 0)
    pred = [*mine, right0, right1, left0, left1, far0, far1]
    gene_coef, spot_coef, scalars = coef_call(ids, genes_slides, sums, spot_rows)
    spatial4 = spatial.reshape(8, RING, genes // 32, spots)
    grad, column_a = grad_call(ids, pred[:6], spatial4, gene_coef, spot_coef, 0)
    types = types + swap(after(types, sums), 1, 0, 0, 0)
    grad, column_b = grad_call(ids, pred[6:], spatial4, gene_coef, spot_coef, 12, (after(grad, types),))

    def back_part(steps, *others):
        return back_call(after(ids, *others), steps, grad, masses, expr)

    rows = genes // 16
    sums_a, far_a = back_part([(2, 1)])
    types = types + swap(after(types, far_a), 3, 0, 0, 0)
    far_got = swap(far_a, 0, 0, 0, 1)
    sums_b, far_b = back_part([(2, 0)], far_a)
    far = far_b + far_got
    far_up, far_down = up(far[:rows], 1), up(far[rows:], -1)
    sums_c, up_a, down_a = back_part([(1, 1), (-1, 1)], far, types)
    up_got, down_got = swap(up_a, 0, 0, 0, 1), swap(down_a, 0, 0, 0, 1)
    sums_d, up_b, down_b = back_part([(1, 0), (-1, 0)], up_a)
    sums_e, own_a, own_b = back_part([(0, 1), (0, 0)], up_b)
    sums_0 = mass_call(after(spot_coef, own_b, far_up, far_down)[32:40], masses)
    far_up, far_down = after((far_up, far_down), sums_0)
    above = jnp.concatenate([up_b[:rows] + up_got[:rows] + far_up, up_b[rows:] + up_got[rows:]])
    below = jnp.concatenate([down_b[:rows] + down_got[:rows], down_b[rows:] + down_got[rows:] + far_down])
    near_up, near_down = up(above, 1), up(below, -1)
    own_a = jnp.concatenate([swap(own_a[:rows], 0, 0, 0, 1), swap(own_a[rows:], 0, 0, 0, 1)])
    last = jnp.concatenate(
        [
            jnp.sum(sums_0 + sums_a + sums_b + sums_c + sums_d + sums_e, axis=0).reshape(blocks, 128),
            scalars,
            jnp.zeros((5, 128), F32),
        ]
    )

    column = jnp.sum(column_a + column_b, axis=0) * share + spot_coef[32] * mass
    map_rows = stacked([spot_coef[32], column])
    map_rows = after(map_rows, above, below)
    map_args = (expr, grad.reshape(2, genes, spots), masses, keep2, map_rows, all_cells * genes)
    steps = cells // 256
    got, types_got = swap(last, 0, 0, 0, 1), swap(after(types, own_b), 0, 1, 0, 0)
    grad_map = map_call(0, steps - 2, *map_args)
    got, types_got = after((got, types_got), grad_map)
    last, types = last + got, types + types_got
    got, types_got = swap(last, 0, 0, 1, 0), swap(types, 0, 3, 0, 0)
    grad_map = map_call(steps - 2, steps, *map_args, done=(after(grad_map, own_a),))
    got, types_got = after((got, types_got), grad_map)
    last, types = last + got, types + types_got
    got = swap(last, 0, 0, 3, 0)
    grad_weighted = after(own_b + own_a, grad_map) + near_up + near_down
    grad_expr = grad_weighted * (keep * (genes * all_spots))[None, :]

    type_fraction = types * share

    grad_filter, loss_terms = finish_call(last, got, sums, scalars, kind2, filt2, all_cells)
    return (loss_terms[0, :5], type_fraction, grad_map, grad_filter.reshape(cells), grad_expr)


def solution(mesh):
    in_specs = (
        P("cells", "spots"),
        P("cells"),
        P(None, "cells"),
        P(None, "spots"),
        P("cells"),
        P("spots"),
        P("spots"),
    )
    out_specs = (P(), P(None, "spots"), P("cells", "spots"), P("cells"), P("spots", "cells"))
    return jax.shard_map(
        on_device, mesh=mesh, in_specs=in_specs, out_specs=out_specs, check_vma=False
    )
```

```python
import functools

import jax
import jax.numpy as jnp
from jax import lax
from jax.experimental import pallas as pl
from jax.experimental.pallas import tpu as pltpu
from jax.sharding import PartitionSpec as P

TYPES = 32
SLIDES = 3
RING = 4
F32 = jnp.float32
BF16 = jnp.bfloat16


def vmem(mib):
    return pltpu.CompilerParams(vmem_limit_bytes=mib << 20)


def fixed(shape):
    return pl.BlockSpec(shape, lambda *_: (0,) * len(shape), pipeline_mode=pl.Buffered(1))


def streamed(array):
    return pltpu.with_memory_space_constraint(array, pltpu.HBM)


RESIDENT = pl.BlockSpec(memory_space=pltpu.VMEM)


def cost(flops, moved):
    return pl.CostEstimate(flops=int(flops) // 8, bytes_accessed=int(moved) // 8, transcendentals=0)


NO_COST = pl.CostEstimate(flops=0, bytes_accessed=0, transcendentals=0)


def route(target):
    def flat(z, x, y, core):
        return ((z % RING * RING + x % RING) * RING + y % RING) * 2 + core

    return [
        (flat(z, x, y, core), flat(*target(z, x, y, core)))
        for z in range(RING)
        for x in range(RING)
        for y in range(RING)
        for core in range(2)
    ]


def send(array, target):
    return lax.ppermute(array, ("cells", "spots"), route(target))


def along(array, step):
    return send(array, lambda z, x, y, c: (z, x + step, y, c) if c == 0 else (z + step, x, y, c))


def across(array, step):
    return send(array, lambda z, x, y, c: (z + step, x, y, c) if c == 0 else (z, x + step, y, c))


def up(array, step):
    return send(array, lambda z, x, y, c: (z, x, y + step, c))


def swap(array, mz, mx, my, mc):
    return send(array, lambda z, x, y, c: (z ^ mz, x ^ mx, y ^ my, c ^ mc))


def swap_along(array, mask):
    return send(array, lambda z, x, y, c: (z, x ^ mask, y, c) if c == 0 else (z ^ mask, x, y, c))


def swap_across(array, mask):
    return send(array, lambda z, x, y, c: (z ^ mask, x, y, c) if c == 0 else (z, x ^ mask, y, c))


def after(value, *others):
    return lax.optimization_barrier((value, *others))[0]


def split(value):
    high = value.astype(BF16)
    return high, (value - high.astype(F32)).astype(BF16)


def product(left, right, dims):
    def one(a, b):
        return lax.dot_general(a, b, (dims, ((), ())), preferred_element_type=F32)

    return one(left[0], right[0]) + one(left[0], right[1]) + one(left[1], right[0])


def gene_group(ids, step, half, sub):
    return ((ids[0] + step) & 3) * RING + ((ids[1] + 2 * half + sub) & 3)


PIECES = [
    (step, half, sub)
    for step, half in ((0, 0), (0, 1), (-1, 0), (-1, 1), (1, 0), (1, 1), (2, 0), (2, 1))
    for sub in range(2)
]


def pick(index, values):
    out = values[0]
    for k, value in enumerate(values[1:]):
        out = jnp.where(index == k + 1, value, out)
    return out


def stacked(rows):
    row = lax.broadcasted_iota(jnp.int32, (8, rows[0].shape[0]), 0)
    out = jnp.zeros(row.shape, F32)
    for k, value in enumerate(rows):
        out = jnp.where(row == k, value[None, :], out)
    return out


def as_column(row):
    return jnp.broadcast_to(row, (128, 128)).T[:, :1]


def expo_kernel(ids, logits, kind, filt, *refs):
    expr, (masses, types, totals, out0, out1) = refs[:4], refs[4:]
    step = pl.program_id(0)
    count = logits.shape[0] // 128

    @pl.when(step == 0)
    def _():
        for out in (types, totals, out0, out1):
            out[...] = jnp.zeros_like(out)

    keeps = []
    lane = lax.broadcasted_iota(jnp.int32, (1, totals.shape[1]), 1)
    cell_sums = jnp.zeros(lane.shape, F32)
    for part in range(count):
        rows = slice(part * 128, part * 128 + 128)
        label = kind[pl.ds(step * count + part, 1), :]
        valid = (label >= 0).astype(F32)
        keep = valid * jax.nn.sigmoid(filt[pl.ds(step * count + part, 1), :])
        keeps.append(keep)
        for k, one in enumerate((valid, keep, keep - keep * keep)):
            cell_sums += jnp.where(lane == k, jnp.sum(one, axis=1, keepdims=True), 0.0)
        expo = jnp.exp(logits[rows]) * as_column(valid)
        masses[0, rows], masses[1, rows] = split(expo)
        whole = jnp.sum(expo, axis=0, keepdims=True)
        kept = jnp.sum(expo * as_column(keep), axis=0, keepdims=True)
        row = lax.broadcasted_iota(jnp.int32, types.shape, 0)
        types[...] += jnp.where(row == jnp.max(label, axis=1, keepdims=True), whole, 0.0)
        row = lax.broadcasted_iota(jnp.int32, totals.shape, 0)
        totals[...] += jnp.where(row == 0, whole, jnp.where(row == 1, kept, 0.0))
    totals[2:3, :] += cell_sums
    weighted = jnp.concatenate([part[...].reshape(-1, logits.shape[0]) for part in expr])
    weighted = weighted * jnp.concatenate(keeps, axis=1)
    part = product(split(weighted), masses, ((1,), (0,)))
    half = part.shape[0] // 2
    out0[...] += part[:half].reshape(out0.shape)
    out1[...] += part[half:].reshape(out1.shape)


def expo_call(ids, parts, logits, kind, filt, expr):
    cells, spots = logits.shape
    blocks, groups, rows, _ = expr.shape
    block = 256

    def genes(part, sub):
        return pl.BlockSpec(
            (blocks, 1, rows, block), lambda i, ids: (0, gene_group(ids, *part, sub), 0, i)
        )

    return pl.pallas_call(
        expo_kernel,
        grid_spec=pltpu.PrefetchScalarGridSpec(
            num_scalar_prefetch=1,
            grid=(cells // block,),
            in_specs=[
                pl.BlockSpec((block, spots), lambda i, w: (i, 0)),
                fixed(kind.shape),
                fixed(filt.shape),
            ]
            + [genes(part, sub) for part in parts for sub in range(2)],
            out_specs=[
                pl.BlockSpec((2, block, spots), lambda i, w: (0, i, 0)),
                fixed((TYPES, spots)),
                fixed((8, spots)),
                fixed((2, blocks, rows, spots)),
                fixed((2, blocks, rows, spots)),
            ],
        ),
        out_shape=[
            jax.ShapeDtypeStruct((2, cells, spots), BF16),
            jax.ShapeDtypeStruct((TYPES, spots), F32),
            jax.ShapeDtypeStruct((8, spots), F32),
            jax.ShapeDtypeStruct((2, blocks, rows, spots), F32),
            jax.ShapeDtypeStruct((2, blocks, rows, spots), F32),
        ],
        compiler_params=vmem(16),
        cost_estimate=cost(0, cells * spots * 8),
        name="expo",
    )(ids, streamed(logits), kind, filt, *[streamed(expr)] * 4)


def pred_kernel(ids, expr_a, expr_b, keep, masses, *refs):
    outs = refs[len(refs) // 2 :] if len(refs) > 2 else refs
    rows = 2 * expr_a.shape[0] * expr_a.shape[2]
    weighted = jnp.concatenate(
        [part[...].reshape(rows // 2, keep.shape[1]) for part in (expr_a, expr_b)]
    )
    part = product(split(weighted * keep[...]), masses, ((1,), (0,)))
    for step, out in enumerate(outs):

        @pl.when(pl.program_id(0) == step)
        def _(step=step, out=out):
            if len(refs) > 2:
                out[...] = part.reshape(out.shape) + refs[step][...]
            else:
                out[...] = part.reshape(out.shape)


def pred_call(ids, parts, expr, keep, masses, more=()):
    blocks, groups, rows, cells = expr.shape
    spots = masses.shape[2]

    def genes(sub):
        def place(i, ids):
            step, half = (pick(i, [part[k] for part in parts]) for k in range(2))
            return (0, gene_group(ids, step, half, sub), 0, 0)

        return pl.BlockSpec((blocks, 1, rows, cells), place)

    return pl.pallas_call(
        pred_kernel,
        grid_spec=pltpu.PrefetchScalarGridSpec(
            num_scalar_prefetch=1,
            grid=(2,),
            in_specs=[
                genes(0),
                genes(1),
                fixed((1, cells)),
                RESIDENT,
            ]
            + [fixed((2, blocks, rows, spots))] * len(more),
            out_specs=[fixed((2, blocks, rows, spots))] * 2,
        ),
        out_shape=[jax.ShapeDtypeStruct((2, blocks, rows, spots), F32)] * 2,
        compiler_params=vmem(16),
        cost_estimate=cost(24 * blocks * rows * cells * spots, 4 * cells * spots + 16 * blocks * rows * (cells + spots)),
        name="pred",
    )(ids, *[streamed(expr)] * 2, keep, masses, *more)


def merge_kernel(own0, own1, got0, got1, *outs):
    for half, (own, got) in enumerate(((own0, got0), (own1, got1))):
        for sub in range(2):
            outs[2 * half + sub][...] = own[sub] + got[sub]


def merge_call(own, got):
    shape = own[0].shape[1:]
    block = (2, *shape[1:])
    return pl.pallas_call(
        merge_kernel,
        grid=(shape[0] // 2,),
        in_specs=[pl.BlockSpec((2, *block), lambda i: (0, i, 0, 0))] * 4,
        out_specs=[pl.BlockSpec(block, lambda i: (i, 0, 0))] * 4,
        out_shape=[jax.ShapeDtypeStruct(shape, F32)] * 4,
        compiler_params=vmem(12),
        cost_estimate=NO_COST,
        name="merge",
    )(*own, *got)


def stats_kernel(ids, piece, spatial, spot, gene, slide_sums):
    rows = piece.shape[0] * piece.shape[1]
    valid, share, mass, slide = (spot[k : k + 1, :] for k in range(4))
    value = piece[...].reshape(rows, piece.shape[2]) * share
    data = spatial[...].reshape(value.shape)
    cross, square = value * data, value * value
    lane = lax.broadcasted_iota(jnp.int32, (rows, 128), 1)
    sums = jnp.zeros((rows, 128), F32)
    for index, one in enumerate((cross, square, data * data)):
        sums = jnp.where(lane == index, jnp.sum(one * valid, axis=1, keepdims=True), sums)
    sums = sums.T
    gene[...] = jnp.zeros_like(gene)
    slide_sums[...] = jnp.zeros_like(slide_sums)
    for index in range(3):
        gene[pl.ds(16 * index + gene_group(ids, 0, 0, 0), 1), :] = sums[index : index + 1, :]
    lane = lax.broadcasted_iota(jnp.int32, (1, 128), 1)
    slides = jnp.zeros((1, 128), F32)
    logs = jnp.log(jnp.where(valid > 0, mass, 1.0))
    for k in range(SLIDES):
        inside = jnp.where(slide == k, valid, 0.0)
        for index, one in enumerate((inside, inside * mass, inside * logs)):
            total = jnp.sum(one, axis=1, keepdims=True)
            slides = jnp.where(lane == 3 * index + k, total, slides)
    slide_sums[0:1, :] = slides
    for index, one in enumerate((cross, square)):
        total = jnp.sum(one, axis=0, keepdims=True)
        for k in range(total.shape[1] // 128):
            at = 48 + 8 * index + k
            gene[at : at + 1, :] = total[:, 128 * k : 128 * k + 128]


def stats_call(ids, piece, spatial, spot):
    blocks, rows, spots = piece.shape
    return pl.pallas_call(
        stats_kernel,
        grid_spec=pltpu.PrefetchScalarGridSpec(
            num_scalar_prefetch=1,
            grid=(1,),
            in_specs=[
                fixed((blocks, rows, spots)),
                pl.BlockSpec((blocks, 1, rows, spots), lambda i, ids: (0, gene_group(ids, 0, 0, 0), 0, 0)),
                fixed((8, spots)),
            ],
            out_specs=[fixed((64, 128)), fixed((8, 128))],
        ),
        out_shape=[jax.ShapeDtypeStruct((64, 128), F32), jax.ShapeDtypeStruct((8, 128), F32)],
        compiler_params=vmem(8),
        cost_estimate=NO_COST,
        name="stats",
    )(ids, piece, streamed(spatial), spot)


def coef_kernel(ids, genes_slides, sums, spot, gene, rows, scalars, pairs):
    valid, share, mass, slide, squares = (spot[k : k + 1, :] for k in range(5))
    genes = float(16 * sums.shape[1])

    def wide(index):
        return jnp.concatenate([sums[index + k : index + k + 1, :] for k in range(8)], axis=1)

    dots, own = wide(48), wide(56)
    dot, aa, bb = genes_slides[0:16, :], genes_slides[16:32, :], genes_slides[32:48, :]
    scale = lax.rsqrt(aa * bb + 1e-06)
    pairs[0:16, :] = dot * scale**3 * bb / genes
    pairs[16:32, :] = scale / genes
    pair = [pairs[pl.ds(k + gene_group(ids, *one), 1), :] for k in (0, 16) for one in PIECES]
    gene[...] = jnp.concatenate([*pair, jnp.zeros((96, 128), F32)]).T
    total = jnp.sum(jnp.sum(dot * scale, axis=1, keepdims=True), axis=0, keepdims=True)
    nvs = jnp.zeros((1, 1), F32)
    density = jnp.zeros((1, 1), F32)
    nk, tk = jnp.ones_like(valid), jnp.ones_like(valid)
    for k in range(SLIDES):
        count, held, logs = (genes_slides[48:49, 3 * j + k : 3 * j + k + 1] for j in range(3))
        some = count > 0
        safe = jnp.where(some, count, 1.0)
        nvs += count
        density += jnp.where(some, jnp.log(jnp.where(some, held, 1.0) / safe) - logs / safe, 0.0)
        here = (slide == k) & (valid > 0)
        nk = jnp.where(here, count, nk)
        tk = jnp.where(here, held, tk)
    scale = lax.rsqrt(own * squares + 1e-06)
    grad_mass = valid / SLIDES * (1.0 / tk - 1.0 / (nk * jnp.where(valid > 0, mass, 1.0)))
    mask = valid * share
    by_pred, by_data = dots * scale**3 * squares / nvs, scale / nvs
    for index, one in enumerate((by_pred * share * mask, by_data * mask, mask, share * mask)):
        rows[8 * index : 8 * index + 8, :] = jnp.broadcast_to(one, (8, one.shape[1]))
    rows[32:40, :] = jnp.concatenate([grad_mass * share, jnp.zeros((7, valid.shape[1]), F32)])
    cosines = jnp.sum(valid * dots * scale, axis=1, keepdims=True)
    lane = lax.broadcasted_iota(jnp.int32, (1, 128), 1)
    out = jnp.zeros((1, 128), F32)
    for index, one in enumerate((total / genes, cosines / nvs, density / SLIDES)):
        out = jnp.where(lane == index, one, out)
    scalars[...] = out


def coef_call(ids, genes_slides, sums, spot):
    spots = spot.shape[1]
    return pl.pallas_call(
        coef_kernel,
        grid_spec=pltpu.PrefetchScalarGridSpec(
            num_scalar_prefetch=1,
            grid=(1,),
            in_specs=[fixed(genes_slides.shape), fixed(sums.shape), fixed((8, spots))],
            out_specs=[fixed((128, 128)), fixed((40, spots)), fixed((1, 128))],
            scratch_shapes=[pltpu.VMEM((32, 128), F32)],
        ),
        out_shape=[
            jax.ShapeDtypeStruct((128, 128), F32),
            jax.ShapeDtypeStruct((40, spots), F32),
            jax.ShapeDtypeStruct((1, 128), F32),
        ],
        compiler_params=vmem(6),
        cost_estimate=NO_COST,
        name="coef",
    )(ids, genes_slides, sums, spot)


def grad_rows(pred, data, gene, spot, lane):
    by_pred = gene[:, lane : lane + 1].reshape(2, 8, 1)
    by_data = gene[:, 16 + lane : 17 + lane].reshape(2, 8, 1)
    pred, data = pred.reshape(2, 8, pred.shape[1]), data.reshape(2, 8, data.shape[1])
    grad = pred * (by_pred * spot[24:32, :] + spot[0:8, :])
    grad = grad - data * (by_data * spot[16:24, :] + spot[8:16, :])
    return grad.reshape(16, grad.shape[2]), jnp.sum(grad * pred, axis=0)


def grad_kernel(ids, *refs, count, lane):
    pred, data, refs = refs[: 2 * count], refs[2 * count : 3 * count], refs[3 * count :]
    gene, spot, grad, column = refs[0], refs[1], refs[-2], refs[-1]

    @pl.when(pl.program_id(0) == 0)
    def _():
        column[...] = jnp.zeros_like(column)

    total = jnp.zeros(column.shape, F32)
    for index, part in enumerate(pred):
        for sub in range(2):
            at = gene_group(ids, *PIECES[lane + 2 * index + sub])
            row = pl.multiple_of((at & 3) * 16, 16)
            to = pl.ds(pl.multiple_of(at * 16, 16) if count > 1 else row, 16)
            for block in range(part.shape[1]):
                rows, inner = grad_rows(
                    part[sub, block],
                    data[index // 2][block, 0, pl.ds(row, 16), :],
                    gene[16 * block : 16 * block + 16, :],
                    spot,
                    lane + 2 * index + sub,
                )
                grad[0, block, to, :], grad[1, block, to, :] = split(rows)
                total += inner
    column[...] += total


def grad_call(ids, pred, spatial, gene, spot, lane, done=()):
    blocks, groups, rows, spots = spatial.shape
    count = len(pred) // 2
    each = 2
    if count > 1:
        grad = pl.BlockSpec((2, each, groups * rows, spots), lambda i, ids: (0, i, 0, 0))
    else:
        grad = pl.BlockSpec((2, each, rows, spots), lambda i, ids: (0, i, (ids[0] + PIECES[lane][0]) & 3, 0))

    def group(k):
        step = PIECES[lane + 4 * k][0]
        return pl.BlockSpec((each, 1, rows, spots), lambda i, ids: (i, (ids[0] + step) & 3, 0, 0))

    return pl.pallas_call(
        functools.partial(grad_kernel, count=count, lane=lane),
        grid_spec=pltpu.PrefetchScalarGridSpec(
            num_scalar_prefetch=1,
            grid=(blocks // each,),
            in_specs=[pl.BlockSpec((2, each, 16, spots), lambda i, ids: (0, i, 0, 0))] * (2 * count)
            + [group(k) for k in range(count)]
            + [pl.BlockSpec((16 * each, 128), lambda i, ids: (i, 0)), fixed(spot.shape)]
            + [pl.BlockSpec(memory_space=pl.ANY)] * len(done),
            out_specs=[grad, fixed((8, spots))],
        ),
        out_shape=[
            jax.ShapeDtypeStruct((2, blocks, groups * rows, spots), BF16),
            jax.ShapeDtypeStruct((8, spots), F32),
        ],
        input_output_aliases={3 * count + 3: 0} if done else {},
        compiler_params=vmem(16),
        cost_estimate=NO_COST,
        name="grad",
    )(ids, *pred, *[streamed(spatial)] * count, gene, spot, *done)


def back_kernel(ids, grad, masses, expr, sums, *outs):
    step = pl.program_id(0)

    @pl.when(step == 0)
    def _():
        sums[...] = jnp.zeros_like(sums)

    part = product((grad[0, 0], grad[1, 0]), masses, ((1,), (1,)))
    sums[...] += jnp.sum((part * expr[...]).reshape(-1, 8, part.shape[1]), axis=0)
    for index, out in enumerate(outs):

        @pl.when(step == index)
        def _(out=out):
            out[...] = part


def back_call(ids, parts, grad, masses, expr):
    _, blocks, rows, spots = grad.shape
    cells = masses.shape[1]
    count = len(parts)

    def block(i, ids):
        step, other = (pick(i, [part[k] for part in parts]) for k in range(2))
        return ((ids[2] + step) & 3) * 2 + (ids[3] ^ other)

    return pl.pallas_call(
        back_kernel,
        grid_spec=pltpu.PrefetchScalarGridSpec(
            num_scalar_prefetch=1,
            grid=(count,),
            in_specs=[
                pl.BlockSpec((2, 1, rows, spots), lambda i, ids: (0, block(i, ids), 0, 0)),
                RESIDENT,
                pl.BlockSpec((rows, cells), lambda i, ids: (block(i, ids), 0)),
            ],
            out_specs=[fixed((8, cells))] + [fixed((rows, cells))] * count,
        ),
        out_shape=[jax.ShapeDtypeStruct((8, cells), F32)]
        + [jax.ShapeDtypeStruct((rows, cells), F32)] * count,
        compiler_params=vmem(20),
        cost_estimate=NO_COST,
        name="back",
    )(ids, grad, masses, streamed(expr))


def mass_kernel(spot, masses, out):
    out[...] = product(split(spot[...]), masses, ((1,), (1,)))


def mass_call(spot, masses):
    _, cells, spots = masses.shape
    return pl.pallas_call(
        mass_kernel,
        grid=(1,),
        in_specs=[fixed((8, spots)), RESIDENT],
        out_specs=fixed((8, cells)),
        out_shape=jax.ShapeDtypeStruct((8, cells), F32),
        compiler_params=vmem(8),
        cost_estimate=pl.CostEstimate(flops=10**10, bytes_accessed=0, transcendentals=0),
        name="mass",
    )(spot, masses)


def map_kernel(expr, grad, masses, keep, spot, *rest, scale, start):
    out = rest[-1]
    step = pl.program_id(0) + start
    inner = product(split(expr[...]), grad, ((0,), (0,))) + spot[0:1, :]
    expo = masses[0].astype(F32) + masses[1].astype(F32)
    for part in range(expr.shape[1] // 128):
        rows = slice(part * 128, part * 128 + 128)
        weight = as_column(keep[pl.ds(step * (expr.shape[1] // 128) + part, 1), :])
        out[rows, :] = (scale * expo[rows]) * (weight * inner[rows] - spot[1:2, :])


def map_call(start, stop, expr, grad, masses, keep, spot, scale, done=()):
    genes, cells = expr.shape
    spots = masses.shape[2]
    block = 256
    return pl.pallas_call(
        functools.partial(map_kernel, scale=scale, start=start),
        grid=(stop - start,),
        in_specs=[
            pl.BlockSpec((genes, block), lambda i: (0, i + start)),
            RESIDENT,
            pl.BlockSpec((2, block, spots), lambda i: (0, i + start, 0)),
            fixed(keep.shape),
            fixed((8, spots)),
        ]
        + [pl.BlockSpec(memory_space=pl.ANY)] * len(done),
        out_specs=pl.BlockSpec((block, spots), lambda i: (i + start, 0)),
        out_shape=jax.ShapeDtypeStruct((cells, spots), F32),
        input_output_aliases={5: 0} if done else {},
        compiler_params=vmem(24),
        cost_estimate=NO_COST,
        name="grad_map",
    )(streamed(expr), grad, masses, keep, spot, *done)


def finish_kernel(last, got, totals, scalars, kind, filt, grad_filter, terms, *, all_cells):
    blocks = kind.shape[0]
    total = last[...] + got[...]
    nvalid, retained, reg_sum = (totals[2:3, k : k + 1] for k in range(3))
    valid = (kind[...] >= 0).astype(F32)
    sigma = jax.nn.sigmoid(filt[...])
    keep = sigma * valid
    shifted = (retained - 0.35 * nvalid) / (0.1 * all_cells)
    count_term = jnp.sqrt(shifted * shifted + 1.0)
    grad_keep = total[:blocks] + shifted / count_term / (0.1 * all_cells) + (1.0 - 2.0 * keep) / nvalid
    grad_filter[...] = valid * sigma * (1.0 - sigma) * grad_keep * all_cells
    lane = lax.broadcasted_iota(jnp.int32, (1, 128), 1)
    out = jnp.zeros((1, 128), F32)
    parts = (scalars[:, 0:1], total[blocks : blocks + 1, 1:2], scalars[:, 2:3], count_term, reg_sum / nvalid)
    for index, one in enumerate(parts):
        out = jnp.where(lane == index, one, out)
    terms[...] = out


def finish_call(last, got, totals, scalars, kind, filt, all_cells):
    return pl.pallas_call(
        functools.partial(finish_kernel, all_cells=float(all_cells)),
        grid=(1,),
        in_specs=[fixed(one.shape) for one in (last, got, totals, scalars, kind, filt)],
        out_specs=[fixed(kind.shape), fixed((1, 128))],
        out_shape=[jax.ShapeDtypeStruct(kind.shape, F32), jax.ShapeDtypeStruct((1, 128), F32)],
        compiler_params=vmem(4),
        cost_estimate=NO_COST,
        name="finish",
    )(last, got, totals, scalars, kind, filt)


def on_device(map_logits, filter_logits, expr, spatial, cell_type, slide_id, spot_mask):
    genes, cells = expr.shape
    spots = map_logits.shape[1]
    all_cells = cells * lax.axis_size("cells")
    all_spots = spots * lax.axis_size("spots")
    cell_place = lax.axis_index("cells")
    z, x = cell_place >> 2, cell_place & 3
    spot_place = lax.axis_index("spots")
    y, core = spot_place >> 1, spot_place & 1
    first = jnp.where(core == 0, x, z)
    second = jnp.where(core == 0, z, x)
    blocks = cells // 128

    valid = (cell_type >= 0).astype(F32)
    sigma = jax.nn.sigmoid(filter_logits)
    keep = sigma * valid
    spot_valid = spot_mask.astype(F32)
    kind2 = cell_type.reshape(blocks, 128)
    filt2 = filter_logits.reshape(blocks, 128)
    keep2 = keep.reshape(blocks, 128)

    expr4 = expr.reshape(8, 16, 16, cells)
    keep_row = keep.reshape(1, cells)

    ids = jnp.stack([first, second, y, core]).astype(jnp.int32)

    def pred_part(one, two, more, *others):
        return pred_call(after(ids, *others), (one, two), expr4, keep_row, masses, more)

    masses, types, totals, *far = expo_call(
        ids, ((2, 0), (2, 1)), map_logits, kind2, filt2, expr4
    )
    far_right, far_left = along(far[0], 1), along(far[1], -1)
    near = pred_part((1, 1), (-1, 0), (), *far)
    near_right, near_left = along(near[0], 1), along(near[1], -1)
    totals = totals + swap_across(totals, 1)
    late = pred_part((1, 0), (-1, 1), (far_right, far_left), totals, *near)
    late_right, late_left = along(late[0], 1), along(late[1], -1)
    totals = totals + swap_across(totals, 3)
    own = pred_part((0, 0), (0, 1), (near_left, near_right), totals, *late)
    mine, *pieces = merge_call(own, (late_right, late_left))
    pieces = [across(piece, step + 1) for step, piece in enumerate(pieces)]
    totals = totals + swap_along(after(totals, mine), 1)
    totals = totals + swap_along(totals, 3)
    spatial_squares = jnp.sum(after(spatial, mine) ** 2, axis=0)
    share = 1.0 / totals[0]
    mass = totals[1] * share
    spot_rows = stacked([spot_valid, share, mass, slide_id.astype(F32), spatial_squares])
    piece = after(mine + pieces[0] + pieces[1] + pieces[2], spot_rows)

    got = [across(piece, step) for step in (1, 2, 3)]
    sums, slides = stats_call(
        ids,
        piece,
        spatial.reshape(8, 16, 16, spots),
        spot_rows,
    )
    sums = sums + swap_along(sums, 1)
    sums = sums + swap_along(sums, 3)
    mine = after((jnp.stack([piece, got[2]]), jnp.stack([got[1], got[0]])), sums)
    right0, left1 = along(mine[0], 1), along(mine[1], -1)
    right1, left0 = along(mine[1], 1), along(mine[0], -1)
    sums = sums + swap_across(after(sums, *mine), 1)
    sums = sums + swap_across(sums, 3)
    right0, left1, sums = lax.optimization_barrier((right0, left1, sums))
    far0, far1 = along(right0, 1), along(left1, -1)
    genes_slides = jnp.concatenate([sums[:48], slides])
    genes_slides = genes_slides + swap(genes_slides, 0, 0, 0, 1)
    genes_slides = genes_slides + swap(genes_slides, 0, 0, 1, 0)
    genes_slides = after(genes_slides, right1, left0)
    genes_slides = genes_slides + swap(genes_slides, 0, 0, 3, 0)
    pred = [*mine, right0, right1, left0, left1, far0, far1]
    gene_coef, spot_coef, scalars = coef_call(ids, genes_slides, sums, spot_rows)
    spatial4 = spatial.reshape(8, RING, genes // 32, spots)
    grad, column_a = grad_call(ids, pred[:6], spatial4, gene_coef, spot_coef, 0)
    types = types + swap(after(types, sums), 1, 0, 0, 0)
    grad, column_b = grad_call(ids, pred[6:], spatial4, gene_coef, spot_coef, 12, (after(grad, types),))

    def back_part(steps, *others):
        return back_call(after(ids, *others), steps, grad, masses, expr)

    rows = genes // 16
    sums_a, far_a = back_part([(2, 1)])
    types = types + swap(after(types, far_a), 3, 0, 0, 0)
    far_got = swap(far_a, 0, 0, 0, 1)
    sums_b, far_b = back_part([(2, 0)], far_a)
    far = far_b + far_got
    far_up, far_down = up(far[:rows], 1), up(far[rows:], -1)
    sums_c, up_a, down_a = back_part([(1, 1), (-1, 1)], far, types)
    up_got, down_got = swap(up_a, 0, 0, 0, 1), swap(down_a, 0, 0, 0, 1)
    sums_d, up_b, down_b = back_part([(1, 0), (-1, 0)], up_a)
    sums_e, own_a, own_b = back_part([(0, 1), (0, 0)], up_b)
    sums_0 = mass_call(after(spot_coef, own_b, far_up, far_down)[32:40], masses)
    far_up, far_down = after((far_up, far_down), sums_0)
    above = jnp.concatenate([up_b[:rows] + up_got[:rows] + far_up, up_b[rows:] + up_got[rows:]])
    below = jnp.concatenate([down_b[:rows] + down_got[:rows], down_b[rows:] + down_got[rows:] + far_down])
    near_up, near_down = up(above, 1), up(below, -1)
    own_a = jnp.concatenate([swap(own_a[:rows], 0, 0, 0, 1), swap(own_a[rows:], 0, 0, 0, 1)])
    last = jnp.concatenate(
        [
            jnp.sum(sums_0 + sums_a + sums_b + sums_c + sums_d + sums_e, axis=0).reshape(blocks, 128),
            scalars,
            jnp.zeros((5, 128), F32),
        ]
    )

    column = jnp.sum(column_a + column_b, axis=0) * share + spot_coef[32] * mass
    map_rows = stacked([spot_coef[32], column])
    map_rows = after(map_rows, above, below)
    map_args = (expr, grad.reshape(2, genes, spots), masses, keep2, map_rows, all_cells * genes)
    steps = cells // 256
    got, types_got = swap(last, 0, 0, 0, 1), swap(after(types, own_b), 0, 1, 0, 0)
    grad_map = map_call(0, steps - 2, *map_args)
    got, types_got = after((got, types_got), grad_map)
    last, types = last + got, types + types_got
    got, types_got = swap(last, 0, 0, 1, 0), swap(types, 0, 3, 0, 0)
    grad_map = map_call(steps - 2, steps, *map_args, done=(after(grad_map, own_a),))
    got, types_got = after((got, types_got), grad_map)
    last, types = last + got, types + types_got
    got = swap(last, 0, 0, 3, 0)
    grad_weighted = after(own_b + own_a, grad_map) + near_up + near_down
    grad_expr = grad_weighted * (keep * (genes * all_spots))[None, :]

    type_fraction = types * share

    grad_filter, loss_terms = finish_call(last, got, totals, scalars, kind2, filt2, all_cells)
    return (loss_terms[0, :5], type_fraction, grad_map, grad_filter.reshape(cells), grad_expr)


def solution(mesh):
    in_specs = (
        P("cells", "spots"),
        P("cells"),
        P(None, "cells"),
        P(None, "spots"),
        P("cells"),
        P("spots"),
        P("spots"),
    )
    out_specs = (P(), P(None, "spots"), P("cells", "spots"), P("cells"), P("spots", "cells"))
    return jax.shard_map(
        on_device, mesh=mesh, in_specs=in_specs, out_specs=out_specs, check_vma=False
    )
```

```python
import functools

import jax
import jax.numpy as jnp
from jax import lax
from jax.experimental import pallas as pl
from jax.experimental.pallas import tpu as pltpu
from jax.sharding import PartitionSpec as P

TYPES = 32
SLIDES = 3
RING = 4
F32 = jnp.float32
BF16 = jnp.bfloat16


def vmem(mib):
    return pltpu.CompilerParams(vmem_limit_bytes=mib << 20)


def fixed(shape):
    return pl.BlockSpec(shape, lambda *_: (0,) * len(shape), pipeline_mode=pl.Buffered(1))


def streamed(array):
    return pltpu.with_memory_space_constraint(array, pltpu.HBM)


RESIDENT = pl.BlockSpec(memory_space=pltpu.VMEM)


def cost(flops, moved):
    return pl.CostEstimate(flops=int(flops) // 8, bytes_accessed=int(moved) // 8, transcendentals=0)


NO_COST = pl.CostEstimate(flops=0, bytes_accessed=0, transcendentals=0)


def route(target):
    def flat(z, x, y, core):
        return ((z % RING * RING + x % RING) * RING + y % RING) * 2 + core

    return [
        (flat(z, x, y, core), flat(*target(z, x, y, core)))
        for z in range(RING)
        for x in range(RING)
        for y in range(RING)
        for core in range(2)
    ]


def send(array, target):
    return lax.ppermute(array, ("cells", "spots"), route(target))


def along(array, step):
    return send(array, lambda z, x, y, c: (z, x + step, y, c) if c == 0 else (z + step, x, y, c))


def across(array, step):
    return send(array, lambda z, x, y, c: (z + step, x, y, c) if c == 0 else (z, x + step, y, c))


def up(array, step):
    return send(array, lambda z, x, y, c: (z, x, y + step, c))


def swap(array, mz, mx, my, mc):
    return send(array, lambda z, x, y, c: (z ^ mz, x ^ mx, y ^ my, c ^ mc))


def swap_along(array, mask):
    return send(array, lambda z, x, y, c: (z, x ^ mask, y, c) if c == 0 else (z ^ mask, x, y, c))


def swap_across(array, mask):
    return send(array, lambda z, x, y, c: (z ^ mask, x, y, c) if c == 0 else (z, x ^ mask, y, c))


def after(value, *others):
    return lax.optimization_barrier((value, *others))[0]


def split(value):
    high = value.astype(BF16)
    return high, (value - high.astype(F32)).astype(BF16)


def product(left, right, dims):
    def one(a, b):
        return lax.dot_general(a, b, (dims, ((), ())), preferred_element_type=F32)

    return one(left[0], right[0]) + one(left[0], right[1]) + one(left[1], right[0])


def gene_group(ids, step, half, sub):
    return ((ids[0] + step) & 3) * RING + ((ids[1] + 2 * half + sub) & 3)


PIECES = [
    (step, half, sub)
    for step, half in ((0, 0), (0, 1), (-1, 0), (-1, 1), (1, 0), (1, 1), (2, 0), (2, 1))
    for sub in range(2)
]


def pick(index, values):
    out = values[0]
    for k, value in enumerate(values[1:]):
        out = jnp.where(index == k + 1, value, out)
    return out


def stacked(rows):
    row = lax.broadcasted_iota(jnp.int32, (8, rows[0].shape[0]), 0)
    out = jnp.zeros(row.shape, F32)
    for k, value in enumerate(rows):
        out = jnp.where(row == k, value[None, :], out)
    return out


def as_column(row):
    return jnp.broadcast_to(row, (128, 128)).T[:, :1]


def expo_kernel(ids, logits, kind, filt, *refs):
    expr, (masses, types, totals, out0, out1) = refs[:4], refs[4:]
    step = pl.program_id(0)
    count = logits.shape[0] // 128

    @pl.when(step == 0)
    def _():
        for out in (types, totals, out0, out1):
            out[...] = jnp.zeros_like(out)

    keeps = []
    lane = lax.broadcasted_iota(jnp.int32, (1, totals.shape[1]), 1)
    cell_sums = jnp.zeros(lane.shape, F32)
    for part in range(count):
        rows = slice(part * 128, part * 128 + 128)
        label = kind[pl.ds(step * count + part, 1), :]
        valid = (label >= 0).astype(F32)
        keep = valid * jax.nn.sigmoid(filt[pl.ds(step * count + part, 1), :])
        keeps.append(keep)
        for k, one in enumerate((valid, keep, keep - keep * keep)):
            cell_sums += jnp.where(lane == k, jnp.sum(one, axis=1, keepdims=True), 0.0)
        expo = jnp.exp(logits[rows]) * as_column(valid)
        masses[0, rows], masses[1, rows] = split(expo)
        whole = jnp.sum(expo, axis=0, keepdims=True)
        kept = jnp.sum(expo * as_column(keep), axis=0, keepdims=True)
        row = lax.broadcasted_iota(jnp.int32, types.shape, 0)
        types[...] += jnp.where(row == jnp.max(label, axis=1, keepdims=True), whole, 0.0)
        row = lax.broadcasted_iota(jnp.int32, totals.shape, 0)
        totals[...] += jnp.where(row == 0, whole, jnp.where(row == 1, kept, 0.0))
    totals[2:3, :] += cell_sums
    weighted = jnp.concatenate([part[...].reshape(-1, logits.shape[0]) for part in expr])
    weighted = weighted * jnp.concatenate(keeps, axis=1)
    part = product(split(weighted), masses, ((1,), (0,)))
    half = part.shape[0] // 2
    out0[...] += part[:half].reshape(out0.shape)
    out1[...] += part[half:].reshape(out1.shape)


def expo_call(ids, parts, logits, kind, filt, expr):
    cells, spots = logits.shape
    blocks, groups, rows, _ = expr.shape
    block = 256

    def genes(part, sub):
        return pl.BlockSpec(
            (blocks, 1, rows, block), lambda i, ids: (0, gene_group(ids, *part, sub), 0, i)
        )

    return pl.pallas_call(
        expo_kernel,
        grid_spec=pltpu.PrefetchScalarGridSpec(
            num_scalar_prefetch=1,
            grid=(cells // block,),
            in_specs=[
                pl.BlockSpec((block, spots), lambda i, w: (i, 0)),
                fixed(kind.shape),
                fixed(filt.shape),
            ]
            + [genes(part, sub) for part in parts for sub in range(2)],
            out_specs=[
                pl.BlockSpec((2, block, spots), lambda i, w: (0, i, 0)),
                fixed((TYPES, spots)),
                fixed((8, spots)),
                fixed((2, blocks, rows, spots)),
                fixed((2, blocks, rows, spots)),
            ],
        ),
        out_shape=[
            jax.ShapeDtypeStruct((2, cells, spots), BF16),
            jax.ShapeDtypeStruct((TYPES, spots), F32),
            jax.ShapeDtypeStruct((8, spots), F32),
            jax.ShapeDtypeStruct((2, blocks, rows, spots), F32),
            jax.ShapeDtypeStruct((2, blocks, rows, spots), F32),
        ],
        compiler_params=vmem(16),
        cost_estimate=cost(0, cells * spots * 8),
        name="expo",
    )(ids, streamed(logits), kind, filt, *[streamed(expr)] * 4)


def pred_kernel(ids, expr_a, expr_b, keep, masses, *refs):
    outs = refs[len(refs) // 2 :] if len(refs) > 2 else refs
    rows = 2 * expr_a.shape[0] * expr_a.shape[2]
    weighted = jnp.concatenate(
        [part[...].reshape(rows // 2, keep.shape[1]) for part in (expr_a, expr_b)]
    )
    part = product(split(weighted * keep[...]), masses, ((1,), (0,)))
    for step, out in enumerate(outs):

        @pl.when(pl.program_id(0) == step)
        def _(step=step, out=out):
            if len(refs) > 2:
                out[...] = part.reshape(out.shape) + refs[step][...]
            else:
                out[...] = part.reshape(out.shape)


def pred_call(ids, parts, expr, keep, masses, more=()):
    blocks, groups, rows, cells = expr.shape
    spots = masses.shape[2]

    def genes(sub):
        def place(i, ids):
            step, half = (pick(i, [part[k] for part in parts]) for k in range(2))
            return (0, gene_group(ids, step, half, sub), 0, 0)

        return pl.BlockSpec((blocks, 1, rows, cells), place)

    return pl.pallas_call(
        pred_kernel,
        grid_spec=pltpu.PrefetchScalarGridSpec(
            num_scalar_prefetch=1,
            grid=(2,),
            in_specs=[
                genes(0),
                genes(1),
                fixed((1, cells)),
                RESIDENT,
            ]
            + [fixed((2, blocks, rows, spots))] * len(more),
            out_specs=[fixed((2, blocks, rows, spots))] * 2,
        ),
        out_shape=[jax.ShapeDtypeStruct((2, blocks, rows, spots), F32)] * 2,
        compiler_params=vmem(16),
        cost_estimate=cost(24 * blocks * rows * cells * spots, 4 * cells * spots + 16 * blocks * rows * (cells + spots)),
        name="pred",
    )(ids, *[streamed(expr)] * 2, keep, masses, *more)


def merge_kernel(own0, own1, got0, got1, *outs):
    for half, (own, got) in enumerate(((own0, got0), (own1, got1))):
        for sub in range(2):
            outs[2 * half + sub][...] = own[sub] + got[sub]


def merge_call(own, got):
    shape = own[0].shape[1:]
    block = (2, *shape[1:])
    return pl.pallas_call(
        merge_kernel,
        grid=(shape[0] // 2,),
        in_specs=[pl.BlockSpec((2, *block), lambda i: (0, i, 0, 0))] * 4,
        out_specs=[pl.BlockSpec(block, lambda i: (i, 0, 0))] * 4,
        out_shape=[jax.ShapeDtypeStruct(shape, F32)] * 4,
        compiler_params=vmem(12),
        cost_estimate=NO_COST,
        name="merge",
    )(*own, *got)


def stats_kernel(ids, piece, spatial, spot, gene, slide_sums):
    rows = piece.shape[0] * piece.shape[1]
    valid, share, mass, slide = (spot[k : k + 1, :] for k in range(4))
    value = piece[...].reshape(rows, piece.shape[2]) * share
    data = spatial[...].reshape(value.shape)
    cross, square = value * data, value * value
    lane = lax.broadcasted_iota(jnp.int32, (rows, 128), 1)
    sums = jnp.zeros((rows, 128), F32)
    for index, one in enumerate((cross, square, data * data)):
        sums = jnp.where(lane == index, jnp.sum(one * valid, axis=1, keepdims=True), sums)
    sums = sums.T
    gene[...] = jnp.zeros_like(gene)
    slide_sums[...] = jnp.zeros_like(slide_sums)
    for index in range(3):
        gene[pl.ds(16 * index + gene_group(ids, 0, 0, 0), 1), :] = sums[index : index + 1, :]
    lane = lax.broadcasted_iota(jnp.int32, (1, 128), 1)
    slides = jnp.zeros((1, 128), F32)
    logs = jnp.log(jnp.where(valid > 0, mass, 1.0))
    for k in range(SLIDES):
        inside = jnp.where(slide == k, valid, 0.0)
        for index, one in enumerate((inside, inside * mass, inside * logs)):
            total = jnp.sum(one, axis=1, keepdims=True)
            slides = jnp.where(lane == 3 * index + k, total, slides)
    slide_sums[0:1, :] = slides
    for index, one in enumerate((cross, square)):
        total = jnp.sum(one, axis=0, keepdims=True)
        for k in range(total.shape[1] // 128):
            at = 48 + 8 * index + k
            gene[at : at + 1, :] = total[:, 128 * k : 128 * k + 128]


def stats_call(ids, piece, spatial, spot):
    blocks, rows, spots = piece.shape
    return pl.pallas_call(
        stats_kernel,
        grid_spec=pltpu.PrefetchScalarGridSpec(
            num_scalar_prefetch=1,
            grid=(1,),
            in_specs=[
                fixed((blocks, rows, spots)),
                pl.BlockSpec((blocks, 1, rows, spots), lambda i, ids: (0, gene_group(ids, 0, 0, 0), 0, 0)),
                fixed((8, spots)),
            ],
            out_specs=[fixed((64, 128)), fixed((8, 128))],
        ),
        out_shape=[jax.ShapeDtypeStruct((64, 128), F32), jax.ShapeDtypeStruct((8, 128), F32)],
        compiler_params=vmem(8),
        cost_estimate=NO_COST,
        name="stats",
    )(ids, piece, streamed(spatial), spot)


def coef_kernel(ids, genes_slides, sums, spot, gene, rows, scalars, pairs):
    valid, share, mass, slide, squares = (spot[k : k + 1, :] for k in range(5))
    genes = float(16 * sums.shape[1])

    def wide(index):
        return jnp.concatenate([sums[index + k : index + k + 1, :] for k in range(8)], axis=1)

    dots, own = wide(48), wide(56)
    dot, aa, bb = genes_slides[0:16, :], genes_slides[16:32, :], genes_slides[32:48, :]
    scale = lax.rsqrt(aa * bb + 1e-06)
    pairs[0:16, :] = dot * scale**3 * bb / genes
    pairs[16:32, :] = scale / genes
    pair = [pairs[pl.ds(k + gene_group(ids, *one), 1), :] for k in (0, 16) for one in PIECES]
    gene[...] = jnp.concatenate([*pair, jnp.zeros((96, 128), F32)]).T
    total = jnp.sum(jnp.sum(dot * scale, axis=1, keepdims=True), axis=0, keepdims=True)
    nvs = jnp.zeros((1, 1), F32)
    density = jnp.zeros((1, 1), F32)
    nk, tk = jnp.ones_like(valid), jnp.ones_like(valid)
    for k in range(SLIDES):
        count, held, logs = (genes_slides[48:49, 3 * j + k : 3 * j + k + 1] for j in range(3))
        some = count > 0
        safe = jnp.where(some, count, 1.0)
        nvs += count
        density += jnp.where(some, jnp.log(jnp.where(some, held, 1.0) / safe) - logs / safe, 0.0)
        here = (slide == k) & (valid > 0)
        nk = jnp.where(here, count, nk)
        tk = jnp.where(here, held, tk)
    scale = lax.rsqrt(own * squares + 1e-06)
    grad_mass = valid / SLIDES * (1.0 / tk - 1.0 / (nk * jnp.where(valid > 0, mass, 1.0)))
    mask = valid * share
    by_pred, by_data = dots * scale**3 * squares / nvs, scale / nvs
    for index, one in enumerate((by_pred * share * mask, by_data * mask, mask, share * mask)):
        rows[8 * index : 8 * index + 8, :] = jnp.broadcast_to(one, (8, one.shape[1]))
    rows[32:40, :] = jnp.concatenate([grad_mass * share, jnp.zeros((7, valid.shape[1]), F32)])
    cosines = jnp.sum(valid * dots * scale, axis=1, keepdims=True)
    lane = lax.broadcasted_iota(jnp.int32, (1, 128), 1)
    out = jnp.zeros((1, 128), F32)
    for index, one in enumerate((total / genes, cosines / nvs, density / SLIDES)):
        out = jnp.where(lane == index, one, out)
    scalars[...] = out


def coef_call(ids, genes_slides, sums, spot):
    spots = spot.shape[1]
    return pl.pallas_call(
        coef_kernel,
        grid_spec=pltpu.PrefetchScalarGridSpec(
            num_scalar_prefetch=1,
            grid=(1,),
            in_specs=[fixed(genes_slides.shape), fixed(sums.shape), fixed((8, spots))],
            out_specs=[fixed((128, 128)), fixed((40, spots)), fixed((1, 128))],
            scratch_shapes=[pltpu.VMEM((32, 128), F32)],
        ),
        out_shape=[
            jax.ShapeDtypeStruct((128, 128), F32),
            jax.ShapeDtypeStruct((40, spots), F32),
            jax.ShapeDtypeStruct((1, 128), F32),
        ],
        compiler_params=vmem(6),
        cost_estimate=NO_COST,
        name="coef",
    )(ids, genes_slides, sums, spot)


def grad_rows(pred, data, gene, spot, lane):
    by_pred = gene[:, lane : lane + 1].reshape(2, 8, 1)
    by_data = gene[:, 16 + lane : 17 + lane].reshape(2, 8, 1)
    pred, data = pred.reshape(2, 8, pred.shape[1]), data.reshape(2, 8, data.shape[1])
    grad = pred * (by_pred * spot[24:32, :] + spot[0:8, :])
    grad = grad - data * (by_data * spot[16:24, :] + spot[8:16, :])
    return grad.reshape(16, grad.shape[2]), jnp.sum(grad * pred, axis=0)


def grad_kernel(ids, *refs, count, lane):
    pred, data, refs = refs[: 2 * count], refs[2 * count : 3 * count], refs[3 * count :]
    gene, spot, grad, column = refs[0], refs[1], refs[-2], refs[-1]

    @pl.when(pl.program_id(0) == 0)
    def _():
        column[...] = jnp.zeros_like(column)

    total = jnp.zeros(column.shape, F32)
    for index, part in enumerate(pred):
        for sub in range(2):
            at = gene_group(ids, *PIECES[lane + 2 * index + sub])
            row = pl.multiple_of((at & 3) * 16, 16)
            to = pl.ds(pl.multiple_of(at * 16, 16) if count > 1 else row, 16)
            for block in range(part.shape[1]):
                rows, inner = grad_rows(
                    part[sub, block],
                    data[index // 2][block, 0, pl.ds(row, 16), :],
                    gene[16 * block : 16 * block + 16, :],
                    spot,
                    lane + 2 * index + sub,
                )
                grad[0, block, to, :], grad[1, block, to, :] = split(rows)
                total += inner
    column[...] += total


def grad_call(ids, pred, spatial, gene, spot, lane, chips, done=()):
    blocks, groups, rows, spots = spatial.shape
    count = len(pred) // 2
    each = 2

    def chip(i, ids):
        return (ids[2] + pick(i, chips)) & 3

    if count > 1:
        grad = pl.BlockSpec(
            (2, each, groups * rows, spots), lambda i, ids: (0, chip(i, ids), 0, 0)
        )
    else:
        grad = pl.BlockSpec(
            (2, each, rows, spots),
            lambda i, ids: (0, chip(i, ids), (ids[0] + PIECES[lane][0]) & 3, 0),
        )

    def group(k):
        step = PIECES[lane + 4 * k][0]
        return pl.BlockSpec(
            (each, 1, rows, spots), lambda i, ids: (chip(i, ids), (ids[0] + step) & 3, 0, 0)
        )

    return pl.pallas_call(
        functools.partial(grad_kernel, count=count, lane=lane),
        grid_spec=pltpu.PrefetchScalarGridSpec(
            num_scalar_prefetch=1,
            grid=(len(chips),),
            in_specs=[pl.BlockSpec((2, each, 16, spots), lambda i, ids: (0, chip(i, ids), 0, 0))]
            * (2 * count)
            + [group(k) for k in range(count)]
            + [
                pl.BlockSpec((16 * each, 128), lambda i, ids: (chip(i, ids), 0)),
                fixed(spot.shape),
            ]
            + [pl.BlockSpec(memory_space=pl.ANY)] * len(done),
            out_specs=[grad, fixed((8, spots))],
        ),
        out_shape=[
            jax.ShapeDtypeStruct((2, blocks, groups * rows, spots), BF16),
            jax.ShapeDtypeStruct((8, spots), F32),
        ],
        input_output_aliases={3 * count + 3: 0} if done else {},
        compiler_params=vmem(16),
        cost_estimate=NO_COST,
        name="grad",
    )(ids, *pred, *[streamed(spatial)] * count, gene, spot, *done)


def back_kernel(ids, grad, masses, expr, *refs, extra):
    sums, *outs = refs[extra:]
    step = pl.program_id(0)
    left = grad[0, 0], grad[1, 0]
    rows = left[0].shape[0]
    if extra:
        pair = split(jnp.concatenate([refs[0][...], jnp.zeros_like(refs[0])]))
        left = [jnp.concatenate(both) for both in zip(left, pair)]
    part = product(left, masses, ((1,), (1,)))

    @pl.when(step == 0)
    def _():
        sums[...] = part[rows : rows + 8] if extra else jnp.zeros_like(sums)

    part = part[:rows]
    sums[...] += jnp.sum((part * expr[...]).reshape(-1, 8, part.shape[1]), axis=0)
    for index, out in enumerate(outs):

        @pl.when(step == index)
        def _(out=out):
            out[...] = part


def back_call(ids, parts, grad, masses, expr, spot=None):
    _, blocks, rows, spots = grad.shape
    cells = masses.shape[1]
    count = len(parts)
    extra = [] if spot is None else [spot]

    def block(i, ids):
        step, other = (pick(i, [part[k] for part in parts]) for k in range(2))
        return ((ids[2] + step) & 3) * 2 + (ids[3] ^ other)

    return pl.pallas_call(
        functools.partial(back_kernel, extra=len(extra)),
        grid_spec=pltpu.PrefetchScalarGridSpec(
            num_scalar_prefetch=1,
            grid=(count,),
            in_specs=[
                pl.BlockSpec((2, 1, rows, spots), lambda i, ids: (0, block(i, ids), 0, 0)),
                RESIDENT,
                pl.BlockSpec((rows, cells), lambda i, ids: (block(i, ids), 0)),
            ]
            + [pl.BlockSpec((8, spots), lambda i, ids: (4, 0))] * len(extra),
            out_specs=[fixed((8, cells))] + [fixed((rows, cells))] * count,
        ),
        out_shape=[jax.ShapeDtypeStruct((8, cells), F32)]
        + [jax.ShapeDtypeStruct((rows, cells), F32)] * count,
        compiler_params=vmem(20),
        cost_estimate=NO_COST,
        name="back",
    )(ids, grad, masses, streamed(expr), *extra)


def lift_kernel(above, below, far_up, far_down, out_above, out_below):
    rows = far_up.shape[0]
    out_above[:rows, :] = above[:rows, :] + far_up[...]
    out_above[rows:, :] = above[rows:, :]
    out_below[:rows, :] = below[:rows, :]
    out_below[rows:, :] = below[rows:, :] + far_down[...]


def lift_call(above, below, far_up, far_down):
    rows, cells = far_up.shape
    block = 256
    far = pl.BlockSpec((rows, block), lambda i: (0, i))
    whole = pl.BlockSpec((2 * rows, block), lambda i: (0, i))
    return pl.pallas_call(
        lift_kernel,
        grid=(cells // block,),
        in_specs=[whole, whole, far, far],
        out_specs=[whole, whole],
        out_shape=[jax.ShapeDtypeStruct(above.shape, F32)] * 2,
        compiler_params=vmem(8),
        cost_estimate=pl.CostEstimate(flops=10**10, bytes_accessed=0, transcendentals=0),
        name="lift",
    )(above, below, far_up, far_down)


def map_kernel(expr, grad, masses, keep, spot, *rest, scale, start):
    out = rest[-1]
    step = pl.program_id(0) + start
    inner = product(split(expr[...]), grad, ((0,), (0,))) + spot[0:1, :]
    expo = masses[0].astype(F32) + masses[1].astype(F32)
    for part in range(expr.shape[1] // 128):
        rows = slice(part * 128, part * 128 + 128)
        weight = as_column(keep[pl.ds(step * (expr.shape[1] // 128) + part, 1), :])
        out[rows, :] = (scale * expo[rows]) * (weight * inner[rows] - spot[1:2, :])


def map_call(start, stop, expr, grad, masses, keep, spot, scale, done=()):
    genes, cells = expr.shape
    spots = masses.shape[2]
    block = 256
    return pl.pallas_call(
        functools.partial(map_kernel, scale=scale, start=start),
        grid=(stop - start,),
        in_specs=[
            pl.BlockSpec((genes, block), lambda i: (0, i + start)),
            RESIDENT,
            pl.BlockSpec((2, block, spots), lambda i: (0, i + start, 0)),
            fixed(keep.shape),
            fixed((8, spots)),
        ]
        + [pl.BlockSpec(memory_space=pl.ANY)] * len(done),
        out_specs=pl.BlockSpec((block, spots), lambda i: (i + start, 0)),
        out_shape=jax.ShapeDtypeStruct((cells, spots), F32),
        input_output_aliases={5: 0} if done else {},
        compiler_params=vmem(24),
        cost_estimate=NO_COST,
        name="grad_map",
    )(streamed(expr), grad, masses, keep, spot, *done)


def finish_kernel(last, got1, got2, got3, totals, scalars, kind, filt, grad_filter, terms, *, all_cells):
    blocks = kind.shape[0]
    total = (last[...] + got2[...]) + (got1[...] + got3[...])
    nvalid, retained, reg_sum = (totals[2:3, k : k + 1] for k in range(3))
    valid = (kind[...] >= 0).astype(F32)
    sigma = jax.nn.sigmoid(filt[...])
    keep = sigma * valid
    shifted = (retained - 0.35 * nvalid) / (0.1 * all_cells)
    count_term = jnp.sqrt(shifted * shifted + 1.0)
    grad_keep = total[:blocks] + shifted / count_term / (0.1 * all_cells) + (1.0 - 2.0 * keep) / nvalid
    grad_filter[...] = valid * sigma * (1.0 - sigma) * grad_keep * all_cells
    lane = lax.broadcasted_iota(jnp.int32, (1, 128), 1)
    out = jnp.zeros((1, 128), F32)
    parts = (scalars[:, 0:1], total[blocks : blocks + 1, 1:2], scalars[:, 2:3], count_term, reg_sum / nvalid)
    for index, one in enumerate(parts):
        out = jnp.where(lane == index, one, out)
    terms[...] = out


def finish_call(last, got, totals, scalars, kind, filt, all_cells):
    return pl.pallas_call(
        functools.partial(finish_kernel, all_cells=float(all_cells)),
        grid=(1,),
        in_specs=[fixed(one.shape) for one in (last, *got, totals, scalars, kind, filt)],
        out_specs=[fixed(kind.shape), fixed((1, 128))],
        out_shape=[jax.ShapeDtypeStruct(kind.shape, F32), jax.ShapeDtypeStruct((1, 128), F32)],
        compiler_params=vmem(4),
        cost_estimate=NO_COST,
        name="finish",
    )(last, *got, totals, scalars, kind, filt)


def on_device(map_logits, filter_logits, expr, spatial, cell_type, slide_id, spot_mask):
    genes, cells = expr.shape
    spots = map_logits.shape[1]
    all_cells = cells * lax.axis_size("cells")
    all_spots = spots * lax.axis_size("spots")
    cell_place = lax.axis_index("cells")
    z, x = cell_place >> 2, cell_place & 3
    spot_place = lax.axis_index("spots")
    y, core = spot_place >> 1, spot_place & 1
    first = jnp.where(core == 0, x, z)
    second = jnp.where(core == 0, z, x)
    blocks = cells // 128

    valid = (cell_type >= 0).astype(F32)
    sigma = jax.nn.sigmoid(filter_logits)
    keep = sigma * valid
    spot_valid = spot_mask.astype(F32)
    kind2 = cell_type.reshape(blocks, 128)
    filt2 = filter_logits.reshape(blocks, 128)
    keep2 = keep.reshape(blocks, 128)

    expr4 = expr.reshape(8, 16, 16, cells)
    keep_row = keep.reshape(1, cells)

    ids = jnp.stack([first, second, y, core]).astype(jnp.int32)

    def pred_part(one, two, more, *others):
        return pred_call(after(ids, *others), (one, two), expr4, keep_row, masses, more)

    masses, types, totals, *far = expo_call(
        ids, ((2, 0), (2, 1)), map_logits, kind2, filt2, expr4
    )
    far_right, far_left = along(far[0], 1), along(far[1], -1)
    near = pred_part((1, 1), (-1, 0), (), *far)
    near_right, near_left = along(near[0], 1), along(near[1], -1)
    totals = totals + swap_across(totals, 1)
    late = pred_part((1, 0), (-1, 1), (far_right, far_left), totals, *near)
    late_right, late_left = along(late[0], 1), along(late[1], -1)
    totals = totals + swap_across(totals, 3)
    own = pred_part((0, 0), (0, 1), (near_left, near_right), totals, *late)
    mine, *pieces = merge_call(own, (late_right, late_left))
    pieces = [across(piece, step + 1) for step, piece in enumerate(pieces)]
    sums = after(jnp.concatenate([types, totals]), mine)
    sums = sums + swap_along(sums, 1)
    sums = sums + swap_along(sums, 3)
    types, totals = sums[:TYPES], sums[TYPES:]
    spatial_squares = jnp.sum(after(spatial, mine) ** 2, axis=0)
    share = 1.0 / totals[0]
    mass = totals[1] * share
    spot_rows = stacked([spot_valid, share, mass, slide_id.astype(F32), spatial_squares])
    piece = after(mine + pieces[0] + pieces[1] + pieces[2], spot_rows)

    got = [across(piece, step) for step in (1, 2, 3)]
    sums, slides = stats_call(
        ids,
        piece,
        spatial.reshape(8, 16, 16, spots),
        spot_rows,
    )
    sums = sums + swap_along(sums, 1)
    sums = sums + swap_along(sums, 3)
    mine = after((jnp.stack([piece, got[2]]), jnp.stack([got[1], got[0]])), sums)
    right0, left1 = along(mine[0], 1), along(mine[1], -1)
    right1, left0 = along(mine[1], 1), along(mine[0], -1)
    sums = sums + swap_across(after(sums, *mine), 1)
    sums = sums + swap_across(sums, 3)
    right0, left1, sums = lax.optimization_barrier((right0, left1, sums))
    far0, far1 = along(right0, 1), along(left1, -1)
    genes_slides = jnp.concatenate([sums[:48], slides])
    genes_slides = genes_slides + swap(genes_slides, 0, 0, 0, 1)
    genes_slides = genes_slides + swap(genes_slides, 0, 0, 1, 0)
    genes_slides = after(genes_slides, right1, left0)
    genes_slides = genes_slides + swap(genes_slides, 0, 0, 3, 0)
    pred = [*mine, right0, right1, left0, left1, far0, far1]
    gene_coef, spot_coef, scalars = coef_call(ids, genes_slides, sums, spot_rows)
    spatial4 = spatial.reshape(8, RING, genes // 32, spots)
    grad, column_a = grad_call(ids, pred[:6], spatial4, gene_coef, spot_coef, 0, (0, 1, 2, 3))

    def last_grad(chips, grad, *others):
        return grad_call(
            after(ids, *others), pred[6:], spatial4, gene_coef, spot_coef, 12, chips, (grad,)
        )

    def back_part(steps, grad, spot, *others):
        return back_call(after(ids, *others), steps, grad, masses, expr, spot)

    rows = genes // 16
    grad, column_b = last_grad((2,), grad)
    sums_a, far_a = back_part([(2, 1)], grad, spot_coef)
    far_got = swap(far_a, 0, 0, 0, 1)
    sums_b, far_b = back_part([(2, 0)], grad, None, far_a)
    far = far_b + far_got
    far_up, far_down = up(far[:rows], 1), up(far[rows:], -1)
    grad, column_c = last_grad((1, -1, 0), grad, far)
    sums_c, up_a, down_a, up_b, down_b = back_part([(1, 1), (-1, 1), (1, 0), (-1, 0)], grad, None)
    up_got, down_got = swap(up_a, 0, 0, 0, 1), swap(down_a, 0, 0, 0, 1)
    types = types + swap_across(after(types, up_b), 1)
    sums_d, own_a, own_b = back_part([(0, 1), (0, 0)], grad, None, up_b)
    above, below = lift_call(up_b, down_b, *after((far_up, far_down), own_b))
    above, below = above + up_got, below + down_got
    near_up, near_down = up(above, 1), up(below, -1)
    own_a = jnp.concatenate([swap(own_a[:rows], 0, 0, 0, 1), swap(own_a[rows:], 0, 0, 0, 1)])
    last = jnp.concatenate(
        [
            jnp.sum(sums_a + sums_b + sums_c + sums_d, axis=0).reshape(blocks, 128),
            scalars,
            jnp.zeros((5, 128), F32),
        ]
    )

    column = jnp.sum(column_a + column_b + column_c, axis=0) * share + spot_coef[32] * mass
    map_rows = stacked([spot_coef[32], column])
    map_rows = after(map_rows, above, below)
    map_args = (expr, grad.reshape(2, genes, spots), masses, keep2, map_rows, all_cells * genes)
    steps = cells // 256
    got, types_got = swap(last, 0, 0, 0, 1), swap_across(after(types, above, below), 3)
    grad_map = map_call(0, steps - 2, *map_args)
    got, types_got = after((got, types_got), grad_map)
    last, types = last + got, types + types_got
    got = [up(last, step) for step in (1, 2, 3)]
    grad_map = map_call(steps - 2, steps, *map_args, done=(after(grad_map, own_a),))
    got = after(tuple(got), grad_map)
    grad_weighted = after(own_b + own_a, grad_map) + near_up + near_down
    grad_expr = grad_weighted * (keep * (genes * all_spots))[None, :]

    type_fraction = types * share

    grad_filter, loss_terms = finish_call(last, got, totals, scalars, kind2, filt2, all_cells)
    return (loss_terms[0, :5], type_fraction, grad_map, grad_filter.reshape(cells), grad_expr)


def solution(mesh):
    in_specs = (
        P("cells", "spots"),
        P("cells"),
        P(None, "cells"),
        P(None, "spots"),
        P("cells"),
        P("spots"),
        P("spots"),
    )
    out_specs = (P(), P(None, "spots"), P("cells", "spots"), P("cells"), P("spots", "cells"))
    return jax.shard_map(
        on_device, mesh=mesh, in_specs=in_specs, out_specs=out_specs, check_vma=False
    )
```

```python
import functools

import jax
import jax.numpy as jnp
from jax import lax
from jax.experimental import pallas as pl
from jax.experimental.pallas import tpu as pltpu
from jax.sharding import PartitionSpec as P

TYPES = 32
SLIDES = 3
RING = 4
F32 = jnp.float32
BF16 = jnp.bfloat16


def vmem(mib):
    return pltpu.CompilerParams(vmem_limit_bytes=mib << 20)


def fixed(shape):
    return pl.BlockSpec(shape, lambda *_: (0,) * len(shape), pipeline_mode=pl.Buffered(1))


def streamed(array):
    return pltpu.with_memory_space_constraint(array, pltpu.HBM)


RESIDENT = pl.BlockSpec(memory_space=pltpu.VMEM)


def cost(flops, moved):
    return pl.CostEstimate(flops=int(flops) // 8, bytes_accessed=int(moved) // 8, transcendentals=0)


NO_COST = pl.CostEstimate(flops=0, bytes_accessed=0, transcendentals=0)


def route(target):
    def flat(z, x, y, core):
        return ((z % RING * RING + x % RING) * RING + y % RING) * 2 + core

    return [
        (flat(z, x, y, core), flat(*target(z, x, y, core)))
        for z in range(RING)
        for x in range(RING)
        for y in range(RING)
        for core in range(2)
    ]


def send(array, target):
    return lax.ppermute(array, ("cells", "spots"), route(target))


def along(array, step):
    return send(array, lambda z, x, y, c: (z, x + step, y, c) if c == 0 else (z + step, x, y, c))


def across(array, step):
    return send(array, lambda z, x, y, c: (z + step, x, y, c) if c == 0 else (z, x + step, y, c))


def up(array, step):
    return send(array, lambda z, x, y, c: (z, x, y + step, c))


def swap(array, mz, mx, my, mc):
    return send(array, lambda z, x, y, c: (z ^ mz, x ^ mx, y ^ my, c ^ mc))


def swap_along(array, mask):
    return send(array, lambda z, x, y, c: (z, x ^ mask, y, c) if c == 0 else (z ^ mask, x, y, c))


def swap_across(array, mask):
    return send(array, lambda z, x, y, c: (z ^ mask, x, y, c) if c == 0 else (z, x ^ mask, y, c))


def after(value, *others):
    return lax.optimization_barrier((value, *others))[0]


def split(value):
    high = value.astype(BF16)
    return high, (value - high.astype(F32)).astype(BF16)


def product(left, right, dims):
    def one(a, b):
        return lax.dot_general(a, b, (dims, ((), ())), preferred_element_type=F32)

    return one(left[0], right[0]) + one(left[0], right[1]) + one(left[1], right[0])


def gene_group(ids, step, half, sub):
    return ((ids[0] + step) & 3) * RING + ((ids[1] + 2 * half + sub) & 3)


PIECES = [
    (step, half, sub)
    for step, half in ((0, 0), (0, 1), (-1, 0), (-1, 1), (1, 0), (1, 1), (2, 0), (2, 1))
    for sub in range(2)
]


def pick(index, values):
    out = values[0]
    for k, value in enumerate(values[1:]):
        out = jnp.where(index == k + 1, value, out)
    return out


def stacked(rows):
    row = lax.broadcasted_iota(jnp.int32, (8, rows[0].shape[0]), 0)
    out = jnp.zeros(row.shape, F32)
    for k, value in enumerate(rows):
        out = jnp.where(row == k, value[None, :], out)
    return out


def as_column(row):
    return jnp.broadcast_to(row, (128, 128)).T[:, :1]


def expo_kernel(ids, logits, kind, filt, *refs):
    expr, (masses, types, totals, out0, out1) = refs[:4], refs[4:]
    step = pl.program_id(0)
    count = logits.shape[0] // 128

    @pl.when(step == 0)
    def _():
        for out in (types, totals, out0, out1):
            out[...] = jnp.zeros_like(out)

    keeps = []
    lane = lax.broadcasted_iota(jnp.int32, (1, totals.shape[1]), 1)
    cell_sums = jnp.zeros(lane.shape, F32)
    for part in range(count):
        rows = slice(part * 128, part * 128 + 128)
        label = kind[pl.ds(step * count + part, 1), :]
        valid = (label >= 0).astype(F32)
        keep = valid * jax.nn.sigmoid(filt[pl.ds(step * count + part, 1), :])
        keeps.append(keep)
        for k, one in enumerate((valid, keep, keep - keep * keep)):
            cell_sums += jnp.where(lane == k, jnp.sum(one, axis=1, keepdims=True), 0.0)
        expo = jnp.exp(logits[rows]) * as_column(valid)
        masses[0, rows], masses[1, rows] = split(expo)
        whole = jnp.sum(expo, axis=0, keepdims=True)
        kept = jnp.sum(expo * as_column(keep), axis=0, keepdims=True)
        row = lax.broadcasted_iota(jnp.int32, types.shape, 0)
        types[...] += jnp.where(row == jnp.max(label, axis=1, keepdims=True), whole, 0.0)
        row = lax.broadcasted_iota(jnp.int32, totals.shape, 0)
        totals[...] += jnp.where(row == 0, whole, jnp.where(row == 1, kept, 0.0))
    totals[2:3, :] += cell_sums
    weighted = jnp.concatenate([part[...].reshape(-1, logits.shape[0]) for part in expr])
    weighted = weighted * jnp.concatenate(keeps, axis=1)
    part = product(split(weighted), masses, ((1,), (0,)))
    half = part.shape[0] // 2
    for index, out in enumerate((out0, out1)):
        new = part[index * half : index * half + half].reshape(-1, 8, part.shape[1])
        out[: half // 8] += new
        out[half // 8] = totals[...]


def expo_call(ids, parts, logits, kind, filt, expr):
    cells, spots = logits.shape
    blocks, groups, rows, _ = expr.shape
    block = 256

    def genes(part, sub):
        return pl.BlockSpec(
            (blocks, 1, rows, block), lambda i, ids: (0, gene_group(ids, *part, sub), 0, i)
        )

    return pl.pallas_call(
        expo_kernel,
        grid_spec=pltpu.PrefetchScalarGridSpec(
            num_scalar_prefetch=1,
            grid=(cells // block,),
            in_specs=[
                pl.BlockSpec((block, spots), lambda i, w: (i, 0)),
                fixed(kind.shape),
                fixed(filt.shape),
            ]
            + [genes(part, sub) for part in parts for sub in range(2)],
            out_specs=[
                pl.BlockSpec((2, block, spots), lambda i, w: (0, i, 0)),
                fixed((TYPES, spots)),
                fixed((8, spots)),
                fixed((blocks * rows // 4 + 1, 8, spots)),
                fixed((blocks * rows // 4 + 1, 8, spots)),
            ],
        ),
        out_shape=[
            jax.ShapeDtypeStruct((2, cells, spots), BF16),
            jax.ShapeDtypeStruct((TYPES, spots), F32),
            jax.ShapeDtypeStruct((8, spots), F32),
            jax.ShapeDtypeStruct((blocks * rows // 4 + 1, 8, spots), F32),
            jax.ShapeDtypeStruct((blocks * rows // 4 + 1, 8, spots), F32),
        ],
        compiler_params=vmem(16),
        cost_estimate=cost(0, cells * spots * 8),
        name="expo",
    )(ids, streamed(logits), kind, filt, *[streamed(expr)] * 4)


def pred_kernel(ids, expr_a, expr_b, keep, masses, totals, *refs):
    more, outs = refs[:-2], refs[-2:]
    rows = 2 * expr_a.shape[0] * expr_a.shape[2]
    weighted = jnp.concatenate(
        [part[...].reshape(rows // 2, keep.shape[1]) for part in (expr_a, expr_b)]
    )
    part = product(split(weighted * keep[...]), masses, ((1,), (0,)))
    part = part.reshape(rows // 8, 8, part.shape[1])
    for step, out in enumerate(outs):

        @pl.when(pl.program_id(0) == step)
        def _(step=step, out=out):
            if more:
                out[: rows // 8] = part + more[step][: rows // 8]
                out[rows // 8] = totals[...] + more[step][rows // 8]
            else:
                out[: rows // 8] = part
                out[rows // 8] = totals[...]


def pred_call(ids, parts, expr, keep, masses, totals, more=()):
    blocks, groups, rows, cells = expr.shape
    spots = masses.shape[2]
    tiles = blocks * rows // 4 + 1

    def genes(sub):
        def place(i, ids):
            step, half = (pick(i, [part[k] for part in parts]) for k in range(2))
            return (0, gene_group(ids, step, half, sub), 0, 0)

        return pl.BlockSpec((blocks, 1, rows, cells), place)

    return pl.pallas_call(
        pred_kernel,
        grid_spec=pltpu.PrefetchScalarGridSpec(
            num_scalar_prefetch=1,
            grid=(2,),
            in_specs=[
                genes(0),
                genes(1),
                fixed((1, cells)),
                RESIDENT,
                fixed((8, spots)),
            ]
            + [fixed((tiles, 8, spots))] * len(more),
            out_specs=[fixed((tiles, 8, spots))] * 2,
        ),
        out_shape=[jax.ShapeDtypeStruct((tiles, 8, spots), F32)] * 2,
        compiler_params=vmem(16),
        cost_estimate=cost(24 * blocks * rows * cells * spots, 4 * cells * spots + 16 * blocks * rows * (cells + spots)),
        name="pred",
    )(ids, *[streamed(expr)] * 2, keep, masses, totals, *more)


def merge_kernel(own0, own1, got0, got1, *outs):
    tiles = outs[0].shape[0] - 1
    for half, (own, got) in enumerate(((own0, got0), (own1, got1))):
        for sub in range(2):
            out = outs[2 * half + sub]
            out[:tiles] = own[sub * tiles : sub * tiles + tiles] + got[sub * tiles : sub * tiles + tiles]
            out[tiles] = own[2 * tiles] + got[2 * tiles]


def merge_call(own, got):
    tiles, _, spots = own[0].shape
    block = 256
    whole = pl.BlockSpec((tiles, 8, block), lambda i: (0, 0, i))
    piece = (tiles // 2 + 1, 8, spots)
    return pl.pallas_call(
        merge_kernel,
        grid=(spots // block,),
        in_specs=[whole] * 4,
        out_specs=[pl.BlockSpec((tiles // 2 + 1, 8, block), lambda i: (0, 0, i))] * 4,
        out_shape=[jax.ShapeDtypeStruct(piece, F32)] * 4,
        compiler_params=vmem(12),
        cost_estimate=NO_COST,
        name="merge",
    )(*own, *got)


def halve_kernel(expr, out):
    out[0], out[1] = split(expr[...])


def halve_call(ids, expr):
    genes, cells = expr.shape
    block = 256
    return pl.pallas_call(
        lambda ids, *refs: halve_kernel(*refs),
        grid_spec=pltpu.PrefetchScalarGridSpec(
            num_scalar_prefetch=1,
            grid=(genes // block,),
            in_specs=[pl.BlockSpec((block, cells), lambda i, ids: (i, 0))],
            out_specs=pl.BlockSpec((2, block, cells), lambda i, ids: (0, i, 0)),
        ),
        out_shape=jax.ShapeDtypeStruct((2, genes, cells), BF16),
        compiler_params=vmem(8),
        cost_estimate=NO_COST,
        name="halve",
    )(ids, streamed(expr))


def stats_kernel(ids, piece, spatial, spot, totals, gene, slide_sums):
    rows = piece.shape[0] * piece.shape[1]
    valid, slide = spot[0:1, :], spot[1:2, :]
    share = 1.0 / totals[0:1, :]
    mass = totals[1:2, :] * share
    value = piece[...].reshape(rows, piece.shape[2]) * share
    data = spatial[...].reshape(value.shape)
    cross, square = value * data, value * value
    lane = lax.broadcasted_iota(jnp.int32, (rows, 128), 1)
    sums = jnp.zeros((rows, 128), F32)
    for index, one in enumerate((cross, square, data * data)):
        sums = jnp.where(lane == index, jnp.sum(one * valid, axis=1, keepdims=True), sums)
    sums = sums.T
    gene[...] = jnp.zeros_like(gene)
    slide_sums[...] = jnp.zeros_like(slide_sums)
    for index in range(3):
        gene[pl.ds(16 * index + gene_group(ids, 0, 0, 0), 1), :] = sums[index : index + 1, :]
    lane = lax.broadcasted_iota(jnp.int32, (1, 128), 1)
    slides = jnp.zeros((1, 128), F32)
    logs = jnp.log(jnp.where(valid > 0, mass, 1.0))
    for k in range(SLIDES):
        inside = jnp.where(slide == k, valid, 0.0)
        for index, one in enumerate((inside, inside * mass, inside * logs)):
            total = jnp.sum(one, axis=1, keepdims=True)
            slides = jnp.where(lane == 3 * index + k, total, slides)
    slide_sums[0:1, :] = slides
    for index, one in enumerate((cross, square)):
        total = jnp.sum(one, axis=0, keepdims=True)
        for k in range(total.shape[1] // 128):
            at = 48 + 8 * index + k
            gene[at : at + 1, :] = total[:, 128 * k : 128 * k + 128]


def stats_call(ids, piece, spatial, spot, totals):
    blocks, rows, spots = piece.shape
    return pl.pallas_call(
        stats_kernel,
        grid_spec=pltpu.PrefetchScalarGridSpec(
            num_scalar_prefetch=1,
            grid=(1,),
            in_specs=[
                fixed((blocks, rows, spots)),
                pl.BlockSpec((blocks, 1, rows, spots), lambda i, ids: (0, gene_group(ids, 0, 0, 0), 0, 0)),
                fixed((8, spots)),
                fixed((8, spots)),
            ],
            out_specs=[fixed((64, 128)), fixed((8, 128))],
        ),
        out_shape=[jax.ShapeDtypeStruct((64, 128), F32), jax.ShapeDtypeStruct((8, 128), F32)],
        compiler_params=vmem(8),
        cost_estimate=NO_COST,
        name="stats",
    )(ids, piece, streamed(spatial), spot, totals)


def coef_kernel(ids, genes_slides, sums, spot, totals, gene, rows, scalars, pairs):
    valid, slide, squares = (spot[k : k + 1, :] for k in range(3))
    share = 1.0 / totals[0:1, :]
    mass = totals[1:2, :] * share
    genes = float(16 * sums.shape[1])

    def wide(index):
        return jnp.concatenate([sums[index + k : index + k + 1, :] for k in range(8)], axis=1)

    dots, own = wide(48), wide(56)
    dot, aa, bb = genes_slides[0:16, :], genes_slides[16:32, :], genes_slides[32:48, :]
    scale = lax.rsqrt(aa * bb + 1e-06)
    pairs[0:16, :] = dot * scale**3 * bb / genes
    pairs[16:32, :] = scale / genes
    pair = [pairs[pl.ds(k + gene_group(ids, *one), 1), :] for k in (0, 16) for one in PIECES]
    gene[...] = jnp.concatenate([*pair, jnp.zeros((96, 128), F32)]).T
    total = jnp.sum(jnp.sum(dot * scale, axis=1, keepdims=True), axis=0, keepdims=True)
    nvs = jnp.zeros((1, 1), F32)
    density = jnp.zeros((1, 1), F32)
    nk, tk = jnp.ones_like(valid), jnp.ones_like(valid)
    for k in range(SLIDES):
        count, held, logs = (genes_slides[48:49, 3 * j + k : 3 * j + k + 1] for j in range(3))
        some = count > 0
        safe = jnp.where(some, count, 1.0)
        nvs += count
        density += jnp.where(some, jnp.log(jnp.where(some, held, 1.0) / safe) - logs / safe, 0.0)
        here = (slide == k) & (valid > 0)
        nk = jnp.where(here, count, nk)
        tk = jnp.where(here, held, tk)
    scale = lax.rsqrt(own * squares + 1e-06)
    grad_mass = valid / SLIDES * (1.0 / tk - 1.0 / (nk * jnp.where(valid > 0, mass, 1.0)))
    mask = valid * share
    by_pred, by_data = dots * scale**3 * squares / nvs, scale / nvs
    for index, one in enumerate((by_pred * share * mask, by_data * mask, mask, share * mask)):
        rows[8 * index : 8 * index + 8, :] = jnp.broadcast_to(one, (8, one.shape[1]))
    rows[32:40, :] = jnp.concatenate([grad_mass * share, jnp.zeros((7, valid.shape[1]), F32)])
    cosines = jnp.sum(valid * dots * scale, axis=1, keepdims=True)
    lane = lax.broadcasted_iota(jnp.int32, (1, 128), 1)
    out = jnp.zeros((1, 128), F32)
    for index, one in enumerate((total / genes, cosines / nvs, density / SLIDES)):
        out = jnp.where(lane == index, one, out)
    scalars[...] = out


def coef_call(ids, genes_slides, sums, spot, totals):
    spots = spot.shape[1]
    return pl.pallas_call(
        coef_kernel,
        grid_spec=pltpu.PrefetchScalarGridSpec(
            num_scalar_prefetch=1,
            grid=(1,),
            in_specs=[fixed(genes_slides.shape), fixed(sums.shape), fixed((8, spots)), fixed((8, spots))],
            out_specs=[fixed((128, 128)), fixed((40, spots)), fixed((1, 128))],
            scratch_shapes=[pltpu.VMEM((32, 128), F32)],
        ),
        out_shape=[
            jax.ShapeDtypeStruct((128, 128), F32),
            jax.ShapeDtypeStruct((40, spots), F32),
            jax.ShapeDtypeStruct((1, 128), F32),
        ],
        compiler_params=vmem(6),
        cost_estimate=NO_COST,
        name="coef",
    )(ids, genes_slides, sums, spot, totals)


def grad_rows(pred, data, gene, spot, lane):
    by_pred = gene[:, lane : lane + 1].reshape(2, 8, 1)
    by_data = gene[:, 16 + lane : 17 + lane].reshape(2, 8, 1)
    pred, data = pred.reshape(2, 8, pred.shape[1]), data.reshape(2, 8, data.shape[1])
    grad = pred * (by_pred * spot[24:32, :] + spot[0:8, :])
    grad = grad - data * (by_data * spot[16:24, :] + spot[8:16, :])
    return grad.reshape(16, grad.shape[2]), jnp.sum(grad * pred, axis=0)


def grad_kernel(ids, *refs, count, lane):
    pred, data, refs = refs[: 2 * count], refs[2 * count : 3 * count], refs[3 * count :]
    gene, spot, grad, column = refs[0], refs[1], refs[-2], refs[-1]

    @pl.when(pl.program_id(0) == 0)
    def _():
        column[...] = jnp.zeros_like(column)

    total = jnp.zeros(column.shape, F32)
    for index, part in enumerate(pred):
        for sub in range(2):
            at = gene_group(ids, *PIECES[lane + 2 * index + sub])
            row = pl.multiple_of((at & 3) * 16, 16)
            to = pl.ds(pl.multiple_of(at * 16, 16) if count > 1 else row, 16)
            for block in range(part.shape[1]):
                rows, inner = grad_rows(
                    part[sub, block],
                    data[index // 2][block, 0, pl.ds(row, 16), :],
                    gene[16 * block : 16 * block + 16, :],
                    spot,
                    lane + 2 * index + sub,
                )
                grad[0, block, to, :], grad[1, block, to, :] = split(rows)
                total += inner
    column[...] += total


def grad_call(ids, pred, spatial, gene, spot, lane, chips, done=()):
    blocks, groups, rows, spots = spatial.shape
    count = len(pred) // 2
    each = 2

    def chip(i, ids):
        return (ids[2] + pick(i, chips)) & 3

    if count > 1:
        grad = pl.BlockSpec(
            (2, each, groups * rows, spots), lambda i, ids: (0, chip(i, ids), 0, 0)
        )
    else:
        grad = pl.BlockSpec(
            (2, each, rows, spots),
            lambda i, ids: (0, chip(i, ids), (ids[0] + PIECES[lane][0]) & 3, 0),
        )

    def group(k):
        step = PIECES[lane + 4 * k][0]
        return pl.BlockSpec(
            (each, 1, rows, spots), lambda i, ids: (chip(i, ids), (ids[0] + step) & 3, 0, 0)
        )

    return pl.pallas_call(
        functools.partial(grad_kernel, count=count, lane=lane),
        grid_spec=pltpu.PrefetchScalarGridSpec(
            num_scalar_prefetch=1,
            grid=(len(chips),),
            in_specs=[pl.BlockSpec((2, each, 16, spots), lambda i, ids: (0, chip(i, ids), 0, 0))]
            * (2 * count)
            + [group(k) for k in range(count)]
            + [
                pl.BlockSpec((16 * each, 128), lambda i, ids: (chip(i, ids), 0)),
                fixed(spot.shape),
            ]
            + [pl.BlockSpec(memory_space=pl.ANY)] * len(done),
            out_specs=[grad, fixed((8, spots))],
        ),
        out_shape=[
            jax.ShapeDtypeStruct((2, blocks, groups * rows, spots), BF16),
            jax.ShapeDtypeStruct((8, spots), F32),
        ],
        input_output_aliases={3 * count + 3: 0} if done else {},
        compiler_params=vmem(16),
        cost_estimate=NO_COST,
        name="grad",
    )(ids, *pred, *[streamed(spatial)] * count, gene, spot, *done)


def back_kernel(ids, grad, masses, expr, *refs, extra):
    sums, *outs = refs[extra:]
    step = pl.program_id(0)
    left = grad[0, 0], grad[1, 0]
    rows = left[0].shape[0]
    if extra:
        pair = split(jnp.concatenate([refs[0][...], jnp.zeros_like(refs[0])]))
        left = [jnp.concatenate(both) for both in zip(left, pair)]
    part = product(left, masses, ((1,), (1,)))

    @pl.when(step == 0)
    def _():
        sums[...] = part[rows : rows + 8] if extra else jnp.zeros_like(sums)

    part = part[:rows]
    sums[...] += jnp.sum((part * expr[...]).reshape(-1, 8, part.shape[1]), axis=0)
    for index, out in enumerate(outs):

        @pl.when(step == index)
        def _(out=out):
            out[...] = part


def back_call(ids, parts, grad, masses, expr, spot=None):
    _, blocks, rows, spots = grad.shape
    cells = masses.shape[1]
    count = len(parts)
    extra = [] if spot is None else [spot]

    def block(i, ids):
        step, other = (pick(i, [part[k] for part in parts]) for k in range(2))
        return ((ids[2] + step) & 3) * 2 + (ids[3] ^ other)

    return pl.pallas_call(
        functools.partial(back_kernel, extra=len(extra)),
        grid_spec=pltpu.PrefetchScalarGridSpec(
            num_scalar_prefetch=1,
            grid=(count,),
            in_specs=[
                pl.BlockSpec((2, 1, rows, spots), lambda i, ids: (0, block(i, ids), 0, 0)),
                RESIDENT,
                pl.BlockSpec((rows, cells), lambda i, ids: (block(i, ids), 0)),
            ]
            + [pl.BlockSpec((8, spots), lambda i, ids: (4, 0))] * len(extra),
            out_specs=[fixed((8, cells))] + [fixed((rows, cells))] * count,
        ),
        out_shape=[jax.ShapeDtypeStruct((8, cells), F32)]
        + [jax.ShapeDtypeStruct((rows, cells), F32)] * count,
        compiler_params=vmem(20),
        cost_estimate=NO_COST,
        name="back",
    )(ids, grad, masses, streamed(expr), *extra)


def lift_kernel(above, below, far_up, far_down, out_above, out_below):
    rows = far_up.shape[0]
    out_above[:rows, :] = above[:rows, :] + far_up[...]
    out_above[rows:, :] = above[rows:, :]
    out_below[:rows, :] = below[:rows, :]
    out_below[rows:, :] = below[rows:, :] + far_down[...]


def lift_call(above, below, far_up, far_down):
    rows, cells = far_up.shape
    block = 256
    far = pl.BlockSpec((rows, block), lambda i: (0, i))
    whole = pl.BlockSpec((2 * rows, block), lambda i: (0, i))
    return pl.pallas_call(
        lift_kernel,
        grid=(cells // block,),
        in_specs=[whole, whole, far, far],
        out_specs=[whole, whole],
        out_shape=[jax.ShapeDtypeStruct(above.shape, F32)] * 2,
        compiler_params=vmem(8),
        cost_estimate=pl.CostEstimate(flops=10**10, bytes_accessed=0, transcendentals=0),
        name="lift",
    )(above, below, far_up, far_down)


def map_kernel(expr, grad, masses, keep, spot, *rest, scale, start):
    out = rest[-1]
    step = pl.program_id(0) + start
    columns = pl.ds(pl.multiple_of(step * masses.shape[1], masses.shape[1]), masses.shape[1])
    pair = expr[0, :, columns], expr[1, :, columns]
    inner = product(pair, grad, ((0,), (0,))) + spot[0:1, :]
    expo = masses[0].astype(F32) + masses[1].astype(F32)
    for part in range(masses.shape[1] // 128):
        rows = slice(part * 128, part * 128 + 128)
        weight = as_column(keep[pl.ds(step * (masses.shape[1] // 128) + part, 1), :])
        out[rows, :] = (scale * expo[rows]) * (weight * inner[rows] - spot[1:2, :])


def map_call(start, stop, expr, grad, masses, keep, spot, scale, done=()):
    _, genes, cells = expr.shape
    spots = masses.shape[2]
    block = 256
    return pl.pallas_call(
        functools.partial(map_kernel, scale=scale, start=start),
        grid=(stop - start,),
        in_specs=[
            RESIDENT,
            RESIDENT,
            pl.BlockSpec((2, block, spots), lambda i: (0, i + start, 0)),
            fixed(keep.shape),
            fixed((8, spots)),
        ]
        + [pl.BlockSpec(memory_space=pl.ANY)] * len(done),
        out_specs=pl.BlockSpec((block, spots), lambda i: (i + start, 0)),
        out_shape=jax.ShapeDtypeStruct((cells, spots), F32),
        input_output_aliases={5: 0} if done else {},
        compiler_params=vmem(24),
        cost_estimate=NO_COST,
        name="grad_map",
    )(expr, grad, masses, keep, spot, *done)


def finish_kernel(last, got1, got2, got3, totals, scalars, kind, filt, grad_filter, terms, *, all_cells):
    blocks = kind.shape[0]
    total = (last[...] + got2[...]) + (got1[...] + got3[...])
    nvalid, retained, reg_sum = (totals[2:3, k : k + 1] for k in range(3))
    valid = (kind[...] >= 0).astype(F32)
    sigma = jax.nn.sigmoid(filt[...])
    keep = sigma * valid
    shifted = (retained - 0.35 * nvalid) / (0.1 * all_cells)
    count_term = jnp.sqrt(shifted * shifted + 1.0)
    grad_keep = total[:blocks] + shifted / count_term / (0.1 * all_cells) + (1.0 - 2.0 * keep) / nvalid
    grad_filter[...] = valid * sigma * (1.0 - sigma) * grad_keep * all_cells
    lane = lax.broadcasted_iota(jnp.int32, (1, 128), 1)
    out = jnp.zeros((1, 128), F32)
    parts = (scalars[:, 0:1], total[blocks : blocks + 1, 1:2], scalars[:, 2:3], count_term, reg_sum / nvalid)
    for index, one in enumerate(parts):
        out = jnp.where(lane == index, one, out)
    terms[...] = out


def finish_call(last, got, totals, scalars, kind, filt, all_cells):
    return pl.pallas_call(
        functools.partial(finish_kernel, all_cells=float(all_cells)),
        grid=(1,),
        in_specs=[fixed(one.shape) for one in (last, *got, totals, scalars, kind, filt)],
        out_specs=[fixed(kind.shape), fixed((1, 128))],
        out_shape=[jax.ShapeDtypeStruct(kind.shape, F32), jax.ShapeDtypeStruct((1, 128), F32)],
        compiler_params=vmem(4),
        cost_estimate=NO_COST,
        name="finish",
    )(last, *got, totals, scalars, kind, filt)


def on_device(map_logits, filter_logits, expr, spatial, cell_type, slide_id, spot_mask):
    genes, cells = expr.shape
    spots = map_logits.shape[1]
    all_cells = cells * lax.axis_size("cells")
    all_spots = spots * lax.axis_size("spots")
    cell_place = lax.axis_index("cells")
    z, x = cell_place >> 2, cell_place & 3
    spot_place = lax.axis_index("spots")
    y, core = spot_place >> 1, spot_place & 1
    first = jnp.where(core == 0, x, z)
    second = jnp.where(core == 0, z, x)
    blocks = cells // 128

    valid = (cell_type >= 0).astype(F32)
    sigma = jax.nn.sigmoid(filter_logits)
    keep = sigma * valid
    spot_valid = spot_mask.astype(F32)
    kind2 = cell_type.reshape(blocks, 128)
    filt2 = filter_logits.reshape(blocks, 128)
    keep2 = keep.reshape(blocks, 128)

    expr4 = expr.reshape(8, 16, 16, cells)
    keep_row = keep.reshape(1, cells)

    ids = jnp.stack([first, second, y, core]).astype(jnp.int32)

    def pred_part(one, two, more, *others):
        return pred_call(after(ids, *others), (one, two), expr4, keep_row, masses, totals, more)

    masses, types, totals, *far = expo_call(
        ids, ((2, 0), (2, 1)), map_logits, kind2, filt2, expr4
    )
    far_right, far_left = along(far[0], 1), along(far[1], -1)
    near = pred_part((1, 1), (-1, 0), (), *far)
    near_right, near_left = along(near[0], 1), along(near[1], -1)
    late = pred_part((1, 0), (-1, 1), (far_right, far_left), *near)
    late_right, late_left = along(late[0], 1), along(late[1], -1)
    own = pred_part((0, 0), (0, 1), (near_left, near_right), *late)
    mine, *pieces = merge_call(own, (late_right, late_left))
    pieces = [across(piece, step + 1) for step, piece in enumerate(pieces)]
    halves = halve_call(after(ids, mine), expr)
    types = types + swap_along(after(types, halves), 1)
    spatial_squares = jnp.sum(after(spatial, mine) ** 2, axis=0)
    spot_rows = stacked([spot_valid, slide_id.astype(F32), spatial_squares])
    mine = after(mine, spot_rows, halves, types)
    piece = mine + pieces[0] + pieces[1] + pieces[2]
    totals = piece[-1]
    piece = piece[:-1].reshape(8, 16, spots)
    share = 1.0 / totals[0]
    mass = totals[1] * share

    got = [across(piece, step) for step in (1, 2, 3)]
    sums, slides = stats_call(
        ids,
        piece,
        spatial.reshape(8, 16, 16, spots),
        spot_rows,
        totals,
    )
    sums = sums + swap_along(sums, 1)
    sums = sums + swap_along(sums, 3)
    types = types + swap_along(after(types, slides), 3)
    mine = after((jnp.stack([piece, got[2]]), jnp.stack([got[1], got[0]])), sums, types)
    right0, left1 = along(mine[0], 1), along(mine[1], -1)
    right1, left0 = along(mine[1], 1), along(mine[0], -1)
    sums = sums + swap_across(after(sums, *mine), 1)
    sums = sums + swap_across(sums, 3)
    right0, left1, sums = lax.optimization_barrier((right0, left1, sums))
    far0, far1 = along(right0, 1), along(left1, -1)
    genes_slides = jnp.concatenate([sums[:48], slides])
    genes_slides = genes_slides + swap(genes_slides, 0, 0, 0, 1)
    genes_slides = genes_slides + swap(genes_slides, 0, 0, 1, 0)
    genes_slides = after(genes_slides, right1, left0)
    genes_slides = genes_slides + swap(genes_slides, 0, 0, 3, 0)
    pred = [*mine, right0, right1, left0, left1, far0, far1]
    gene_coef, spot_coef, scalars = coef_call(ids, genes_slides, sums, spot_rows, totals)
    spatial4 = spatial.reshape(8, RING, genes // 32, spots)
    grad, column_a = grad_call(ids, pred[:6], spatial4, gene_coef, spot_coef, 0, (0, 1, 2, 3))

    def last_grad(chips, grad, *others):
        return grad_call(
            after(ids, *others), pred[6:], spatial4, gene_coef, spot_coef, 12, chips, (grad,)
        )

    def back_part(steps, grad, spot, *others):
        return back_call(after(ids, *others), steps, grad, masses, expr, spot)

    rows = genes // 16
    grad, column_b = last_grad((2,), grad)
    sums_a, far_a = back_part([(2, 1)], grad, spot_coef)
    far_got = swap(far_a, 0, 0, 0, 1)
    sums_b, far_b = back_part([(2, 0)], grad, None, far_a)
    far = far_b + far_got
    far_up, far_down = up(far[:rows], 1), up(far[rows:], -1)
    grad, column_c = last_grad((1, -1, 0), grad, far)
    sums_c, up_a, down_a, up_b, down_b = back_part([(1, 1), (-1, 1), (1, 0), (-1, 0)], grad, None)
    up_got, down_got = swap(up_a, 0, 0, 0, 1), swap(down_a, 0, 0, 0, 1)
    above, below = lift_call(up_b, down_b, far_up, far_down)
    above, below = above + up_got, below + down_got
    near_up, near_down = up(above, 1), up(below, -1)
    sums_d, own_a, own_b = back_part([(0, 1), (0, 0)], grad, None, above, below)
    types = types + swap_across(after(types, above), 1)
    own_a = jnp.concatenate([swap(own_a[:rows], 0, 0, 0, 1), swap(own_a[rows:], 0, 0, 0, 1)])
    last = jnp.concatenate(
        [
            jnp.sum(sums_a + sums_b + sums_c + sums_d, axis=0).reshape(blocks, 128),
            scalars,
            jnp.zeros((5, 128), F32),
        ]
    )

    column = jnp.sum(column_a + column_b + column_c, axis=0) * share + spot_coef[32] * mass
    map_rows = stacked([spot_coef[32], column])
    map_rows = after(map_rows, above, below)
    map_args = (halves, grad.reshape(2, genes, spots), masses, keep2, map_rows, all_cells * genes)
    steps = cells // 256
    got, types_got = swap(last, 0, 0, 0, 1), swap_across(after(types, own_b), 3)
    grad_map = map_call(0, steps - 2, *map_args)
    got, types_got = after((got, types_got), grad_map)
    last, types = last + got, types + types_got
    got = [up(last, step) for step in (1, 2, 3)]
    grad_map = map_call(steps - 2, steps, *map_args, done=(after(grad_map, own_a),))
    got = after(tuple(got), grad_map)
    grad_weighted = after(own_b + own_a, grad_map) + near_up + near_down
    grad_expr = grad_weighted * (keep * (genes * all_spots))[None, :]

    type_fraction = types * share

    grad_filter, loss_terms = finish_call(last, got, totals, scalars, kind2, filt2, all_cells)
    return (loss_terms[0, :5], type_fraction, grad_map, grad_filter.reshape(cells), grad_expr)


def solution(mesh):
    in_specs = (
        P("cells", "spots"),
        P("cells"),
        P(None, "cells"),
        P(None, "spots"),
        P("cells"),
        P("spots"),
        P("spots"),
    )
    out_specs = (P(), P(None, "spots"), P("cells", "spots"), P("cells"), P("spots", "cells"))
    return jax.shard_map(
        on_device, mesh=mesh, in_specs=in_specs, out_specs=out_specs, check_vma=False
    )
```

```python
import functools

import jax
import jax.numpy as jnp
from jax import lax
from jax.experimental import pallas as pl
from jax.experimental.pallas import tpu as pltpu
from jax.sharding import PartitionSpec as P

TYPES = 32
SLIDES = 3
RING = 4
F32 = jnp.float32
BF16 = jnp.bfloat16


def vmem(mib):
    return pltpu.CompilerParams(vmem_limit_bytes=mib << 20)


def fixed(shape):
    return pl.BlockSpec(shape, lambda *_: (0,) * len(shape), pipeline_mode=pl.Buffered(1))


def streamed(array):
    return pltpu.with_memory_space_constraint(array, pltpu.HBM)


RESIDENT = pl.BlockSpec(memory_space=pltpu.VMEM)


def cost(flops, moved):
    return pl.CostEstimate(flops=int(flops) // 8, bytes_accessed=int(moved) // 8, transcendentals=0)


NO_COST = pl.CostEstimate(flops=0, bytes_accessed=0, transcendentals=0)


def route(target):
    def flat(z, x, y, core):
        return ((z % RING * RING + x % RING) * RING + y % RING) * 2 + core

    return [
        (flat(z, x, y, core), flat(*target(z, x, y, core)))
        for z in range(RING)
        for x in range(RING)
        for y in range(RING)
        for core in range(2)
    ]


def send(array, target):
    return lax.ppermute(array, ("cells", "spots"), route(target))


def along(array, step):
    return send(array, lambda z, x, y, c: (z, x + step, y, c) if c == 0 else (z + step, x, y, c))


def across(array, step):
    return send(array, lambda z, x, y, c: (z + step, x, y, c) if c == 0 else (z, x + step, y, c))


def up(array, step):
    return send(array, lambda z, x, y, c: (z, x, y + step, c))


def swap(array, mz, mx, my, mc):
    return send(array, lambda z, x, y, c: (z ^ mz, x ^ mx, y ^ my, c ^ mc))


def swap_along(array, mask):
    return send(array, lambda z, x, y, c: (z, x ^ mask, y, c) if c == 0 else (z ^ mask, x, y, c))


def swap_across(array, mask):
    return send(array, lambda z, x, y, c: (z ^ mask, x, y, c) if c == 0 else (z, x ^ mask, y, c))


def after(value, *others):
    return lax.optimization_barrier((value, *others))[0]


def split(value):
    high = value.astype(BF16)
    return high, (value - high.astype(F32)).astype(BF16)


def product(left, right, dims):
    def one(a, b):
        return lax.dot_general(a, b, (dims, ((), ())), preferred_element_type=F32)

    return one(left[0], right[0]) + one(left[0], right[1]) + one(left[1], right[0])


def gene_group(ids, step, half, sub):
    return ((ids[0] + step) & 3) * RING + ((ids[1] + 2 * half + sub) & 3)


PIECES = [
    (step, half, sub)
    for step, half in ((0, 0), (0, 1), (-1, 0), (-1, 1), (1, 0), (1, 1), (2, 0), (2, 1))
    for sub in range(2)
]


def pick(index, values):
    out = values[0]
    for k, value in enumerate(values[1:]):
        out = jnp.where(index == k + 1, value, out)
    return out


def stacked(rows):
    row = lax.broadcasted_iota(jnp.int32, (8, rows[0].shape[0]), 0)
    out = jnp.zeros(row.shape, F32)
    for k, value in enumerate(rows):
        out = jnp.where(row == k, value[None, :], out)
    return out


def as_column(row):
    return jnp.broadcast_to(row, (128, 128)).T[:, :1]


def expo_kernel(ids, logits, kind, filt, *refs):
    expr, (masses, types, totals, out0, out1) = refs[:4], refs[4:]
    step = pl.program_id(0)
    count = logits.shape[0] // 128

    @pl.when(step == 0)
    def _():
        for out in (types, totals, out0, out1):
            out[...] = jnp.zeros_like(out)

    keeps = []
    lane = lax.broadcasted_iota(jnp.int32, (1, totals.shape[1]), 1)
    cell_sums = jnp.zeros(lane.shape, F32)
    for part in range(count):
        rows = slice(part * 128, part * 128 + 128)
        label = kind[pl.ds(step * count + part, 1), :]
        valid = (label >= 0).astype(F32)
        keep = valid * jax.nn.sigmoid(filt[pl.ds(step * count + part, 1), :])
        keeps.append(keep)
        for k, one in enumerate((valid, keep, keep - keep * keep)):
            cell_sums += jnp.where(lane == k, jnp.sum(one, axis=1, keepdims=True), 0.0)
        expo = jnp.exp(logits[rows]) * as_column(valid)
        masses[0, rows], masses[1, rows] = split(expo)
        whole = jnp.sum(expo, axis=0, keepdims=True)
        kept = jnp.sum(expo * as_column(keep), axis=0, keepdims=True)
        row = lax.broadcasted_iota(jnp.int32, types.shape, 0)
        types[...] += jnp.where(row == jnp.max(label, axis=1, keepdims=True), whole, 0.0)
        row = lax.broadcasted_iota(jnp.int32, totals.shape, 0)
        totals[...] += jnp.where(row == 0, whole, jnp.where(row == 1, kept, 0.0))
    totals[2:3, :] += cell_sums
    weighted = jnp.concatenate([part[...].reshape(-1, logits.shape[0]) for part in expr])
    weighted = weighted * jnp.concatenate(keeps, axis=1)
    part = product(split(weighted), masses, ((1,), (0,)))
    half = part.shape[0] // 2
    for index, out in enumerate((out0, out1)):
        new = part[index * half : index * half + half].reshape(-1, 8, part.shape[1])
        out[: half // 8] += new
        out[half // 8] = totals[...]


def expo_call(ids, parts, logits, kind, filt, expr):
    cells, spots = logits.shape
    blocks, groups, rows, _ = expr.shape
    block = 256

    def genes(part, sub):
        return pl.BlockSpec(
            (blocks, 1, rows, block), lambda i, ids: (0, gene_group(ids, *part, sub), 0, i)
        )

    return pl.pallas_call(
        expo_kernel,
        grid_spec=pltpu.PrefetchScalarGridSpec(
            num_scalar_prefetch=1,
            grid=(cells // block,),
            in_specs=[
                pl.BlockSpec((block, spots), lambda i, w: (i, 0)),
                fixed(kind.shape),
                fixed(filt.shape),
            ]
            + [genes(part, sub) for part in parts for sub in range(2)],
            out_specs=[
                pl.BlockSpec((2, block, spots), lambda i, w: (0, i, 0)),
                fixed((TYPES, spots)),
                fixed((8, spots)),
                fixed((blocks * rows // 4 + 1, 8, spots)),
                fixed((blocks * rows // 4 + 1, 8, spots)),
            ],
        ),
        out_shape=[
            jax.ShapeDtypeStruct((2, cells, spots), BF16),
            jax.ShapeDtypeStruct((TYPES, spots), F32),
            jax.ShapeDtypeStruct((8, spots), F32),
            jax.ShapeDtypeStruct((blocks * rows // 4 + 1, 8, spots), F32),
            jax.ShapeDtypeStruct((blocks * rows // 4 + 1, 8, spots), F32),
        ],
        compiler_params=vmem(16),
        cost_estimate=cost(0, cells * spots * 8),
        name="expo",
    )(ids, streamed(logits), kind, filt, *[streamed(expr)] * 4)


def pred_kernel(ids, expr_a, expr_b, keep, masses, totals, *refs):
    more, outs = refs[:-2], refs[-2:]
    rows = 2 * expr_a.shape[0] * expr_a.shape[2]
    weighted = jnp.concatenate(
        [part[...].reshape(rows // 2, keep.shape[1]) for part in (expr_a, expr_b)]
    )
    part = product(split(weighted * keep[...]), masses, ((1,), (0,)))
    part = part.reshape(rows // 8, 8, part.shape[1])
    for step, out in enumerate(outs):

        @pl.when(pl.program_id(0) == step)
        def _(step=step, out=out):
            if more:
                out[: rows // 8] = part + more[step][: rows // 8]
                out[rows // 8] = totals[...] + more[step][rows // 8]
            else:
                out[: rows // 8] = part
                out[rows // 8] = totals[...]


def pred_call(ids, parts, expr, keep, masses, totals, more=()):
    blocks, groups, rows, cells = expr.shape
    spots = masses.shape[2]
    tiles = blocks * rows // 4 + 1

    def genes(sub):
        def place(i, ids):
            step, half = (pick(i, [part[k] for part in parts]) for k in range(2))
            return (0, gene_group(ids, step, half, sub), 0, 0)

        return pl.BlockSpec((blocks, 1, rows, cells), place)

    return pl.pallas_call(
        pred_kernel,
        grid_spec=pltpu.PrefetchScalarGridSpec(
            num_scalar_prefetch=1,
            grid=(2,),
            in_specs=[
                genes(0),
                genes(1),
                fixed((1, cells)),
                RESIDENT,
                fixed((8, spots)),
            ]
            + [fixed((tiles, 8, spots))] * len(more),
            out_specs=[fixed((tiles, 8, spots))] * 2,
        ),
        out_shape=[jax.ShapeDtypeStruct((tiles, 8, spots), F32)] * 2,
        compiler_params=vmem(16),
        cost_estimate=cost(24 * blocks * rows * cells * spots, 4 * cells * spots + 16 * blocks * rows * (cells + spots)),
        name="pred",
    )(ids, *[streamed(expr)] * 2, keep, masses, totals, *more)


def merge_kernel(own0, own1, got0, got1, *outs):
    tiles = outs[0].shape[0] - 1
    for half, (own, got) in enumerate(((own0, got0), (own1, got1))):
        for sub in range(2):
            out = outs[2 * half + sub]
            out[:tiles] = own[sub * tiles : sub * tiles + tiles] + got[sub * tiles : sub * tiles + tiles]
            out[tiles] = own[2 * tiles] + got[2 * tiles]


def merge_call(own, got):
    tiles, _, spots = own[0].shape
    block = 256
    whole = pl.BlockSpec((tiles, 8, block), lambda i: (0, 0, i))
    piece = (tiles // 2 + 1, 8, spots)
    return pl.pallas_call(
        merge_kernel,
        grid=(spots // block,),
        in_specs=[whole] * 4,
        out_specs=[pl.BlockSpec((tiles // 2 + 1, 8, block), lambda i: (0, 0, i))] * 4,
        out_shape=[jax.ShapeDtypeStruct(piece, F32)] * 4,
        compiler_params=vmem(12),
        cost_estimate=NO_COST,
        name="merge",
    )(*own, *got)


def stats_kernel(ids, piece, spatial, spot, totals, gene, slide_sums):
    rows = piece.shape[0] * piece.shape[1]
    valid, slide = spot[0:1, :], spot[1:2, :]
    share = 1.0 / totals[0:1, :]
    mass = totals[1:2, :] * share
    value = piece[...].reshape(rows, piece.shape[2]) * share
    data = spatial[...].reshape(value.shape)
    cross, square = value * data, value * value
    lane = lax.broadcasted_iota(jnp.int32, (rows, 128), 1)
    sums = jnp.zeros((rows, 128), F32)
    for index, one in enumerate((cross, square, data * data)):
        sums = jnp.where(lane == index, jnp.sum(one * valid, axis=1, keepdims=True), sums)
    sums = sums.T
    gene[...] = jnp.zeros_like(gene)
    slide_sums[...] = jnp.zeros_like(slide_sums)
    for index in range(3):
        gene[pl.ds(16 * index + gene_group(ids, 0, 0, 0), 1), :] = sums[index : index + 1, :]
    lane = lax.broadcasted_iota(jnp.int32, (1, 128), 1)
    slides = jnp.zeros((1, 128), F32)
    logs = jnp.log(jnp.where(valid > 0, mass, 1.0))
    for k in range(SLIDES):
        inside = jnp.where(slide == k, valid, 0.0)
        for index, one in enumerate((inside, inside * mass, inside * logs)):
            total = jnp.sum(one, axis=1, keepdims=True)
            slides = jnp.where(lane == 3 * index + k, total, slides)
    slide_sums[0:1, :] = slides
    for index, one in enumerate((cross, square)):
        total = jnp.sum(one, axis=0, keepdims=True)
        for k in range(total.shape[1] // 128):
            at = 48 + 8 * index + k
            gene[at : at + 1, :] = total[:, 128 * k : 128 * k + 128]


def stats_call(ids, piece, spatial, spot, totals):
    blocks, rows, spots = piece.shape
    return pl.pallas_call(
        stats_kernel,
        grid_spec=pltpu.PrefetchScalarGridSpec(
            num_scalar_prefetch=1,
            grid=(1,),
            in_specs=[
                fixed((blocks, rows, spots)),
                pl.BlockSpec((blocks, 1, rows, spots), lambda i, ids: (0, gene_group(ids, 0, 0, 0), 0, 0)),
                fixed((8, spots)),
                fixed((8, spots)),
            ],
            out_specs=[fixed((64, 128)), fixed((8, 128))],
        ),
        out_shape=[jax.ShapeDtypeStruct((64, 128), F32), jax.ShapeDtypeStruct((8, 128), F32)],
        compiler_params=vmem(8),
        cost_estimate=NO_COST,
        name="stats",
    )(ids, piece, streamed(spatial), spot, totals)


def coef_kernel(ids, genes_slides, sums, spot, totals, gene, rows, scalars, pairs):
    valid, slide, squares = (spot[k : k + 1, :] for k in range(3))
    share = 1.0 / totals[0:1, :]
    mass = totals[1:2, :] * share
    genes = float(16 * sums.shape[1])

    def wide(index):
        return jnp.concatenate([sums[index + k : index + k + 1, :] for k in range(8)], axis=1)

    dots, own = wide(48), wide(56)
    dot, aa, bb = genes_slides[0:16, :], genes_slides[16:32, :], genes_slides[32:48, :]
    scale = lax.rsqrt(aa * bb + 1e-06)
    pairs[0:16, :] = dot * scale**3 * bb / genes
    pairs[16:32, :] = scale / genes
    pair = [pairs[pl.ds(k + gene_group(ids, *one), 1), :] for k in (0, 16) for one in PIECES]
    gene[...] = jnp.concatenate([*pair, jnp.zeros((96, 128), F32)]).T
    total = jnp.sum(jnp.sum(dot * scale, axis=1, keepdims=True), axis=0, keepdims=True)
    nvs = jnp.zeros((1, 1), F32)
    density = jnp.zeros((1, 1), F32)
    nk, tk = jnp.ones_like(valid), jnp.ones_like(valid)
    for k in range(SLIDES):
        count, held, logs = (genes_slides[48:49, 3 * j + k : 3 * j + k + 1] for j in range(3))
        some = count > 0
        safe = jnp.where(some, count, 1.0)
        nvs += count
        density += jnp.where(some, jnp.log(jnp.where(some, held, 1.0) / safe) - logs / safe, 0.0)
        here = (slide == k) & (valid > 0)
        nk = jnp.where(here, count, nk)
        tk = jnp.where(here, held, tk)
    scale = lax.rsqrt(own * squares + 1e-06)
    grad_mass = valid / SLIDES * (1.0 / tk - 1.0 / (nk * jnp.where(valid > 0, mass, 1.0)))
    mask = valid * share
    by_pred, by_data = dots * scale**3 * squares / nvs, scale / nvs
    for index, one in enumerate((by_pred * share * mask, by_data * mask, mask, share * mask)):
        rows[8 * index : 8 * index + 8, :] = jnp.broadcast_to(one, (8, one.shape[1]))
    rows[32:40, :] = jnp.concatenate([grad_mass * share, jnp.zeros((7, valid.shape[1]), F32)])
    cosines = jnp.sum(valid * dots * scale, axis=1, keepdims=True)
    lane = lax.broadcasted_iota(jnp.int32, (1, 128), 1)
    out = jnp.zeros((1, 128), F32)
    for index, one in enumerate((total / genes, cosines / nvs, density / SLIDES)):
        out = jnp.where(lane == index, one, out)
    scalars[...] = out


def coef_call(ids, genes_slides, sums, spot, totals):
    spots = spot.shape[1]
    return pl.pallas_call(
        coef_kernel,
        grid_spec=pltpu.PrefetchScalarGridSpec(
            num_scalar_prefetch=1,
            grid=(1,),
            in_specs=[fixed(genes_slides.shape), fixed(sums.shape), fixed((8, spots)), fixed((8, spots))],
            out_specs=[fixed((128, 128)), fixed((40, spots)), fixed((1, 128))],
            scratch_shapes=[pltpu.VMEM((32, 128), F32)],
        ),
        out_shape=[
            jax.ShapeDtypeStruct((128, 128), F32),
            jax.ShapeDtypeStruct((40, spots), F32),
            jax.ShapeDtypeStruct((1, 128), F32),
        ],
        compiler_params=vmem(6),
        cost_estimate=NO_COST,
        name="coef",
    )(ids, genes_slides, sums, spot, totals)


def grad_rows(pred, data, gene, spot, lane):
    by_pred = gene[:, lane : lane + 1].reshape(2, 8, 1)
    by_data = gene[:, 16 + lane : 17 + lane].reshape(2, 8, 1)
    pred, data = pred.reshape(2, 8, pred.shape[1]), data.reshape(2, 8, data.shape[1])
    grad = pred * (by_pred * spot[24:32, :] + spot[0:8, :])
    grad = grad - data * (by_data * spot[16:24, :] + spot[8:16, :])
    return grad.reshape(16, grad.shape[2]), jnp.sum(grad * pred, axis=0)


def grad_kernel(ids, *refs, count, lane):
    pred, data, refs = refs[: 2 * count], refs[2 * count : 3 * count], refs[3 * count :]
    gene, spot, grad, column = refs[0], refs[1], refs[-2], refs[-1]

    @pl.when(pl.program_id(0) == 0)
    def _():
        column[...] = jnp.zeros_like(column)

    total = jnp.zeros(column.shape, F32)
    for index, part in enumerate(pred):
        for sub in range(2):
            at = gene_group(ids, *PIECES[lane + 2 * index + sub])
            row = pl.multiple_of((at & 3) * 16, 16)
            to = pl.ds(pl.multiple_of(at * 16, 16) if count > 1 else row, 16)
            for block in range(part.shape[1]):
                rows, inner = grad_rows(
                    part[sub, block],
                    data[index // 2][block, 0, pl.ds(row, 16), :],
                    gene[16 * block : 16 * block + 16, :],
                    spot,
                    lane + 2 * index + sub,
                )
                grad[0, block, to, :], grad[1, block, to, :] = split(rows)
                total += inner
    column[...] += total


def grad_call(ids, pred, spatial, gene, spot, lane, chips, done=()):
    blocks, groups, rows, spots = spatial.shape
    count = len(pred) // 2
    each = 2

    def chip(i, ids):
        return (ids[2] + pick(i, chips)) & 3

    if count > 1:
        grad = pl.BlockSpec(
            (2, each, groups * rows, spots), lambda i, ids: (0, chip(i, ids), 0, 0)
        )
    else:
        grad = pl.BlockSpec(
            (2, each, rows, spots),
            lambda i, ids: (0, chip(i, ids), (ids[0] + PIECES[lane][0]) & 3, 0),
        )

    def group(k):
        step = PIECES[lane + 4 * k][0]
        return pl.BlockSpec(
            (each, 1, rows, spots), lambda i, ids: (chip(i, ids), (ids[0] + step) & 3, 0, 0)
        )

    return pl.pallas_call(
        functools.partial(grad_kernel, count=count, lane=lane),
        grid_spec=pltpu.PrefetchScalarGridSpec(
            num_scalar_prefetch=1,
            grid=(len(chips),),
            in_specs=[pl.BlockSpec((2, each, 16, spots), lambda i, ids: (0, chip(i, ids), 0, 0))]
            * (2 * count)
            + [group(k) for k in range(count)]
            + [
                pl.BlockSpec((16 * each, 128), lambda i, ids: (chip(i, ids), 0)),
                fixed(spot.shape),
            ]
            + [pl.BlockSpec(memory_space=pl.ANY)] * len(done),
            out_specs=[grad, fixed((8, spots))],
        ),
        out_shape=[
            jax.ShapeDtypeStruct((2, blocks, groups * rows, spots), BF16),
            jax.ShapeDtypeStruct((8, spots), F32),
        ],
        input_output_aliases={3 * count + 3: 0} if done else {},
        compiler_params=vmem(16),
        cost_estimate=NO_COST,
        name="grad",
    )(ids, *pred, *[streamed(spatial)] * count, gene, spot, *done)


def back_kernel(ids, grad, masses, expr, *refs, extra):
    sums, *outs = refs[extra:]
    step = pl.program_id(0)
    left = grad[0, 0], grad[1, 0]
    rows = left[0].shape[0]
    if extra:
        pair = split(jnp.concatenate([refs[0][...], jnp.zeros_like(refs[0])]))
        left = [jnp.concatenate(both) for both in zip(left, pair)]
    part = product(left, masses, ((1,), (1,)))

    @pl.when(step == 0)
    def _():
        sums[...] = part[rows : rows + 8] if extra else jnp.zeros_like(sums)

    part = part[:rows]
    sums[...] += jnp.sum((part * expr[...]).reshape(-1, 8, part.shape[1]), axis=0)
    for index, out in enumerate(outs):

        @pl.when(step == index)
        def _(out=out):
            out[...] = part


def back_call(ids, parts, grad, masses, expr, spot=None):
    _, blocks, rows, spots = grad.shape
    cells = masses.shape[1]
    count = len(parts)
    extra = [] if spot is None else [spot]

    def block(i, ids):
        step, other = (pick(i, [part[k] for part in parts]) for k in range(2))
        return ((ids[2] + step) & 3) * 2 + (ids[3] ^ other)

    return pl.pallas_call(
        functools.partial(back_kernel, extra=len(extra)),
        grid_spec=pltpu.PrefetchScalarGridSpec(
            num_scalar_prefetch=1,
            grid=(count,),
            in_specs=[
                pl.BlockSpec((2, 1, rows, spots), lambda i, ids: (0, block(i, ids), 0, 0)),
                RESIDENT,
                pl.BlockSpec((rows, cells), lambda i, ids: (block(i, ids), 0)),
            ]
            + [pl.BlockSpec((8, spots), lambda i, ids: (4, 0))] * len(extra),
            out_specs=[fixed((8, cells))] + [fixed((rows, cells))] * count,
        ),
        out_shape=[jax.ShapeDtypeStruct((8, cells), F32)]
        + [jax.ShapeDtypeStruct((rows, cells), F32)] * count,
        compiler_params=vmem(20),
        cost_estimate=NO_COST,
        name="back",
    )(ids, grad, masses, streamed(expr), *extra)


def lift_kernel(above, below, far_up, far_down, out_above, out_below):
    rows = far_up.shape[0]
    out_above[:rows, :] = above[:rows, :] + far_up[...]
    out_above[rows:, :] = above[rows:, :]
    out_below[:rows, :] = below[:rows, :]
    out_below[rows:, :] = below[rows:, :] + far_down[...]


def lift_call(above, below, far_up, far_down):
    rows, cells = far_up.shape
    block = 256
    far = pl.BlockSpec((rows, block), lambda i: (0, i))
    whole = pl.BlockSpec((2 * rows, block), lambda i: (0, i))
    return pl.pallas_call(
        lift_kernel,
        grid=(cells // block,),
        in_specs=[whole, whole, far, far],
        out_specs=[whole, whole],
        out_shape=[jax.ShapeDtypeStruct(above.shape, F32)] * 2,
        compiler_params=vmem(8),
        cost_estimate=pl.CostEstimate(flops=10**10, bytes_accessed=0, transcendentals=0),
        name="lift",
    )(above, below, far_up, far_down)


def map_kernel(expr, grad, masses, keep, spot, *rest, scale, start):
    out = rest[-1]
    step = pl.program_id(0) + start
    inner = product(split(expr[...]), grad, ((0,), (0,))) + spot[0:1, :]
    expo = masses[0].astype(F32) + masses[1].astype(F32)
    for part in range(masses.shape[1] // 128):
        rows = slice(part * 128, part * 128 + 128)
        weight = as_column(keep[pl.ds(step * (masses.shape[1] // 128) + part, 1), :])
        out[rows, :] = (scale * expo[rows]) * (weight * inner[rows] - spot[1:2, :])


def map_call(start, stop, expr, grad, masses, keep, spot, scale, done=()):
    genes, cells = expr.shape
    spots = masses.shape[2]
    block = 256
    return pl.pallas_call(
        functools.partial(map_kernel, scale=scale, start=start),
        grid=(stop - start,),
        in_specs=[
            pl.BlockSpec((genes, block), lambda i: (0, i + start)),
            RESIDENT,
            pl.BlockSpec((2, block, spots), lambda i: (0, i + start, 0)),
            fixed(keep.shape),
            fixed((8, spots)),
        ]
        + [pl.BlockSpec(memory_space=pl.ANY)] * len(done),
        out_specs=pl.BlockSpec((block, spots), lambda i: (i + start, 0)),
        out_shape=jax.ShapeDtypeStruct((cells, spots), F32),
        input_output_aliases={5: 0} if done else {},
        compiler_params=vmem(24),
        cost_estimate=NO_COST,
        name="grad_map",
    )(streamed(expr), grad, masses, keep, spot, *done)


def finish_kernel(last, got1, got2, got3, totals, scalars, kind, filt, grad_filter, terms, *, all_cells):
    blocks = kind.shape[0]
    total = (last[...] + got2[...]) + (got1[...] + got3[...])
    nvalid, retained, reg_sum = (totals[2:3, k : k + 1] for k in range(3))
    valid = (kind[...] >= 0).astype(F32)
    sigma = jax.nn.sigmoid(filt[...])
    keep = sigma * valid
    shifted = (retained - 0.35 * nvalid) / (0.1 * all_cells)
    count_term = jnp.sqrt(shifted * shifted + 1.0)
    grad_keep = total[:blocks] + shifted / count_term / (0.1 * all_cells) + (1.0 - 2.0 * keep) / nvalid
    grad_filter[...] = valid * sigma * (1.0 - sigma) * grad_keep * all_cells
    lane = lax.broadcasted_iota(jnp.int32, (1, 128), 1)
    out = jnp.zeros((1, 128), F32)
    parts = (scalars[:, 0:1], total[blocks : blocks + 1, 1:2], scalars[:, 2:3], count_term, reg_sum / nvalid)
    for index, one in enumerate(parts):
        out = jnp.where(lane == index, one, out)
    terms[...] = out


def finish_call(last, got, totals, scalars, kind, filt, all_cells):
    return pl.pallas_call(
        functools.partial(finish_kernel, all_cells=float(all_cells)),
        grid=(1,),
        in_specs=[fixed(one.shape) for one in (last, *got, totals, scalars, kind, filt)],
        out_specs=[fixed(kind.shape), fixed((1, 128))],
        out_shape=[jax.ShapeDtypeStruct(kind.shape, F32), jax.ShapeDtypeStruct((1, 128), F32)],
        compiler_params=vmem(4),
        cost_estimate=NO_COST,
        name="finish",
    )(last, *got, totals, scalars, kind, filt)


def on_device(map_logits, filter_logits, expr, spatial, cell_type, slide_id, spot_mask):
    genes, cells = expr.shape
    spots = map_logits.shape[1]
    all_cells = cells * lax.axis_size("cells")
    all_spots = spots * lax.axis_size("spots")
    cell_place = lax.axis_index("cells")
    z, x = cell_place >> 2, cell_place & 3
    spot_place = lax.axis_index("spots")
    y, core = spot_place >> 1, spot_place & 1
    first = jnp.where(core == 0, x, z)
    second = jnp.where(core == 0, z, x)
    blocks = cells // 128

    valid = (cell_type >= 0).astype(F32)
    sigma = jax.nn.sigmoid(filter_logits)
    keep = sigma * valid
    spot_valid = spot_mask.astype(F32)
    kind2 = cell_type.reshape(blocks, 128)
    filt2 = filter_logits.reshape(blocks, 128)
    keep2 = keep.reshape(blocks, 128)

    expr4 = expr.reshape(8, 16, 16, cells)
    keep_row = keep.reshape(1, cells)

    ids = jnp.stack([first, second, y, core]).astype(jnp.int32)

    def pred_part(one, two, more, *others):
        return pred_call(after(ids, *others), (one, two), expr4, keep_row, masses, totals, more)

    masses, types, totals, *far = expo_call(
        ids, ((2, 0), (2, 1)), map_logits, kind2, filt2, expr4
    )
    far_right, far_left = along(far[0], 1), along(far[1], -1)
    near = pred_part((1, 1), (-1, 0), (), *far)
    near_right, near_left = along(near[0], 1), along(near[1], -1)
    late = pred_part((1, 0), (-1, 1), (far_right, far_left), *near)
    late_right, late_left = along(late[0], 1), along(late[1], -1)
    own = pred_part((0, 0), (0, 1), (near_left, near_right), *late)
    mine, *pieces = merge_call(own, (late_right, late_left))
    pieces = [across(piece, step + 1) for step, piece in enumerate(pieces)]
    spatial_squares = jnp.sum(after(spatial, mine) ** 2, axis=0)
    types = types + swap_along(after(types, spatial_squares), 1)
    spot_rows = stacked([spot_valid, slide_id.astype(F32), spatial_squares])
    mine = after(mine, spot_rows, types)
    piece = mine + pieces[0] + pieces[1] + pieces[2]
    totals = piece[-1]
    piece = piece[:-1].reshape(8, 16, spots)
    share = 1.0 / totals[0]
    mass = totals[1] * share

    got = [across(piece, step) for step in (1, 2, 3)]
    sums, slides = stats_call(
        ids,
        piece,
        spatial.reshape(8, 16, 16, spots),
        spot_rows,
        totals,
    )
    sums = sums + swap_along(sums, 1)
    sums = sums + swap_along(sums, 3)
    types = types + swap_along(after(types, slides), 3)
    mine = after((jnp.stack([piece, got[2]]), jnp.stack([got[1], got[0]])), sums, types)
    right0, left1 = along(mine[0], 1), along(mine[1], -1)
    right1, left0 = along(mine[1], 1), along(mine[0], -1)
    sums = sums + swap_across(after(sums, *mine), 1)
    sums = sums + swap_across(sums, 3)
    right0, left1, sums = lax.optimization_barrier((right0, left1, sums))
    far0, far1 = along(right0, 1), along(left1, -1)
    genes_slides = jnp.concatenate([sums[:48], slides])
    genes_slides = genes_slides + swap(genes_slides, 0, 0, 0, 1)
    genes_slides = genes_slides + swap(genes_slides, 0, 0, 1, 0)
    genes_slides = after(genes_slides, right1, left0)
    genes_slides = genes_slides + swap(genes_slides, 0, 0, 3, 0)
    pred = [*mine, right0, right1, left0, left1, far0, far1]
    gene_coef, spot_coef, scalars = coef_call(ids, genes_slides, sums, spot_rows, totals)
    spatial4 = spatial.reshape(8, RING, genes // 32, spots)
    grad, column_a = grad_call(ids, pred[:6], spatial4, gene_coef, spot_coef, 0, (0, 1, 2, 3))

    def last_grad(chips, grad, *others):
        return grad_call(
            after(ids, *others), pred[6:], spatial4, gene_coef, spot_coef, 12, chips, (grad,)
        )

    def back_part(steps, grad, spot, *others):
        return back_call(after(ids, *others), steps, grad, masses, expr, spot)

    rows = genes // 16
    grad, column_b = last_grad((2,), grad)
    sums_a, far_a = back_part([(2, 1)], grad, spot_coef)
    far_got = swap(far_a, 0, 0, 0, 1)
    sums_b, far_b = back_part([(2, 0)], grad, None, far_a)
    far = far_b + far_got
    far_up, far_down = up(far[:rows], 1), up(far[rows:], -1)
    grad, column_c = last_grad((1, -1, 0), grad, far)
    sums_c, up_a, down_a, up_b, down_b = back_part([(1, 1), (-1, 1), (1, 0), (-1, 0)], grad, None)
    up_got, down_got = swap(up_a, 0, 0, 0, 1), swap(down_a, 0, 0, 0, 1)
    above, below = lift_call(up_b, down_b, far_up, far_down)
    above, below = above + up_got, below + down_got
    near_up, near_down = up(above, 1), up(below, -1)
    sums_d, own_a, own_b = back_part([(0, 1), (0, 0)], grad, None, above, below)
    types = types + swap_across(after(types, above), 1)
    own_a = jnp.concatenate([swap(own_a[:rows], 0, 0, 0, 1), swap(own_a[rows:], 0, 0, 0, 1)])
    last = jnp.concatenate(
        [
            jnp.sum(sums_a + sums_b + sums_c + sums_d, axis=0).reshape(blocks, 128),
            scalars,
            jnp.zeros((5, 128), F32),
        ]
    )

    column = jnp.sum(column_a + column_b + column_c, axis=0) * share + spot_coef[32] * mass
    map_rows = stacked([spot_coef[32], column])
    map_rows = after(map_rows, above, below)
    map_args = (expr, grad.reshape(2, genes, spots), masses, keep2, map_rows, all_cells * genes)
    steps = cells // 256
    got, types_got = swap(last, 0, 0, 0, 1), swap_across(after(types, own_b), 3)
    grad_map = map_call(0, steps - 2, *map_args)
    got, types_got = after((got, types_got), grad_map)
    last, types = last + got, types + types_got
    got = [up(last, step) for step in (1, 2, 3)]
    grad_map = map_call(steps - 2, steps, *map_args, done=(after(grad_map, own_a),))
    got = after(tuple(got), grad_map)
    grad_weighted = after(own_b + own_a, grad_map) + near_up + near_down
    grad_expr = grad_weighted * (keep * (genes * all_spots))[None, :]

    type_fraction = types * share

    grad_filter, loss_terms = finish_call(last, got, totals, scalars, kind2, filt2, all_cells)
    return (loss_terms[0, :5], type_fraction, grad_map, grad_filter.reshape(cells), grad_expr)


def solution(mesh):
    in_specs = (
        P("cells", "spots"),
        P("cells"),
        P(None, "cells"),
        P(None, "spots"),
        P("cells"),
        P("spots"),
        P("spots"),
    )
    out_specs = (P(), P(None, "spots"), P("cells", "spots"), P("cells"), P("spots", "cells"))
    return jax.shard_map(
        on_device, mesh=mesh, in_specs=in_specs, out_specs=out_specs, check_vma=False
    )
```

```python
import functools

import jax
import jax.numpy as jnp
from jax import lax
from jax.experimental import pallas as pl
from jax.experimental.pallas import tpu as pltpu
from jax.sharding import PartitionSpec as P

TYPES = 32
SLIDES = 3
RING = 4
F32 = jnp.float32
BF16 = jnp.bfloat16


def vmem(mib):
    return pltpu.CompilerParams(vmem_limit_bytes=mib << 20)


def fixed(shape):
    return pl.BlockSpec(shape, lambda *_: (0,) * len(shape), pipeline_mode=pl.Buffered(1))


def streamed(array):
    return pltpu.with_memory_space_constraint(array, pltpu.HBM)


RESIDENT = pl.BlockSpec(memory_space=pltpu.VMEM)


def cost(flops, moved):
    return pl.CostEstimate(flops=int(flops) // 8, bytes_accessed=int(moved) // 8, transcendentals=0)


NO_COST = pl.CostEstimate(flops=0, bytes_accessed=0, transcendentals=0)


def route(target):
    def flat(z, x, y, core):
        return ((z % RING * RING + x % RING) * RING + y % RING) * 2 + core

    return [
        (flat(z, x, y, core), flat(*target(z, x, y, core)))
        for z in range(RING)
        for x in range(RING)
        for y in range(RING)
        for core in range(2)
    ]


def send(array, target):
    return lax.ppermute(array, ("cells", "spots"), route(target))


def along(array, step):
    return send(array, lambda z, x, y, c: (z, x + step, y, c) if c == 0 else (z + step, x, y, c))


def across(array, step):
    return send(array, lambda z, x, y, c: (z + step, x, y, c) if c == 0 else (z, x + step, y, c))


def up(array, step):
    return send(array, lambda z, x, y, c: (z, x, y + step, c))


def swap(array, mz, mx, my, mc):
    return send(array, lambda z, x, y, c: (z ^ mz, x ^ mx, y ^ my, c ^ mc))


def swap_along(array, mask):
    return send(array, lambda z, x, y, c: (z, x ^ mask, y, c) if c == 0 else (z ^ mask, x, y, c))


def swap_across(array, mask):
    return send(array, lambda z, x, y, c: (z ^ mask, x, y, c) if c == 0 else (z, x ^ mask, y, c))


def after(value, *others):
    return lax.optimization_barrier((value, *others))[0]


def split(value):
    high = value.astype(BF16)
    return high, (value - high.astype(F32)).astype(BF16)


def product(left, right, dims):
    def one(a, b):
        return lax.dot_general(a, b, (dims, ((), ())), preferred_element_type=F32)

    return one(left[0], right[0]) + one(left[0], right[1]) + one(left[1], right[0])


def gene_group(ids, step, half, sub):
    return ((ids[0] + step) & 3) * RING + ((ids[1] + 2 * half + sub) & 3)


PIECES = [
    (step, half, sub)
    for step, half in ((0, 0), (0, 1), (-1, 0), (-1, 1), (1, 0), (1, 1), (2, 0), (2, 1))
    for sub in range(2)
]


def pick(index, values):
    out = values[0]
    for k, value in enumerate(values[1:]):
        out = jnp.where(index == k + 1, value, out)
    return out


def stacked(rows):
    row = lax.broadcasted_iota(jnp.int32, (8, rows[0].shape[0]), 0)
    out = jnp.zeros(row.shape, F32)
    for k, value in enumerate(rows):
        out = jnp.where(row == k, value[None, :], out)
    return out


def as_column(row):
    return jnp.broadcast_to(row, (128, 128)).T[:, :1]


def expo_kernel(ids, logits, kind, filt, *refs):
    expr, (masses, types, totals, out0, out1) = refs[:4], refs[4:]
    step = pl.program_id(0)
    count = logits.shape[0] // 128

    @pl.when(step == 0)
    def _():
        for out in (types, totals, out0, out1):
            out[...] = jnp.zeros_like(out)

    keeps = []
    lane = lax.broadcasted_iota(jnp.int32, (1, totals.shape[1]), 1)
    cell_sums = jnp.zeros(lane.shape, F32)
    for part in range(count):
        rows = slice(part * 128, part * 128 + 128)
        label = kind[pl.ds(step * count + part, 1), :]
        valid = (label >= 0).astype(F32)
        keep = valid * jax.nn.sigmoid(filt[pl.ds(step * count + part, 1), :])
        keeps.append(keep)
        for k, one in enumerate((valid, keep, keep - keep * keep)):
            cell_sums += jnp.where(lane == k, jnp.sum(one, axis=1, keepdims=True), 0.0)
        expo = jnp.exp(logits[rows]) * as_column(valid)
        masses[0, rows], masses[1, rows] = split(expo)
        whole = jnp.sum(expo, axis=0, keepdims=True)
        kept = jnp.sum(expo * as_column(keep), axis=0, keepdims=True)
        row = lax.broadcasted_iota(jnp.int32, types.shape, 0)
        types[...] += jnp.where(row == jnp.max(label, axis=1, keepdims=True), whole, 0.0)
        row = lax.broadcasted_iota(jnp.int32, totals.shape, 0)
        totals[...] += jnp.where(row == 0, whole, jnp.where(row == 1, kept, 0.0))
    totals[2:3, :] += cell_sums
    weighted = jnp.concatenate([part[...].reshape(-1, logits.shape[0]) for part in expr])
    weighted = weighted * jnp.concatenate(keeps, axis=1)
    part = product(split(weighted), masses, ((1,), (0,)))
    half = part.shape[0] // 2
    for index, out in enumerate((out0, out1)):
        new = part[index * half : index * half + half].reshape(-1, 8, part.shape[1])
        out[: half // 8] += new
        out[half // 8] = totals[...]


def expo_call(ids, parts, logits, kind, filt, expr):
    cells, spots = logits.shape
    blocks, groups, rows, _ = expr.shape
    block = 256

    def genes(part, sub):
        return pl.BlockSpec(
            (blocks, 1, rows, block), lambda i, ids: (0, gene_group(ids, *part, sub), 0, i)
        )

    return pl.pallas_call(
        expo_kernel,
        grid_spec=pltpu.PrefetchScalarGridSpec(
            num_scalar_prefetch=1,
            grid=(cells // block,),
            in_specs=[
                pl.BlockSpec((block, spots), lambda i, w: (i, 0)),
                fixed(kind.shape),
                fixed(filt.shape),
            ]
            + [genes(part, sub) for part in parts for sub in range(2)],
            out_specs=[
                pl.BlockSpec((2, block, spots), lambda i, w: (0, i, 0)),
                fixed((TYPES, spots)),
                fixed((8, spots)),
                fixed((blocks * rows // 4 + 1, 8, spots)),
                fixed((blocks * rows // 4 + 1, 8, spots)),
            ],
        ),
        out_shape=[
            jax.ShapeDtypeStruct((2, cells, spots), BF16),
            jax.ShapeDtypeStruct((TYPES, spots), F32),
            jax.ShapeDtypeStruct((8, spots), F32),
            jax.ShapeDtypeStruct((blocks * rows // 4 + 1, 8, spots), F32),
            jax.ShapeDtypeStruct((blocks * rows // 4 + 1, 8, spots), F32),
        ],
        compiler_params=vmem(16),
        cost_estimate=cost(0, cells * spots * 8),
        name="expo",
    )(ids, streamed(logits), kind, filt, *[streamed(expr)] * 4)


def pred_kernel(ids, expr_a, expr_b, keep, masses, totals, *refs):
    more, outs = refs[:-2], refs[-2:]
    rows = 2 * expr_a.shape[0] * expr_a.shape[2]
    weighted = jnp.concatenate(
        [part[...].reshape(rows // 2, keep.shape[1]) for part in (expr_a, expr_b)]
    )
    part = product(split(weighted * keep[...]), masses, ((1,), (0,)))
    part = part.reshape(rows // 8, 8, part.shape[1])
    for step, out in enumerate(outs):

        @pl.when(pl.program_id(0) == step)
        def _(step=step, out=out):
            if more:
                out[: rows // 8] = part + more[step][: rows // 8]
                out[rows // 8] = totals[...] + more[step][rows // 8]
            else:
                out[: rows // 8] = part
                out[rows // 8] = totals[...]


def pred_call(ids, parts, expr, keep, masses, totals, more=()):
    blocks, groups, rows, cells = expr.shape
    spots = masses.shape[2]
    tiles = blocks * rows // 4 + 1

    def genes(sub):
        def place(i, ids):
            step, half = (pick(i, [part[k] for part in parts]) for k in range(2))
            return (0, gene_group(ids, step, half, sub), 0, 0)

        return pl.BlockSpec((blocks, 1, rows, cells), place)

    return pl.pallas_call(
        pred_kernel,
        grid_spec=pltpu.PrefetchScalarGridSpec(
            num_scalar_prefetch=1,
            grid=(2,),
            in_specs=[
                genes(0),
                genes(1),
                fixed((1, cells)),
                RESIDENT,
                fixed((8, spots)),
            ]
            + [RESIDENT] * len(more),
            out_specs=[RESIDENT] * 2,
        ),
        out_shape=[jax.ShapeDtypeStruct((tiles, 8, spots), F32)] * 2,
        compiler_params=vmem(16),
        cost_estimate=cost(24 * blocks * rows * cells * spots, 4 * cells * spots + 16 * blocks * rows * (cells + spots)),
        name="pred",
    )(ids, *[streamed(expr)] * 2, keep, masses, totals, *more)


def merge_kernel(own0, own1, got0, got1, *outs):
    tiles = outs[0].shape[0] - 1
    for half, (own, got) in enumerate(((own0, got0), (own1, got1))):
        for sub in range(2):
            out = outs[2 * half + sub]
            out[:tiles] = own[sub * tiles : sub * tiles + tiles] + got[sub * tiles : sub * tiles + tiles]
            out[tiles] = own[2 * tiles] + got[2 * tiles]


def merge_call(own, got):
    tiles, _, spots = own[0].shape
    block = 256
    whole = pl.BlockSpec((tiles, 8, block), lambda i: (0, 0, i))
    piece = (tiles // 2 + 1, 8, spots)
    return pl.pallas_call(
        merge_kernel,
        grid=(spots // block,),
        in_specs=[whole] * 4,
        out_specs=[pl.BlockSpec((tiles // 2 + 1, 8, block), lambda i: (0, 0, i))] * 4,
        out_shape=[jax.ShapeDtypeStruct(piece, F32)] * 4,
        compiler_params=vmem(12),
        cost_estimate=NO_COST,
        name="merge",
    )(*own, *got)


def stats_kernel(ids, piece, spatial, spot, totals, gene, slide_sums):
    rows = piece.shape[0] * piece.shape[1]
    valid, slide = spot[0:1, :], spot[1:2, :]
    share = 1.0 / totals[0:1, :]
    mass = totals[1:2, :] * share
    value = piece[...].reshape(rows, piece.shape[2]) * share
    data = spatial[...].reshape(value.shape)
    cross, square = value * data, value * value
    lane = lax.broadcasted_iota(jnp.int32, (rows, 128), 1)
    sums = jnp.zeros((rows, 128), F32)
    for index, one in enumerate((cross, square, data * data)):
        sums = jnp.where(lane == index, jnp.sum(one * valid, axis=1, keepdims=True), sums)
    sums = sums.T
    gene[...] = jnp.zeros_like(gene)
    slide_sums[...] = jnp.zeros_like(slide_sums)
    for index in range(3):
        gene[pl.ds(16 * index + gene_group(ids, 0, 0, 0), 1), :] = sums[index : index + 1, :]
    lane = lax.broadcasted_iota(jnp.int32, (1, 128), 1)
    slides = jnp.zeros((1, 128), F32)
    logs = jnp.log(jnp.where(valid > 0, mass, 1.0))
    for k in range(SLIDES):
        inside = jnp.where(slide == k, valid, 0.0)
        for index, one in enumerate((inside, inside * mass, inside * logs)):
            total = jnp.sum(one, axis=1, keepdims=True)
            slides = jnp.where(lane == 3 * index + k, total, slides)
    slide_sums[0:1, :] = slides
    for index, one in enumerate((cross, square)):
        total = jnp.sum(one, axis=0, keepdims=True)
        for k in range(total.shape[1] // 128):
            at = 48 + 8 * index + k
            gene[at : at + 1, :] = total[:, 128 * k : 128 * k + 128]


def stats_call(ids, piece, spatial, spot, totals):
    blocks, rows, spots = piece.shape
    return pl.pallas_call(
        stats_kernel,
        grid_spec=pltpu.PrefetchScalarGridSpec(
            num_scalar_prefetch=1,
            grid=(1,),
            in_specs=[
                fixed((blocks, rows, spots)),
                pl.BlockSpec((blocks, 1, rows, spots), lambda i, ids: (0, gene_group(ids, 0, 0, 0), 0, 0)),
                fixed((8, spots)),
                fixed((8, spots)),
            ],
            out_specs=[fixed((64, 128)), fixed((8, 128))],
        ),
        out_shape=[jax.ShapeDtypeStruct((64, 128), F32), jax.ShapeDtypeStruct((8, 128), F32)],
        compiler_params=vmem(8),
        cost_estimate=NO_COST,
        name="stats",
    )(ids, piece, streamed(spatial), spot, totals)


def coef_kernel(ids, genes_slides, sums, spot, totals, gene, rows, scalars, pairs):
    valid, slide, squares = (spot[k : k + 1, :] for k in range(3))
    share = 1.0 / totals[0:1, :]
    mass = totals[1:2, :] * share
    genes = float(16 * sums.shape[1])

    def wide(index):
        return jnp.concatenate([sums[index + k : index + k + 1, :] for k in range(8)], axis=1)

    dots, own = wide(48), wide(56)
    dot, aa, bb = genes_slides[0:16, :], genes_slides[16:32, :], genes_slides[32:48, :]
    scale = lax.rsqrt(aa * bb + 1e-06)
    pairs[0:16, :] = dot * scale**3 * bb / genes
    pairs[16:32, :] = scale / genes
    pair = [pairs[pl.ds(k + gene_group(ids, *one), 1), :] for k in (0, 16) for one in PIECES]
    gene[...] = jnp.concatenate([*pair, jnp.zeros((96, 128), F32)]).T
    total = jnp.sum(jnp.sum(dot * scale, axis=1, keepdims=True), axis=0, keepdims=True)
    nvs = jnp.zeros((1, 1), F32)
    density = jnp.zeros((1, 1), F32)
    nk, tk = jnp.ones_like(valid), jnp.ones_like(valid)
    for k in range(SLIDES):
        count, held, logs = (genes_slides[48:49, 3 * j + k : 3 * j + k + 1] for j in range(3))
        some = count > 0
        safe = jnp.where(some, count, 1.0)
        nvs += count
        density += jnp.where(some, jnp.log(jnp.where(some, held, 1.0) / safe) - logs / safe, 0.0)
        here = (slide == k) & (valid > 0)
        nk = jnp.where(here, count, nk)
        tk = jnp.where(here, held, tk)
    scale = lax.rsqrt(own * squares + 1e-06)
    grad_mass = valid / SLIDES * (1.0 / tk - 1.0 / (nk * jnp.where(valid > 0, mass, 1.0)))
    mask = valid * share
    by_pred, by_data = dots * scale**3 * squares / nvs, scale / nvs
    for index, one in enumerate((by_pred * share * mask, by_data * mask, mask, share * mask)):
        rows[8 * index : 8 * index + 8, :] = jnp.broadcast_to(one, (8, one.shape[1]))
    rows[32:40, :] = jnp.concatenate([grad_mass * share, jnp.zeros((7, valid.shape[1]), F32)])
    cosines = jnp.sum(valid * dots * scale, axis=1, keepdims=True)
    lane = lax.broadcasted_iota(jnp.int32, (1, 128), 1)
    out = jnp.zeros((1, 128), F32)
    for index, one in enumerate((total / genes, cosines / nvs, density / SLIDES)):
        out = jnp.where(lane == index, one, out)
    scalars[...] = out


def coef_call(ids, genes_slides, sums, spot, totals):
    spots = spot.shape[1]
    return pl.pallas_call(
        coef_kernel,
        grid_spec=pltpu.PrefetchScalarGridSpec(
            num_scalar_prefetch=1,
            grid=(1,),
            in_specs=[fixed(genes_slides.shape), fixed(sums.shape), fixed((8, spots)), fixed((8, spots))],
            out_specs=[fixed((128, 128)), fixed((40, spots)), fixed((1, 128))],
            scratch_shapes=[pltpu.VMEM((32, 128), F32)],
        ),
        out_shape=[
            jax.ShapeDtypeStruct((128, 128), F32),
            jax.ShapeDtypeStruct((40, spots), F32),
            jax.ShapeDtypeStruct((1, 128), F32),
        ],
        compiler_params=vmem(6),
        cost_estimate=NO_COST,
        name="coef",
    )(ids, genes_slides, sums, spot, totals)


def grad_rows(pred, data, gene, spot, lane):
    by_pred = gene[:, lane : lane + 1].reshape(2, 8, 1)
    by_data = gene[:, 16 + lane : 17 + lane].reshape(2, 8, 1)
    pred, data = pred.reshape(2, 8, pred.shape[1]), data.reshape(2, 8, data.shape[1])
    grad = pred * (by_pred * spot[24:32, :] + spot[0:8, :])
    grad = grad - data * (by_data * spot[16:24, :] + spot[8:16, :])
    return grad.reshape(16, grad.shape[2]), jnp.sum(grad * pred, axis=0)


def grad_kernel(ids, *refs, count, lane, chips):
    pred, data, refs = refs[: 2 * count], refs[2 * count : 3 * count], refs[3 * count :]
    gene, spot, grad, column = refs[0], refs[1], refs[-2], refs[-1]
    step = pl.program_id(0)
    chip = (ids[2] + pick(step, chips)) & 3

    @pl.when(step == 0)
    def _():
        column[...] = jnp.zeros_like(column)

    total = jnp.zeros(column.shape, F32)
    for index, part in enumerate(pred):
        for sub in range(2):
            at = gene_group(ids, *PIECES[lane + 2 * index + sub])
            row = pl.multiple_of((at & 3) * 16, 16)
            to = pl.ds(pl.multiple_of(at * 16, 16), 16)
            for half in range(2):
                block = chip * 2 + half
                rows, inner = grad_rows(
                    part[sub, block],
                    data[index // 2][half, 0, pl.ds(row, 16), :],
                    gene[16 * half : 16 * half + 16, :],
                    spot,
                    lane + 2 * index + sub,
                )
                grad[0, block, to, :], grad[1, block, to, :] = split(rows)
                total += inner
    column[...] += total


def grad_call(ids, pred, spatial, gene, spot, lane, chips, done=()):
    blocks, groups, rows, spots = spatial.shape
    count = len(pred) // 2

    def chip(i, ids):
        return (ids[2] + pick(i, chips)) & 3

    def group(k):
        step = PIECES[lane + 4 * k][0]
        return pl.BlockSpec(
            (2, 1, rows, spots), lambda i, ids: (chip(i, ids), (ids[0] + step) & 3, 0, 0)
        )

    return pl.pallas_call(
        functools.partial(grad_kernel, count=count, lane=lane, chips=chips),
        grid_spec=pltpu.PrefetchScalarGridSpec(
            num_scalar_prefetch=1,
            grid=(len(chips),),
            in_specs=[RESIDENT] * (2 * count)
            + [group(k) for k in range(count)]
            + [pl.BlockSpec((32, 128), lambda i, ids: (chip(i, ids), 0)), fixed(spot.shape)]
            + [RESIDENT] * len(done),
            out_specs=[RESIDENT, fixed((8, spots))],
        ),
        out_shape=[
            jax.ShapeDtypeStruct((2, blocks, groups * rows, spots), BF16),
            jax.ShapeDtypeStruct((8, spots), F32),
        ],
        input_output_aliases={3 * count + 3: 0} if done else {},
        compiler_params=vmem(12),
        cost_estimate=NO_COST,
        name="grad",
    )(ids, *pred, *[streamed(spatial)] * count, gene, spot, *done)


def back_kernel(ids, grad, masses, expr, *refs, parts, extra):
    sums, *outs = refs[extra:-2]
    held, ready = refs[-2:]
    step = pl.program_id(0)
    rows = grad.shape[2]

    def block(part):
        return ((ids[2] + part[0]) & 3) * 2 + (ids[3] ^ part[1])

    def fetch(k):
        start = pl.multiple_of(block(parts[k]) * rows, rows)
        return pltpu.make_async_copy(expr.at[pl.ds(start, rows), :], held.at[k], ready.at[k])

    @pl.when(step == 0)
    def _():
        for k in range(len(parts)):
            fetch(k).start()

    here = block([pick(step, [part[k] for part in parts]) for k in range(2)])
    left = grad[0, here], grad[1, here]
    if extra:
        pair = split(jnp.concatenate([refs[0][...], jnp.zeros_like(refs[0])]))
        left = [jnp.concatenate(both) for both in zip(left, pair)]
    part = product(left, masses, ((1,), (1,)))

    @pl.when(step == 0)
    def _():
        sums[...] = part[rows : rows + 8] if extra else jnp.zeros_like(sums)

    part = part[:rows]
    for k, out in enumerate(outs):

        @pl.when(step == k)
        def _(k=k, out=out):
            out[...] = part
            fetch(k).wait()

    sums[...] += jnp.sum((part * held[step]).reshape(-1, 8, part.shape[1]), axis=0)


def back_call(ids, parts, grad, masses, expr, spot=None):
    _, blocks, rows, spots = grad.shape
    cells = masses.shape[1]
    count = len(parts)
    extra = [] if spot is None else [spot]
    return pl.pallas_call(
        functools.partial(back_kernel, parts=parts, extra=len(extra)),
        grid_spec=pltpu.PrefetchScalarGridSpec(
            num_scalar_prefetch=1,
            grid=(count,),
            in_specs=[RESIDENT, RESIDENT, pl.BlockSpec(memory_space=pl.ANY)]
            + [pl.BlockSpec((8, spots), lambda i, ids: (4, 0))] * len(extra),
            out_specs=[fixed((8, cells))] + [RESIDENT] * count,
            scratch_shapes=[
                pltpu.VMEM((count, rows, cells), F32),
                pltpu.SemaphoreType.DMA((count,)),
            ],
        ),
        out_shape=[jax.ShapeDtypeStruct((8, cells), F32)]
        + [jax.ShapeDtypeStruct((rows, cells), F32)] * count,
        compiler_params=vmem(16),
        cost_estimate=NO_COST,
        name="back",
    )(ids, grad, masses, streamed(expr), *extra)


def lift_kernel(above, below, far_up, far_down, out_above, out_below):
    rows = far_up.shape[0]
    out_above[:rows, :] = above[:rows, :] + far_up[...]
    out_above[rows:, :] = above[rows:, :]
    out_below[:rows, :] = below[:rows, :]
    out_below[rows:, :] = below[rows:, :] + far_down[...]


def lift_call(above, below, far_up, far_down):
    rows, cells = far_up.shape
    block = 256
    far = pl.BlockSpec((rows, block), lambda i: (0, i))
    whole = pl.BlockSpec((2 * rows, block), lambda i: (0, i))
    return pl.pallas_call(
        lift_kernel,
        grid=(cells // block,),
        in_specs=[whole, whole, far, far],
        out_specs=[whole, whole],
        out_shape=[jax.ShapeDtypeStruct(above.shape, F32)] * 2,
        compiler_params=vmem(8),
        cost_estimate=pl.CostEstimate(flops=10**10, bytes_accessed=0, transcendentals=0),
        name="lift",
    )(above, below, far_up, far_down)


def map_kernel(expr, grad, masses, keep, spot, *rest, scale, start):
    out, held, ready = rest[-3:]
    index = pl.program_id(0)
    quarter, block = held.shape[2:]
    count = held.shape[1]

    def fetch(at, k):
        columns = pl.ds(pl.multiple_of((at + start) * block, block), block)
        return pltpu.make_async_copy(
            expr.at[pl.ds(k * quarter, quarter), columns], held.at[at & 1, k], ready.at[at & 1, k]
        )

    @pl.when(index == 0)
    def _():
        for k in range(count):
            fetch(index, k).start()

    @pl.when(index + 1 < pl.num_programs(0))
    def _():
        for k in range(count):
            fetch(index + 1, k).start()

    inner = spot[0:1, :]
    for k in range(count):
        fetch(index, k).wait()
        rows = slice(k * quarter, k * quarter + quarter)
        pair = grad[0, rows, :], grad[1, rows, :]
        inner = inner + product(split(held[index & 1, k]), pair, ((0,), (0,)))
    at = pl.multiple_of((index + start) * block, block)
    expo = masses[0, pl.ds(at, block), :].astype(F32) + masses[1, pl.ds(at, block), :].astype(F32)
    for part in range(block // 128):
        rows = slice(part * 128, part * 128 + 128)
        weight = as_column(keep[pl.ds((index + start) * (block // 128) + part, 1), :])
        out[rows, :] = (scale * expo[rows]) * (weight * inner[rows] - spot[1:2, :])


def map_call(start, stop, expr, grad, masses, keep, spot, scale, done=()):
    genes, cells = expr.shape
    spots = masses.shape[2]
    block, count = 256, 4
    return pl.pallas_call(
        functools.partial(map_kernel, scale=scale, start=start),
        grid=(stop - start,),
        in_specs=[
            pl.BlockSpec(memory_space=pl.ANY),
            RESIDENT,
            RESIDENT,
            fixed(keep.shape),
            fixed((8, spots)),
        ]
        + [pl.BlockSpec(memory_space=pl.ANY)] * len(done),
        out_specs=pl.BlockSpec((block, spots), lambda i: (i + start, 0)),
        out_shape=jax.ShapeDtypeStruct((cells, spots), F32),
        scratch_shapes=[
            pltpu.VMEM((2, count, genes // count, block), F32),
            pltpu.SemaphoreType.DMA((2, count)),
        ],
        input_output_aliases={5: 0} if done else {},
        compiler_params=vmem(24),
        cost_estimate=NO_COST,
        name="grad_map",
    )(streamed(expr), grad, masses, keep, spot, *done)


def finish_kernel(last, got1, got2, got3, totals, scalars, kind, filt, grad_filter, terms, *, all_cells):
    blocks = kind.shape[0]
    total = (last[...] + got2[...]) + (got1[...] + got3[...])
    nvalid, retained, reg_sum = (totals[2:3, k : k + 1] for k in range(3))
    valid = (kind[...] >= 0).astype(F32)
    sigma = jax.nn.sigmoid(filt[...])
    keep = sigma * valid
    shifted = (retained - 0.35 * nvalid) / (0.1 * all_cells)
    count_term = jnp.sqrt(shifted * shifted + 1.0)
    grad_keep = total[:blocks] + shifted / count_term / (0.1 * all_cells) + (1.0 - 2.0 * keep) / nvalid
    grad_filter[...] = valid * sigma * (1.0 - sigma) * grad_keep * all_cells
    lane = lax.broadcasted_iota(jnp.int32, (1, 128), 1)
    out = jnp.zeros((1, 128), F32)
    parts = (scalars[:, 0:1], total[blocks : blocks + 1, 1:2], scalars[:, 2:3], count_term, reg_sum / nvalid)
    for index, one in enumerate(parts):
        out = jnp.where(lane == index, one, out)
    terms[...] = out


def finish_call(last, got, totals, scalars, kind, filt, all_cells):
    return pl.pallas_call(
        functools.partial(finish_kernel, all_cells=float(all_cells)),
        grid=(1,),
        in_specs=[fixed(one.shape) for one in (last, *got, totals, scalars, kind, filt)],
        out_specs=[fixed(kind.shape), fixed((1, 128))],
        out_shape=[jax.ShapeDtypeStruct(kind.shape, F32), jax.ShapeDtypeStruct((1, 128), F32)],
        compiler_params=vmem(4),
        cost_estimate=NO_COST,
        name="finish",
    )(last, *got, totals, scalars, kind, filt)


def on_device(map_logits, filter_logits, expr, spatial, cell_type, slide_id, spot_mask):
    genes, cells = expr.shape
    spots = map_logits.shape[1]
    all_cells = cells * lax.axis_size("cells")
    all_spots = spots * lax.axis_size("spots")
    cell_place = lax.axis_index("cells")
    z, x = cell_place >> 2, cell_place & 3
    spot_place = lax.axis_index("spots")
    y, core = spot_place >> 1, spot_place & 1
    first = jnp.where(core == 0, x, z)
    second = jnp.where(core == 0, z, x)
    blocks = cells // 128

    valid = (cell_type >= 0).astype(F32)
    sigma = jax.nn.sigmoid(filter_logits)
    keep = sigma * valid
    spot_valid = spot_mask.astype(F32)
    kind2 = cell_type.reshape(blocks, 128)
    filt2 = filter_logits.reshape(blocks, 128)
    keep2 = keep.reshape(blocks, 128)

    expr4 = expr.reshape(8, 16, 16, cells)
    keep_row = keep.reshape(1, cells)

    ids = jnp.stack([first, second, y, core]).astype(jnp.int32)

    def pred_part(one, two, more, *others):
        return pred_call(after(ids, *others), (one, two), expr4, keep_row, masses, totals, more)

    masses, types, totals, *far = expo_call(
        ids, ((2, 0), (2, 1)), map_logits, kind2, filt2, expr4
    )
    far_right, far_left = along(far[0], 1), along(far[1], -1)
    near = pred_part((1, 1), (-1, 0), (), *far)
    near_right, near_left = along(near[0], 1), along(near[1], -1)
    late = pred_part((1, 0), (-1, 1), (far_right, far_left), *near)
    late_right, late_left = along(late[0], 1), along(late[1], -1)
    own = pred_part((0, 0), (0, 1), (near_left, near_right), *late)
    mine, *pieces = merge_call(own, (late_right, late_left))
    pieces = [across(piece, step + 1) for step, piece in enumerate(pieces)]
    spatial_squares = jnp.sum(after(spatial, mine) ** 2, axis=0)
    types = types + swap_along(after(types, spatial_squares), 1)
    spot_rows = stacked([spot_valid, slide_id.astype(F32), spatial_squares])
    mine = after(mine, spot_rows, types)
    piece = mine + pieces[0] + pieces[1] + pieces[2]
    totals = piece[-1]
    piece = piece[:-1].reshape(8, 16, spots)
    share = 1.0 / totals[0]
    mass = totals[1] * share

    got = [across(piece, step) for step in (1, 2, 3)]
    sums, slides = stats_call(
        ids,
        piece,
        spatial.reshape(8, 16, 16, spots),
        spot_rows,
        totals,
    )
    sums = sums + swap_along(sums, 1)
    sums = sums + swap_along(sums, 3)
    types = types + swap_along(after(types, slides), 3)
    mine = after((jnp.stack([piece, got[2]]), jnp.stack([got[1], got[0]])), sums, types)
    right0, left1 = along(mine[0], 1), along(mine[1], -1)
    right1, left0 = along(mine[1], 1), along(mine[0], -1)
    sums = sums + swap_across(after(sums, *mine), 1)
    sums = sums + swap_across(sums, 3)
    right0, left1, sums = lax.optimization_barrier((right0, left1, sums))
    far0, far1 = along(right0, 1), along(left1, -1)
    genes_slides = jnp.concatenate([sums[:48], slides])
    genes_slides = genes_slides + swap(genes_slides, 0, 0, 0, 1)
    genes_slides = genes_slides + swap(genes_slides, 0, 0, 1, 0)
    genes_slides = after(genes_slides, right1, left0)
    genes_slides = genes_slides + swap(genes_slides, 0, 0, 3, 0)
    pred = [*mine, right0, right1, left0, left1, far0, far1]
    gene_coef, spot_coef, scalars = coef_call(ids, genes_slides, sums, spot_rows, totals)
    spatial4 = spatial.reshape(8, RING, genes // 32, spots)
    grad, column_a = grad_call(ids, pred[:6], spatial4, gene_coef, spot_coef, 0, (0, 1, 2, 3))

    def last_grad(chips, grad, *others):
        return grad_call(
            after(ids, *others), pred[6:], spatial4, gene_coef, spot_coef, 12, chips, (grad,)
        )

    def back_part(steps, grad, spot, *others):
        return back_call(after(ids, *others), steps, grad, masses, expr, spot)

    rows = genes // 16
    grad, column_b = last_grad((2,), grad)
    sums_a, far_a = back_part([(2, 1)], grad, spot_coef)
    far_got = swap(far_a, 0, 0, 0, 1)
    sums_b, far_b = back_part([(2, 0)], grad, None, far_a)
    far = far_b + far_got
    far_up, far_down = up(far[:rows], 1), up(far[rows:], -1)
    grad, column_c = last_grad((1, -1, 0), grad, far)
    sums_c, up_a, down_a, up_b, down_b = back_part([(1, 1), (-1, 1), (1, 0), (-1, 0)], grad, None)
    up_got, down_got = swap(up_a, 0, 0, 0, 1), swap(down_a, 0, 0, 0, 1)
    above, below = lift_call(up_b, down_b, far_up, far_down)
    above, below = above + up_got, below + down_got
    near_up, near_down = up(above, 1), up(below, -1)
    sums_d, own_a, own_b = back_part([(0, 1), (0, 0)], grad, None, above, below)
    types = types + swap_across(after(types, above), 1)
    own_a = jnp.concatenate([swap(own_a[:rows], 0, 0, 0, 1), swap(own_a[rows:], 0, 0, 0, 1)])
    last = jnp.concatenate(
        [
            jnp.sum(sums_a + sums_b + sums_c + sums_d, axis=0).reshape(blocks, 128),
            scalars,
            jnp.zeros((5, 128), F32),
        ]
    )

    column = jnp.sum(column_a + column_b + column_c, axis=0) * share + spot_coef[32] * mass
    map_rows = stacked([spot_coef[32], column])
    map_rows = after(map_rows, above, below)
    map_args = (expr, grad.reshape(2, genes, spots), masses, keep2, map_rows, all_cells * genes)
    steps = cells // 256
    got, types_got = swap(last, 0, 0, 0, 1), swap_across(after(types, own_b), 3)
    grad_map = map_call(0, steps - 2, *map_args)
    got, types_got = after((got, types_got), grad_map)
    last, types = last + got, types + types_got
    got = [up(last, step) for step in (1, 2, 3)]
    grad_map = map_call(steps - 2, steps, *map_args, done=(after(grad_map, own_a),))
    got = after(tuple(got), grad_map)
    grad_weighted = after(own_b + own_a, grad_map) + near_up + near_down
    grad_expr = grad_weighted * (keep * (genes * all_spots))[None, :]

    type_fraction = types * share

    grad_filter, loss_terms = finish_call(last, got, totals, scalars, kind2, filt2, all_cells)
    return (loss_terms[0, :5], type_fraction, grad_map, grad_filter.reshape(cells), grad_expr)


def solution(mesh):
    in_specs = (
        P("cells", "spots"),
        P("cells"),
        P(None, "cells"),
        P(None, "spots"),
        P("cells"),
        P("spots"),
        P("spots"),
    )
    out_specs = (P(), P(None, "spots"), P("cells", "spots"), P("cells"), P("spots", "cells"))
    return jax.shard_map(
        on_device, mesh=mesh, in_specs=in_specs, out_specs=out_specs, check_vma=False
    )
```

```python
import functools

import jax
import jax.numpy as jnp
from jax import lax
from jax.experimental import pallas as pl
from jax.experimental.pallas import tpu as pltpu
from jax.sharding import PartitionSpec as P

TYPES = 32
SLIDES = 3
RING = 4
F32 = jnp.float32
BF16 = jnp.bfloat16


def vmem(mib):
    return pltpu.CompilerParams(vmem_limit_bytes=mib << 20)


def fixed(shape):
    return pl.BlockSpec(shape, lambda *_: (0,) * len(shape), pipeline_mode=pl.Buffered(1))


def streamed(array):
    return pltpu.with_memory_space_constraint(array, pltpu.HBM)


RESIDENT = pl.BlockSpec(memory_space=pltpu.VMEM)


def cost(flops, moved):
    return pl.CostEstimate(flops=int(flops) // 8, bytes_accessed=int(moved) // 8, transcendentals=0)


NO_COST = pl.CostEstimate(flops=0, bytes_accessed=0, transcendentals=0)


def route(target):
    def flat(z, x, y, core):
        return ((z % RING * RING + x % RING) * RING + y % RING) * 2 + core

    return [
        (flat(z, x, y, core), flat(*target(z, x, y, core)))
        for z in range(RING)
        for x in range(RING)
        for y in range(RING)
        for core in range(2)
    ]


def send(array, target):
    return lax.ppermute(array, ("cells", "spots"), route(target))


def along(array, step):
    return send(array, lambda z, x, y, c: (z, x + step, y, c) if c == 0 else (z + step, x, y, c))


def across(array, step):
    return send(array, lambda z, x, y, c: (z + step, x, y, c) if c == 0 else (z, x + step, y, c))


def up(array, step):
    return send(array, lambda z, x, y, c: (z, x, y + step, c))


def swap(array, mz, mx, my, mc):
    return send(array, lambda z, x, y, c: (z ^ mz, x ^ mx, y ^ my, c ^ mc))


def swap_along(array, mask):
    return send(array, lambda z, x, y, c: (z, x ^ mask, y, c) if c == 0 else (z ^ mask, x, y, c))


def swap_across(array, mask):
    return send(array, lambda z, x, y, c: (z ^ mask, x, y, c) if c == 0 else (z, x ^ mask, y, c))


def after(value, *others):
    return lax.optimization_barrier((value, *others))[0]


def split(value):
    high = value.astype(BF16)
    return high, (value - high.astype(F32)).astype(BF16)


def product(left, right, dims):
    def one(a, b):
        return lax.dot_general(a, b, (dims, ((), ())), preferred_element_type=F32)

    return one(left[0], right[0]) + one(left[0], right[1]) + one(left[1], right[0])


def gene_group(ids, step, half, sub):
    return ((ids[0] + step) & 3) * RING + ((ids[1] + 2 * half + sub) & 3)


PIECES = [
    (step, half, sub)
    for step, half in ((0, 0), (0, 1), (-1, 0), (-1, 1), (1, 0), (1, 1), (2, 0), (2, 1))
    for sub in range(2)
]


def pick(index, values):
    out = values[0]
    for k, value in enumerate(values[1:]):
        out = jnp.where(index == k + 1, value, out)
    return out


def stacked(rows):
    row = lax.broadcasted_iota(jnp.int32, (8, rows[0].shape[0]), 0)
    out = jnp.zeros(row.shape, F32)
    for k, value in enumerate(rows):
        out = jnp.where(row == k, value[None, :], out)
    return out


def as_column(row):
    return jnp.broadcast_to(row, (128, 128)).T[:, :1]


def expo_kernel(ids, logits, kind, filt, *refs):
    expr, (masses, types, totals, out0, out1) = refs[:4], refs[4:]
    step = pl.program_id(0)
    count = logits.shape[0] // 128

    @pl.when(step == 0)
    def _():
        for out in (types, totals, out0, out1):
            out[...] = jnp.zeros_like(out)

    keeps = []
    lane = lax.broadcasted_iota(jnp.int32, (1, totals.shape[1]), 1)
    cell_sums = jnp.zeros(lane.shape, F32)
    for part in range(count):
        rows = slice(part * 128, part * 128 + 128)
        label = kind[pl.ds(step * count + part, 1), :]
        valid = (label >= 0).astype(F32)
        keep = valid * jax.nn.sigmoid(filt[pl.ds(step * count + part, 1), :])
        keeps.append(keep)
        for k, one in enumerate((valid, keep, keep - keep * keep)):
            cell_sums += jnp.where(lane == k, jnp.sum(one, axis=1, keepdims=True), 0.0)
        expo = jnp.exp(logits[rows]) * as_column(valid)
        masses[0, rows], masses[1, rows] = split(expo)
        whole = jnp.sum(expo, axis=0, keepdims=True)
        kept = jnp.sum(expo * as_column(keep), axis=0, keepdims=True)
        row = lax.broadcasted_iota(jnp.int32, types.shape, 0)
        types[...] += jnp.where(row == jnp.max(label, axis=1, keepdims=True), whole, 0.0)
        row = lax.broadcasted_iota(jnp.int32, totals.shape, 0)
        totals[...] += jnp.where(row == 0, whole, jnp.where(row == 1, kept, 0.0))
    totals[2:3, :] += cell_sums
    weighted = jnp.concatenate([part[...].reshape(-1, logits.shape[0]) for part in expr])
    weighted = weighted * jnp.concatenate(keeps, axis=1)
    part = product(split(weighted), masses, ((1,), (0,)))
    half = part.shape[0] // 2
    for index, out in enumerate((out0, out1)):
        new = part[index * half : index * half + half].reshape(-1, 8, part.shape[1])
        out[: half // 8] += new
        out[half // 8] = totals[...]


def expo_call(ids, parts, logits, kind, filt, expr):
    cells, spots = logits.shape
    blocks, groups, rows, _ = expr.shape
    block = 256

    def genes(part, sub):
        return pl.BlockSpec(
            (blocks, 1, rows, block), lambda i, ids: (0, gene_group(ids, *part, sub), 0, i)
        )

    return pl.pallas_call(
        expo_kernel,
        grid_spec=pltpu.PrefetchScalarGridSpec(
            num_scalar_prefetch=1,
            grid=(cells // block,),
            in_specs=[
                pl.BlockSpec((block, spots), lambda i, w: (i, 0)),
                fixed(kind.shape),
                fixed(filt.shape),
            ]
            + [genes(part, sub) for part in parts for sub in range(2)],
            out_specs=[
                pl.BlockSpec((2, block, spots), lambda i, w: (0, i, 0)),
                fixed((TYPES, spots)),
                fixed((8, spots)),
                fixed((blocks * rows // 4 + 1, 8, spots)),
                fixed((blocks * rows // 4 + 1, 8, spots)),
            ],
        ),
        out_shape=[
            jax.ShapeDtypeStruct((2, cells, spots), BF16),
            jax.ShapeDtypeStruct((TYPES, spots), F32),
            jax.ShapeDtypeStruct((8, spots), F32),
            jax.ShapeDtypeStruct((blocks * rows // 4 + 1, 8, spots), F32),
            jax.ShapeDtypeStruct((blocks * rows // 4 + 1, 8, spots), F32),
        ],
        compiler_params=vmem(16),
        cost_estimate=cost(0, cells * spots * 8),
        name="expo",
    )(ids, streamed(logits), kind, filt, *[streamed(expr)] * 4)


def pred_kernel(ids, expr_a, expr_b, keep, masses, totals, *refs):
    more, outs = refs[:-2], refs[-2:]
    rows = 2 * expr_a.shape[0] * expr_a.shape[2]
    weighted = jnp.concatenate(
        [part[...].reshape(rows // 2, keep.shape[1]) for part in (expr_a, expr_b)]
    )
    part = product(split(weighted * keep[...]), masses, ((1,), (0,)))
    part = part.reshape(rows // 8, 8, part.shape[1])
    for step, out in enumerate(outs):

        @pl.when(pl.program_id(0) == step)
        def _(step=step, out=out):
            if more:
                out[: rows // 8] = part + more[step][: rows // 8]
                out[rows // 8] = totals[...] + more[step][rows // 8]
            else:
                out[: rows // 8] = part
                out[rows // 8] = totals[...]


def pred_call(ids, parts, expr, keep, masses, totals, more=()):
    blocks, groups, rows, cells = expr.shape
    spots = masses.shape[2]
    tiles = blocks * rows // 4 + 1

    def genes(sub):
        def place(i, ids):
            step, half = (pick(i, [part[k] for part in parts]) for k in range(2))
            return (0, gene_group(ids, step, half, sub), 0, 0)

        return pl.BlockSpec((blocks, 1, rows, cells), place)

    return pl.pallas_call(
        pred_kernel,
        grid_spec=pltpu.PrefetchScalarGridSpec(
            num_scalar_prefetch=1,
            grid=(2,),
            in_specs=[
                genes(0),
                genes(1),
                fixed((1, cells)),
                RESIDENT,
                fixed((8, spots)),
            ]
            + [RESIDENT] * len(more),
            out_specs=[RESIDENT] * 2,
        ),
        out_shape=[jax.ShapeDtypeStruct((tiles, 8, spots), F32)] * 2,
        compiler_params=vmem(16),
        cost_estimate=cost(24 * blocks * rows * cells * spots, 4 * cells * spots + 16 * blocks * rows * (cells + spots)),
        name="pred",
    )(ids, *[streamed(expr)] * 2, keep, masses, totals, *more)


def merge_kernel(own0, own1, got0, got1, *outs):
    tiles = outs[0].shape[0] - 1
    for half, (own, got) in enumerate(((own0, got0), (own1, got1))):
        for sub in range(2):
            out = outs[2 * half + sub]
            out[:tiles] = own[sub * tiles : sub * tiles + tiles] + got[sub * tiles : sub * tiles + tiles]
            out[tiles] = own[2 * tiles] + got[2 * tiles]


def merge_call(own, got):
    tiles, _, spots = own[0].shape
    block = 256
    whole = pl.BlockSpec((tiles, 8, block), lambda i: (0, 0, i))
    piece = (tiles // 2 + 1, 8, spots)
    return pl.pallas_call(
        merge_kernel,
        grid=(spots // block,),
        in_specs=[whole] * 4,
        out_specs=[pl.BlockSpec((tiles // 2 + 1, 8, block), lambda i: (0, 0, i))] * 4,
        out_shape=[jax.ShapeDtypeStruct(piece, F32)] * 4,
        compiler_params=vmem(12),
        cost_estimate=NO_COST,
        name="merge",
    )(*own, *got)


def stats_kernel(ids, piece, spatial, spot, totals, gene, slide_sums):
    rows = piece.shape[0] * piece.shape[1]
    valid, slide = spot[0:1, :], spot[1:2, :]
    share = 1.0 / totals[0:1, :]
    mass = totals[1:2, :] * share
    value = piece[...].reshape(rows, piece.shape[2]) * share
    data = spatial[...].reshape(value.shape)
    cross, square = value * data, value * value
    lane = lax.broadcasted_iota(jnp.int32, (rows, 128), 1)
    sums = jnp.zeros((rows, 128), F32)
    for index, one in enumerate((cross, square, data * data)):
        sums = jnp.where(lane == index, jnp.sum(one * valid, axis=1, keepdims=True), sums)
    sums = sums.T
    gene[...] = jnp.zeros_like(gene)
    slide_sums[...] = jnp.zeros_like(slide_sums)
    for index in range(3):
        gene[pl.ds(16 * index + gene_group(ids, 0, 0, 0), 1), :] = sums[index : index + 1, :]
    lane = lax.broadcasted_iota(jnp.int32, (1, 128), 1)
    slides = jnp.zeros((1, 128), F32)
    logs = jnp.log(jnp.where(valid > 0, mass, 1.0))
    for k in range(SLIDES):
        inside = jnp.where(slide == k, valid, 0.0)
        for index, one in enumerate((inside, inside * mass, inside * logs)):
            total = jnp.sum(one, axis=1, keepdims=True)
            slides = jnp.where(lane == 3 * index + k, total, slides)
    slide_sums[0:1, :] = slides
    for index, one in enumerate((cross, square)):
        total = jnp.sum(one, axis=0, keepdims=True)
        for k in range(total.shape[1] // 128):
            at = 48 + 8 * index + k
            gene[at : at + 1, :] = total[:, 128 * k : 128 * k + 128]


def stats_call(ids, piece, spatial, spot, totals):
    blocks, rows, spots = piece.shape
    return pl.pallas_call(
        stats_kernel,
        grid_spec=pltpu.PrefetchScalarGridSpec(
            num_scalar_prefetch=1,
            grid=(1,),
            in_specs=[
                fixed((blocks, rows, spots)),
                pl.BlockSpec((blocks, 1, rows, spots), lambda i, ids: (0, gene_group(ids, 0, 0, 0), 0, 0)),
                fixed((8, spots)),
                fixed((8, spots)),
            ],
            out_specs=[fixed((64, 128)), fixed((8, 128))],
        ),
        out_shape=[jax.ShapeDtypeStruct((64, 128), F32), jax.ShapeDtypeStruct((8, 128), F32)],
        compiler_params=vmem(8),
        cost_estimate=NO_COST,
        name="stats",
    )(ids, piece, streamed(spatial), spot, totals)


def coef_kernel(ids, genes_slides, sums, spot, totals, gene, rows, scalars, pairs):
    valid, slide, squares = (spot[k : k + 1, :] for k in range(3))
    share = 1.0 / totals[0:1, :]
    mass = totals[1:2, :] * share
    genes = float(16 * sums.shape[1])

    def wide(index):
        return jnp.concatenate([sums[index + k : index + k + 1, :] for k in range(8)], axis=1)

    dots, own = wide(48), wide(56)
    dot, aa, bb = genes_slides[0:16, :], genes_slides[16:32, :], genes_slides[32:48, :]
    scale = lax.rsqrt(aa * bb + 1e-06)
    pairs[0:16, :] = dot * scale**3 * bb / genes
    pairs[16:32, :] = scale / genes
    pair = [pairs[pl.ds(k + gene_group(ids, *one), 1), :] for k in (0, 16) for one in PIECES]
    gene[...] = jnp.concatenate([*pair, jnp.zeros((96, 128), F32)]).T
    total = jnp.sum(jnp.sum(dot * scale, axis=1, keepdims=True), axis=0, keepdims=True)
    nvs = jnp.zeros((1, 1), F32)
    density = jnp.zeros((1, 1), F32)
    nk, tk = jnp.ones_like(valid), jnp.ones_like(valid)
    for k in range(SLIDES):
        count, held, logs = (genes_slides[48:49, 3 * j + k : 3 * j + k + 1] for j in range(3))
        some = count > 0
        safe = jnp.where(some, count, 1.0)
        nvs += count
        density += jnp.where(some, jnp.log(jnp.where(some, held, 1.0) / safe) - logs / safe, 0.0)
        here = (slide == k) & (valid > 0)
        nk = jnp.where(here, count, nk)
        tk = jnp.where(here, held, tk)
    scale = lax.rsqrt(own * squares + 1e-06)
    grad_mass = valid / SLIDES * (1.0 / tk - 1.0 / (nk * jnp.where(valid > 0, mass, 1.0)))
    mask = valid * share
    by_pred, by_data = dots * scale**3 * squares / nvs, scale / nvs
    for index, one in enumerate((by_pred * share * mask, by_data * mask, mask, share * mask)):
        rows[8 * index : 8 * index + 8, :] = jnp.broadcast_to(one, (8, one.shape[1]))
    rows[32:40, :] = jnp.concatenate([grad_mass * share, jnp.zeros((7, valid.shape[1]), F32)])
    cosines = jnp.sum(valid * dots * scale, axis=1, keepdims=True)
    lane = lax.broadcasted_iota(jnp.int32, (1, 128), 1)
    out = jnp.zeros((1, 128), F32)
    for index, one in enumerate((total / genes, cosines / nvs, density / SLIDES)):
        out = jnp.where(lane == index, one, out)
    scalars[...] = out


def coef_call(ids, genes_slides, sums, spot, totals):
    spots = spot.shape[1]
    return pl.pallas_call(
        coef_kernel,
        grid_spec=pltpu.PrefetchScalarGridSpec(
            num_scalar_prefetch=1,
            grid=(1,),
            in_specs=[fixed(genes_slides.shape), fixed(sums.shape), fixed((8, spots)), fixed((8, spots))],
            out_specs=[fixed((128, 128)), fixed((40, spots)), fixed((1, 128))],
            scratch_shapes=[pltpu.VMEM((32, 128), F32)],
        ),
        out_shape=[
            jax.ShapeDtypeStruct((128, 128), F32),
            jax.ShapeDtypeStruct((40, spots), F32),
            jax.ShapeDtypeStruct((1, 128), F32),
        ],
        compiler_params=vmem(6),
        cost_estimate=NO_COST,
        name="coef",
    )(ids, genes_slides, sums, spot, totals)


def grad_rows(pred, data, gene, spot, lane):
    by_pred = gene[:, lane : lane + 1].reshape(2, 8, 1)
    by_data = gene[:, 16 + lane : 17 + lane].reshape(2, 8, 1)
    pred, data = pred.reshape(2, 8, pred.shape[1]), data.reshape(2, 8, data.shape[1])
    grad = pred * (by_pred * spot[24:32, :] + spot[0:8, :])
    grad = grad - data * (by_data * spot[16:24, :] + spot[8:16, :])
    return grad.reshape(16, grad.shape[2]), jnp.sum(grad * pred, axis=0)


def grad_kernel(ids, *refs, count, lane, chips):
    pred, data, refs = refs[: 2 * count], refs[2 * count : 3 * count], refs[3 * count :]
    gene, spot, grad, column = refs[0], refs[1], refs[-2], refs[-1]
    step = pl.program_id(0)
    chip = (ids[2] + pick(step, chips)) & 3

    @pl.when(step == 0)
    def _():
        column[...] = jnp.zeros_like(column)

    total = jnp.zeros(column.shape, F32)
    for index, part in enumerate(pred):
        for sub in range(2):
            at = gene_group(ids, *PIECES[lane + 2 * index + sub])
            row = pl.multiple_of((at & 3) * 16, 16)
            to = pl.ds(pl.multiple_of(at * 16, 16), 16)
            for half in range(2):
                block = chip * 2 + half
                rows, inner = grad_rows(
                    part[sub, block],
                    data[index // 2][half, 0, pl.ds(row, 16), :],
                    gene[16 * half : 16 * half + 16, :],
                    spot,
                    lane + 2 * index + sub,
                )
                grad[0, block, to, :], grad[1, block, to, :] = split(rows)
                total += inner
    column[...] += total


def grad_call(ids, pred, spatial, gene, spot, lane, chips, done=()):
    blocks, groups, rows, spots = spatial.shape
    count = len(pred) // 2

    def chip(i, ids):
        return (ids[2] + pick(i, chips)) & 3

    def group(k):
        step = PIECES[lane + 4 * k][0]
        return pl.BlockSpec(
            (2, 1, rows, spots), lambda i, ids: (chip(i, ids), (ids[0] + step) & 3, 0, 0)
        )

    return pl.pallas_call(
        functools.partial(grad_kernel, count=count, lane=lane, chips=chips),
        grid_spec=pltpu.PrefetchScalarGridSpec(
            num_scalar_prefetch=1,
            grid=(len(chips),),
            in_specs=[RESIDENT] * (2 * count)
            + [group(k) for k in range(count)]
            + [pl.BlockSpec((32, 128), lambda i, ids: (chip(i, ids), 0)), fixed(spot.shape)]
            + [RESIDENT] * len(done),
            out_specs=[RESIDENT, fixed((8, spots))],
        ),
        out_shape=[
            jax.ShapeDtypeStruct((2, blocks, groups * rows, spots), BF16),
            jax.ShapeDtypeStruct((8, spots), F32),
        ],
        input_output_aliases={3 * count + 3: 0} if done else {},
        compiler_params=vmem(12),
        cost_estimate=NO_COST,
        name="grad",
    )(ids, *pred, *[streamed(spatial)] * count, gene, spot, *done)


def back_kernel(ids, grad, masses, expr, *refs, parts, first, last):
    more, (sums, *outs), (held, ready) = refs[: first + 4 * last], refs[first + 4 * last : -2], refs[-2:]
    step = pl.program_id(0)
    rows = grad.shape[2]

    def block(part):
        return ((ids[2] + part[0]) & 3) * 2 + (ids[3] ^ part[1])

    def fetch(k):
        start = pl.multiple_of(block(parts[k]) * rows, rows)
        return pltpu.make_async_copy(expr.at[pl.ds(start, rows), :], held.at[k], ready.at[k])

    @pl.when(step == 0)
    def _():
        for k in range(len(parts)):
            fetch(k).start()

    here = block([pick(step, [part[k] for part in parts]) for k in range(2)])
    left = grad[0, here], grad[1, here]
    if first:
        pair = split(jnp.concatenate([more[0][...], jnp.zeros_like(more[0])]))
        left = [jnp.concatenate(both) for both in zip(left, pair)]
    part = product(left, masses, ((1,), (1,)))

    @pl.when(step == 0)
    def _():
        if first:
            sums[...] = part[rows : rows + 8]
        elif last:
            sums[...] = more[0][...] + more[1][...] + more[2][...]
        else:
            sums[...] = jnp.zeros_like(sums)

    part = part[:rows]
    for k, out in enumerate(outs):

        @pl.when(step == k)
        def _(k=k, out=out):
            out[:rows, :] = part
            fetch(k).wait()

    sums[...] += jnp.sum((part * held[step]).reshape(-1, 8, part.shape[1]), axis=0)
    if last:

        @pl.when(step == len(parts) - 1)
        def _():
            total = jnp.sum(sums[...], axis=0, keepdims=True)
            sums[...] = jnp.zeros_like(sums)
            sums[0:1, :] = total
            sums[1:2, 0:128] = more[3][...]
            outs[0][rows:, :] = sums[...]


def back_call(ids, parts, grad, masses, expr, first=(), last=()):
    _, blocks, rows, spots = grad.shape
    cells = masses.shape[1]
    shapes = [(rows, cells)] * len(parts)
    if last:
        shapes[0] = (rows + 8, cells)
    return pl.pallas_call(
        functools.partial(back_kernel, parts=parts, first=len(first), last=len(last) // 4),
        grid_spec=pltpu.PrefetchScalarGridSpec(
            num_scalar_prefetch=1,
            grid=(len(parts),),
            in_specs=[RESIDENT, RESIDENT, pl.BlockSpec(memory_space=pl.ANY)]
            + [pl.BlockSpec((8, spots), lambda i, ids: (4, 0))] * len(first)
            + [fixed(one.shape) for one in last],
            out_specs=[fixed((8, cells))] + [RESIDENT] * len(parts),
            scratch_shapes=[
                pltpu.VMEM((len(parts), rows, cells), F32),
                pltpu.SemaphoreType.DMA((len(parts),)),
            ],
        ),
        out_shape=[jax.ShapeDtypeStruct((8, cells), F32)]
        + [jax.ShapeDtypeStruct(shape, F32) for shape in shapes],
        compiler_params=vmem(16),
        cost_estimate=NO_COST,
        name="back",
    )(ids, grad, masses, streamed(expr), *first, *last)


def lift_kernel(above, below, far_up, far_down, out_above, out_below):
    rows = far_up.shape[0]
    out_above[:rows, :] = above[:rows, :] + far_up[...]
    out_above[rows:, :] = above[rows:, :]
    out_below[:rows, :] = below[:rows, :]
    out_below[rows:, :] = below[rows:, :] + far_down[...]


def lift_call(above, below, far_up, far_down):
    rows, cells = far_up.shape
    block = 256
    far = pl.BlockSpec((rows, block), lambda i: (0, i))
    whole = pl.BlockSpec((2 * rows, block), lambda i: (0, i))
    return pl.pallas_call(
        lift_kernel,
        grid=(cells // block,),
        in_specs=[whole, whole, far, far],
        out_specs=[whole, whole],
        out_shape=[jax.ShapeDtypeStruct(above.shape, F32)] * 2,
        compiler_params=vmem(8),
        cost_estimate=pl.CostEstimate(flops=10**10, bytes_accessed=0, transcendentals=0),
        name="lift",
    )(above, below, far_up, far_down)


def map_kernel(expr, grad, masses, keep, spot, out, held, ready, *, scale):
    index = pl.program_id(0)
    quarter, block = held.shape[2:]
    count = held.shape[1]

    def fetch(at, k):
        columns = pl.ds(pl.multiple_of(at * block, block), block)
        return pltpu.make_async_copy(
            expr.at[pl.ds(k * quarter, quarter), columns], held.at[at & 1, k], ready.at[at & 1, k]
        )

    @pl.when(index == 0)
    def _():
        for k in range(count):
            fetch(index, k).start()

    @pl.when(index + 1 < pl.num_programs(0))
    def _():
        for k in range(count):
            fetch(index + 1, k).start()

    inner = spot[0:1, :]
    for k in range(count):
        fetch(index, k).wait()
        rows = slice(k * quarter, k * quarter + quarter)
        pair = grad[0, rows, :], grad[1, rows, :]
        inner = inner + product(split(held[index & 1, k]), pair, ((0,), (0,)))
    at = pl.multiple_of(index * block, block)
    expo = masses[0, pl.ds(at, block), :].astype(F32) + masses[1, pl.ds(at, block), :].astype(F32)
    for part in range(block // 128):
        rows = slice(part * 128, part * 128 + 128)
        weight = as_column(keep[pl.ds(index * (block // 128) + part, 1), :])
        out[rows, :] = (scale * expo[rows]) * (weight * inner[rows] - spot[1:2, :])


def map_call(expr, grad, masses, keep, spot, scale):
    genes, cells = expr.shape
    spots = masses.shape[2]
    block, count = 256, 4
    return pl.pallas_call(
        functools.partial(map_kernel, scale=scale),
        grid=(cells // block,),
        in_specs=[
            pl.BlockSpec(memory_space=pl.ANY),
            RESIDENT,
            RESIDENT,
            fixed(keep.shape),
            fixed((8, spots)),
        ],
        out_specs=pl.BlockSpec((block, spots), lambda i: (i, 0)),
        out_shape=jax.ShapeDtypeStruct((cells, spots), F32),
        scratch_shapes=[
            pltpu.VMEM((2, count, genes // count, block), F32),
            pltpu.SemaphoreType.DMA((2, count)),
        ],
        compiler_params=vmem(24),
        cost_estimate=NO_COST,
        name="grad_map",
    )(streamed(expr), grad, masses, keep, spot)


def finish_kernel(last, got1, got2, got3, totals, scalars, kind, filt, grad_filter, terms, *, all_cells):
    total = (last[...] + got2[...]) + (got1[...] + got3[...])
    nvalid, retained, reg_sum = (totals[2:3, k : k + 1] for k in range(3))
    valid = (kind[...] >= 0).astype(F32)
    sigma = jax.nn.sigmoid(filt[...])
    keep = sigma * valid
    shifted = (retained - 0.35 * nvalid) / (0.1 * all_cells)
    count_term = jnp.sqrt(shifted * shifted + 1.0)
    grad_keep = total[0:1, :] + shifted / count_term / (0.1 * all_cells) + (1.0 - 2.0 * keep) / nvalid
    grad_filter[...] = valid * sigma * (1.0 - sigma) * grad_keep * all_cells
    lane = lax.broadcasted_iota(jnp.int32, (1, 128), 1)
    out = jnp.zeros((1, 128), F32)
    parts = (scalars[:, 0:1], total[1:2, 1:2], scalars[:, 2:3], count_term, reg_sum / nvalid)
    for index, one in enumerate(parts):
        out = jnp.where(lane == index, one, out)
    terms[...] = out


def finish_call(last, got, totals, scalars, kind, filt, all_cells):
    return pl.pallas_call(
        functools.partial(finish_kernel, all_cells=float(all_cells)),
        grid=(1,),
        in_specs=[fixed(one.shape) for one in (last, *got, totals, scalars, kind, filt)],
        out_specs=[fixed(kind.shape), fixed((1, 128))],
        out_shape=[jax.ShapeDtypeStruct(kind.shape, F32), jax.ShapeDtypeStruct((1, 128), F32)],
        compiler_params=vmem(4),
        cost_estimate=NO_COST,
        name="finish",
    )(last, *got, totals, scalars, kind, filt)


def on_device(map_logits, filter_logits, expr, spatial, cell_type, slide_id, spot_mask):
    genes, cells = expr.shape
    spots = map_logits.shape[1]
    all_cells = cells * lax.axis_size("cells")
    all_spots = spots * lax.axis_size("spots")
    cell_place = lax.axis_index("cells")
    z, x = cell_place >> 2, cell_place & 3
    spot_place = lax.axis_index("spots")
    y, core = spot_place >> 1, spot_place & 1
    first = jnp.where(core == 0, x, z)
    second = jnp.where(core == 0, z, x)
    blocks = cells // 128

    valid = (cell_type >= 0).astype(F32)
    sigma = jax.nn.sigmoid(filter_logits)
    keep = sigma * valid
    spot_valid = spot_mask.astype(F32)
    kind2 = cell_type.reshape(blocks, 128)
    filt2 = filter_logits.reshape(blocks, 128)
    keep2 = keep.reshape(blocks, 128)

    expr4 = expr.reshape(8, 16, 16, cells)
    keep_row = keep.reshape(1, cells)

    ids = jnp.stack([first, second, y, core]).astype(jnp.int32)

    def pred_part(one, two, more, *others):
        return pred_call(after(ids, *others), (one, two), expr4, keep_row, masses, totals, more)

    masses, types, totals, *far = expo_call(
        ids, ((2, 0), (2, 1)), map_logits, kind2, filt2, expr4
    )
    far_right, far_left = along(far[0], 1), along(far[1], -1)
    near = pred_part((1, 1), (-1, 0), (), *far)
    near_right, near_left = along(near[0], 1), along(near[1], -1)
    late = pred_part((1, 0), (-1, 1), (far_right, far_left), *near)
    late_right, late_left = along(late[0], 1), along(late[1], -1)
    own = pred_part((0, 0), (0, 1), (near_left, near_right), *late)
    types = types + swap_across(after(types, *own), 1)
    mine, *pieces = merge_call(own, (late_right, late_left))
    pieces = [across(piece, step + 1) for step, piece in enumerate(pieces)]
    spatial_squares = jnp.sum(after(spatial, mine) ** 2, axis=0)
    types = types + swap_along(after(types, spatial_squares), 1)
    types = types + swap_along(types, 3)
    spot_rows = stacked([spot_valid, slide_id.astype(F32), spatial_squares])
    mine = after(mine, spot_rows, types)
    piece = mine + pieces[0] + pieces[1] + pieces[2]
    totals = piece[-1]
    piece = piece[:-1].reshape(8, 16, spots)
    share = 1.0 / totals[0]
    mass = totals[1] * share

    got = [across(piece, step) for step in (1, 2, 3)]
    sums, slides = stats_call(
        ids,
        piece,
        spatial.reshape(8, 16, 16, spots),
        spot_rows,
        totals,
    )
    sums = sums + swap_along(sums, 1)
    sums = sums + swap_along(sums, 3)
    mine = after((jnp.stack([piece, got[2]]), jnp.stack([got[1], got[0]])), sums)
    right0, left1 = along(mine[0], 1), along(mine[1], -1)
    right1, left0 = along(mine[1], 1), along(mine[0], -1)
    sums = sums + swap_across(after(sums, *mine), 1)
    sums = sums + swap_across(sums, 3)
    right0, left1, sums = lax.optimization_barrier((right0, left1, sums))
    far0, far1 = along(right0, 1), along(left1, -1)
    genes_slides = jnp.concatenate([sums[:48], slides])
    genes_slides = genes_slides + swap(genes_slides, 0, 0, 0, 1)
    genes_slides = genes_slides + swap(genes_slides, 0, 0, 1, 0)
    genes_slides = after(genes_slides, right1, left0)
    genes_slides = genes_slides + swap(genes_slides, 0, 0, 3, 0)
    pred = [*mine, right0, right1, left0, left1, far0, far1]
    gene_coef, spot_coef, scalars = coef_call(ids, genes_slides, sums, spot_rows, totals)
    spatial4 = spatial.reshape(8, RING, genes // 32, spots)
    grad, column_a = grad_call(ids, pred[:6], spatial4, gene_coef, spot_coef, 0, (0, 1, 2, 3))

    def last_grad(chips, grad, *others):
        return grad_call(
            after(ids, *others), pred[6:], spatial4, gene_coef, spot_coef, 12, chips, (grad,)
        )

    def back_part(steps, grad, *others, **rows):
        return back_call(after(ids, *others), steps, grad, masses, expr, **rows)

    rows = genes // 16
    grad, column_b = last_grad((2,), grad)
    sums_a, far_a = back_part([(2, 1)], grad, first=[spot_coef])
    far_got = swap(far_a, 0, 0, 0, 1)
    sums_b, far_b = back_part([(2, 0)], grad, far_a)
    far = far_b + far_got
    far_up, far_down = up(far[:rows], 1), up(far[rows:], -1)
    grad, column_c = last_grad((1, -1, 0), grad, far)
    sums_c, up_a, down_a, up_b, down_b = back_part([(1, 1), (-1, 1), (1, 0), (-1, 0)], grad)
    up_got, down_got = swap(up_a, 0, 0, 0, 1), swap(down_a, 0, 0, 0, 1)
    last, own_a, own_b = back_part(
        [(0, 1), (0, 0)], grad, up_b, last=[sums_a, sums_b, sums_c, scalars]
    )
    above, below = lift_call(up_b, down_b, *after((far_up, far_down), own_b))
    above, below = above + up_got, below + down_got
    near_up, near_down = up(above, 1), up(below, -1)
    own_got = swap(after(own_a, far_up, far_down), 0, 0, 0, 1)
    last = last + own_got[2 * rows :]
    own = own_b + own_got[: 2 * rows]

    column = jnp.sum(column_a + column_b + column_c, axis=0) * share + spot_coef[32] * mass
    map_rows = stacked([spot_coef[32], column])
    map_rows = after(map_rows, above, below, last)
    map_args = (expr, grad.reshape(2, genes, spots), masses, keep2, map_rows, all_cells * genes)
    got = [up(last, step) for step in (1, 2, 3)]
    grad_map = map_call(*map_args)
    got = after(tuple(got), grad_map)
    types = types + swap_across(after(types, grad_map), 3)
    grad_weighted = after(own, grad_map) + near_up + near_down
    grad_expr = grad_weighted * (keep * (genes * all_spots))[None, :]

    type_fraction = types * share

    grad_filter, loss_terms = finish_call(
        last, got, totals, scalars, cell_type.reshape(1, cells), filter_logits.reshape(1, cells), all_cells
    )
    return (loss_terms[0, :5], type_fraction, grad_map, grad_filter.reshape(cells), grad_expr)


def solution(mesh):
    in_specs = (
        P("cells", "spots"),
        P("cells"),
        P(None, "cells"),
        P(None, "spots"),
        P("cells"),
        P("spots"),
        P("spots"),
    )
    out_specs = (P(), P(None, "spots"), P("cells", "spots"), P("cells"), P("spots", "cells"))
    return jax.shard_map(
        on_device, mesh=mesh, in_specs=in_specs, out_specs=out_specs, check_vma=False
    )
```

```python
import functools

import jax
import jax.numpy as jnp
from jax import lax
from jax.experimental import pallas as pl
from jax.experimental.pallas import tpu as pltpu
from jax.sharding import PartitionSpec as P

TYPES = 32
SLIDES = 3
RING = 4
F32 = jnp.float32
BF16 = jnp.bfloat16


def vmem(mib):
    return pltpu.CompilerParams(vmem_limit_bytes=mib << 20)


def fixed(shape):
    return pl.BlockSpec(shape, lambda *_: (0,) * len(shape), pipeline_mode=pl.Buffered(1))


def streamed(array):
    return pltpu.with_memory_space_constraint(array, pltpu.HBM)


RESIDENT = pl.BlockSpec(memory_space=pltpu.VMEM)


def cost(flops, moved):
    return pl.CostEstimate(flops=int(flops) // 8, bytes_accessed=int(moved) // 8, transcendentals=0)


NO_COST = pl.CostEstimate(flops=0, bytes_accessed=0, transcendentals=0)


def route(target):
    def flat(z, x, y, core):
        return ((z % RING * RING + x % RING) * RING + y % RING) * 2 + core

    return [
        (flat(z, x, y, core), flat(*target(z, x, y, core)))
        for z in range(RING)
        for x in range(RING)
        for y in range(RING)
        for core in range(2)
    ]


def send(array, target):
    return lax.ppermute(array, ("cells", "spots"), route(target))


def along(array, step):
    return send(array, lambda z, x, y, c: (z, x + step, y, c) if c == 0 else (z + step, x, y, c))


def across(array, step):
    return send(array, lambda z, x, y, c: (z + step, x, y, c) if c == 0 else (z, x + step, y, c))


def up(array, step):
    return send(array, lambda z, x, y, c: (z, x, y + step, c))


def swap(array, mz, mx, my, mc):
    return send(array, lambda z, x, y, c: (z ^ mz, x ^ mx, y ^ my, c ^ mc))


def swap_along(array, mask):
    return send(array, lambda z, x, y, c: (z, x ^ mask, y, c) if c == 0 else (z ^ mask, x, y, c))


def swap_across(array, mask):
    return send(array, lambda z, x, y, c: (z ^ mask, x, y, c) if c == 0 else (z, x ^ mask, y, c))


def after(value, *others):
    return lax.optimization_barrier((value, *others))[0]


def split(value):
    high = value.astype(BF16)
    return high, (value - high.astype(F32)).astype(BF16)


def product(left, right, dims):
    def one(a, b):
        return lax.dot_general(a, b, (dims, ((), ())), preferred_element_type=F32)

    return one(left[0], right[0]) + one(left[0], right[1]) + one(left[1], right[0])


def gene_group(ids, step, half, sub):
    return ((ids[0] + step) & 3) * RING + ((ids[1] + 2 * half + sub) & 3)


PIECES = [
    (step, half, sub)
    for step, half in ((0, 0), (0, 1), (-1, 0), (-1, 1), (1, 0), (1, 1), (2, 0), (2, 1))
    for sub in range(2)
]


def pick(index, values):
    out = values[0]
    for k, value in enumerate(values[1:]):
        out = jnp.where(index == k + 1, value, out)
    return out


def stacked(rows):
    row = lax.broadcasted_iota(jnp.int32, (8, rows[0].shape[0]), 0)
    out = jnp.zeros(row.shape, F32)
    for k, value in enumerate(rows):
        out = jnp.where(row == k, value[None, :], out)
    return out


def as_column(row):
    return jnp.broadcast_to(row, (128, 128)).T[:, :1]


def expo_kernel(ids, logits, kind, filt, *refs):
    expr, (masses, types, totals, out0, out1) = refs[:4], refs[4:]
    step = pl.program_id(0)
    count = logits.shape[0] // 128

    @pl.when(step == 0)
    def _():
        for out in (types, totals, out0, out1):
            out[...] = jnp.zeros_like(out)

    keeps = []
    lane = lax.broadcasted_iota(jnp.int32, (1, totals.shape[1]), 1)
    cell_sums = jnp.zeros(lane.shape, F32)
    for part in range(count):
        rows = slice(part * 128, part * 128 + 128)
        label = kind[pl.ds(step * count + part, 1), :]
        valid = (label >= 0).astype(F32)
        keep = valid * jax.nn.sigmoid(filt[pl.ds(step * count + part, 1), :])
        keeps.append(keep)
        for k, one in enumerate((valid, keep, keep - keep * keep)):
            cell_sums += jnp.where(lane == k, jnp.sum(one, axis=1, keepdims=True), 0.0)
        expo = jnp.exp(logits[rows]) * as_column(valid)
        masses[0, rows], masses[1, rows] = split(expo)
        whole = jnp.sum(expo, axis=0, keepdims=True)
        kept = jnp.sum(expo * as_column(keep), axis=0, keepdims=True)
        row = lax.broadcasted_iota(jnp.int32, types.shape, 0)
        types[...] += jnp.where(row == jnp.max(label, axis=1, keepdims=True), whole, 0.0)
        row = lax.broadcasted_iota(jnp.int32, totals.shape, 0)
        totals[...] += jnp.where(row == 0, whole, jnp.where(row == 1, kept, 0.0))
    totals[2:3, :] += cell_sums
    weighted = jnp.concatenate([part[...].reshape(-1, logits.shape[0]) for part in expr])
    weighted = weighted * jnp.concatenate(keeps, axis=1)
    part = product(split(weighted), masses, ((1,), (0,)))
    half = part.shape[0] // 2
    for index, out in enumerate((out0, out1)):
        new = part[index * half : index * half + half].reshape(-1, 8, part.shape[1])
        out[: half // 8] += new
        out[half // 8] = totals[...]


def expo_call(ids, parts, logits, kind, filt, expr):
    cells, spots = logits.shape
    blocks, groups, rows, _ = expr.shape
    block = 256

    def genes(part, sub):
        return pl.BlockSpec(
            (blocks, 1, rows, block), lambda i, ids: (0, gene_group(ids, *part, sub), 0, i)
        )

    return pl.pallas_call(
        expo_kernel,
        grid_spec=pltpu.PrefetchScalarGridSpec(
            num_scalar_prefetch=1,
            grid=(cells // block,),
            in_specs=[
                pl.BlockSpec((block, spots), lambda i, w: (i, 0)),
                fixed(kind.shape),
                fixed(filt.shape),
            ]
            + [genes(part, sub) for part in parts for sub in range(2)],
            out_specs=[
                pl.BlockSpec((2, block, spots), lambda i, w: (0, i, 0)),
                fixed((TYPES, spots)),
                fixed((8, spots)),
                fixed((blocks * rows // 4 + 1, 8, spots)),
                fixed((blocks * rows // 4 + 1, 8, spots)),
            ],
        ),
        out_shape=[
            jax.ShapeDtypeStruct((2, cells, spots), BF16),
            jax.ShapeDtypeStruct((TYPES, spots), F32),
            jax.ShapeDtypeStruct((8, spots), F32),
            jax.ShapeDtypeStruct((blocks * rows // 4 + 1, 8, spots), F32),
            jax.ShapeDtypeStruct((blocks * rows // 4 + 1, 8, spots), F32),
        ],
        compiler_params=vmem(16),
        cost_estimate=cost(0, cells * spots * 8),
        name="expo",
    )(ids, streamed(logits), kind, filt, *[streamed(expr)] * 4)


def pred_kernel(ids, expr_a, expr_b, keep, masses, totals, *refs):
    more, outs = refs[:-2], refs[-2:]
    rows = 2 * expr_a.shape[0] * expr_a.shape[2]
    weighted = jnp.concatenate(
        [part[...].reshape(rows // 2, keep.shape[1]) for part in (expr_a, expr_b)]
    )
    part = product(split(weighted * keep[...]), masses, ((1,), (0,)))
    part = part.reshape(rows // 8, 8, part.shape[1])
    for step, out in enumerate(outs):

        @pl.when(pl.program_id(0) == step)
        def _(step=step, out=out):
            if more:
                out[: rows // 8] = part + more[step][: rows // 8]
                out[rows // 8] = totals[...] + more[step][rows // 8]
            else:
                out[: rows // 8] = part
                out[rows // 8] = totals[...]


def pred_call(ids, parts, expr, keep, masses, totals, more=()):
    blocks, groups, rows, cells = expr.shape
    spots = masses.shape[2]
    tiles = blocks * rows // 4 + 1

    def genes(sub):
        def place(i, ids):
            step, half = (pick(i, [part[k] for part in parts]) for k in range(2))
            return (0, gene_group(ids, step, half, sub), 0, 0)

        return pl.BlockSpec((blocks, 1, rows, cells), place)

    return pl.pallas_call(
        pred_kernel,
        grid_spec=pltpu.PrefetchScalarGridSpec(
            num_scalar_prefetch=1,
            grid=(2,),
            in_specs=[
                genes(0),
                genes(1),
                fixed((1, cells)),
                RESIDENT,
                fixed((8, spots)),
            ]
            + [RESIDENT] * len(more),
            out_specs=[RESIDENT] * 2,
        ),
        out_shape=[jax.ShapeDtypeStruct((tiles, 8, spots), F32)] * 2,
        compiler_params=vmem(16),
        cost_estimate=cost(24 * blocks * rows * cells * spots, 4 * cells * spots + 16 * blocks * rows * (cells + spots)),
        name="pred",
    )(ids, *[streamed(expr)] * 2, keep, masses, totals, *more)


def merge_kernel(own0, own1, got0, got1, *outs):
    tiles = outs[0].shape[0] - 1
    for half, (own, got) in enumerate(((own0, got0), (own1, got1))):
        for sub in range(2):
            out = outs[2 * half + sub]
            out[:tiles] = own[sub * tiles : sub * tiles + tiles] + got[sub * tiles : sub * tiles + tiles]
            out[tiles] = own[2 * tiles] + got[2 * tiles]


def merge_call(own, got):
    tiles, _, spots = own[0].shape
    block = 256
    whole = pl.BlockSpec((tiles, 8, block), lambda i: (0, 0, i))
    piece = (tiles // 2 + 1, 8, spots)
    return pl.pallas_call(
        merge_kernel,
        grid=(spots // block,),
        in_specs=[whole] * 4,
        out_specs=[pl.BlockSpec((tiles // 2 + 1, 8, block), lambda i: (0, 0, i))] * 4,
        out_shape=[jax.ShapeDtypeStruct(piece, F32)] * 4,
        compiler_params=vmem(12),
        cost_estimate=NO_COST,
        name="merge",
    )(*own, *got)


def stats_kernel(ids, piece, spatial, spot, totals, gene, slide_sums):
    rows = piece.shape[0] * piece.shape[1]
    valid, slide = spot[0:1, :], spot[1:2, :]
    share = 1.0 / totals[0:1, :]
    mass = totals[1:2, :] * share
    value = piece[...].reshape(rows, piece.shape[2]) * share
    data = spatial[...].reshape(value.shape)
    cross, square = value * data, value * value
    lane = lax.broadcasted_iota(jnp.int32, (rows, 128), 1)
    sums = jnp.zeros((rows, 128), F32)
    for index, one in enumerate((cross, square, data * data)):
        sums = jnp.where(lane == index, jnp.sum(one * valid, axis=1, keepdims=True), sums)
    sums = sums.T
    gene[...] = jnp.zeros_like(gene)
    slide_sums[...] = jnp.zeros_like(slide_sums)
    for index in range(3):
        gene[pl.ds(16 * index + gene_group(ids, 0, 0, 0), 1), :] = sums[index : index + 1, :]
    lane = lax.broadcasted_iota(jnp.int32, (1, 128), 1)
    slides = jnp.zeros((1, 128), F32)
    logs = jnp.log(jnp.where(valid > 0, mass, 1.0))
    for k in range(SLIDES):
        inside = jnp.where(slide == k, valid, 0.0)
        for index, one in enumerate((inside, inside * mass, inside * logs)):
            total = jnp.sum(one, axis=1, keepdims=True)
            slides = jnp.where(lane == 3 * index + k, total, slides)
    slide_sums[0:1, :] = slides
    for index, one in enumerate((cross, square)):
        total = jnp.sum(one, axis=0, keepdims=True)
        for k in range(total.shape[1] // 128):
            at = 48 + 8 * index + k
            gene[at : at + 1, :] = total[:, 128 * k : 128 * k + 128]


def stats_call(ids, piece, spatial, spot, totals):
    blocks, rows, spots = piece.shape
    return pl.pallas_call(
        stats_kernel,
        grid_spec=pltpu.PrefetchScalarGridSpec(
            num_scalar_prefetch=1,
            grid=(1,),
            in_specs=[
                fixed((blocks, rows, spots)),
                pl.BlockSpec((blocks, 1, rows, spots), lambda i, ids: (0, gene_group(ids, 0, 0, 0), 0, 0)),
                fixed((8, spots)),
                fixed((8, spots)),
            ],
            out_specs=[fixed((64, 128)), fixed((8, 128))],
        ),
        out_shape=[jax.ShapeDtypeStruct((64, 128), F32), jax.ShapeDtypeStruct((8, 128), F32)],
        compiler_params=vmem(8),
        cost_estimate=NO_COST,
        name="stats",
    )(ids, piece, streamed(spatial), spot, totals)


def coef_kernel(ids, genes_slides, sums, spot, totals, gene, rows, scalars, pairs):
    valid, slide, squares = (spot[k : k + 1, :] for k in range(3))
    share = 1.0 / totals[0:1, :]
    mass = totals[1:2, :] * share
    genes = float(16 * sums.shape[1])

    def wide(index):
        return jnp.concatenate([sums[index + k : index + k + 1, :] for k in range(8)], axis=1)

    dots, own = wide(48), wide(56)
    dot, aa, bb = genes_slides[0:16, :], genes_slides[16:32, :], genes_slides[32:48, :]
    scale = lax.rsqrt(aa * bb + 1e-06)
    pairs[0:16, :] = dot * scale**3 * bb / genes
    pairs[16:32, :] = scale / genes
    pair = [pairs[pl.ds(k + gene_group(ids, *one), 1), :] for k in (0, 16) for one in PIECES]
    gene[...] = jnp.concatenate([*pair, jnp.zeros((96, 128), F32)]).T
    total = jnp.sum(jnp.sum(dot * scale, axis=1, keepdims=True), axis=0, keepdims=True)
    nvs = jnp.zeros((1, 1), F32)
    density = jnp.zeros((1, 1), F32)
    nk, tk = jnp.ones_like(valid), jnp.ones_like(valid)
    for k in range(SLIDES):
        count, held, logs = (genes_slides[48:49, 3 * j + k : 3 * j + k + 1] for j in range(3))
        some = count > 0
        safe = jnp.where(some, count, 1.0)
        nvs += count
        density += jnp.where(some, jnp.log(jnp.where(some, held, 1.0) / safe) - logs / safe, 0.0)
        here = (slide == k) & (valid > 0)
        nk = jnp.where(here, count, nk)
        tk = jnp.where(here, held, tk)
    scale = lax.rsqrt(own * squares + 1e-06)
    grad_mass = valid / SLIDES * (1.0 / tk - 1.0 / (nk * jnp.where(valid > 0, mass, 1.0)))
    mask = valid * share
    by_pred, by_data = dots * scale**3 * squares / nvs, scale / nvs
    for index, one in enumerate((by_pred * share * mask, by_data * mask, mask, share * mask)):
        rows[8 * index : 8 * index + 8, :] = jnp.broadcast_to(one, (8, one.shape[1]))
    rows[32:40, :] = jnp.concatenate([grad_mass * share, jnp.zeros((7, valid.shape[1]), F32)])
    cosines = jnp.sum(valid * dots * scale, axis=1, keepdims=True)
    lane = lax.broadcasted_iota(jnp.int32, (1, 128), 1)
    out = jnp.zeros((1, 128), F32)
    for index, one in enumerate((total / genes, cosines / nvs, density / SLIDES)):
        out = jnp.where(lane == index, one, out)
    scalars[...] = out


def coef_call(ids, genes_slides, sums, spot, totals):
    spots = spot.shape[1]
    return pl.pallas_call(
        coef_kernel,
        grid_spec=pltpu.PrefetchScalarGridSpec(
            num_scalar_prefetch=1,
            grid=(1,),
            in_specs=[fixed(genes_slides.shape), fixed(sums.shape), fixed((8, spots)), fixed((8, spots))],
            out_specs=[fixed((128, 128)), fixed((40, spots)), fixed((1, 128))],
            scratch_shapes=[pltpu.VMEM((32, 128), F32)],
        ),
        out_shape=[
            jax.ShapeDtypeStruct((128, 128), F32),
            jax.ShapeDtypeStruct((40, spots), F32),
            jax.ShapeDtypeStruct((1, 128), F32),
        ],
        compiler_params=vmem(6),
        cost_estimate=NO_COST,
        name="coef",
    )(ids, genes_slides, sums, spot, totals)


def grad_rows(pred, data, gene, spot, lane):
    by_pred = gene[:, lane : lane + 1].reshape(2, 8, 1)
    by_data = gene[:, 16 + lane : 17 + lane].reshape(2, 8, 1)
    pred, data = pred.reshape(2, 8, pred.shape[1]), data.reshape(2, 8, data.shape[1])
    grad = pred * (by_pred * spot[24:32, :] + spot[0:8, :])
    grad = grad - data * (by_data * spot[16:24, :] + spot[8:16, :])
    return grad.reshape(16, grad.shape[2]), jnp.sum(grad * pred, axis=0)


def grad_kernel(ids, *refs, count, lane, chips):
    pred, data, refs = refs[: 2 * count], refs[2 * count : 3 * count], refs[3 * count :]
    gene, spot, grad, column = refs[0], refs[1], refs[-2], refs[-1]
    step = pl.program_id(0)
    chip = (ids[2] + pick(step, chips)) & 3

    @pl.when(step == 0)
    def _():
        column[...] = jnp.zeros_like(column)

    def half_of(half, _):
        block = chip * 2 + half
        factors = gene[pl.ds(pl.multiple_of(16 * half, 16), 16), :]
        total = jnp.zeros(column.shape, F32)
        for index, part in enumerate(pred):
            for sub in range(2):
                at = gene_group(ids, *PIECES[lane + 2 * index + sub])
                row = pl.multiple_of((at & 3) * 16, 16)
                to = pl.ds(pl.multiple_of(at * 16, 16), 16)
                rows, inner = grad_rows(
                    part[sub, block],
                    data[index // 2][half, 0, pl.ds(row, 16), :],
                    factors,
                    spot,
                    lane + 2 * index + sub,
                )
                grad[0, block, to, :], grad[1, block, to, :] = split(rows)
                total += inner
        column[...] += total
        return 0

    lax.fori_loop(0, 2, half_of, 0)


def grad_call(ids, pred, spatial, gene, spot, lane, chips, done=()):
    blocks, groups, rows, spots = spatial.shape
    count = len(pred) // 2

    def chip(i, ids):
        return (ids[2] + pick(i, chips)) & 3

    def group(k):
        step = PIECES[lane + 4 * k][0]
        return pl.BlockSpec(
            (2, 1, rows, spots), lambda i, ids: (chip(i, ids), (ids[0] + step) & 3, 0, 0)
        )

    return pl.pallas_call(
        functools.partial(grad_kernel, count=count, lane=lane, chips=chips),
        grid_spec=pltpu.PrefetchScalarGridSpec(
            num_scalar_prefetch=1,
            grid=(len(chips),),
            in_specs=[RESIDENT] * (2 * count)
            + [group(k) for k in range(count)]
            + [pl.BlockSpec((32, 128), lambda i, ids: (chip(i, ids), 0)), fixed(spot.shape)]
            + [RESIDENT] * len(done),
            out_specs=[RESIDENT, fixed((8, spots))],
        ),
        out_shape=[
            jax.ShapeDtypeStruct((2, blocks, groups * rows, spots), BF16),
            jax.ShapeDtypeStruct((8, spots), F32),
        ],
        input_output_aliases={3 * count + 3: 0} if done else {},
        compiler_params=vmem(12),
        cost_estimate=NO_COST,
        name="grad",
    )(ids, *pred, *[streamed(spatial)] * count, gene, spot, *done)


def back_kernel(ids, grad, masses, expr, *refs, parts, first, last):
    more, (sums, *outs), (held, ready) = refs[: first + 4 * last], refs[first + 4 * last : -2], refs[-2:]
    step = pl.program_id(0)
    rows = grad.shape[2]

    def block(part):
        return ((ids[2] + part[0]) & 3) * 2 + (ids[3] ^ part[1])

    def fetch(k):
        start = pl.multiple_of(block(parts[k]) * rows, rows)
        return pltpu.make_async_copy(expr.at[pl.ds(start, rows), :], held.at[k], ready.at[k])

    @pl.when(step == 0)
    def _():
        for k in range(len(parts)):
            fetch(k).start()

    here = block([pick(step, [part[k] for part in parts]) for k in range(2)])
    left = grad[0, here], grad[1, here]
    if first:
        pair = split(jnp.concatenate([more[0][...], jnp.zeros_like(more[0])]))
        left = [jnp.concatenate(both) for both in zip(left, pair)]
    part = product(left, masses, ((1,), (1,)))

    @pl.when(step == 0)
    def _():
        if first:
            sums[...] = part[rows : rows + 8]
        elif last:
            sums[...] = more[0][...] + more[1][...] + more[2][...]
        else:
            sums[...] = jnp.zeros_like(sums)

    part = part[:rows]
    for k, out in enumerate(outs):

        @pl.when(step == k)
        def _(k=k, out=out):
            out[...] = part
            fetch(k).wait()

    sums[...] += jnp.sum((part * held[step]).reshape(-1, 8, part.shape[1]), axis=0)
    if last:

        @pl.when(step == len(parts) - 1)
        def _():
            total = jnp.sum(sums[...], axis=0, keepdims=True)
            sums[...] = jnp.zeros_like(sums)
            sums[0:1, :] = total
            sums[1:2, 0:128] = more[3][...]


def back_call(ids, parts, grad, masses, expr, first=(), last=()):
    _, blocks, rows, spots = grad.shape
    cells = masses.shape[1]
    return pl.pallas_call(
        functools.partial(back_kernel, parts=parts, first=len(first), last=len(last) // 4),
        grid_spec=pltpu.PrefetchScalarGridSpec(
            num_scalar_prefetch=1,
            grid=(len(parts),),
            in_specs=[RESIDENT, RESIDENT, pl.BlockSpec(memory_space=pl.ANY)]
            + [pl.BlockSpec((8, spots), lambda i, ids: (4, 0))] * len(first)
            + [fixed(one.shape) for one in last],
            out_specs=[fixed((8, cells))] + [RESIDENT] * len(parts),
            scratch_shapes=[
                pltpu.VMEM((len(parts), rows, cells), F32),
                pltpu.SemaphoreType.DMA((len(parts),)),
            ],
        ),
        out_shape=[jax.ShapeDtypeStruct((8, cells), F32)]
        + [jax.ShapeDtypeStruct((rows, cells), F32)] * len(parts),
        compiler_params=vmem(22),
        cost_estimate=NO_COST,
        name="back",
    )(ids, grad, masses, streamed(expr), *first, *last)


def lift_kernel(above, below, far_up, far_down, out_above, out_below):
    rows = far_up.shape[0]
    out_above[:rows, :] = above[:rows, :] + far_up[...]
    out_above[rows:, :] = above[rows:, :]
    out_below[:rows, :] = below[:rows, :]
    out_below[rows:, :] = below[rows:, :] + far_down[...]


def lift_call(above, below, far_up, far_down):
    rows, cells = far_up.shape
    block = 256
    far = pl.BlockSpec((rows, block), lambda i: (0, i))
    whole = pl.BlockSpec((2 * rows, block), lambda i: (0, i))
    return pl.pallas_call(
        lift_kernel,
        grid=(cells // block,),
        in_specs=[whole, whole, far, far],
        out_specs=[whole, whole],
        out_shape=[jax.ShapeDtypeStruct(above.shape, F32)] * 2,
        compiler_params=vmem(8),
        cost_estimate=pl.CostEstimate(flops=10**10, bytes_accessed=0, transcendentals=0),
        name="lift",
    )(above, below, far_up, far_down)


def join_kernel(above, below, got_above, got_below, out_above, out_below):
    out_above[...] = above[...] + got_above[...]
    out_below[...] = below[...] + got_below[...]


def join_call(above, below, got_above, got_below):
    rows, cells = above.shape
    whole = pl.BlockSpec((rows, 256), lambda i: (0, i))
    return pl.pallas_call(
        join_kernel,
        grid=(cells // 256,),
        in_specs=[whole] * 4,
        out_specs=[whole] * 2,
        out_shape=[jax.ShapeDtypeStruct(above.shape, F32)] * 2,
        compiler_params=vmem(8),
        cost_estimate=NO_COST,
        name="join",
    )(above, below, got_above, got_below)


def map_kernel(expr, grad, masses, keep, spot, out, held, ready, *, scale):
    index = pl.program_id(0)
    quarter, block = held.shape[2:]
    count = held.shape[1]

    def fetch(at, k):
        columns = pl.ds(pl.multiple_of(at * block, block), block)
        return pltpu.make_async_copy(
            expr.at[pl.ds(k * quarter, quarter), columns], held.at[at & 1, k], ready.at[at & 1, k]
        )

    @pl.when(index == 0)
    def _():
        for k in range(count):
            fetch(index, k).start()

    @pl.when(index + 1 < pl.num_programs(0))
    def _():
        for k in range(count):
            fetch(index + 1, k).start()

    inner = spot[0:1, :]
    for k in range(count):
        fetch(index, k).wait()
        rows = slice(k * quarter, k * quarter + quarter)
        pair = grad[0, rows, :], grad[1, rows, :]
        inner = inner + product(split(held[index & 1, k]), pair, ((0,), (0,)))
    at = pl.multiple_of(index * block, block)
    expo = masses[0, pl.ds(at, block), :].astype(F32) + masses[1, pl.ds(at, block), :].astype(F32)
    for part in range(block // 128):
        rows = slice(part * 128, part * 128 + 128)
        weight = as_column(keep[pl.ds(index * (block // 128) + part, 1), :])
        out[rows, :] = (scale * expo[rows]) * (weight * inner[rows] - spot[1:2, :])


def map_call(expr, grad, masses, keep, spot, scale):
    genes, cells = expr.shape
    spots = masses.shape[2]
    block, count = 256, 4
    return pl.pallas_call(
        functools.partial(map_kernel, scale=scale),
        grid=(cells // block,),
        in_specs=[
            pl.BlockSpec(memory_space=pl.ANY),
            RESIDENT,
            RESIDENT,
            fixed(keep.shape),
            fixed((8, spots)),
        ],
        out_specs=pl.BlockSpec((block, spots), lambda i: (i, 0)),
        out_shape=jax.ShapeDtypeStruct((cells, spots), F32),
        scratch_shapes=[
            pltpu.VMEM((2, count, genes // count, block), F32),
            pltpu.SemaphoreType.DMA((2, count)),
        ],
        compiler_params=vmem(24),
        cost_estimate=NO_COST,
        name="grad_map",
    )(streamed(expr), grad, masses, keep, spot)


def finish_kernel(last, got1, got2, got3, totals, scalars, kind, filt, grad_filter, terms, *, all_cells):
    total = (last[...] + got2[...]) + (got1[...] + got3[...])
    nvalid, retained, reg_sum = (totals[2:3, k : k + 1] for k in range(3))
    valid = (kind[...] >= 0).astype(F32)
    sigma = jax.nn.sigmoid(filt[...])
    keep = sigma * valid
    shifted = (retained - 0.35 * nvalid) / (0.1 * all_cells)
    count_term = jnp.sqrt(shifted * shifted + 1.0)
    grad_keep = total[0:1, :] + shifted / count_term / (0.1 * all_cells) + (1.0 - 2.0 * keep) / nvalid
    row = valid * sigma * (1.0 - sigma) * grad_keep * all_cells
    for k in range(grad_filter.shape[0]):
        grad_filter[k : k + 1, :] = row[:, 128 * k : 128 * k + 128]
    lane = lax.broadcasted_iota(jnp.int32, (1, 128), 1)
    out = jnp.zeros((1, 128), F32)
    parts = (scalars[:, 0:1], total[1:2, 1:2], scalars[:, 2:3], count_term, reg_sum / nvalid)
    for index, one in enumerate(parts):
        out = jnp.where(lane == index, one, out)
    terms[...] = out


def finish_call(last, got, totals, scalars, kind, filt, all_cells):
    return pl.pallas_call(
        functools.partial(finish_kernel, all_cells=float(all_cells)),
        grid=(1,),
        in_specs=[fixed(one.shape) for one in (last, *got, totals, scalars, kind, filt)],
        out_specs=[fixed((kind.shape[1] // 128, 128)), fixed((1, 128))],
        out_shape=[
            jax.ShapeDtypeStruct((kind.shape[1] // 128, 128), F32),
            jax.ShapeDtypeStruct((1, 128), F32),
        ],
        compiler_params=vmem(4),
        cost_estimate=NO_COST,
        name="finish",
    )(last, *got, totals, scalars, kind, filt)


def on_device(map_logits, filter_logits, expr, spatial, cell_type, slide_id, spot_mask):
    genes, cells = expr.shape
    spots = map_logits.shape[1]
    all_cells = cells * lax.axis_size("cells")
    all_spots = spots * lax.axis_size("spots")
    cell_place = lax.axis_index("cells")
    z, x = cell_place >> 2, cell_place & 3
    spot_place = lax.axis_index("spots")
    y, core = spot_place >> 1, spot_place & 1
    first = jnp.where(core == 0, x, z)
    second = jnp.where(core == 0, z, x)
    blocks = cells // 128

    valid = (cell_type >= 0).astype(F32)
    sigma = jax.nn.sigmoid(filter_logits)
    keep = sigma * valid
    spot_valid = spot_mask.astype(F32)
    kind2 = cell_type.reshape(blocks, 128)
    filt2 = filter_logits.reshape(blocks, 128)
    keep2 = keep.reshape(blocks, 128)

    expr4 = expr.reshape(8, 16, 16, cells)
    keep_row = keep.reshape(1, cells)

    ids = jnp.stack([first, second, y, core]).astype(jnp.int32)

    def pred_part(one, two, more, *others):
        return pred_call(after(ids, *others), (one, two), expr4, keep_row, masses, totals, more)

    masses, types, totals, *far = expo_call(
        ids, ((2, 0), (2, 1)), map_logits, kind2, filt2, expr4
    )
    far_right, far_left = along(far[0], 1), along(far[1], -1)
    near = pred_part((1, 1), (-1, 0), (), *far)
    near_right, near_left = along(near[0], 1), along(near[1], -1)
    late = pred_part((1, 0), (-1, 1), (far_right, far_left), *near)
    late_right, late_left = along(late[0], 1), along(late[1], -1)
    own = pred_part((0, 0), (0, 1), (near_left, near_right), *late)
    mine, *pieces = merge_call(own, (late_right, late_left))
    pieces = [across(piece, step + 1) for step, piece in enumerate(pieces)]
    spatial_squares = jnp.sum(after(spatial, mine) ** 2, axis=0)
    types = types + swap_along(after(types, spatial_squares), 1)
    types = types + swap_along(types, 3)
    spot_rows = stacked([spot_valid, slide_id.astype(F32), spatial_squares])
    mine = after(mine, spot_rows, types)
    piece = mine + pieces[0] + pieces[1] + pieces[2]
    totals = piece[-1]
    piece = piece[:-1].reshape(8, 16, spots)
    share = 1.0 / totals[0]
    mass = totals[1] * share

    got = [across(piece, step) for step in (1, 2, 3)]
    sums, slides = stats_call(
        ids,
        piece,
        spatial.reshape(8, 16, 16, spots),
        spot_rows,
        totals,
    )
    sums = sums + swap_along(sums, 1)
    sums = sums + swap_along(sums, 3)
    mine = after((jnp.stack([piece, got[2]]), jnp.stack([got[1], got[0]])), sums)
    right0, left1 = along(mine[0], 1), along(mine[1], -1)
    right1, left0 = along(mine[1], 1), along(mine[0], -1)
    sums = sums + swap_across(after(sums, *mine), 1)
    sums = sums + swap_across(sums, 3)
    right0, left1, sums = lax.optimization_barrier((right0, left1, sums))
    far0, far1 = along(right0, 1), along(left1, -1)
    genes_slides = jnp.concatenate([sums[:48], slides])
    genes_slides = genes_slides + swap(genes_slides, 0, 0, 0, 1)
    genes_slides = genes_slides + swap(genes_slides, 0, 0, 1, 0)
    genes_slides = after(genes_slides, right1, left0)
    genes_slides = genes_slides + swap(genes_slides, 0, 0, 3, 0)
    pred = [*mine, right0, right1, left0, left1, far0, far1]
    gene_coef, spot_coef, scalars = coef_call(ids, genes_slides, sums, spot_rows, totals)
    spatial4 = spatial.reshape(8, RING, genes // 32, spots)
    grad, column_a = grad_call(ids, pred[:6], spatial4, gene_coef, spot_coef, 0, (0, 1, 2, 3))

    def last_grad(chips, grad, *others):
        return grad_call(
            after(ids, *others), pred[6:], spatial4, gene_coef, spot_coef, 12, chips, (grad,)
        )

    def back_part(steps, grad, *others, **rows):
        return back_call(after(ids, *others), steps, grad, masses, expr, **rows)

    rows = genes // 16
    grad, column_b = last_grad((2,), grad)
    sums_a, far_a = back_part([(2, 1)], grad, first=[spot_coef])
    far_got = swap(far_a, 0, 0, 0, 1)
    sums_b, far_b = back_part([(2, 0)], grad, far_a)
    far = far_b + far_got
    far_up, far_down = up(far[:rows], 1), up(far[rows:], -1)
    grad, column_c = last_grad((1, -1, 0), grad, far)
    sums_c, up_a, down_a, own_a, up_b, down_b = back_part(
        [(1, 1), (-1, 1), (0, 1), (1, 0), (-1, 0)], grad
    )
    up_got, down_got, own_got = (swap(one, 0, 0, 0, 1) for one in (up_a, down_a, own_a))
    above, below = lift_call(up_b, down_b, far_up, far_down)
    above, below = join_call(above, below, up_got, down_got)
    near_up, near_down = up(above, 1), up(below, -1)
    types_got = swap_across(after(types, above), 1)
    last, own_b = back_part(
        [(0, 0)], grad, above, below, own_got, last=[sums_a, sums_b, sums_c, scalars]
    )
    types = types + after(types_got, own_b)
    own = own_b + own_got

    column = jnp.sum(column_a + column_b + column_c, axis=0) * share + spot_coef[32] * mass
    map_rows = stacked([spot_coef[32], column])
    map_args = (expr, grad.reshape(2, genes, spots), masses, keep2, map_rows, all_cells * genes)
    types_got = swap_across(types, 3)
    last = last + swap(last, 0, 0, 0, 1)
    got = [up(last, step) for step in (1, 2, 3)]
    types = types + types_got
    grad_map = map_call(*after(map_args[:-1], last, types), map_args[-1])
    got = after(tuple(got), grad_map)
    grad_weighted = after(own, grad_map) + near_up + near_down
    grad_expr = grad_weighted * (keep * (genes * all_spots))[None, :]

    type_fraction = types * share

    grad_filter, loss_terms = finish_call(
        last, got, totals, scalars, cell_type.reshape(1, cells), filter_logits.reshape(1, cells), all_cells
    )
    return (loss_terms[0, :5], type_fraction, grad_map, grad_filter.reshape(cells), grad_expr)


def solution(mesh):
    in_specs = (
        P("cells", "spots"),
        P("cells"),
        P(None, "cells"),
        P(None, "spots"),
        P("cells"),
        P("spots"),
        P("spots"),
    )
    out_specs = (P(), P(None, "spots"), P("cells", "spots"), P("cells"), P("spots", "cells"))
    return jax.shard_map(
        on_device, mesh=mesh, in_specs=in_specs, out_specs=out_specs, check_vma=False
    )
```

```python
import functools

import jax
import jax.numpy as jnp
from jax import lax
from jax.experimental import pallas as pl
from jax.experimental.pallas import tpu as pltpu
from jax.sharding import PartitionSpec as P

TYPES = 32
SLIDES = 3
RING = 4
F32 = jnp.float32
BF16 = jnp.bfloat16


def vmem(mib):
    return pltpu.CompilerParams(vmem_limit_bytes=mib << 20)


def fixed(shape):
    return pl.BlockSpec(shape, lambda *_: (0,) * len(shape), pipeline_mode=pl.Buffered(1))


def streamed(array):
    return pltpu.with_memory_space_constraint(array, pltpu.HBM)


RESIDENT = pl.BlockSpec(memory_space=pltpu.VMEM)


def cost(flops, moved):
    return pl.CostEstimate(flops=int(flops) // 8, bytes_accessed=int(moved) // 8, transcendentals=0)


NO_COST = pl.CostEstimate(flops=0, bytes_accessed=0, transcendentals=0)


def route(target):
    def flat(z, x, y, core):
        return ((z % RING * RING + x % RING) * RING + y % RING) * 2 + core

    return [
        (flat(z, x, y, core), flat(*target(z, x, y, core)))
        for z in range(RING)
        for x in range(RING)
        for y in range(RING)
        for core in range(2)
    ]


def send(array, target):
    return lax.ppermute(array, ("cells", "spots"), route(target))


def along(array, step):
    return send(array, lambda z, x, y, c: (z, x + step, y, c) if c == 0 else (z + step, x, y, c))


def across(array, step):
    return send(array, lambda z, x, y, c: (z + step, x, y, c) if c == 0 else (z, x + step, y, c))


def up(array, step):
    return send(array, lambda z, x, y, c: (z, x, y + step, c))


def swap(array, mz, mx, my, mc):
    return send(array, lambda z, x, y, c: (z ^ mz, x ^ mx, y ^ my, c ^ mc))


def swap_along(array, mask):
    return send(array, lambda z, x, y, c: (z, x ^ mask, y, c) if c == 0 else (z ^ mask, x, y, c))


def swap_across(array, mask):
    return send(array, lambda z, x, y, c: (z ^ mask, x, y, c) if c == 0 else (z, x ^ mask, y, c))


def after(value, *others):
    return lax.optimization_barrier((value, *others))[0]


def split(value):
    high = value.astype(BF16)
    return high, (value - high.astype(F32)).astype(BF16)


def product(left, right, dims):
    def one(a, b):
        return lax.dot_general(a, b, (dims, ((), ())), preferred_element_type=F32)

    return one(left[0], right[0]) + one(left[0], right[1]) + one(left[1], right[0])


def gene_group(ids, step, half, sub):
    return ((ids[0] + step) & 3) * RING + ((ids[1] + 2 * half + sub) & 3)


PIECES = [
    (step, half, sub)
    for step, half in ((0, 0), (0, 1), (-1, 0), (-1, 1), (1, 0), (1, 1), (2, 0), (2, 1))
    for sub in range(2)
]


def pick(index, values):
    out = values[0]
    for k, value in enumerate(values[1:]):
        out = jnp.where(index == k + 1, value, out)
    return out


def stacked(rows):
    row = lax.broadcasted_iota(jnp.int32, (8, rows[0].shape[0]), 0)
    out = jnp.zeros(row.shape, F32)
    for k, value in enumerate(rows):
        out = jnp.where(row == k, value[None, :], out)
    return out


def as_column(row):
    return jnp.broadcast_to(row, (128, 128)).T[:, :1]


def expo_kernel(ids, logits, kind, filt, *refs):
    expr, (masses, types, totals, out0, out1) = refs[:4], refs[4:]
    step = pl.program_id(0)
    count = logits.shape[0] // 128

    @pl.when(step == 0)
    def _():
        for out in (types, totals, out0, out1):
            out[...] = jnp.zeros_like(out)

    keeps = []
    lane = lax.broadcasted_iota(jnp.int32, (1, totals.shape[1]), 1)
    cell_sums = jnp.zeros(lane.shape, F32)
    for part in range(count):
        rows = slice(part * 128, part * 128 + 128)
        label = kind[pl.ds(step * count + part, 1), :]
        valid = (label >= 0).astype(F32)
        keep = valid * jax.nn.sigmoid(filt[pl.ds(step * count + part, 1), :])
        keeps.append(keep)
        for k, one in enumerate((valid, keep, keep - keep * keep)):
            cell_sums += jnp.where(lane == k, jnp.sum(one, axis=1, keepdims=True), 0.0)
        expo = jnp.exp(logits[rows]) * as_column(valid)
        masses[0, rows], masses[1, rows] = split(expo)
        whole = jnp.sum(expo, axis=0, keepdims=True)
        kept = jnp.sum(expo * as_column(keep), axis=0, keepdims=True)
        row = lax.broadcasted_iota(jnp.int32, types.shape, 0)
        types[...] += jnp.where(row == jnp.max(label, axis=1, keepdims=True), whole, 0.0)
        row = lax.broadcasted_iota(jnp.int32, totals.shape, 0)
        totals[...] += jnp.where(row == 0, whole, jnp.where(row == 1, kept, 0.0))
    totals[2:3, :] += cell_sums
    weighted = jnp.concatenate([part[...].reshape(-1, logits.shape[0]) for part in expr])
    weighted = weighted * jnp.concatenate(keeps, axis=1)
    part = product(split(weighted), masses, ((1,), (0,)))
    half = part.shape[0] // 2
    for index, out in enumerate((out0, out1)):
        new = part[index * half : index * half + half].reshape(-1, 8, part.shape[1])
        out[: half // 8] += new
        out[half // 8] = totals[...]


def expo_call(ids, parts, logits, kind, filt, expr):
    cells, spots = logits.shape
    blocks, groups, rows, _ = expr.shape
    block = 256

    def genes(part, sub):
        return pl.BlockSpec(
            (blocks, 1, rows, block), lambda i, ids: (0, gene_group(ids, *part, sub), 0, i)
        )

    return pl.pallas_call(
        expo_kernel,
        grid_spec=pltpu.PrefetchScalarGridSpec(
            num_scalar_prefetch=1,
            grid=(cells // block,),
            in_specs=[
                pl.BlockSpec((block, spots), lambda i, w: (i, 0)),
                fixed(kind.shape),
                fixed(filt.shape),
            ]
            + [genes(part, sub) for part in parts for sub in range(2)],
            out_specs=[
                pl.BlockSpec((2, block, spots), lambda i, w: (0, i, 0)),
                fixed((TYPES, spots)),
                fixed((8, spots)),
                fixed((blocks * rows // 4 + 1, 8, spots)),
                fixed((blocks * rows // 4 + 1, 8, spots)),
            ],
        ),
        out_shape=[
            jax.ShapeDtypeStruct((2, cells, spots), BF16),
            jax.ShapeDtypeStruct((TYPES, spots), F32),
            jax.ShapeDtypeStruct((8, spots), F32),
            jax.ShapeDtypeStruct((blocks * rows // 4 + 1, 8, spots), F32),
            jax.ShapeDtypeStruct((blocks * rows // 4 + 1, 8, spots), F32),
        ],
        compiler_params=vmem(16),
        cost_estimate=cost(0, cells * spots * 8),
        name="expo",
    )(ids, streamed(logits), streamed(kind), streamed(filt), *[streamed(expr)] * 4)


def pred_kernel(ids, expr_a, expr_b, keep, masses, totals, *refs, cuts):
    more, outs = refs[:-2], refs[-2:]
    rows = 2 * expr_a.shape[0] * expr_a.shape[2]
    weighted = jnp.concatenate(
        [part[...].reshape(rows // 2, keep.shape[1]) for part in (expr_a, expr_b)]
    )
    weighted = split(weighted * keep[...])
    width = masses.shape[2] // cuts

    def half(index, _):
        columns = pl.ds(pl.multiple_of(index * width, width), width)
        part = product(weighted, (masses[0, :, columns], masses[1, :, columns]), ((1,), (0,)))
        part = part.reshape(rows // 8, 8, width)
        for step, out in enumerate(outs):

            @pl.when(pl.program_id(0) == step)
            def _(step=step, out=out):
                if more:
                    out[: rows // 8, :, columns] = part + more[step][: rows // 8, :, columns]
                    out[rows // 8, :, columns] = totals[:, columns] + more[step][rows // 8, :, columns]
                else:
                    out[: rows // 8, :, columns] = part
                    out[rows // 8, :, columns] = totals[:, columns]

        return 0

    lax.fori_loop(0, cuts, half, 0)


def pred_call(ids, parts, expr, keep, masses, totals, more, cuts):
    blocks, groups, rows, cells = expr.shape
    spots = masses.shape[2]
    tiles = blocks * rows // 4 + 1

    def genes(sub):
        def place(i, ids):
            step, half = (pick(i, [part[k] for part in parts]) for k in range(2))
            return (0, gene_group(ids, step, half, sub), 0, 0)

        return pl.BlockSpec((blocks, 1, rows, cells), place)

    return pl.pallas_call(
        functools.partial(pred_kernel, cuts=cuts),
        grid_spec=pltpu.PrefetchScalarGridSpec(
            num_scalar_prefetch=1,
            grid=(2,),
            in_specs=[
                genes(0),
                genes(1),
                fixed((1, cells)),
                RESIDENT,
                fixed((8, spots)),
            ]
            + [RESIDENT] * len(more),
            out_specs=[RESIDENT] * 2,
        ),
        out_shape=[jax.ShapeDtypeStruct((tiles, 8, spots), F32)] * 2,
        compiler_params=vmem(16),
        cost_estimate=cost(24 * blocks * rows * cells * spots, 4 * cells * spots + 16 * blocks * rows * (cells + spots)),
        name="pred",
    )(ids, *[streamed(expr)] * 2, keep, masses, totals, *more)


def merge_kernel(own0, own1, got0, got1, *outs):
    tiles = outs[0].shape[0] - 1
    for half, (own, got) in enumerate(((own0, got0), (own1, got1))):
        for sub in range(2):
            out = outs[2 * half + sub]
            out[:tiles] = own[sub * tiles : sub * tiles + tiles] + got[sub * tiles : sub * tiles + tiles]
            out[tiles] = own[2 * tiles] + got[2 * tiles]


def merge_call(own, got):
    tiles, _, spots = own[0].shape
    block = 256
    whole = pl.BlockSpec((tiles, 8, block), lambda i: (0, 0, i))
    piece = (tiles // 2 + 1, 8, spots)
    return pl.pallas_call(
        merge_kernel,
        grid=(spots // block,),
        in_specs=[whole] * 4,
        out_specs=[pl.BlockSpec((tiles // 2 + 1, 8, block), lambda i: (0, 0, i))] * 4,
        out_shape=[jax.ShapeDtypeStruct(piece, F32)] * 4,
        compiler_params=vmem(12),
        cost_estimate=NO_COST,
        name="merge",
    )(*own, *got)


def stats_kernel(ids, piece, spatial, spot, totals, gene, slide_sums):
    rows = piece.shape[0] * piece.shape[1]
    valid, slide = spot[0:1, :], spot[1:2, :]
    share = 1.0 / totals[0:1, :]
    mass = totals[1:2, :] * share
    value = piece[...].reshape(rows, piece.shape[2]) * share
    data = spatial[...].reshape(value.shape)
    cross, square = value * data, value * value
    lane = lax.broadcasted_iota(jnp.int32, (rows, 128), 1)
    sums = jnp.zeros((rows, 128), F32)
    for index, one in enumerate((cross, square, data * data)):
        sums = jnp.where(lane == index, jnp.sum(one * valid, axis=1, keepdims=True), sums)
    sums = sums.T
    gene[...] = jnp.zeros_like(gene)
    slide_sums[...] = jnp.zeros_like(slide_sums)
    for index in range(3):
        gene[pl.ds(16 * index + gene_group(ids, 0, 0, 0), 1), :] = sums[index : index + 1, :]
    lane = lax.broadcasted_iota(jnp.int32, (1, 128), 1)
    slides = jnp.zeros((1, 128), F32)
    logs = jnp.log(jnp.where(valid > 0, mass, 1.0))
    for k in range(SLIDES):
        inside = jnp.where(slide == k, valid, 0.0)
        for index, one in enumerate((inside, inside * mass, inside * logs)):
            total = jnp.sum(one, axis=1, keepdims=True)
            slides = jnp.where(lane == 3 * index + k, total, slides)
    slide_sums[0:1, :] = slides
    for index, one in enumerate((cross, square)):
        total = jnp.sum(one, axis=0, keepdims=True)
        for k in range(total.shape[1] // 128):
            at = 48 + 8 * index + k
            gene[at : at + 1, :] = total[:, 128 * k : 128 * k + 128]


def stats_call(ids, piece, spatial, spot, totals):
    blocks, rows, spots = piece.shape
    return pl.pallas_call(
        stats_kernel,
        grid_spec=pltpu.PrefetchScalarGridSpec(
            num_scalar_prefetch=1,
            grid=(1,),
            in_specs=[
                fixed((blocks, rows, spots)),
                pl.BlockSpec((blocks, 1, rows, spots), lambda i, ids: (0, gene_group(ids, 0, 0, 0), 0, 0)),
                fixed((8, spots)),
                fixed((8, spots)),
            ],
            out_specs=[fixed((64, 128)), fixed((8, 128))],
        ),
        out_shape=[jax.ShapeDtypeStruct((64, 128), F32), jax.ShapeDtypeStruct((8, 128), F32)],
        compiler_params=vmem(8),
        cost_estimate=NO_COST,
        name="stats",
    )(ids, piece, streamed(spatial), spot, totals)


def coef_kernel(ids, genes_slides, sums, spot, totals, gene, rows, scalars, pairs):
    valid, slide, squares = (spot[k : k + 1, :] for k in range(3))
    share = 1.0 / totals[0:1, :]
    mass = totals[1:2, :] * share
    genes = float(16 * sums.shape[1])

    def wide(index):
        return jnp.concatenate([sums[index + k : index + k + 1, :] for k in range(8)], axis=1)

    dots, own = wide(48), wide(56)
    dot, aa, bb = genes_slides[0:16, :], genes_slides[16:32, :], genes_slides[32:48, :]
    scale = lax.rsqrt(aa * bb + 1e-06)
    pairs[0:16, :] = dot * scale**3 * bb / genes
    pairs[16:32, :] = scale / genes
    pair = [pairs[pl.ds(k + gene_group(ids, *one), 1), :] for k in (0, 16) for one in PIECES]
    gene[...] = jnp.concatenate([*pair, jnp.zeros((96, 128), F32)]).T
    total = jnp.sum(jnp.sum(dot * scale, axis=1, keepdims=True), axis=0, keepdims=True)
    nvs = jnp.zeros((1, 1), F32)
    density = jnp.zeros((1, 1), F32)
    nk, tk = jnp.ones_like(valid), jnp.ones_like(valid)
    for k in range(SLIDES):
        count, held, logs = (genes_slides[48:49, 3 * j + k : 3 * j + k + 1] for j in range(3))
        some = count > 0
        safe = jnp.where(some, count, 1.0)
        nvs += count
        density += jnp.where(some, jnp.log(jnp.where(some, held, 1.0) / safe) - logs / safe, 0.0)
        here = (slide == k) & (valid > 0)
        nk = jnp.where(here, count, nk)
        tk = jnp.where(here, held, tk)
    scale = lax.rsqrt(own * squares + 1e-06)
    grad_mass = valid / SLIDES * (1.0 / tk - 1.0 / (nk * jnp.where(valid > 0, mass, 1.0)))
    mask = valid * share
    by_pred, by_data = dots * scale**3 * squares / nvs, scale / nvs
    for index, one in enumerate((by_pred * share * mask, by_data * mask, mask, share * mask)):
        rows[8 * index : 8 * index + 8, :] = jnp.broadcast_to(one, (8, one.shape[1]))
    rows[32:40, :] = jnp.concatenate([grad_mass * share, jnp.zeros((7, valid.shape[1]), F32)])
    cosines = jnp.sum(valid * dots * scale, axis=1, keepdims=True)
    lane = lax.broadcasted_iota(jnp.int32, (1, 128), 1)
    out = jnp.zeros((1, 128), F32)
    for index, one in enumerate((total / genes, cosines / nvs, density / SLIDES)):
        out = jnp.where(lane == index, one, out)
    scalars[...] = out


def coef_call(ids, genes_slides, sums, spot, totals):
    spots = spot.shape[1]
    return pl.pallas_call(
        coef_kernel,
        grid_spec=pltpu.PrefetchScalarGridSpec(
            num_scalar_prefetch=1,
            grid=(1,),
            in_specs=[fixed(genes_slides.shape), fixed(sums.shape), fixed((8, spots)), fixed((8, spots))],
            out_specs=[fixed((128, 128)), fixed((40, spots)), fixed((1, 128))],
            scratch_shapes=[pltpu.VMEM((32, 128), F32)],
        ),
        out_shape=[
            jax.ShapeDtypeStruct((128, 128), F32),
            jax.ShapeDtypeStruct((40, spots), F32),
            jax.ShapeDtypeStruct((1, 128), F32),
        ],
        compiler_params=vmem(6),
        cost_estimate=NO_COST,
        name="coef",
    )(ids, genes_slides, sums, spot, totals)


def grad_rows(pred, data, gene, spot, lane):
    by_pred = gene[:, lane : lane + 1].reshape(2, 8, 1)
    by_data = gene[:, 16 + lane : 17 + lane].reshape(2, 8, 1)
    pred, data = pred.reshape(2, 8, pred.shape[1]), data.reshape(2, 8, data.shape[1])
    grad = pred * (by_pred * spot[24:32, :] + spot[0:8, :])
    grad = grad - data * (by_data * spot[16:24, :] + spot[8:16, :])
    return grad.reshape(16, grad.shape[2]), jnp.sum(grad * pred, axis=0)


def grad_kernel(ids, *refs, count, lane, chips):
    pred, data, refs = refs[: 2 * count], refs[2 * count : 3 * count], refs[3 * count :]
    gene, spot, grad, column = refs[0], refs[1], refs[-2], refs[-1]
    step = pl.program_id(0)
    chip = (ids[2] + pick(step, chips)) & 3

    @pl.when(step == 0)
    def _():
        column[...] = jnp.zeros_like(column)

    def half_of(half, _):
        block = chip * 2 + half
        factors = gene[pl.ds(pl.multiple_of(16 * half, 16), 16), :]
        total = jnp.zeros(column.shape, F32)
        for index, part in enumerate(pred):
            for sub in range(2):
                at = gene_group(ids, *PIECES[lane + 2 * index + sub])
                row = pl.multiple_of((at & 3) * 16, 16)
                to = pl.ds(pl.multiple_of(at * 16, 16), 16)
                rows, inner = grad_rows(
                    part[sub, block],
                    data[index // 2][half, 0, pl.ds(row, 16), :],
                    factors,
                    spot,
                    lane + 2 * index + sub,
                )
                grad[0, block, to, :], grad[1, block, to, :] = split(rows)
                total += inner
        column[...] += total
        return 0

    lax.fori_loop(0, 2, half_of, 0)


def grad_call(ids, pred, spatial, gene, spot, lane, chips, done=()):
    blocks, groups, rows, spots = spatial.shape
    count = len(pred) // 2

    def chip(i, ids):
        return (ids[2] + pick(i, chips)) & 3

    def group(k):
        step = PIECES[lane + 4 * k][0]
        return pl.BlockSpec(
            (2, 1, rows, spots), lambda i, ids: (chip(i, ids), (ids[0] + step) & 3, 0, 0)
        )

    return pl.pallas_call(
        functools.partial(grad_kernel, count=count, lane=lane, chips=chips),
        grid_spec=pltpu.PrefetchScalarGridSpec(
            num_scalar_prefetch=1,
            grid=(len(chips),),
            in_specs=[RESIDENT] * (2 * count)
            + [group(k) for k in range(count)]
            + [pl.BlockSpec((32, 128), lambda i, ids: (chip(i, ids), 0)), fixed(spot.shape)]
            + [RESIDENT] * len(done),
            out_specs=[RESIDENT, fixed((8, spots))],
        ),
        out_shape=[
            jax.ShapeDtypeStruct((2, blocks, groups * rows, spots), BF16),
            jax.ShapeDtypeStruct((8, spots), F32),
        ],
        input_output_aliases={3 * count + 3: 0} if done else {},
        compiler_params=vmem(12),
        cost_estimate=NO_COST,
        name="grad",
    )(ids, *pred, *[streamed(spatial)] * count, gene, spot, *done)


def back_kernel(ids, grad, masses, expr, *refs, parts, first, last):
    more, (sums, *outs), (held, ready) = refs[: first + 5 * last], refs[first + 5 * last : -2], refs[-2:]
    step = pl.program_id(0)
    rows = grad.shape[2]

    def block(part):
        return ((ids[2] + part[0]) & 3) * 2 + (ids[3] ^ part[1])

    def fetch(k):
        start = pl.multiple_of(block(parts[k]) * rows, rows)
        return pltpu.make_async_copy(expr.at[pl.ds(start, rows), :], held.at[k], ready.at[k])

    @pl.when(step == 0)
    def _():
        for k in range(len(parts)):
            fetch(k).start()

    @pl.when(step == 0)
    def _():
        if last:
            sums[...] = more[0][...] + more[1][...] + more[2][...] + more[3][...]
        else:
            sums[...] = jnp.zeros_like(sums)

    here = block([pick(step, [part[k] for part in parts]) for k in range(2)])
    left = grad[0, here], grad[1, here]
    if first:
        pair = split(jnp.concatenate([more[0][...], jnp.zeros_like(more[0])]))
        left = [jnp.concatenate(both) for both in zip(left, pair)]
    part = product(left, masses, ((1,), (1,)))
    if first:
        sums[...] = part[rows : rows + 8]
        part = part[:rows]
    for k, out in enumerate(outs):

        @pl.when(step == k)
        def _(k=k, out=out):
            out[...] = part
            fetch(k).wait()

    sums[...] += jnp.sum((part * held[step]).reshape(-1, 8, part.shape[1]), axis=0)
    if last:

        @pl.when(step == len(parts) - 1)
        def _():
            total = jnp.sum(sums[...], axis=0, keepdims=True)
            sums[...] = jnp.zeros_like(sums)
            sums[0:1, :] = total
            sums[1:2, 0:128] = more[4][...]


def back_call(ids, parts, grad, masses, expr, first=(), last=()):
    _, blocks, rows, spots = grad.shape
    cells = masses.shape[1]
    return pl.pallas_call(
        functools.partial(back_kernel, parts=parts, first=len(first), last=len(last) // 5),
        grid_spec=pltpu.PrefetchScalarGridSpec(
            num_scalar_prefetch=1,
            grid=(len(parts),),
            in_specs=[RESIDENT, RESIDENT, pl.BlockSpec(memory_space=pl.ANY)]
            + [pl.BlockSpec((8, spots), lambda i, ids: (4, 0))] * len(first)
            + [fixed(one.shape) for one in last],
            out_specs=[fixed((8, cells))] + [RESIDENT] * len(parts),
            scratch_shapes=[
                pltpu.VMEM((len(parts), rows, cells), F32),
                pltpu.SemaphoreType.DMA((len(parts),)),
            ],
        ),
        out_shape=[jax.ShapeDtypeStruct((8, cells), F32)]
        + [jax.ShapeDtypeStruct((rows, cells), F32)] * len(parts),
        compiler_params=vmem(22),
        cost_estimate=NO_COST,
        name="back",
    )(ids, grad, masses, streamed(expr), *first, *last)


def lift_kernel(above, below, far_up, far_down, out_above, out_below):
    rows = far_up.shape[0]
    out_above[:rows, :] = above[:rows, :] + far_up[...]
    out_above[rows:, :] = above[rows:, :]
    out_below[:rows, :] = below[:rows, :]
    out_below[rows:, :] = below[rows:, :] + far_down[...]


def lift_call(above, below, far_up, far_down):
    rows, cells = far_up.shape
    block = 256
    far = pl.BlockSpec((rows, block), lambda i: (0, i))
    whole = pl.BlockSpec((2 * rows, block), lambda i: (0, i))
    return pl.pallas_call(
        lift_kernel,
        grid=(cells // block,),
        in_specs=[whole, whole, far, far],
        out_specs=[whole, whole],
        out_shape=[jax.ShapeDtypeStruct(above.shape, F32)] * 2,
        compiler_params=vmem(8),
        cost_estimate=pl.CostEstimate(flops=10**10, bytes_accessed=0, transcendentals=0),
        name="lift",
    )(above, below, far_up, far_down)


def join_kernel(above, below, got_above, got_below, out_above, out_below):
    out_above[...] = above[...] + got_above[...]
    out_below[...] = below[...] + got_below[...]


def join_call(above, below, got_above, got_below):
    rows, cells = above.shape
    whole = pl.BlockSpec((rows, 256), lambda i: (0, i))
    return pl.pallas_call(
        join_kernel,
        grid=(cells // 256,),
        in_specs=[whole] * 4,
        out_specs=[whole] * 2,
        out_shape=[jax.ShapeDtypeStruct(above.shape, F32)] * 2,
        compiler_params=vmem(8),
        cost_estimate=NO_COST,
        name="join",
    )(above, below, got_above, got_below)


def map_kernel(expr, grad, masses, keep, spot, out, held, ready, *, scale):
    index = pl.program_id(0)
    quarter, block = held.shape[2:]
    count = held.shape[1]

    def fetch(at, k):
        columns = pl.ds(pl.multiple_of(at * block, block), block)
        return pltpu.make_async_copy(
            expr.at[pl.ds(k * quarter, quarter), columns], held.at[at & 1, k], ready.at[at & 1, k]
        )

    @pl.when(index == 0)
    def _():
        for k in range(count):
            fetch(index, k).start()

    @pl.when(index + 1 < pl.num_programs(0))
    def _():
        for k in range(count):
            fetch(index + 1, k).start()

    inner = spot[0:1, :]
    for k in range(count):
        fetch(index, k).wait()
        rows = slice(k * quarter, k * quarter + quarter)
        pair = grad[0, rows, :], grad[1, rows, :]
        inner = inner + product(split(held[index & 1, k]), pair, ((0,), (0,)))
    at = pl.multiple_of(index * block, block)
    expo = masses[0, pl.ds(at, block), :].astype(F32) + masses[1, pl.ds(at, block), :].astype(F32)
    for part in range(block // 128):
        rows = slice(part * 128, part * 128 + 128)
        weight = as_column(keep[pl.ds(index * (block // 128) + part, 1), :])
        out[rows, :] = (scale * expo[rows]) * (weight * inner[rows] - spot[1:2, :])


def map_call(expr, grad, masses, keep, spot, scale):
    genes, cells = expr.shape
    spots = masses.shape[2]
    block, count = 256, 4
    return pl.pallas_call(
        functools.partial(map_kernel, scale=scale),
        grid=(cells // block,),
        in_specs=[
            pl.BlockSpec(memory_space=pl.ANY),
            RESIDENT,
            RESIDENT,
            fixed(keep.shape),
            fixed((8, spots)),
        ],
        out_specs=pl.BlockSpec((block, spots), lambda i: (i, 0)),
        out_shape=jax.ShapeDtypeStruct((cells, spots), F32),
        scratch_shapes=[
            pltpu.VMEM((2, count, genes // count, block), F32),
            pltpu.SemaphoreType.DMA((2, count)),
        ],
        compiler_params=vmem(24),
        cost_estimate=NO_COST,
        name="grad_map",
    )(streamed(expr), grad, masses, keep, spot)


def finish_kernel(last, got1, got2, got3, totals, scalars, kind, filt, grad_filter, terms, *, all_cells):
    total = (last[...] + got2[...]) + (got1[...] + got3[...])
    nvalid, retained, reg_sum = (totals[2:3, k : k + 1] for k in range(3))
    valid = (kind[...] >= 0).astype(F32)
    sigma = jax.nn.sigmoid(filt[...])
    keep = sigma * valid
    shifted = (retained - 0.35 * nvalid) / (0.1 * all_cells)
    count_term = jnp.sqrt(shifted * shifted + 1.0)
    grad_keep = total[0:1, :] + shifted / count_term / (0.1 * all_cells) + (1.0 - 2.0 * keep) / nvalid
    row = valid * sigma * (1.0 - sigma) * grad_keep * all_cells
    for k in range(grad_filter.shape[0]):
        grad_filter[k : k + 1, :] = row[:, 128 * k : 128 * k + 128]
    lane = lax.broadcasted_iota(jnp.int32, (1, 128), 1)
    out = jnp.zeros((1, 128), F32)
    parts = (scalars[:, 0:1], total[1:2, 1:2], scalars[:, 2:3], count_term, reg_sum / nvalid)
    for index, one in enumerate(parts):
        out = jnp.where(lane == index, one, out)
    terms[...] = out


def finish_call(last, got, totals, scalars, kind, filt, all_cells):
    return pl.pallas_call(
        functools.partial(finish_kernel, all_cells=float(all_cells)),
        grid=(1,),
        in_specs=[fixed(one.shape) for one in (last, *got, totals, scalars, kind, filt)],
        out_specs=[fixed((kind.shape[1] // 128, 128)), fixed((1, 128))],
        out_shape=[
            jax.ShapeDtypeStruct((kind.shape[1] // 128, 128), F32),
            jax.ShapeDtypeStruct((1, 128), F32),
        ],
        compiler_params=vmem(4),
        cost_estimate=NO_COST,
        name="finish",
    )(last, *got, totals, scalars, kind, filt)


def on_device(map_logits, filter_logits, expr, spatial, cell_type, slide_id, spot_mask):
    genes, cells = expr.shape
    spots = map_logits.shape[1]
    all_cells = cells * lax.axis_size("cells")
    all_spots = spots * lax.axis_size("spots")
    cell_place = lax.axis_index("cells")
    z, x = cell_place >> 2, cell_place & 3
    spot_place = lax.axis_index("spots")
    y, core = spot_place >> 1, spot_place & 1
    first = jnp.where(core == 0, x, z)
    second = jnp.where(core == 0, z, x)
    blocks = cells // 128

    valid = (cell_type >= 0).astype(F32)
    sigma = jax.nn.sigmoid(filter_logits)
    keep = sigma * valid
    spot_valid = spot_mask.astype(F32)
    kind2 = cell_type.reshape(blocks, 128)
    filt2 = filter_logits.reshape(blocks, 128)
    keep2 = keep.reshape(blocks, 128)

    expr4 = expr.reshape(8, 16, 16, cells)
    keep_row = keep.reshape(1, cells)

    ids = jnp.stack([first, second, y, core]).astype(jnp.int32)

    def pred_part(one, two, more, cuts, *others):
        return pred_call(after(ids, *others), (one, two), expr4, keep_row, masses, totals, more, cuts)

    masses, types, totals, *far = expo_call(
        ids, ((2, 0), (2, 1)), map_logits, kind2, filt2, expr4
    )
    far_right, far_left = along(far[0], 1), along(far[1], -1)
    near = pred_part((1, 1), (-1, 0), (), 2, *far)
    near_right, near_left = along(near[0], 1), along(near[1], -1)
    late = pred_part((1, 0), (-1, 1), (far_right, far_left), 1, *near)
    late_right, late_left = along(late[0], 1), along(late[1], -1)
    own = pred_part((0, 0), (0, 1), (near_left, near_right), 2, *late)
    mine, *pieces = merge_call(own, (late_right, late_left))
    pieces = [across(piece, step + 1) for step, piece in enumerate(pieces)]
    spatial_squares = jnp.sum(after(spatial, mine) ** 2, axis=0)
    types = types + swap_along(after(types, spatial_squares), 1)
    types = types + swap_along(types, 3)
    spot_rows = stacked([spot_valid, slide_id.astype(F32), spatial_squares])
    mine = after(mine, spot_rows, types)
    piece = mine + pieces[0] + pieces[1] + pieces[2]
    totals = piece[-1]
    piece = piece[:-1].reshape(8, 16, spots)
    share = 1.0 / totals[0]
    mass = totals[1] * share

    got = [across(piece, step) for step in (1, 2, 3)]
    sums, slides = stats_call(
        ids,
        piece,
        spatial.reshape(8, 16, 16, spots),
        spot_rows,
        totals,
    )
    sums = sums + swap_along(sums, 1)
    sums = sums + swap_along(sums, 3)
    mine = after((jnp.stack([piece, got[2]]), jnp.stack([got[1], got[0]])), sums)
    right0, left1 = along(mine[0], 1), along(mine[1], -1)
    right1, left0 = along(mine[1], 1), along(mine[0], -1)
    sums = sums + swap_across(after(sums, *mine), 1)
    sums = sums + swap_across(sums, 3)
    right0, left1, sums = lax.optimization_barrier((right0, left1, sums))
    far0, far1 = along(right0, 1), along(left1, -1)
    genes_slides = jnp.concatenate([sums[:48], slides])
    genes_slides = genes_slides + swap(genes_slides, 0, 0, 0, 1)
    genes_slides = genes_slides + swap(genes_slides, 0, 0, 1, 0)
    genes_slides = after(genes_slides, right1, left0)
    genes_slides = genes_slides + swap(genes_slides, 0, 0, 3, 0)
    pred = [*mine, right0, right1, left0, left1, far0, far1]
    gene_coef, spot_coef, scalars = coef_call(ids, genes_slides, sums, spot_rows, totals)
    spatial4 = spatial.reshape(8, RING, genes // 32, spots)
    grad, column_a = grad_call(ids, pred[:6], spatial4, gene_coef, spot_coef, 0, (0, 1, 2, 3))

    def last_grad(chips, grad, *others):
        return grad_call(
            after(ids, *others), pred[6:], spatial4, gene_coef, spot_coef, 12, chips, (grad,)
        )

    def back_part(steps, grad, *others, **rows):
        return back_call(after(ids, *others), steps, grad, masses, expr, **rows)

    rows = genes // 16
    grad, column_b = last_grad((2,), grad)
    sums_a, far_a = back_part([(2, 1)], grad, first=[spot_coef])
    far_got = swap(far_a, 0, 0, 0, 1)
    sums_b, far_b = back_part([(2, 0)], grad, far_a)
    far = far_b + far_got
    far_up, far_down = up(far[:rows], 1), up(far[rows:], -1)
    grad, column_c = last_grad((1, -1, 0), grad, far)
    sums_c, up_a, down_a, own_a = back_part([(1, 1), (-1, 1), (0, 1)], grad)
    up_got, down_got, own_got = (swap(one, 0, 0, 0, 1) for one in (up_a, down_a, own_a))
    sums_d, up_b, down_b = back_part([(1, 0), (-1, 0)], grad, up_a)
    above, below = lift_call(up_b, down_b, far_up, far_down)
    types = types + swap_across(after(types, above), 1)
    above, below = join_call(above, below, up_got, down_got)
    near_up, near_down = up(above, 1), up(below, -1)
    types_got = swap_across(types, 3)
    last, own_b = back_part(
        [(0, 0)], grad, above, below, own_got, types, last=[sums_a, sums_b, sums_c, sums_d, scalars]
    )
    types = types + after(types_got, own_b)
    own = own_b + own_got

    column = jnp.sum(column_a + column_b + column_c, axis=0) * share + spot_coef[32] * mass
    map_rows = stacked([spot_coef[32], column])
    map_args = (expr, grad.reshape(2, genes, spots), masses, keep2, map_rows, all_cells * genes)
    last = last + swap(last, 0, 0, 0, 1)
    got = [up(last, step) for step in (1, 2, 3)]
    grad_map = map_call(*after(map_args[:-1], last, types), map_args[-1])
    got = after(tuple(got), grad_map)
    grad_weighted = after(own, grad_map) + near_up + near_down
    grad_expr = grad_weighted * (keep * (genes * all_spots))[None, :]

    type_fraction = types * share

    grad_filter, loss_terms = finish_call(
        last, got, totals, scalars, cell_type.reshape(1, cells), filter_logits.reshape(1, cells), all_cells
    )
    return (loss_terms[0, :5], type_fraction, grad_map, grad_filter.reshape(cells), grad_expr)


def solution(mesh):
    in_specs = (
        P("cells", "spots"),
        P("cells"),
        P(None, "cells"),
        P(None, "spots"),
        P("cells"),
        P("spots"),
        P("spots"),
    )
    out_specs = (P(), P(None, "spots"), P("cells", "spots"), P("cells"), P("spots", "cells"))
    return jax.shard_map(
        on_device, mesh=mesh, in_specs=in_specs, out_specs=out_specs, check_vma=False
    )
```

```python
import functools

import jax
import jax.numpy as jnp
from jax import lax
from jax.experimental import pallas as pl
from jax.experimental.pallas import tpu as pltpu
from jax.sharding import PartitionSpec as P

TYPES = 32
SLIDES = 3
RING = 4
F32 = jnp.float32
BF16 = jnp.bfloat16


def vmem(mib):
    return pltpu.CompilerParams(vmem_limit_bytes=mib << 20)


def fixed(shape):
    return pl.BlockSpec(shape, lambda *_: (0,) * len(shape), pipeline_mode=pl.Buffered(1))


def streamed(array):
    return pltpu.with_memory_space_constraint(array, pltpu.HBM)


RESIDENT = pl.BlockSpec(memory_space=pltpu.VMEM)


def cost(flops, moved):
    return pl.CostEstimate(flops=int(flops) // 8, bytes_accessed=int(moved) // 8, transcendentals=0)


NO_COST = pl.CostEstimate(flops=0, bytes_accessed=0, transcendentals=0)


def route(target):
    def flat(z, x, y, core):
        return ((z % RING * RING + x % RING) * RING + y % RING) * 2 + core

    return [
        (flat(z, x, y, core), flat(*target(z, x, y, core)))
        for z in range(RING)
        for x in range(RING)
        for y in range(RING)
        for core in range(2)
    ]


def send(array, target):
    return lax.ppermute(array, ("cells", "spots"), route(target))


def along(array, step):
    return send(array, lambda z, x, y, c: (z, x + step, y, c) if c == 0 else (z + step, x, y, c))


def across(array, step):
    return send(array, lambda z, x, y, c: (z + step, x, y, c) if c == 0 else (z, x + step, y, c))


def up(array, step):
    return send(array, lambda z, x, y, c: (z, x, y + step, c))


def swap(array, mz, mx, my, mc):
    return send(array, lambda z, x, y, c: (z ^ mz, x ^ mx, y ^ my, c ^ mc))


def swap_along(array, mask):
    return send(array, lambda z, x, y, c: (z, x ^ mask, y, c) if c == 0 else (z ^ mask, x, y, c))


def swap_across(array, mask):
    return send(array, lambda z, x, y, c: (z ^ mask, x, y, c) if c == 0 else (z, x ^ mask, y, c))


def after(value, *others):
    return lax.optimization_barrier((value, *others))[0]


def split(value):
    high = value.astype(BF16)
    return high, (value - high.astype(F32)).astype(BF16)


def product(left, right, dims):
    def one(a, b):
        return lax.dot_general(a, b, (dims, ((), ())), preferred_element_type=F32)

    return one(left[0], right[0]) + one(left[0], right[1]) + one(left[1], right[0])


def gene_group(ids, step, half, sub):
    return ((ids[0] + step) & 3) * RING + ((ids[1] + 2 * half + sub) & 3)


PIECES = [
    (step, half, sub)
    for step, half in ((0, 0), (0, 1), (-1, 0), (-1, 1), (1, 0), (1, 1), (2, 0), (2, 1))
    for sub in range(2)
]


def pick(index, values):
    out = values[0]
    for k, value in enumerate(values[1:]):
        out = jnp.where(index == k + 1, value, out)
    return out


def stacked(rows):
    row = lax.broadcasted_iota(jnp.int32, (8, rows[0].shape[0]), 0)
    out = jnp.zeros(row.shape, F32)
    for k, value in enumerate(rows):
        out = jnp.where(row == k, value[None, :], out)
    return out


def as_column(row):
    return jnp.broadcast_to(row, (128, 128)).T[:, :1]


def expo_kernel(ids, logits, kind, filt, *refs):
    expr, (masses, types, totals, out0, out1) = refs[:4], refs[4:]
    step = pl.program_id(0)
    count = logits.shape[0] // 128

    @pl.when(step == 0)
    def _():
        for out in (types, totals, out0, out1):
            out[...] = jnp.zeros_like(out)

    keeps = []
    lane = lax.broadcasted_iota(jnp.int32, (1, totals.shape[1]), 1)
    cell_sums = jnp.zeros(lane.shape, F32)
    for part in range(count):
        rows = slice(part * 128, part * 128 + 128)
        label = kind[pl.ds(step * count + part, 1), :]
        valid = (label >= 0).astype(F32)
        keep = valid * jax.nn.sigmoid(filt[pl.ds(step * count + part, 1), :])
        keeps.append(keep)
        for k, one in enumerate((valid, keep, keep - keep * keep)):
            cell_sums += jnp.where(lane == k, jnp.sum(one, axis=1, keepdims=True), 0.0)
        expo = jnp.exp(logits[rows]) * as_column(valid)
        masses[0, rows], masses[1, rows] = split(expo)
        whole = jnp.sum(expo, axis=0, keepdims=True)
        kept = jnp.sum(expo * as_column(keep), axis=0, keepdims=True)
        row = lax.broadcasted_iota(jnp.int32, types.shape, 0)
        types[...] += jnp.where(row == jnp.max(label, axis=1, keepdims=True), whole, 0.0)
        row = lax.broadcasted_iota(jnp.int32, totals.shape, 0)
        totals[...] += jnp.where(row == 0, whole, jnp.where(row == 1, kept, 0.0))
    totals[2:3, :] += cell_sums
    weighted = jnp.concatenate([part[...].reshape(-1, logits.shape[0]) for part in expr])
    weighted = weighted * jnp.concatenate(keeps, axis=1)
    part = product(split(weighted), masses, ((1,), (0,)))
    half = part.shape[0] // 2
    for index, out in enumerate((out0, out1)):
        new = part[index * half : index * half + half].reshape(-1, 8, part.shape[1])
        out[: half // 8] += new
        out[half // 8] = totals[...]


def expo_call(ids, parts, logits, kind, filt, expr):
    cells, spots = logits.shape
    blocks, groups, rows, _ = expr.shape
    block = 256

    def genes(part, sub):
        return pl.BlockSpec(
            (blocks, 1, rows, block), lambda i, ids: (0, gene_group(ids, *part, sub), 0, i)
        )

    return pl.pallas_call(
        expo_kernel,
        grid_spec=pltpu.PrefetchScalarGridSpec(
            num_scalar_prefetch=1,
            grid=(cells // block,),
            in_specs=[
                pl.BlockSpec((block, spots), lambda i, w: (i, 0)),
                fixed(kind.shape),
                fixed(filt.shape),
            ]
            + [genes(part, sub) for part in parts for sub in range(2)],
            out_specs=[
                pl.BlockSpec((2, block, spots), lambda i, w: (0, i, 0)),
                fixed((TYPES, spots)),
                fixed((8, spots)),
                fixed((blocks * rows // 4 + 1, 8, spots)),
                fixed((blocks * rows // 4 + 1, 8, spots)),
            ],
        ),
        out_shape=[
            jax.ShapeDtypeStruct((2, cells, spots), BF16),
            jax.ShapeDtypeStruct((TYPES, spots), F32),
            jax.ShapeDtypeStruct((8, spots), F32),
            jax.ShapeDtypeStruct((blocks * rows // 4 + 1, 8, spots), F32),
            jax.ShapeDtypeStruct((blocks * rows // 4 + 1, 8, spots), F32),
        ],
        compiler_params=vmem(16),
        cost_estimate=cost(0, cells * spots * 8),
        name="expo",
    )(ids, streamed(logits), streamed(kind), streamed(filt), *[streamed(expr)] * 4)


def pred_kernel(ids, expr_a, expr_b, keep, masses, totals, *refs, cuts):
    more, outs = refs[:-2], refs[-2:]
    rows = 2 * expr_a.shape[0] * expr_a.shape[2]
    weighted = jnp.concatenate(
        [part[...].reshape(rows // 2, keep.shape[1]) for part in (expr_a, expr_b)]
    )
    weighted = split(weighted * keep[...])
    width = masses.shape[2] // cuts

    def half(index, _):
        columns = pl.ds(pl.multiple_of(index * width, width), width)
        part = product(weighted, (masses[0, :, columns], masses[1, :, columns]), ((1,), (0,)))
        part = part.reshape(rows // 8, 8, width)
        for step, out in enumerate(outs):

            @pl.when(pl.program_id(0) == step)
            def _(step=step, out=out):
                if more:
                    out[: rows // 8, :, columns] = part + more[step][: rows // 8, :, columns]
                    out[rows // 8, :, columns] = totals[:, columns] + more[step][rows // 8, :, columns]
                else:
                    out[: rows // 8, :, columns] = part
                    out[rows // 8, :, columns] = totals[:, columns]

        return 0

    lax.fori_loop(0, cuts, half, 0)


def pred_call(ids, parts, expr, keep, masses, totals, more, cuts):
    blocks, groups, rows, cells = expr.shape
    spots = masses.shape[2]
    tiles = blocks * rows // 4 + 1

    def genes(sub):
        def place(i, ids):
            step, half = (pick(i, [part[k] for part in parts]) for k in range(2))
            return (0, gene_group(ids, step, half, sub), 0, 0)

        return pl.BlockSpec((blocks, 1, rows, cells), place)

    return pl.pallas_call(
        functools.partial(pred_kernel, cuts=cuts),
        grid_spec=pltpu.PrefetchScalarGridSpec(
            num_scalar_prefetch=1,
            grid=(2,),
            in_specs=[
                genes(0),
                genes(1),
                fixed((1, cells)),
                RESIDENT,
                fixed((8, spots)),
            ]
            + [RESIDENT] * len(more),
            out_specs=[RESIDENT] * 2,
        ),
        out_shape=[jax.ShapeDtypeStruct((tiles, 8, spots), F32)] * 2,
        compiler_params=vmem(16),
        cost_estimate=cost(24 * blocks * rows * cells * spots, 4 * cells * spots + 16 * blocks * rows * (cells + spots)),
        name="pred",
    )(ids, *[streamed(expr)] * 2, keep, masses, totals, *more)


def merge_kernel(own0, own1, got0, got1, *outs):
    tiles = outs[0].shape[0] - 1
    for half, (own, got) in enumerate(((own0, got0), (own1, got1))):
        for sub in range(2):
            out = outs[2 * half + sub]
            out[:tiles] = own[sub * tiles : sub * tiles + tiles] + got[sub * tiles : sub * tiles + tiles]
            out[tiles] = own[2 * tiles] + got[2 * tiles]


def merge_call(own, got):
    tiles, _, spots = own[0].shape
    block = 256
    whole = pl.BlockSpec((tiles, 8, block), lambda i: (0, 0, i))
    piece = (tiles // 2 + 1, 8, spots)
    return pl.pallas_call(
        merge_kernel,
        grid=(spots // block,),
        in_specs=[whole] * 4,
        out_specs=[pl.BlockSpec((tiles // 2 + 1, 8, block), lambda i: (0, 0, i))] * 4,
        out_shape=[jax.ShapeDtypeStruct(piece, F32)] * 4,
        compiler_params=vmem(12),
        cost_estimate=NO_COST,
        name="merge",
    )(*own, *got)


def stats_kernel(ids, piece, spatial, spot, totals, gene, slide_sums):
    rows = piece.shape[0] * piece.shape[1]
    valid, slide = spot[0:1, :], spot[1:2, :]
    share = 1.0 / totals[0:1, :]
    mass = totals[1:2, :] * share
    value = piece[...].reshape(rows, piece.shape[2]) * share
    data = spatial[...].reshape(value.shape)
    cross, square = value * data, value * value
    lane = lax.broadcasted_iota(jnp.int32, (rows, 128), 1)
    sums = jnp.zeros((rows, 128), F32)
    for index, one in enumerate((cross, square, data * data)):
        sums = jnp.where(lane == index, jnp.sum(one * valid, axis=1, keepdims=True), sums)
    sums = sums.T
    gene[...] = jnp.zeros_like(gene)
    slide_sums[...] = jnp.zeros_like(slide_sums)
    for index in range(3):
        gene[pl.ds(16 * index + gene_group(ids, 0, 0, 0), 1), :] = sums[index : index + 1, :]
    lane = lax.broadcasted_iota(jnp.int32, (1, 128), 1)
    slides = jnp.zeros((1, 128), F32)
    logs = jnp.log(jnp.where(valid > 0, mass, 1.0))
    for k in range(SLIDES):
        inside = jnp.where(slide == k, valid, 0.0)
        for index, one in enumerate((inside, inside * mass, inside * logs)):
            total = jnp.sum(one, axis=1, keepdims=True)
            slides = jnp.where(lane == 3 * index + k, total, slides)
    slide_sums[0:1, :] = slides
    for index, one in enumerate((cross, square)):
        total = jnp.sum(one, axis=0, keepdims=True)
        for k in range(total.shape[1] // 128):
            at = 48 + 8 * index + k
            gene[at : at + 1, :] = total[:, 128 * k : 128 * k + 128]


def stats_call(ids, piece, spatial, spot, totals):
    blocks, rows, spots = piece.shape
    return pl.pallas_call(
        stats_kernel,
        grid_spec=pltpu.PrefetchScalarGridSpec(
            num_scalar_prefetch=1,
            grid=(1,),
            in_specs=[
                fixed((blocks, rows, spots)),
                pl.BlockSpec((blocks, 1, rows, spots), lambda i, ids: (0, gene_group(ids, 0, 0, 0), 0, 0)),
                fixed((8, spots)),
                fixed((8, spots)),
            ],
            out_specs=[fixed((64, 128)), fixed((8, 128))],
        ),
        out_shape=[jax.ShapeDtypeStruct((64, 128), F32), jax.ShapeDtypeStruct((8, 128), F32)],
        compiler_params=vmem(8),
        cost_estimate=NO_COST,
        name="stats",
    )(ids, piece, spatial, spot, totals)


def coef_kernel(ids, genes_slides, sums, spot, totals, gene, rows, scalars, pairs):
    valid, slide, squares = (spot[k : k + 1, :] for k in range(3))
    share = 1.0 / totals[0:1, :]
    mass = totals[1:2, :] * share
    genes = float(16 * sums.shape[1])

    def wide(index):
        return jnp.concatenate([sums[index + k : index + k + 1, :] for k in range(8)], axis=1)

    dots, own = wide(48), wide(56)
    dot, aa, bb = genes_slides[0:16, :], genes_slides[16:32, :], genes_slides[32:48, :]
    scale = lax.rsqrt(aa * bb + 1e-06)
    pairs[0:16, :] = dot * scale**3 * bb / genes
    pairs[16:32, :] = scale / genes
    pair = [pairs[pl.ds(k + gene_group(ids, *one), 1), :] for k in (0, 16) for one in PIECES]
    gene[...] = jnp.concatenate([*pair, jnp.zeros((96, 128), F32)]).T
    total = jnp.sum(jnp.sum(dot * scale, axis=1, keepdims=True), axis=0, keepdims=True)
    nvs = jnp.zeros((1, 1), F32)
    density = jnp.zeros((1, 1), F32)
    nk, tk = jnp.ones_like(valid), jnp.ones_like(valid)
    for k in range(SLIDES):
        count, held, logs = (genes_slides[48:49, 3 * j + k : 3 * j + k + 1] for j in range(3))
        some = count > 0
        safe = jnp.where(some, count, 1.0)
        nvs += count
        density += jnp.where(some, jnp.log(jnp.where(some, held, 1.0) / safe) - logs / safe, 0.0)
        here = (slide == k) & (valid > 0)
        nk = jnp.where(here, count, nk)
        tk = jnp.where(here, held, tk)
    scale = lax.rsqrt(own * squares + 1e-06)
    grad_mass = valid / SLIDES * (1.0 / tk - 1.0 / (nk * jnp.where(valid > 0, mass, 1.0)))
    mask = valid * share
    by_pred, by_data = dots * scale**3 * squares / nvs, scale / nvs
    for index, one in enumerate((by_pred * share * mask, by_data * mask, mask, share * mask)):
        rows[8 * index : 8 * index + 8, :] = jnp.broadcast_to(one, (8, one.shape[1]))
    rows[32:40, :] = jnp.concatenate([grad_mass * share, jnp.zeros((7, valid.shape[1]), F32)])
    cosines = jnp.sum(valid * dots * scale, axis=1, keepdims=True)
    lane = lax.broadcasted_iota(jnp.int32, (1, 128), 1)
    out = jnp.zeros((1, 128), F32)
    for index, one in enumerate((total / genes, cosines / nvs, density / SLIDES)):
        out = jnp.where(lane == index, one, out)
    scalars[...] = out


def coef_call(ids, genes_slides, sums, spot, totals):
    spots = spot.shape[1]
    return pl.pallas_call(
        coef_kernel,
        grid_spec=pltpu.PrefetchScalarGridSpec(
            num_scalar_prefetch=1,
            grid=(1,),
            in_specs=[fixed(genes_slides.shape), fixed(sums.shape), fixed((8, spots)), fixed((8, spots))],
            out_specs=[fixed((128, 128)), fixed((40, spots)), fixed((1, 128))],
            scratch_shapes=[pltpu.VMEM((32, 128), F32)],
        ),
        out_shape=[
            jax.ShapeDtypeStruct((128, 128), F32),
            jax.ShapeDtypeStruct((40, spots), F32),
            jax.ShapeDtypeStruct((1, 128), F32),
        ],
        compiler_params=vmem(6),
        cost_estimate=NO_COST,
        name="coef",
    )(ids, genes_slides, sums, spot, totals)


def grad_rows(pred, data, gene, spot, lane):
    by_pred = gene[:, lane : lane + 1].reshape(2, 8, 1)
    by_data = gene[:, 16 + lane : 17 + lane].reshape(2, 8, 1)
    pred, data = pred.reshape(2, 8, pred.shape[1]), data.reshape(2, 8, data.shape[1])
    grad = pred * (by_pred * spot[24:32, :] + spot[0:8, :])
    grad = grad - data * (by_data * spot[16:24, :] + spot[8:16, :])
    return grad.reshape(16, grad.shape[2]), jnp.sum(grad * pred, axis=0)


def grad_kernel(ids, *refs, count, lane, chips):
    pred, data, refs = refs[: 2 * count], refs[2 * count : 3 * count], refs[3 * count :]
    gene, spot, grad, column = refs[0], refs[1], refs[-2], refs[-1]
    step = pl.program_id(0)
    chip = (ids[2] + pick(step, chips)) & 3

    @pl.when(step == 0)
    def _():
        column[...] = jnp.zeros_like(column)

    def half_of(half, _):
        block = chip * 2 + half
        factors = gene[pl.ds(pl.multiple_of(16 * half, 16), 16), :]
        total = jnp.zeros(column.shape, F32)
        for index, part in enumerate(pred):
            for sub in range(2):
                at = gene_group(ids, *PIECES[lane + 2 * index + sub])
                row = pl.multiple_of((at & 3) * 16, 16)
                to = pl.ds(pl.multiple_of(at * 16, 16), 16)
                rows, inner = grad_rows(
                    part[sub, block],
                    data[index // 2][half, 0, pl.ds(row, 16), :],
                    factors,
                    spot,
                    lane + 2 * index + sub,
                )
                grad[0, block, to, :], grad[1, block, to, :] = split(rows)
                total += inner
        column[...] += total
        return 0

    lax.fori_loop(0, 2, half_of, 0)


def grad_call(ids, pred, spatial, gene, spot, lane, chips, done=()):
    blocks, groups, rows, spots = spatial.shape
    count = len(pred) // 2

    def chip(i, ids):
        return (ids[2] + pick(i, chips)) & 3

    def group(k):
        step = PIECES[lane + 4 * k][0]
        return pl.BlockSpec(
            (2, 1, rows, spots), lambda i, ids: (chip(i, ids), (ids[0] + step) & 3, 0, 0)
        )

    return pl.pallas_call(
        functools.partial(grad_kernel, count=count, lane=lane, chips=chips),
        grid_spec=pltpu.PrefetchScalarGridSpec(
            num_scalar_prefetch=1,
            grid=(len(chips),),
            in_specs=[RESIDENT] * (2 * count)
            + [group(k) for k in range(count)]
            + [pl.BlockSpec((32, 128), lambda i, ids: (chip(i, ids), 0)), fixed(spot.shape)]
            + [RESIDENT] * len(done),
            out_specs=[RESIDENT, fixed((8, spots))],
        ),
        out_shape=[
            jax.ShapeDtypeStruct((2, blocks, groups * rows, spots), BF16),
            jax.ShapeDtypeStruct((8, spots), F32),
        ],
        input_output_aliases={3 * count + 3: 0} if done else {},
        compiler_params=vmem(12),
        cost_estimate=NO_COST,
        name="grad",
    )(ids, *pred, *[spatial] * count, gene, spot, *done)


def back_kernel(ids, grad, masses, expr, *refs, parts, first, last):
    more, (sums, *outs), (held, ready) = refs[: first + 4 * last], refs[first + 4 * last : -2], refs[-2:]
    step = pl.program_id(0)
    rows = grad.shape[2]

    def block(part):
        return ((ids[2] + part[0]) & 3) * 2 + (ids[3] ^ part[1])

    def fetch(k):
        start = pl.multiple_of(block(parts[k]) * rows, rows)
        return pltpu.make_async_copy(expr.at[pl.ds(start, rows), :], held.at[k], ready.at[k])

    @pl.when(step == 0)
    def _():
        for k in range(len(parts)):
            fetch(k).start()

    @pl.when(step == 0)
    def _():
        if last:
            sums[...] = more[0][...] + more[1][...] + more[2][...]
        else:
            sums[...] = jnp.zeros_like(sums)

    here = block([pick(step, [part[k] for part in parts]) for k in range(2)])
    left = grad[0, here], grad[1, here]
    if first:
        pair = split(jnp.concatenate([more[0][...], jnp.zeros_like(more[0])]))
        left = [jnp.concatenate(both) for both in zip(left, pair)]
    part = product(left, masses, ((1,), (1,)))
    if first:
        sums[...] = part[rows : rows + 8]
        part = part[:rows]
    for k, out in enumerate(outs):

        @pl.when(step == k)
        def _(k=k, out=out):
            out[...] = part
            fetch(k).wait()

    sums[...] += jnp.sum((part * held[step]).reshape(-1, 8, part.shape[1]), axis=0)
    if last:

        @pl.when(step == len(parts) - 1)
        def _():
            total = jnp.sum(sums[...], axis=0, keepdims=True)
            sums[...] = jnp.zeros_like(sums)
            sums[0:1, :] = total
            sums[1:2, 0:128] = more[3][...]


def back_call(ids, parts, grad, masses, expr, first=(), last=()):
    _, blocks, rows, spots = grad.shape
    cells = masses.shape[1]
    return pl.pallas_call(
        functools.partial(back_kernel, parts=parts, first=len(first), last=len(last) // 4),
        grid_spec=pltpu.PrefetchScalarGridSpec(
            num_scalar_prefetch=1,
            grid=(len(parts),),
            in_specs=[RESIDENT, RESIDENT, pl.BlockSpec(memory_space=pl.ANY)]
            + [pl.BlockSpec((8, spots), lambda i, ids: (4, 0))] * len(first)
            + [fixed(one.shape) for one in last],
            out_specs=[fixed((8, cells))] + [RESIDENT] * len(parts),
            scratch_shapes=[
                pltpu.VMEM((len(parts), rows, cells), F32),
                pltpu.SemaphoreType.DMA((len(parts),)),
            ],
        ),
        out_shape=[jax.ShapeDtypeStruct((8, cells), F32)]
        + [jax.ShapeDtypeStruct((rows, cells), F32)] * len(parts),
        compiler_params=vmem(22),
        cost_estimate=NO_COST,
        name="back",
    )(ids, grad, masses, streamed(expr), *first, *last)


def lift_kernel(above, below, far_up, far_down, out_above, out_below):
    rows = far_up.shape[0]
    out_above[:rows, :] = above[:rows, :] + far_up[...]
    out_above[rows:, :] = above[rows:, :]
    out_below[:rows, :] = below[:rows, :]
    out_below[rows:, :] = below[rows:, :] + far_down[...]


def lift_call(above, below, far_up, far_down):
    rows, cells = far_up.shape
    block = 256
    far = pl.BlockSpec((rows, block), lambda i: (0, i))
    whole = pl.BlockSpec((2 * rows, block), lambda i: (0, i))
    return pl.pallas_call(
        lift_kernel,
        grid=(cells // block,),
        in_specs=[whole, whole, far, far],
        out_specs=[whole, whole],
        out_shape=[jax.ShapeDtypeStruct(above.shape, F32)] * 2,
        compiler_params=vmem(8),
        cost_estimate=pl.CostEstimate(flops=10**10, bytes_accessed=0, transcendentals=0),
        name="lift",
    )(above, below, far_up, far_down)


def join_kernel(above, below, got_above, got_below, out_above, out_below):
    out_above[...] = above[...] + got_above[...]
    out_below[...] = below[...] + got_below[...]


def join_call(above, below, got_above, got_below):
    rows, cells = above.shape
    whole = pl.BlockSpec((rows, 256), lambda i: (0, i))
    return pl.pallas_call(
        join_kernel,
        grid=(cells // 256,),
        in_specs=[whole] * 4,
        out_specs=[whole] * 2,
        out_shape=[jax.ShapeDtypeStruct(above.shape, F32)] * 2,
        compiler_params=vmem(8),
        cost_estimate=NO_COST,
        name="join",
    )(above, below, got_above, got_below)


def map_kernel(expr, grad, masses, keep, spot, out, held, ready, *, scale):
    index = pl.program_id(0)
    quarter, block = held.shape[2:]
    count = held.shape[1]

    def fetch(at, k):
        columns = pl.ds(pl.multiple_of(at * block, block), block)
        return pltpu.make_async_copy(
            expr.at[pl.ds(k * quarter, quarter), columns], held.at[at & 1, k], ready.at[at & 1, k]
        )

    @pl.when(index == 0)
    def _():
        for k in range(count):
            fetch(index, k).start()

    @pl.when(index + 1 < pl.num_programs(0))
    def _():
        for k in range(count):
            fetch(index + 1, k).start()

    inner = spot[0:1, :]
    for k in range(count):
        fetch(index, k).wait()
        rows = slice(k * quarter, k * quarter + quarter)
        pair = grad[0, rows, :], grad[1, rows, :]
        inner = inner + product(split(held[index & 1, k]), pair, ((0,), (0,)))
    at = pl.multiple_of(index * block, block)
    expo = masses[0, pl.ds(at, block), :].astype(F32) + masses[1, pl.ds(at, block), :].astype(F32)
    for part in range(block // 128):
        rows = slice(part * 128, part * 128 + 128)
        weight = as_column(keep[pl.ds(index * (block // 128) + part, 1), :])
        out[rows, :] = (scale * expo[rows]) * (weight * inner[rows] - spot[1:2, :])


def map_call(expr, grad, masses, keep, spot, scale):
    genes, cells = expr.shape
    spots = masses.shape[2]
    block, count = 256, 4
    return pl.pallas_call(
        functools.partial(map_kernel, scale=scale),
        grid=(cells // block,),
        in_specs=[
            pl.BlockSpec(memory_space=pl.ANY),
            RESIDENT,
            RESIDENT,
            fixed(keep.shape),
            fixed((8, spots)),
        ],
        out_specs=pl.BlockSpec((block, spots), lambda i: (i, 0)),
        out_shape=jax.ShapeDtypeStruct((cells, spots), F32),
        scratch_shapes=[
            pltpu.VMEM((2, count, genes // count, block), F32),
            pltpu.SemaphoreType.DMA((2, count)),
        ],
        compiler_params=vmem(24),
        cost_estimate=NO_COST,
        name="grad_map",
    )(streamed(expr), grad, masses, keep, spot)


def finish_kernel(last, got1, got2, got3, totals, scalars, kind, filt, grad_filter, terms, *, all_cells):
    total = (last[...] + got2[...]) + (got1[...] + got3[...])
    nvalid, retained, reg_sum = (totals[2:3, k : k + 1] for k in range(3))
    valid = (kind[...] >= 0).astype(F32)
    sigma = jax.nn.sigmoid(filt[...])
    keep = sigma * valid
    shifted = (retained - 0.35 * nvalid) / (0.1 * all_cells)
    count_term = jnp.sqrt(shifted * shifted + 1.0)
    grad_keep = total[0:1, :] + shifted / count_term / (0.1 * all_cells) + (1.0 - 2.0 * keep) / nvalid
    row = valid * sigma * (1.0 - sigma) * grad_keep * all_cells
    for k in range(grad_filter.shape[0]):
        grad_filter[k : k + 1, :] = row[:, 128 * k : 128 * k + 128]
    lane = lax.broadcasted_iota(jnp.int32, (1, 128), 1)
    out = jnp.zeros((1, 128), F32)
    parts = (scalars[:, 0:1], total[1:2, 1:2], scalars[:, 2:3], count_term, reg_sum / nvalid)
    for index, one in enumerate(parts):
        out = jnp.where(lane == index, one, out)
    terms[...] = out


def finish_call(last, got, totals, scalars, kind, filt, all_cells):
    return pl.pallas_call(
        functools.partial(finish_kernel, all_cells=float(all_cells)),
        grid=(1,),
        in_specs=[fixed(one.shape) for one in (last, *got, totals, scalars, kind, filt)],
        out_specs=[fixed((kind.shape[1] // 128, 128)), fixed((1, 128))],
        out_shape=[
            jax.ShapeDtypeStruct((kind.shape[1] // 128, 128), F32),
            jax.ShapeDtypeStruct((1, 128), F32),
        ],
        compiler_params=vmem(4),
        cost_estimate=NO_COST,
        name="finish",
    )(last, *got, totals, scalars, kind, filt)


def on_device(map_logits, filter_logits, expr, spatial, cell_type, slide_id, spot_mask):
    genes, cells = expr.shape
    spots = map_logits.shape[1]
    all_cells = cells * lax.axis_size("cells")
    all_spots = spots * lax.axis_size("spots")
    cell_place = lax.axis_index("cells")
    z, x = cell_place >> 2, cell_place & 3
    spot_place = lax.axis_index("spots")
    y, core = spot_place >> 1, spot_place & 1
    first = jnp.where(core == 0, x, z)
    second = jnp.where(core == 0, z, x)
    blocks = cells // 128

    valid = (cell_type >= 0).astype(F32)
    sigma = jax.nn.sigmoid(filter_logits)
    keep = sigma * valid
    spot_valid = spot_mask.astype(F32)
    kind2 = cell_type.reshape(blocks, 128)
    filt2 = filter_logits.reshape(blocks, 128)
    keep2 = keep.reshape(blocks, 128)

    expr4 = expr.reshape(8, 16, 16, cells)
    keep_row = keep.reshape(1, cells)

    ids = jnp.stack([first, second, y, core]).astype(jnp.int32)

    def pred_part(one, two, more, cuts, *others):
        return pred_call(after(ids, *others), (one, two), expr4, keep_row, masses, totals, more, cuts)

    masses, types, totals, *far = expo_call(
        ids, ((2, 0), (2, 1)), map_logits, kind2, filt2, expr4
    )
    far_right, far_left = along(far[0], 1), along(far[1], -1)
    near = pred_part((1, 1), (-1, 0), (), 2, *far)
    near_right, near_left = along(near[0], 1), along(near[1], -1)
    late = pred_part((1, 0), (-1, 1), (far_right, far_left), 1, *near)
    late_right, late_left = along(late[0], 1), along(late[1], -1)
    own = pred_part((0, 0), (0, 1), (near_left, near_right), 2, *late)
    mine, *pieces = merge_call(own, (late_right, late_left))
    pieces = [across(piece, step + 1) for step, piece in enumerate(pieces)]
    spatial_squares = jnp.sum(after(spatial, mine) ** 2, axis=0)
    types = types + swap_along(after(types, spatial_squares), 1)
    types = types + swap_along(types, 3)
    spot_rows = stacked([spot_valid, slide_id.astype(F32), spatial_squares])
    mine = after(mine, spot_rows, types)
    piece = mine + pieces[0] + pieces[1] + pieces[2]
    totals = piece[-1]
    piece = piece[:-1].reshape(8, 16, spots)
    share = 1.0 / totals[0]
    mass = totals[1] * share

    got = [across(piece, step) for step in (1, 2, 3)]
    sums, slides = stats_call(
        ids,
        piece,
        spatial.reshape(8, 16, 16, spots),
        spot_rows,
        totals,
    )
    sums = sums + swap_along(sums, 1)
    sums = sums + swap_along(sums, 3)
    mine = after((jnp.stack([piece, got[2]]), jnp.stack([got[1], got[0]])), sums)
    right0, left1 = along(mine[0], 1), along(mine[1], -1)
    right1, left0 = along(mine[1], 1), along(mine[0], -1)
    sums = sums + swap_across(after(sums, *mine), 1)
    sums = sums + swap_across(sums, 3)
    right0, left1, sums = lax.optimization_barrier((right0, left1, sums))
    far0, far1 = along(right0, 1), along(left1, -1)
    genes_slides = jnp.concatenate([sums[:48], slides])
    genes_slides = genes_slides + swap(genes_slides, 0, 0, 0, 1)
    genes_slides = genes_slides + swap(genes_slides, 0, 0, 1, 0)
    genes_slides = after(genes_slides, right1, left0)
    genes_slides = genes_slides + swap(genes_slides, 0, 0, 3, 0)
    pred = [*mine, right0, right1, left0, left1, far0, far1]
    gene_coef, spot_coef, scalars = coef_call(ids, genes_slides, sums, spot_rows, totals)
    spatial4 = spatial.reshape(8, RING, genes // 32, spots)
    grad, column_a = grad_call(ids, pred[:6], spatial4, gene_coef, spot_coef, 0, (0, 1, 2, 3))

    def last_grad(chips, grad, *others):
        return grad_call(
            after(ids, *others), pred[6:], spatial4, gene_coef, spot_coef, 12, chips, (grad,)
        )

    def back_part(steps, grad, *others, **rows):
        return back_call(after(ids, *others), steps, grad, masses, expr, **rows)

    rows = genes // 16
    grad, column_b = last_grad((2,), grad)
    sums_a, far_a = back_part([(2, 1)], grad, first=[spot_coef])
    far_got = swap(far_a, 0, 0, 0, 1)
    sums_b, far_b = back_part([(2, 0)], grad, far_a)
    far = far_b + far_got
    far_up, far_down = up(far[:rows], 1), up(far[rows:], -1)
    grad, column_c = last_grad((1, -1, 0), grad, far)
    sums_c, up_a, down_a, own_a = back_part([(1, 1), (-1, 1), (0, 1)], grad)
    up_got, down_got, own_got = (swap(one, 0, 0, 0, 1) for one in (up_a, down_a, own_a))
    last, up_b, down_b, own_b = back_part(
        [(1, 0), (-1, 0), (0, 0)], grad, up_a, last=[sums_a, sums_b, sums_c, scalars]
    )
    last = last + swap(last, 0, 0, 0, 1)
    above, below = lift_call(up_b, down_b, far_up, far_down)
    above, below = join_call(above, below, up_got, down_got)
    near_up, near_down = up(above, 1), up(below, -1)
    types = types + swap_across(after(types, up_b), 1)
    types = types + swap_across(after(types, above), 3)
    own = own_b + own_got

    column = jnp.sum(column_a + column_b + column_c, axis=0) * share + spot_coef[32] * mass
    map_rows = stacked([spot_coef[32], column])
    map_args = (expr, grad.reshape(2, genes, spots), masses, keep2, map_rows, all_cells * genes)
    got = [up(last, step) for step in (1, 2, 3)]
    grad_map = map_call(*after(map_args[:-1], last, types), map_args[-1])
    got = after(tuple(got), grad_map)
    grad_weighted = after(own, grad_map) + near_up + near_down
    grad_expr = grad_weighted * (keep * (genes * all_spots))[None, :]

    type_fraction = types * share

    grad_filter, loss_terms = finish_call(
        last, got, totals, scalars, cell_type.reshape(1, cells), filter_logits.reshape(1, cells), all_cells
    )
    return (loss_terms[0, :5], type_fraction, grad_map, grad_filter.reshape(cells), grad_expr)


def solution(mesh):
    in_specs = (
        P("cells", "spots"),
        P("cells"),
        P(None, "cells"),
        P(None, "spots"),
        P("cells"),
        P("spots"),
        P("spots"),
    )
    out_specs = (P(), P(None, "spots"), P("cells", "spots"), P("cells"), P("spots", "cells"))
    return jax.shard_map(
        on_device, mesh=mesh, in_specs=in_specs, out_specs=out_specs, check_vma=False
    )
```

```python
import functools

import jax
import jax.numpy as jnp
from jax import lax
from jax.experimental import pallas as pl
from jax.experimental.pallas import tpu as pltpu
from jax.sharding import PartitionSpec as P

TYPES = 32
SLIDES = 3
RING = 4
F32 = jnp.float32
BF16 = jnp.bfloat16


def vmem(mib):
    return pltpu.CompilerParams(vmem_limit_bytes=mib << 20)


def fixed(shape):
    return pl.BlockSpec(shape, lambda *_: (0,) * len(shape), pipeline_mode=pl.Buffered(1))


def streamed(array):
    return pltpu.with_memory_space_constraint(array, pltpu.HBM)


RESIDENT = pl.BlockSpec(memory_space=pltpu.VMEM)


def cost(flops, moved):
    return pl.CostEstimate(flops=int(flops) // 8, bytes_accessed=int(moved) // 8, transcendentals=0)


NO_COST = pl.CostEstimate(flops=0, bytes_accessed=0, transcendentals=0)


def route(target):
    def flat(z, x, y, core):
        return ((z % RING * RING + x % RING) * RING + y % RING) * 2 + core

    return [
        (flat(z, x, y, core), flat(*target(z, x, y, core)))
        for z in range(RING)
        for x in range(RING)
        for y in range(RING)
        for core in range(2)
    ]


def send(array, target):
    return lax.ppermute(array, ("cells", "spots"), route(target))


def along(array, step):
    return send(array, lambda z, x, y, c: (z, x + step, y, c) if c == 0 else (z + step, x, y, c))


def across(array, step):
    return send(array, lambda z, x, y, c: (z + step, x, y, c) if c == 0 else (z, x + step, y, c))


def up(array, step):
    return send(array, lambda z, x, y, c: (z, x, y + step, c))


def swap(array, mz, mx, my, mc):
    return send(array, lambda z, x, y, c: (z ^ mz, x ^ mx, y ^ my, c ^ mc))


def swap_along(array, mask):
    return send(array, lambda z, x, y, c: (z, x ^ mask, y, c) if c == 0 else (z ^ mask, x, y, c))


def swap_across(array, mask):
    return send(array, lambda z, x, y, c: (z ^ mask, x, y, c) if c == 0 else (z, x ^ mask, y, c))


def after(value, *others):
    return lax.optimization_barrier((value, *others))[0]


def split(value):
    high = value.astype(BF16)
    return high, (value - high.astype(F32)).astype(BF16)


def product(left, right, dims):
    def one(a, b):
        return lax.dot_general(a, b, (dims, ((), ())), preferred_element_type=F32)

    return one(left[0], right[0]) + one(left[0], right[1]) + one(left[1], right[0])


def gene_group(ids, step, half, sub):
    return ((ids[0] + step) & 3) * RING + ((ids[1] + 2 * half + sub) & 3)


PIECES = [
    (step, half, sub)
    for step, half in ((0, 0), (0, 1), (-1, 0), (-1, 1), (1, 0), (1, 1), (2, 0), (2, 1))
    for sub in range(2)
]


def pick(index, values):
    out = values[0]
    for k, value in enumerate(values[1:]):
        out = jnp.where(index == k + 1, value, out)
    return out


def stacked(rows):
    row = lax.broadcasted_iota(jnp.int32, (8, rows[0].shape[0]), 0)
    out = jnp.zeros(row.shape, F32)
    for k, value in enumerate(rows):
        out = jnp.where(row == k, value[None, :], out)
    return out


def as_column(row):
    return jnp.broadcast_to(row, (128, 128)).T[:, :1]


def expo_kernel(ids, logits, kind, filt, *refs):
    expr, (masses, types, totals, out0, out1) = refs[:4], refs[4:]
    step = pl.program_id(0)
    count = logits.shape[0] // 128

    @pl.when(step == 0)
    def _():
        for out in (types, totals, out0, out1):
            out[...] = jnp.zeros_like(out)

    keeps = []
    lane = lax.broadcasted_iota(jnp.int32, (1, totals.shape[1]), 1)
    cell_sums = jnp.zeros(lane.shape, F32)
    for part in range(count):
        rows = slice(part * 128, part * 128 + 128)
        label = kind[pl.ds(step * count + part, 1), :]
        valid = (label >= 0).astype(F32)
        keep = valid * jax.nn.sigmoid(filt[pl.ds(step * count + part, 1), :])
        keeps.append(keep)
        for k, one in enumerate((valid, keep, keep - keep * keep)):
            cell_sums += jnp.where(lane == k, jnp.sum(one, axis=1, keepdims=True), 0.0)
        expo = jnp.exp(logits[rows]) * as_column(valid)
        masses[0, rows], masses[1, rows] = split(expo)
        whole = jnp.sum(expo, axis=0, keepdims=True)
        kept = jnp.sum(expo * as_column(keep), axis=0, keepdims=True)
        row = lax.broadcasted_iota(jnp.int32, types.shape, 0)
        types[...] += jnp.where(row == jnp.max(label, axis=1, keepdims=True), whole, 0.0)
        row = lax.broadcasted_iota(jnp.int32, totals.shape, 0)
        totals[...] += jnp.where(row == 0, whole, jnp.where(row == 1, kept, 0.0))
    totals[2:3, :] += cell_sums
    weighted = jnp.concatenate([part[...].reshape(-1, logits.shape[0]) for part in expr])
    weighted = weighted * jnp.concatenate(keeps, axis=1)
    part = product(split(weighted), masses, ((1,), (0,)))
    half = part.shape[0] // 2
    for index, out in enumerate((out0, out1)):
        new = part[index * half : index * half + half].reshape(-1, 8, part.shape[1])
        out[: half // 8] += new
        out[half // 8] = totals[...]


def expo_call(ids, parts, logits, kind, filt, expr):
    cells, spots = logits.shape
    blocks, groups, rows, _ = expr.shape
    block = 256

    def genes(part, sub):
        return pl.BlockSpec(
            (blocks, 1, rows, block), lambda i, ids: (0, gene_group(ids, *part, sub), 0, i)
        )

    return pl.pallas_call(
        expo_kernel,
        grid_spec=pltpu.PrefetchScalarGridSpec(
            num_scalar_prefetch=1,
            grid=(cells // block,),
            in_specs=[
                pl.BlockSpec((block, spots), lambda i, w: (i, 0)),
                fixed(kind.shape),
                fixed(filt.shape),
            ]
            + [genes(part, sub) for part in parts for sub in range(2)],
            out_specs=[
                pl.BlockSpec((2, block, spots), lambda i, w: (0, i, 0)),
                fixed((TYPES, spots)),
                fixed((8, spots)),
                fixed((blocks * rows // 4 + 1, 8, spots)),
                fixed((blocks * rows // 4 + 1, 8, spots)),
            ],
        ),
        out_shape=[
            jax.ShapeDtypeStruct((2, cells, spots), BF16),
            jax.ShapeDtypeStruct((TYPES, spots), F32),
            jax.ShapeDtypeStruct((8, spots), F32),
            jax.ShapeDtypeStruct((blocks * rows // 4 + 1, 8, spots), F32),
            jax.ShapeDtypeStruct((blocks * rows // 4 + 1, 8, spots), F32),
        ],
        compiler_params=vmem(16),
        cost_estimate=cost(0, cells * spots * 8),
        name="expo",
    )(ids, streamed(logits), streamed(kind), streamed(filt), *[streamed(expr)] * 4)


def pred_kernel(ids, expr_a, expr_b, keep, masses, totals, *refs, cuts):
    more, outs = refs[:-2], refs[-2:]
    rows = 2 * expr_a.shape[0] * expr_a.shape[2]
    weighted = jnp.concatenate(
        [part[...].reshape(rows // 2, keep.shape[1]) for part in (expr_a, expr_b)]
    )
    weighted = split(weighted * keep[...])
    width = masses.shape[2] // cuts

    def half(index, _):
        columns = pl.ds(pl.multiple_of(index * width, width), width)
        part = product(weighted, (masses[0, :, columns], masses[1, :, columns]), ((1,), (0,)))
        part = part.reshape(rows // 8, 8, width)
        for step, out in enumerate(outs):

            @pl.when(pl.program_id(0) == step)
            def _(step=step, out=out):
                if more:
                    out[: rows // 8, :, columns] = part + more[step][: rows // 8, :, columns]
                    out[rows // 8, :, columns] = totals[:, columns] + more[step][rows // 8, :, columns]
                else:
                    out[: rows // 8, :, columns] = part
                    out[rows // 8, :, columns] = totals[:, columns]

        return 0

    lax.fori_loop(0, cuts, half, 0)


def pred_call(ids, parts, expr, keep, masses, totals, more, cuts):
    blocks, groups, rows, cells = expr.shape
    spots = masses.shape[2]
    tiles = blocks * rows // 4 + 1

    def genes(sub):
        def place(i, ids):
            step, half = (pick(i, [part[k] for part in parts]) for k in range(2))
            return (0, gene_group(ids, step, half, sub), 0, 0)

        return pl.BlockSpec((blocks, 1, rows, cells), place)

    return pl.pallas_call(
        functools.partial(pred_kernel, cuts=cuts),
        grid_spec=pltpu.PrefetchScalarGridSpec(
            num_scalar_prefetch=1,
            grid=(2,),
            in_specs=[
                genes(0),
                genes(1),
                fixed((1, cells)),
                RESIDENT,
                fixed((8, spots)),
            ]
            + [RESIDENT] * len(more),
            out_specs=[RESIDENT] * 2,
        ),
        out_shape=[jax.ShapeDtypeStruct((tiles, 8, spots), F32)] * 2,
        compiler_params=vmem(16),
        cost_estimate=cost(24 * blocks * rows * cells * spots, 4 * cells * spots + 16 * blocks * rows * (cells + spots)),
        name="pred",
    )(ids, *[streamed(expr)] * 2, keep, masses, totals, *more)


def merge_kernel(own0, own1, got0, got1, *outs):
    tiles = outs[0].shape[0] - 1
    for half, (own, got) in enumerate(((own0, got0), (own1, got1))):
        for sub in range(2):
            out = outs[2 * half + sub]
            out[:tiles] = own[sub * tiles : sub * tiles + tiles] + got[sub * tiles : sub * tiles + tiles]
            out[tiles] = own[2 * tiles] + got[2 * tiles]


def merge_call(own, got):
    tiles, _, spots = own[0].shape
    block = 256
    whole = pl.BlockSpec((tiles, 8, block), lambda i: (0, 0, i))
    piece = (tiles // 2 + 1, 8, spots)
    return pl.pallas_call(
        merge_kernel,
        grid=(spots // block,),
        in_specs=[whole] * 4,
        out_specs=[pl.BlockSpec((tiles // 2 + 1, 8, block), lambda i: (0, 0, i))] * 4,
        out_shape=[jax.ShapeDtypeStruct(piece, F32)] * 4,
        compiler_params=vmem(12),
        cost_estimate=NO_COST,
        name="merge",
    )(*own, *got)


def stats_kernel(ids, piece, spatial, spot, totals, gene, slide_sums):
    rows = piece.shape[0] * piece.shape[1]
    valid, slide = spot[0:1, :], spot[1:2, :]
    share = 1.0 / totals[0:1, :]
    mass = totals[1:2, :] * share
    value = piece[...].reshape(rows, piece.shape[2]) * share
    data = spatial[...].reshape(value.shape)
    cross, square = value * data, value * value
    lane = lax.broadcasted_iota(jnp.int32, (rows, 128), 1)
    sums = jnp.zeros((rows, 128), F32)
    for index, one in enumerate((cross, square, data * data)):
        sums = jnp.where(lane == index, jnp.sum(one * valid, axis=1, keepdims=True), sums)
    sums = sums.T
    gene[...] = jnp.zeros_like(gene)
    slide_sums[...] = jnp.zeros_like(slide_sums)
    for index in range(3):
        gene[pl.ds(16 * index + gene_group(ids, 0, 0, 0), 1), :] = sums[index : index + 1, :]
    lane = lax.broadcasted_iota(jnp.int32, (1, 128), 1)
    slides = jnp.zeros((1, 128), F32)
    logs = jnp.log(jnp.where(valid > 0, mass, 1.0))
    for k in range(SLIDES):
        inside = jnp.where(slide == k, valid, 0.0)
        for index, one in enumerate((inside, inside * mass, inside * logs)):
            total = jnp.sum(one, axis=1, keepdims=True)
            slides = jnp.where(lane == 3 * index + k, total, slides)
    slide_sums[0:1, :] = slides
    for index, one in enumerate((cross, square)):
        total = jnp.sum(one, axis=0, keepdims=True)
        for k in range(total.shape[1] // 128):
            at = 48 + 8 * index + k
            gene[at : at + 1, :] = total[:, 128 * k : 128 * k + 128]


def stats_call(ids, piece, spatial, spot, totals):
    blocks, rows, spots = piece.shape
    return pl.pallas_call(
        stats_kernel,
        grid_spec=pltpu.PrefetchScalarGridSpec(
            num_scalar_prefetch=1,
            grid=(1,),
            in_specs=[
                fixed((blocks, rows, spots)),
                pl.BlockSpec((blocks, 1, rows, spots), lambda i, ids: (0, gene_group(ids, 0, 0, 0), 0, 0)),
                fixed((8, spots)),
                fixed((8, spots)),
            ],
            out_specs=[fixed((64, 128)), fixed((8, 128))],
        ),
        out_shape=[jax.ShapeDtypeStruct((64, 128), F32), jax.ShapeDtypeStruct((8, 128), F32)],
        compiler_params=vmem(8),
        cost_estimate=NO_COST,
        name="stats",
    )(ids, piece, spatial, spot, totals)


def coef_kernel(ids, genes_slides, sums, spot, totals, gene, rows, scalars, pairs):
    valid, slide, squares = (spot[k : k + 1, :] for k in range(3))
    share = 1.0 / totals[0:1, :]
    mass = totals[1:2, :] * share
    genes = float(16 * sums.shape[1])

    def wide(index):
        return jnp.concatenate([sums[index + k : index + k + 1, :] for k in range(8)], axis=1)

    dots, own = wide(48), wide(56)
    dot, aa, bb = genes_slides[0:16, :], genes_slides[16:32, :], genes_slides[32:48, :]
    scale = lax.rsqrt(aa * bb + 1e-06)
    pairs[0:16, :] = dot * scale**3 * bb / genes
    pairs[16:32, :] = scale / genes
    pair = [pairs[pl.ds(k + gene_group(ids, *one), 1), :] for k in (0, 16) for one in PIECES]
    gene[...] = jnp.concatenate([*pair, jnp.zeros((96, 128), F32)]).T
    total = jnp.sum(jnp.sum(dot * scale, axis=1, keepdims=True), axis=0, keepdims=True)
    nvs = jnp.zeros((1, 1), F32)
    density = jnp.zeros((1, 1), F32)
    nk, tk = jnp.ones_like(valid), jnp.ones_like(valid)
    for k in range(SLIDES):
        count, held, logs = (genes_slides[48:49, 3 * j + k : 3 * j + k + 1] for j in range(3))
        some = count > 0
        safe = jnp.where(some, count, 1.0)
        nvs += count
        density += jnp.where(some, jnp.log(jnp.where(some, held, 1.0) / safe) - logs / safe, 0.0)
        here = (slide == k) & (valid > 0)
        nk = jnp.where(here, count, nk)
        tk = jnp.where(here, held, tk)
    scale = lax.rsqrt(own * squares + 1e-06)
    grad_mass = valid / SLIDES * (1.0 / tk - 1.0 / (nk * jnp.where(valid > 0, mass, 1.0)))
    mask = valid * share
    by_pred, by_data = dots * scale**3 * squares / nvs, scale / nvs
    for index, one in enumerate((by_pred * share * mask, by_data * mask, mask, share * mask)):
        rows[8 * index : 8 * index + 8, :] = jnp.broadcast_to(one, (8, one.shape[1]))
    rows[32:40, :] = jnp.concatenate([grad_mass * share, jnp.zeros((7, valid.shape[1]), F32)])
    cosines = jnp.sum(valid * dots * scale, axis=1, keepdims=True)
    lane = lax.broadcasted_iota(jnp.int32, (1, 128), 1)
    out = jnp.zeros((1, 128), F32)
    for index, one in enumerate((total / genes, cosines / nvs, density / SLIDES)):
        out = jnp.where(lane == index, one, out)
    scalars[...] = out


def coef_call(ids, genes_slides, sums, spot, totals):
    spots = spot.shape[1]
    return pl.pallas_call(
        coef_kernel,
        grid_spec=pltpu.PrefetchScalarGridSpec(
            num_scalar_prefetch=1,
            grid=(1,),
            in_specs=[fixed(genes_slides.shape), fixed(sums.shape), fixed((8, spots)), fixed((8, spots))],
            out_specs=[fixed((128, 128)), fixed((40, spots)), fixed((1, 128))],
            scratch_shapes=[pltpu.VMEM((32, 128), F32)],
        ),
        out_shape=[
            jax.ShapeDtypeStruct((128, 128), F32),
            jax.ShapeDtypeStruct((40, spots), F32),
            jax.ShapeDtypeStruct((1, 128), F32),
        ],
        compiler_params=vmem(6),
        cost_estimate=NO_COST,
        name="coef",
    )(ids, genes_slides, sums, spot, totals)


def grad_rows(pred, data, gene, spot, lane):
    by_pred = gene[:, lane : lane + 1].reshape(2, 8, 1)
    by_data = gene[:, 16 + lane : 17 + lane].reshape(2, 8, 1)
    pred, data = pred.reshape(2, 8, pred.shape[1]), data.reshape(2, 8, data.shape[1])
    grad = pred * (by_pred * spot[24:32, :] + spot[0:8, :])
    grad = grad - data * (by_data * spot[16:24, :] + spot[8:16, :])
    return grad.reshape(16, grad.shape[2]), jnp.sum(grad * pred, axis=0)


def grad_kernel(ids, *refs, count, lane, chips):
    pred, data, refs = refs[: 2 * count], refs[2 * count : 3 * count], refs[3 * count :]
    gene, spot, grad, column = refs[0], refs[1], refs[-2], refs[-1]
    step = pl.program_id(0)
    chip = (ids[2] + pick(step, chips)) & 3

    @pl.when(step == 0)
    def _():
        column[...] = jnp.zeros_like(column)

    def half_of(half, _):
        block = chip * 2 + half
        factors = gene[pl.ds(pl.multiple_of(16 * half, 16), 16), :]
        total = jnp.zeros(column.shape, F32)
        for index, part in enumerate(pred):
            for sub in range(2):
                at = gene_group(ids, *PIECES[lane + 2 * index + sub])
                row = pl.multiple_of((at & 3) * 16, 16)
                to = pl.ds(pl.multiple_of(at * 16, 16), 16)
                rows, inner = grad_rows(
                    part[sub, block],
                    data[index // 2][half, 0, pl.ds(row, 16), :],
                    factors,
                    spot,
                    lane + 2 * index + sub,
                )
                grad[0, block, to, :], grad[1, block, to, :] = split(rows)
                total += inner
        column[...] += total
        return 0

    lax.fori_loop(0, 2, half_of, 0)


def grad_call(ids, pred, spatial, gene, spot, lane, chips, done=()):
    blocks, groups, rows, spots = spatial.shape
    count = len(pred) // 2

    def chip(i, ids):
        return (ids[2] + pick(i, chips)) & 3

    def group(k):
        step = PIECES[lane + 4 * k][0]
        return pl.BlockSpec(
            (2, 1, rows, spots), lambda i, ids: (chip(i, ids), (ids[0] + step) & 3, 0, 0)
        )

    return pl.pallas_call(
        functools.partial(grad_kernel, count=count, lane=lane, chips=chips),
        grid_spec=pltpu.PrefetchScalarGridSpec(
            num_scalar_prefetch=1,
            grid=(len(chips),),
            in_specs=[RESIDENT] * (2 * count)
            + [group(k) for k in range(count)]
            + [pl.BlockSpec((32, 128), lambda i, ids: (chip(i, ids), 0)), fixed(spot.shape)]
            + [RESIDENT] * len(done),
            out_specs=[RESIDENT, fixed((8, spots))],
        ),
        out_shape=[
            jax.ShapeDtypeStruct((2, blocks, groups * rows, spots), BF16),
            jax.ShapeDtypeStruct((8, spots), F32),
        ],
        input_output_aliases={3 * count + 3: 0} if done else {},
        compiler_params=vmem(12),
        cost_estimate=NO_COST,
        name="grad",
    )(ids, *pred, *[spatial] * count, gene, spot, *done)


def back_kernel(ids, grad, masses, expr, *refs, parts, first, last):
    more, (sums, *outs), (held, ready) = refs[: first + 4 * last], refs[first + 4 * last : -2], refs[-2:]
    step = pl.program_id(0)
    rows = grad.shape[2]

    def block(part):
        return ((ids[2] + part[0]) & 3) * 2 + (ids[3] ^ part[1])

    def fetch(k):
        start = pl.multiple_of(block(parts[k]) * rows, rows)
        return pltpu.make_async_copy(expr.at[pl.ds(start, rows), :], held.at[k], ready.at[k])

    @pl.when(step == 0)
    def _():
        for k in range(len(parts)):
            fetch(k).start()

    @pl.when(step == 0)
    def _():
        if last:
            sums[...] = more[0][...] + more[1][...] + more[2][...]
        else:
            sums[...] = jnp.zeros_like(sums)

    here = block([pick(step, [part[k] for part in parts]) for k in range(2)])
    left = grad[0, here], grad[1, here]
    if first:
        pair = split(jnp.concatenate([more[0][...], jnp.zeros_like(more[0])]))
        left = [jnp.concatenate(both) for both in zip(left, pair)]
    part = product(left, masses, ((1,), (1,)))
    if first:
        sums[...] = part[rows : rows + 8]
        part = part[:rows]
    for k, out in enumerate(outs):

        @pl.when(step == k)
        def _(k=k, out=out):
            out[...] = part
            fetch(k).wait()

    sums[...] += jnp.sum((part * held[step]).reshape(-1, 8, part.shape[1]), axis=0)
    if last:

        @pl.when(step == len(parts) - 1)
        def _():
            total = jnp.sum(sums[...], axis=0, keepdims=True)
            sums[...] = jnp.zeros_like(sums)
            sums[0:1, :] = total
            sums[1:2, 0:128] = more[3][...]


def back_call(ids, parts, grad, masses, expr, first=(), last=()):
    _, blocks, rows, spots = grad.shape
    cells = masses.shape[1]
    return pl.pallas_call(
        functools.partial(back_kernel, parts=parts, first=len(first), last=len(last) // 4),
        grid_spec=pltpu.PrefetchScalarGridSpec(
            num_scalar_prefetch=1,
            grid=(len(parts),),
            in_specs=[RESIDENT, RESIDENT, pl.BlockSpec(memory_space=pl.ANY)]
            + [pl.BlockSpec((8, spots), lambda i, ids: (4, 0))] * len(first)
            + [fixed(one.shape) for one in last],
            out_specs=[fixed((8, cells))] + [RESIDENT] * len(parts),
            scratch_shapes=[
                pltpu.VMEM((len(parts), rows, cells), F32),
                pltpu.SemaphoreType.DMA((len(parts),)),
            ],
        ),
        out_shape=[jax.ShapeDtypeStruct((8, cells), F32)]
        + [jax.ShapeDtypeStruct((rows, cells), F32)] * len(parts),
        compiler_params=vmem(22),
        cost_estimate=NO_COST,
        name="back",
    )(ids, grad, masses, streamed(expr), *first, *last)


def lift_kernel(above, below, far_up, far_down, out_above, out_below):
    rows = far_up.shape[0]
    out_above[:rows, :] = above[:rows, :] + far_up[...]
    out_above[rows:, :] = above[rows:, :]
    out_below[:rows, :] = below[:rows, :]
    out_below[rows:, :] = below[rows:, :] + far_down[...]


def lift_call(above, below, far_up, far_down):
    rows, cells = far_up.shape
    block = 256
    far = pl.BlockSpec((rows, block), lambda i: (0, i))
    whole = pl.BlockSpec((2 * rows, block), lambda i: (0, i))
    return pl.pallas_call(
        lift_kernel,
        grid=(cells // block,),
        in_specs=[whole, whole, far, far],
        out_specs=[whole, whole],
        out_shape=[jax.ShapeDtypeStruct(above.shape, F32)] * 2,
        compiler_params=vmem(8),
        cost_estimate=pl.CostEstimate(flops=10**10, bytes_accessed=0, transcendentals=0),
        name="lift",
    )(above, below, far_up, far_down)


def join_kernel(above, below, got_above, got_below, out_above, out_below):
    out_above[...] = above[...] + got_above[...]
    out_below[...] = below[...] + got_below[...]


def join_call(above, below, got_above, got_below):
    rows, cells = above.shape
    whole = pl.BlockSpec((rows, 256), lambda i: (0, i))
    return pl.pallas_call(
        join_kernel,
        grid=(cells // 256,),
        in_specs=[whole] * 4,
        out_specs=[whole] * 2,
        out_shape=[jax.ShapeDtypeStruct(above.shape, F32)] * 2,
        compiler_params=vmem(8),
        cost_estimate=NO_COST,
        name="join",
    )(above, below, got_above, got_below)


def map_kernel(expr, grad, masses, keep, spot, out, held, ready, *, scale):
    index = pl.program_id(0)
    quarter, block = held.shape[2:]
    count = held.shape[1]

    def fetch(at, k):
        columns = pl.ds(pl.multiple_of(at * block, block), block)
        return pltpu.make_async_copy(
            expr.at[pl.ds(k * quarter, quarter), columns], held.at[at & 1, k], ready.at[at & 1, k]
        )

    @pl.when(index == 0)
    def _():
        for k in range(count):
            fetch(index, k).start()

    @pl.when(index + 1 < pl.num_programs(0))
    def _():
        for k in range(count):
            fetch(index + 1, k).start()

    inner = spot[0:1, :]
    for k in range(count):
        fetch(index, k).wait()
        rows = slice(k * quarter, k * quarter + quarter)
        pair = grad[0, rows, :], grad[1, rows, :]
        inner = inner + product(split(held[index & 1, k]), pair, ((0,), (0,)))
    at = pl.multiple_of(index * block, block)
    expo = masses[0, pl.ds(at, block), :].astype(F32) + masses[1, pl.ds(at, block), :].astype(F32)
    for part in range(block // 128):
        rows = slice(part * 128, part * 128 + 128)
        weight = as_column(keep[pl.ds(index * (block // 128) + part, 1), :])
        out[rows, :] = (scale * expo[rows]) * (weight * inner[rows] - spot[1:2, :])


def map_call(expr, grad, masses, keep, spot, scale):
    genes, cells = expr.shape
    spots = masses.shape[2]
    block, count = 256, 4
    return pl.pallas_call(
        functools.partial(map_kernel, scale=scale),
        grid=(cells // block,),
        in_specs=[
            pl.BlockSpec(memory_space=pl.ANY),
            RESIDENT,
            RESIDENT,
            fixed(keep.shape),
            fixed((8, spots)),
        ],
        out_specs=pl.BlockSpec((block, spots), lambda i: (i, 0)),
        out_shape=jax.ShapeDtypeStruct((cells, spots), F32),
        scratch_shapes=[
            pltpu.VMEM((2, count, genes // count, block), F32),
            pltpu.SemaphoreType.DMA((2, count)),
        ],
        compiler_params=vmem(24),
        cost_estimate=NO_COST,
        name="grad_map",
    )(streamed(expr), grad, masses, keep, spot)


def finish_kernel(last, got1, got2, got3, totals, scalars, kind, filt, grad_filter, terms, *, all_cells):
    total = (last[...] + got2[...]) + (got1[...] + got3[...])
    nvalid, retained, reg_sum = (totals[2:3, k : k + 1] for k in range(3))
    valid = (kind[...] >= 0).astype(F32)
    sigma = jax.nn.sigmoid(filt[...])
    keep = sigma * valid
    shifted = (retained - 0.35 * nvalid) / (0.1 * all_cells)
    count_term = jnp.sqrt(shifted * shifted + 1.0)
    grad_keep = total[0:1, :] + shifted / count_term / (0.1 * all_cells) + (1.0 - 2.0 * keep) / nvalid
    row = valid * sigma * (1.0 - sigma) * grad_keep * all_cells
    for k in range(grad_filter.shape[0]):
        grad_filter[k : k + 1, :] = row[:, 128 * k : 128 * k + 128]
    lane = lax.broadcasted_iota(jnp.int32, (1, 128), 1)
    out = jnp.zeros((1, 128), F32)
    parts = (scalars[:, 0:1], total[1:2, 1:2], scalars[:, 2:3], count_term, reg_sum / nvalid)
    for index, one in enumerate(parts):
        out = jnp.where(lane == index, one, out)
    terms[...] = out


def finish_call(last, got, totals, scalars, kind, filt, all_cells):
    return pl.pallas_call(
        functools.partial(finish_kernel, all_cells=float(all_cells)),
        grid=(1,),
        in_specs=[fixed(one.shape) for one in (last, *got, totals, scalars, kind, filt)],
        out_specs=[fixed((kind.shape[1] // 128, 128)), fixed((1, 128))],
        out_shape=[
            jax.ShapeDtypeStruct((kind.shape[1] // 128, 128), F32),
            jax.ShapeDtypeStruct((1, 128), F32),
        ],
        compiler_params=vmem(4),
        cost_estimate=NO_COST,
        name="finish",
    )(last, *got, totals, scalars, kind, filt)


def on_device(map_logits, filter_logits, expr, spatial, cell_type, slide_id, spot_mask):
    genes, cells = expr.shape
    spots = map_logits.shape[1]
    all_cells = cells * lax.axis_size("cells")
    all_spots = spots * lax.axis_size("spots")
    cell_place = lax.axis_index("cells")
    z, x = cell_place >> 2, cell_place & 3
    spot_place = lax.axis_index("spots")
    y, core = spot_place >> 1, spot_place & 1
    first = jnp.where(core == 0, x, z)
    second = jnp.where(core == 0, z, x)
    blocks = cells // 128

    valid = (cell_type >= 0).astype(F32)
    sigma = jax.nn.sigmoid(filter_logits)
    keep = sigma * valid
    spot_valid = spot_mask.astype(F32)
    kind2 = cell_type.reshape(blocks, 128)
    filt2 = filter_logits.reshape(blocks, 128)
    keep2 = keep.reshape(blocks, 128)

    expr4 = expr.reshape(8, 16, 16, cells)
    keep_row = keep.reshape(1, cells)

    ids = jnp.stack([first, second, y, core]).astype(jnp.int32)

    def pred_part(one, two, more, cuts, *others):
        return pred_call(after(ids, *others), (one, two), expr4, keep_row, masses, totals, more, cuts)

    masses, types, totals, *far = expo_call(
        ids, ((2, 0), (2, 1)), map_logits, kind2, filt2, expr4
    )
    far_right, far_left = along(far[0], 1), along(far[1], -1)
    near = pred_part((1, 1), (-1, 0), (), 2, *far)
    near_right, near_left = along(near[0], 1), along(near[1], -1)
    late = pred_part((1, 0), (-1, 1), (far_right, far_left), 1, *near)
    late_right, late_left = along(late[0], 1), along(late[1], -1)
    own = pred_part((0, 0), (0, 1), (near_left, near_right), 2, *late)
    mine, *pieces = merge_call(own, (late_right, late_left))
    pieces = [across(piece, step + 1) for step, piece in enumerate(pieces)]
    spatial_squares = jnp.sum(after(spatial, mine) ** 2, axis=0)
    types = types + swap_along(after(types, spatial_squares), 1)
    types = types + swap_along(types, 3)
    spot_rows = stacked([spot_valid, slide_id.astype(F32), spatial_squares])
    mine = after(mine, spot_rows, types)
    piece = mine + pieces[0] + pieces[1] + pieces[2]
    totals = piece[-1]
    piece = piece[:-1].reshape(8, 16, spots)
    share = 1.0 / totals[0]
    mass = totals[1] * share

    got = [across(piece, step) for step in (1, 2, 3)]
    sums, slides = stats_call(
        ids,
        piece,
        spatial.reshape(8, 16, 16, spots),
        spot_rows,
        totals,
    )
    sums = sums + swap_along(sums, 1)
    sums = sums + swap_along(sums, 3)
    mine = after((jnp.stack([piece, got[2]]), jnp.stack([got[1], got[0]])), sums)
    right0, left1 = along(mine[0], 1), along(mine[1], -1)
    right1, left0 = along(mine[1], 1), along(mine[0], -1)
    sums = sums + swap_across(after(sums, *mine), 1)
    sums = sums + swap_across(sums, 3)
    right0, left1, sums = lax.optimization_barrier((right0, left1, sums))
    far0, far1 = along(right0, 1), along(left1, -1)
    genes_slides = jnp.concatenate([sums[:48], slides])
    genes_slides = genes_slides + swap(genes_slides, 0, 0, 0, 1)
    genes_slides = genes_slides + swap(genes_slides, 0, 0, 1, 0)
    genes_slides = after(genes_slides, right1, left0)
    genes_slides = genes_slides + swap(genes_slides, 0, 0, 3, 0)
    pred = [*mine, right0, right1, left0, left1, far0, far1]
    gene_coef, spot_coef, scalars = coef_call(ids, genes_slides, sums, spot_rows, totals)
    spatial4 = spatial.reshape(8, RING, genes // 32, spots)
    grad, column_a = grad_call(ids, pred[:6], spatial4, gene_coef, spot_coef, 0, (0, 1, 2, 3))

    def last_grad(chips, grad, *others):
        return grad_call(
            after(ids, *others), pred[6:], spatial4, gene_coef, spot_coef, 12, chips, (grad,)
        )

    def back_part(steps, grad, *others, **rows):
        return back_call(after(ids, *others), steps, grad, masses, expr, **rows)

    rows = genes // 16
    grad, column_b = last_grad((2,), grad)
    sums_a, far_a = back_part([(2, 1)], grad, first=[spot_coef])
    far_got = swap(far_a, 0, 0, 0, 1)
    sums_b, far_b = back_part([(2, 0)], grad, far_a)
    far = far_b + far_got
    far_up, far_down = up(far[:rows], 1), up(far[rows:], -1)
    grad, column_c = last_grad((1, -1, 0), grad, far)
    sums_c, up_a, down_a, own_a = back_part([(1, 1), (-1, 1), (0, 1)], grad)
    up_got, down_got, own_got = (swap(one, 0, 0, 0, 1) for one in (up_a, down_a, own_a))
    last, up_b, down_b, own_b = back_part(
        [(1, 0), (-1, 0), (0, 0)], grad, up_a, last=[sums_a, sums_b, sums_c, scalars]
    )
    last_got = swap(last, 0, 0, 0, 1)
    types = types + swap_across(after(types, up_a), 1)
    above, below = lift_call(up_b, down_b, *after((far_up, far_down), types))
    above, below = join_call(above, below, up_got, down_got)
    near_up, near_down = up(above, 1), up(below, -1)
    types_got = swap_across(after(types, above), 3)
    own = own_b + own_got

    column = jnp.sum(column_a + column_b + column_c, axis=0) * share + spot_coef[32] * mass
    map_rows = stacked([spot_coef[32], column])
    map_args = (expr, grad.reshape(2, genes, spots), masses, keep2, map_rows, all_cells * genes)
    grad_map = map_call(*map_args)
    types_got, last_got = after((types_got, last_got), grad_map)
    types = types + types_got
    last = after(last + last_got, own)
    got = [up(last, step) for step in (1, 2, 3)]
    grad_weighted = after(own, grad_map) + near_up + near_down
    grad_expr = grad_weighted * (keep * (genes * all_spots))[None, :]

    type_fraction = types * share

    grad_filter, loss_terms = finish_call(
        last, got, totals, scalars, cell_type.reshape(1, cells), filter_logits.reshape(1, cells), all_cells
    )
    return (loss_terms[0, :5], type_fraction, grad_map, grad_filter.reshape(cells), grad_expr)


def solution(mesh):
    in_specs = (
        P("cells", "spots"),
        P("cells"),
        P(None, "cells"),
        P(None, "spots"),
        P("cells"),
        P("spots"),
        P("spots"),
    )
    out_specs = (P(), P(None, "spots"), P("cells", "spots"), P("cells"), P("spots", "cells"))
    return jax.shard_map(
        on_device, mesh=mesh, in_specs=in_specs, out_specs=out_specs, check_vma=False
    )
```

```python
import functools

import jax
import jax.numpy as jnp
from jax import lax
from jax.experimental import pallas as pl
from jax.experimental.pallas import tpu as pltpu
from jax.sharding import PartitionSpec as P

TYPES = 32
SLIDES = 3
RING = 4
F32 = jnp.float32
BF16 = jnp.bfloat16


def vmem(mib):
    return pltpu.CompilerParams(vmem_limit_bytes=mib << 20)


def fixed(shape):
    return pl.BlockSpec(shape, lambda *_: (0,) * len(shape), pipeline_mode=pl.Buffered(1))


def streamed(array):
    return pltpu.with_memory_space_constraint(array, pltpu.HBM)


RESIDENT = pl.BlockSpec(memory_space=pltpu.VMEM)


def cost(flops, moved):
    return pl.CostEstimate(flops=int(flops) // 8, bytes_accessed=int(moved) // 8, transcendentals=0)


NO_COST = pl.CostEstimate(flops=0, bytes_accessed=0, transcendentals=0)


def route(target):
    def flat(z, x, y, core):
        return ((z % RING * RING + x % RING) * RING + y % RING) * 2 + core

    return [
        (flat(z, x, y, core), flat(*target(z, x, y, core)))
        for z in range(RING)
        for x in range(RING)
        for y in range(RING)
        for core in range(2)
    ]


def send(array, target):
    return lax.ppermute(array, ("cells", "spots"), route(target))


def along(array, step):
    return send(array, lambda z, x, y, c: (z, x + step, y, c) if c == 0 else (z + step, x, y, c))


def across(array, step):
    return send(array, lambda z, x, y, c: (z + step, x, y, c) if c == 0 else (z, x + step, y, c))


def up(array, step):
    return send(array, lambda z, x, y, c: (z, x, y + step, c))


def swap(array, mz, mx, my, mc):
    return send(array, lambda z, x, y, c: (z ^ mz, x ^ mx, y ^ my, c ^ mc))


def swap_along(array, mask):
    return send(array, lambda z, x, y, c: (z, x ^ mask, y, c) if c == 0 else (z ^ mask, x, y, c))


def swap_across(array, mask):
    return send(array, lambda z, x, y, c: (z ^ mask, x, y, c) if c == 0 else (z, x ^ mask, y, c))


def after(value, *others):
    return lax.optimization_barrier((value, *others))[0]


def split(value):
    high = value.astype(BF16)
    return high, (value - high.astype(F32)).astype(BF16)


def product(left, right, dims):
    def one(a, b):
        return lax.dot_general(a, b, (dims, ((), ())), preferred_element_type=F32)

    return one(left[0], right[0]) + one(left[0], right[1]) + one(left[1], right[0])


def gene_group(ids, step, half, sub):
    return ((ids[0] + step) & 3) * RING + ((ids[1] + 2 * half + sub) & 3)


PIECES = [
    (step, half, sub)
    for step, half in ((0, 0), (0, 1), (-1, 0), (-1, 1), (1, 0), (1, 1), (2, 0), (2, 1))
    for sub in range(2)
]


def pick(index, values):
    out = values[0]
    for k, value in enumerate(values[1:]):
        out = jnp.where(index == k + 1, value, out)
    return out


def stacked(rows):
    row = lax.broadcasted_iota(jnp.int32, (8, rows[0].shape[0]), 0)
    out = jnp.zeros(row.shape, F32)
    for k, value in enumerate(rows):
        out = jnp.where(row == k, value[None, :], out)
    return out


def as_column(row):
    return jnp.broadcast_to(row, (128, 128)).T[:, :1]


def expo_kernel(ids, logits, kind, filt, *refs):
    expr, (masses, types, totals, out0, out1) = refs[:4], refs[4:]
    step = pl.program_id(0)
    count = logits.shape[0] // 128

    @pl.when(step == 0)
    def _():
        for out in (types, totals, out0, out1):
            out[...] = jnp.zeros_like(out)

    keeps = []
    lane = lax.broadcasted_iota(jnp.int32, (1, totals.shape[1]), 1)
    cell_sums = jnp.zeros(lane.shape, F32)
    for part in range(count):
        rows = slice(part * 128, part * 128 + 128)
        label = kind[pl.ds(step * count + part, 1), :]
        valid = (label >= 0).astype(F32)
        keep = valid * jax.nn.sigmoid(filt[pl.ds(step * count + part, 1), :])
        keeps.append(keep)
        for k, one in enumerate((valid, keep, keep - keep * keep)):
            cell_sums += jnp.where(lane == k, jnp.sum(one, axis=1, keepdims=True), 0.0)
        expo = jnp.exp(logits[rows]) * as_column(valid)
        masses[0, rows], masses[1, rows] = split(expo)
        whole = jnp.sum(expo, axis=0, keepdims=True)
        kept = jnp.sum(expo * as_column(keep), axis=0, keepdims=True)
        row = lax.broadcasted_iota(jnp.int32, types.shape, 0)
        types[...] += jnp.where(row == jnp.max(label, axis=1, keepdims=True), whole, 0.0)
        row = lax.broadcasted_iota(jnp.int32, totals.shape, 0)
        totals[...] += jnp.where(row == 0, whole, jnp.where(row == 1, kept, 0.0))
    totals[2:3, :] += cell_sums
    weighted = jnp.concatenate([part[...].reshape(-1, logits.shape[0]) for part in expr])
    weighted = weighted * jnp.concatenate(keeps, axis=1)
    part = product(split(weighted), masses, ((1,), (0,)))
    half = part.shape[0] // 2
    for index, out in enumerate((out0, out1)):
        new = part[index * half : index * half + half].reshape(-1, 8, part.shape[1])
        out[: half // 8] += new
        out[half // 8] = totals[...]


def expo_call(ids, parts, logits, kind, filt, expr):
    cells, spots = logits.shape
    blocks, groups, rows, _ = expr.shape
    block = 256

    def genes(part, sub):
        return pl.BlockSpec(
            (blocks, 1, rows, block), lambda i, ids: (0, gene_group(ids, *part, sub), 0, i)
        )

    return pl.pallas_call(
        expo_kernel,
        grid_spec=pltpu.PrefetchScalarGridSpec(
            num_scalar_prefetch=1,
            grid=(cells // block,),
            in_specs=[
                pl.BlockSpec((block, spots), lambda i, w: (i, 0)),
                fixed(kind.shape),
                fixed(filt.shape),
            ]
            + [genes(part, sub) for part in parts for sub in range(2)],
            out_specs=[
                pl.BlockSpec((2, block, spots), lambda i, w: (0, i, 0)),
                fixed((TYPES, spots)),
                fixed((8, spots)),
                fixed((blocks * rows // 4 + 1, 8, spots)),
                fixed((blocks * rows // 4 + 1, 8, spots)),
            ],
        ),
        out_shape=[
            jax.ShapeDtypeStruct((2, cells, spots), BF16),
            jax.ShapeDtypeStruct((TYPES, spots), F32),
            jax.ShapeDtypeStruct((8, spots), F32),
            jax.ShapeDtypeStruct((blocks * rows // 4 + 1, 8, spots), F32),
            jax.ShapeDtypeStruct((blocks * rows // 4 + 1, 8, spots), F32),
        ],
        compiler_params=vmem(16),
        cost_estimate=cost(0, cells * spots * 8),
        name="expo",
    )(ids, streamed(logits), streamed(kind), streamed(filt), *[streamed(expr)] * 4)


def pred_kernel(ids, expr_a, expr_b, keep, masses, totals, *refs, cuts):
    more, outs = refs[:-2], refs[-2:]
    rows = 2 * expr_a.shape[0] * expr_a.shape[2]
    weighted = jnp.concatenate(
        [part[...].reshape(rows // 2, keep.shape[1]) for part in (expr_a, expr_b)]
    )
    weighted = split(weighted * keep[...])
    width = masses.shape[2] // cuts

    def half(index, _):
        columns = pl.ds(pl.multiple_of(index * width, width), width)
        part = product(weighted, (masses[0, :, columns], masses[1, :, columns]), ((1,), (0,)))
        part = part.reshape(rows // 8, 8, width)
        for step, out in enumerate(outs):

            @pl.when(pl.program_id(0) == step)
            def _(step=step, out=out):
                if more:
                    out[: rows // 8, :, columns] = part + more[step][: rows // 8, :, columns]
                    out[rows // 8, :, columns] = totals[:, columns] + more[step][rows // 8, :, columns]
                else:
                    out[: rows // 8, :, columns] = part
                    out[rows // 8, :, columns] = totals[:, columns]

        return 0

    lax.fori_loop(0, cuts, half, 0)


def pred_call(ids, parts, expr, keep, masses, totals, more, cuts):
    blocks, groups, rows, cells = expr.shape
    spots = masses.shape[2]
    tiles = blocks * rows // 4 + 1

    def genes(sub):
        def place(i, ids):
            step, half = (pick(i, [part[k] for part in parts]) for k in range(2))
            return (0, gene_group(ids, step, half, sub), 0, 0)

        return pl.BlockSpec((blocks, 1, rows, cells), place)

    return pl.pallas_call(
        functools.partial(pred_kernel, cuts=cuts),
        grid_spec=pltpu.PrefetchScalarGridSpec(
            num_scalar_prefetch=1,
            grid=(2,),
            in_specs=[
                genes(0),
                genes(1),
                fixed((1, cells)),
                RESIDENT,
                fixed((8, spots)),
            ]
            + [RESIDENT] * len(more),
            out_specs=[RESIDENT] * 2,
        ),
        out_shape=[jax.ShapeDtypeStruct((tiles, 8, spots), F32)] * 2,
        compiler_params=vmem(16),
        cost_estimate=cost(24 * blocks * rows * cells * spots, 4 * cells * spots + 16 * blocks * rows * (cells + spots)),
        name="pred",
    )(ids, *[streamed(expr)] * 2, keep, masses, totals, *more)


def merge_kernel(own0, own1, got0, got1, *outs):
    tiles = outs[0].shape[0] - 1
    for half, (own, got) in enumerate(((own0, got0), (own1, got1))):
        for sub in range(2):
            out = outs[2 * half + sub]
            out[:tiles] = own[sub * tiles : sub * tiles + tiles] + got[sub * tiles : sub * tiles + tiles]
            out[tiles] = own[2 * tiles] + got[2 * tiles]


def merge_call(own, got):
    tiles, _, spots = own[0].shape
    block = 256
    whole = pl.BlockSpec((tiles, 8, block), lambda i: (0, 0, i))
    piece = (tiles // 2 + 1, 8, spots)
    return pl.pallas_call(
        merge_kernel,
        grid=(spots // block,),
        in_specs=[whole] * 4,
        out_specs=[pl.BlockSpec((tiles // 2 + 1, 8, block), lambda i: (0, 0, i))] * 4,
        out_shape=[jax.ShapeDtypeStruct(piece, F32)] * 4,
        compiler_params=vmem(12),
        cost_estimate=NO_COST,
        name="merge",
    )(*own, *got)


def stats_kernel(ids, piece, spatial, spot, totals, gene, slide_sums):
    rows = piece.shape[0] * piece.shape[1]
    valid, slide = spot[0:1, :], spot[1:2, :]
    share = 1.0 / totals[0:1, :]
    mass = totals[1:2, :] * share
    value = piece[...].reshape(rows, piece.shape[2]) * share
    data = spatial[...].reshape(value.shape)
    cross, square = value * data, value * value
    lane = lax.broadcasted_iota(jnp.int32, (rows, 128), 1)
    sums = jnp.zeros((rows, 128), F32)
    for index, one in enumerate((cross, square, data * data)):
        sums = jnp.where(lane == index, jnp.sum(one * valid, axis=1, keepdims=True), sums)
    sums = sums.T
    gene[...] = jnp.zeros_like(gene)
    slide_sums[...] = jnp.zeros_like(slide_sums)
    for index in range(3):
        gene[pl.ds(16 * index + gene_group(ids, 0, 0, 0), 1), :] = sums[index : index + 1, :]
    lane = lax.broadcasted_iota(jnp.int32, (1, 128), 1)
    slides = jnp.zeros((1, 128), F32)
    logs = jnp.log(jnp.where(valid > 0, mass, 1.0))
    for k in range(SLIDES):
        inside = jnp.where(slide == k, valid, 0.0)
        for index, one in enumerate((inside, inside * mass, inside * logs)):
            total = jnp.sum(one, axis=1, keepdims=True)
            slides = jnp.where(lane == 3 * index + k, total, slides)
    slide_sums[0:1, :] = slides
    for index, one in enumerate((cross, square)):
        total = jnp.sum(one, axis=0, keepdims=True)
        for k in range(total.shape[1] // 128):
            at = 48 + 8 * index + k
            gene[at : at + 1, :] = total[:, 128 * k : 128 * k + 128]


def stats_call(ids, piece, spatial, spot, totals):
    blocks, rows, spots = piece.shape
    return pl.pallas_call(
        stats_kernel,
        grid_spec=pltpu.PrefetchScalarGridSpec(
            num_scalar_prefetch=1,
            grid=(1,),
            in_specs=[
                fixed((blocks, rows, spots)),
                pl.BlockSpec((blocks, 1, rows, spots), lambda i, ids: (0, gene_group(ids, 0, 0, 0), 0, 0)),
                fixed((8, spots)),
                fixed((8, spots)),
            ],
            out_specs=[fixed((64, 128)), fixed((8, 128))],
        ),
        out_shape=[jax.ShapeDtypeStruct((64, 128), F32), jax.ShapeDtypeStruct((8, 128), F32)],
        compiler_params=vmem(8),
        cost_estimate=NO_COST,
        name="stats",
    )(ids, piece, spatial, spot, totals)


def coef_kernel(ids, genes_slides, sums, spot, totals, gene, rows, scalars, pairs):
    valid, slide, squares = (spot[k : k + 1, :] for k in range(3))
    share = 1.0 / totals[0:1, :]
    mass = totals[1:2, :] * share
    genes = float(16 * sums.shape[1])

    def wide(index):
        return jnp.concatenate([sums[index + k : index + k + 1, :] for k in range(8)], axis=1)

    dots, own = wide(48), wide(56)
    dot, aa, bb = genes_slides[0:16, :], genes_slides[16:32, :], genes_slides[32:48, :]
    scale = lax.rsqrt(aa * bb + 1e-06)
    pairs[0:16, :] = dot * scale**3 * bb / genes
    pairs[16:32, :] = scale / genes
    pair = [pairs[pl.ds(k + gene_group(ids, *one), 1), :] for k in (0, 16) for one in PIECES]
    gene[...] = jnp.concatenate([*pair, jnp.zeros((96, 128), F32)]).T
    total = jnp.sum(jnp.sum(dot * scale, axis=1, keepdims=True), axis=0, keepdims=True)
    nvs = jnp.zeros((1, 1), F32)
    density = jnp.zeros((1, 1), F32)
    nk, tk = jnp.ones_like(valid), jnp.ones_like(valid)
    for k in range(SLIDES):
        count, held, logs = (genes_slides[48:49, 3 * j + k : 3 * j + k + 1] for j in range(3))
        some = count > 0
        safe = jnp.where(some, count, 1.0)
        nvs += count
        density += jnp.where(some, jnp.log(jnp.where(some, held, 1.0) / safe) - logs / safe, 0.0)
        here = (slide == k) & (valid > 0)
        nk = jnp.where(here, count, nk)
        tk = jnp.where(here, held, tk)
    scale = lax.rsqrt(own * squares + 1e-06)
    grad_mass = valid / SLIDES * (1.0 / tk - 1.0 / (nk * jnp.where(valid > 0, mass, 1.0)))
    mask = valid * share
    by_pred, by_data = dots * scale**3 * squares / nvs, scale / nvs
    for index, one in enumerate((by_pred * share * mask, by_data * mask, mask, share * mask)):
        rows[8 * index : 8 * index + 8, :] = jnp.broadcast_to(one, (8, one.shape[1]))
    rows[32:40, :] = jnp.concatenate([grad_mass * share, jnp.zeros((7, valid.shape[1]), F32)])
    cosines = jnp.sum(valid * dots * scale, axis=1, keepdims=True)
    lane = lax.broadcasted_iota(jnp.int32, (1, 128), 1)
    out = jnp.zeros((1, 128), F32)
    for index, one in enumerate((total / genes, cosines / nvs, density / SLIDES)):
        out = jnp.where(lane == index, one, out)
    scalars[...] = out


def coef_call(ids, genes_slides, sums, spot, totals):
    spots = spot.shape[1]
    return pl.pallas_call(
        coef_kernel,
        grid_spec=pltpu.PrefetchScalarGridSpec(
            num_scalar_prefetch=1,
            grid=(1,),
            in_specs=[fixed(genes_slides.shape), fixed(sums.shape), fixed((8, spots)), fixed((8, spots))],
            out_specs=[fixed((128, 128)), fixed((40, spots)), fixed((1, 128))],
            scratch_shapes=[pltpu.VMEM((32, 128), F32)],
        ),
        out_shape=[
            jax.ShapeDtypeStruct((128, 128), F32),
            jax.ShapeDtypeStruct((40, spots), F32),
            jax.ShapeDtypeStruct((1, 128), F32),
        ],
        compiler_params=vmem(6),
        cost_estimate=NO_COST,
        name="coef",
    )(ids, genes_slides, sums, spot, totals)


def grad_rows(pred, data, gene, spot, lane):
    by_pred = gene[:, lane : lane + 1].reshape(2, 8, 1)
    by_data = gene[:, 16 + lane : 17 + lane].reshape(2, 8, 1)
    pred, data = pred.reshape(2, 8, pred.shape[1]), data.reshape(2, 8, data.shape[1])
    grad = pred * (by_pred * spot[24:32, :] + spot[0:8, :])
    grad = grad - data * (by_data * spot[16:24, :] + spot[8:16, :])
    return grad.reshape(16, grad.shape[2]), jnp.sum(grad * pred, axis=0)


def grad_kernel(ids, *refs, count, lane, chips):
    pred, data, refs = refs[: 2 * count], refs[2 * count : 3 * count], refs[3 * count :]
    gene, spot, grad, column = refs[0], refs[1], refs[-2], refs[-1]
    step = pl.program_id(0)
    chip = (ids[2] + pick(step, chips)) & 3

    @pl.when(step == 0)
    def _():
        column[...] = jnp.zeros_like(column)

    def half_of(half, _):
        block = chip * 2 + half
        factors = gene[pl.ds(pl.multiple_of(16 * half, 16), 16), :]
        total = jnp.zeros(column.shape, F32)
        for index, part in enumerate(pred):
            for sub in range(2):
                at = gene_group(ids, *PIECES[lane + 2 * index + sub])
                row = pl.multiple_of((at & 3) * 16, 16)
                to = pl.ds(pl.multiple_of(at * 16, 16), 16)
                rows, inner = grad_rows(
                    part[sub, block],
                    data[index // 2][half, 0, pl.ds(row, 16), :],
                    factors,
                    spot,
                    lane + 2 * index + sub,
                )
                grad[0, block, to, :], grad[1, block, to, :] = split(rows)
                total += inner
        column[...] += total
        return 0

    lax.fori_loop(0, 2, half_of, 0)


def grad_call(ids, pred, spatial, gene, spot, lane, chips, done=()):
    blocks, groups, rows, spots = spatial.shape
    count = len(pred) // 2

    def chip(i, ids):
        return (ids[2] + pick(i, chips)) & 3

    def group(k):
        step = PIECES[lane + 4 * k][0]
        return pl.BlockSpec(
            (2, 1, rows, spots), lambda i, ids: (chip(i, ids), (ids[0] + step) & 3, 0, 0)
        )

    return pl.pallas_call(
        functools.partial(grad_kernel, count=count, lane=lane, chips=chips),
        grid_spec=pltpu.PrefetchScalarGridSpec(
            num_scalar_prefetch=1,
            grid=(len(chips),),
            in_specs=[RESIDENT] * (2 * count)
            + [group(k) for k in range(count)]
            + [pl.BlockSpec((32, 128), lambda i, ids: (chip(i, ids), 0)), fixed(spot.shape)]
            + [RESIDENT] * len(done),
            out_specs=[RESIDENT, fixed((8, spots))],
        ),
        out_shape=[
            jax.ShapeDtypeStruct((2, blocks, groups * rows, spots), BF16),
            jax.ShapeDtypeStruct((8, spots), F32),
        ],
        input_output_aliases={3 * count + 3: 0} if done else {},
        compiler_params=vmem(12),
        cost_estimate=NO_COST,
        name="grad",
    )(ids, *pred, *[spatial] * count, gene, spot, *done)


def back_kernel(ids, grad, masses, expr, *refs, parts, first, last):
    more, (sums, *outs), (held, ready) = refs[: first + 5 * last], refs[first + 5 * last : -2], refs[-2:]
    step = pl.program_id(0)
    rows = grad.shape[2]

    def block(part):
        return ((ids[2] + part[0]) & 3) * 2 + (ids[3] ^ part[1])

    def fetch(k):
        start = pl.multiple_of(block(parts[k]) * rows, rows)
        return pltpu.make_async_copy(expr.at[pl.ds(start, rows), :], held.at[k], ready.at[k])

    @pl.when(step == 0)
    def _():
        for k in range(len(parts)):
            fetch(k).start()

    @pl.when(step == 0)
    def _():
        if last:
            sums[...] = more[0][...] + more[1][...] + more[2][...] + more[3][...]
        else:
            sums[...] = jnp.zeros_like(sums)

    here = block([pick(step, [part[k] for part in parts]) for k in range(2)])
    left = grad[0, here], grad[1, here]
    if first:
        pair = split(jnp.concatenate([more[0][...], jnp.zeros_like(more[0])]))
        left = [jnp.concatenate(both) for both in zip(left, pair)]
    part = product(left, masses, ((1,), (1,)))
    if first:
        sums[...] = part[rows : rows + 8]
        part = part[:rows]
    for k, out in enumerate(outs):

        @pl.when(step == k)
        def _(k=k, out=out):
            out[...] = part
            fetch(k).wait()

    sums[...] += jnp.sum((part * held[step]).reshape(-1, 8, part.shape[1]), axis=0)
    if last:

        @pl.when(step == len(parts) - 1)
        def _():
            total = jnp.sum(sums[...], axis=0, keepdims=True)
            sums[...] = jnp.zeros_like(sums)
            sums[0:1, :] = total
            sums[1:2, 0:128] = more[4][...]


def back_call(ids, parts, grad, masses, expr, first=(), last=()):
    _, blocks, rows, spots = grad.shape
    cells = masses.shape[1]
    return pl.pallas_call(
        functools.partial(back_kernel, parts=parts, first=len(first), last=len(last) // 5),
        grid_spec=pltpu.PrefetchScalarGridSpec(
            num_scalar_prefetch=1,
            grid=(len(parts),),
            in_specs=[RESIDENT, RESIDENT, pl.BlockSpec(memory_space=pl.ANY)]
            + [pl.BlockSpec((8, spots), lambda i, ids: (4, 0))] * len(first)
            + [fixed(one.shape) for one in last],
            out_specs=[fixed((8, cells))] + [RESIDENT] * len(parts),
            scratch_shapes=[
                pltpu.VMEM((len(parts), rows, cells), F32),
                pltpu.SemaphoreType.DMA((len(parts),)),
            ],
        ),
        out_shape=[jax.ShapeDtypeStruct((8, cells), F32)]
        + [jax.ShapeDtypeStruct((rows, cells), F32)] * len(parts),
        compiler_params=vmem(22),
        cost_estimate=NO_COST,
        name="back",
    )(ids, grad, masses, streamed(expr), *first, *last)


def lift_kernel(above, below, far_up, far_down, out_above, out_below):
    rows = far_up.shape[0]
    out_above[:rows, :] = above[:rows, :] + far_up[...]
    out_above[rows:, :] = above[rows:, :]
    out_below[:rows, :] = below[:rows, :]
    out_below[rows:, :] = below[rows:, :] + far_down[...]


def lift_call(above, below, far_up, far_down):
    rows, cells = far_up.shape
    block = 256
    far = pl.BlockSpec((rows, block), lambda i: (0, i))
    whole = pl.BlockSpec((2 * rows, block), lambda i: (0, i))
    return pl.pallas_call(
        lift_kernel,
        grid=(cells // block,),
        in_specs=[whole, whole, far, far],
        out_specs=[whole, whole],
        out_shape=[jax.ShapeDtypeStruct(above.shape, F32)] * 2,
        compiler_params=vmem(8),
        cost_estimate=pl.CostEstimate(flops=10**10, bytes_accessed=0, transcendentals=0),
        name="lift",
    )(above, below, far_up, far_down)


def join_kernel(above, below, got_above, got_below, out_above, out_below):
    out_above[...] = above[...] + got_above[...]
    out_below[...] = below[...] + got_below[...]


def join_call(above, below, got_above, got_below):
    rows, cells = above.shape
    whole = pl.BlockSpec((rows, 256), lambda i: (0, i))
    return pl.pallas_call(
        join_kernel,
        grid=(cells // 256,),
        in_specs=[whole] * 4,
        out_specs=[whole] * 2,
        out_shape=[jax.ShapeDtypeStruct(above.shape, F32)] * 2,
        compiler_params=vmem(8),
        cost_estimate=NO_COST,
        name="join",
    )(above, below, got_above, got_below)


def map_kernel(expr, grad, masses, keep, spot, out, held, ready, *, scale):
    index = pl.program_id(0)
    quarter, block = held.shape[2:]
    count = held.shape[1]

    def fetch(at, k):
        columns = pl.ds(pl.multiple_of(at * block, block), block)
        return pltpu.make_async_copy(
            expr.at[pl.ds(k * quarter, quarter), columns], held.at[at & 1, k], ready.at[at & 1, k]
        )

    @pl.when(index == 0)
    def _():
        for k in range(count):
            fetch(index, k).start()

    @pl.when(index + 1 < pl.num_programs(0))
    def _():
        for k in range(count):
            fetch(index + 1, k).start()

    inner = spot[0:1, :]
    for k in range(count):
        fetch(index, k).wait()
        rows = slice(k * quarter, k * quarter + quarter)
        pair = grad[0, rows, :], grad[1, rows, :]
        inner = inner + product(split(held[index & 1, k]), pair, ((0,), (0,)))
    at = pl.multiple_of(index * block, block)
    expo = masses[0, pl.ds(at, block), :].astype(F32) + masses[1, pl.ds(at, block), :].astype(F32)
    for part in range(block // 128):
        rows = slice(part * 128, part * 128 + 128)
        weight = as_column(keep[pl.ds(index * (block // 128) + part, 1), :])
        out[rows, :] = (scale * expo[rows]) * (weight * inner[rows] - spot[1:2, :])


def map_call(expr, grad, masses, keep, spot, scale):
    genes, cells = expr.shape
    spots = masses.shape[2]
    block, count = 256, 4
    return pl.pallas_call(
        functools.partial(map_kernel, scale=scale),
        grid=(cells // block,),
        in_specs=[
            pl.BlockSpec(memory_space=pl.ANY),
            RESIDENT,
            RESIDENT,
            fixed(keep.shape),
            fixed((8, spots)),
        ],
        out_specs=pl.BlockSpec((block, spots), lambda i: (i, 0)),
        out_shape=jax.ShapeDtypeStruct((cells, spots), F32),
        scratch_shapes=[
            pltpu.VMEM((2, count, genes // count, block), F32),
            pltpu.SemaphoreType.DMA((2, count)),
        ],
        compiler_params=vmem(24),
        cost_estimate=NO_COST,
        name="grad_map",
    )(streamed(expr), grad, masses, keep, spot)


def finish_kernel(last, got1, got2, got3, totals, scalars, kind, filt, grad_filter, terms, *, all_cells):
    total = (last[...] + got2[...]) + (got1[...] + got3[...])
    nvalid, retained, reg_sum = (totals[2:3, k : k + 1] for k in range(3))
    valid = (kind[...] >= 0).astype(F32)
    sigma = jax.nn.sigmoid(filt[...])
    keep = sigma * valid
    shifted = (retained - 0.35 * nvalid) / (0.1 * all_cells)
    count_term = jnp.sqrt(shifted * shifted + 1.0)
    grad_keep = total[0:1, :] + shifted / count_term / (0.1 * all_cells) + (1.0 - 2.0 * keep) / nvalid
    row = valid * sigma * (1.0 - sigma) * grad_keep * all_cells
    for k in range(grad_filter.shape[0]):
        grad_filter[k : k + 1, :] = row[:, 128 * k : 128 * k + 128]
    lane = lax.broadcasted_iota(jnp.int32, (1, 128), 1)
    out = jnp.zeros((1, 128), F32)
    parts = (scalars[:, 0:1], total[1:2, 1:2], scalars[:, 2:3], count_term, reg_sum / nvalid)
    for index, one in enumerate(parts):
        out = jnp.where(lane == index, one, out)
    terms[...] = out


def finish_call(last, got, totals, scalars, kind, filt, all_cells):
    return pl.pallas_call(
        functools.partial(finish_kernel, all_cells=float(all_cells)),
        grid=(1,),
        in_specs=[fixed(one.shape) for one in (last, *got, totals, scalars, kind, filt)],
        out_specs=[fixed((kind.shape[1] // 128, 128)), fixed((1, 128))],
        out_shape=[
            jax.ShapeDtypeStruct((kind.shape[1] // 128, 128), F32),
            jax.ShapeDtypeStruct((1, 128), F32),
        ],
        compiler_params=vmem(4),
        cost_estimate=NO_COST,
        name="finish",
    )(last, *got, totals, scalars, kind, filt)


def on_device(map_logits, filter_logits, expr, spatial, cell_type, slide_id, spot_mask):
    genes, cells = expr.shape
    spots = map_logits.shape[1]
    all_cells = cells * lax.axis_size("cells")
    all_spots = spots * lax.axis_size("spots")
    cell_place = lax.axis_index("cells")
    z, x = cell_place >> 2, cell_place & 3
    spot_place = lax.axis_index("spots")
    y, core = spot_place >> 1, spot_place & 1
    first = jnp.where(core == 0, x, z)
    second = jnp.where(core == 0, z, x)
    blocks = cells // 128

    valid = (cell_type >= 0).astype(F32)
    sigma = jax.nn.sigmoid(filter_logits)
    keep = sigma * valid
    spot_valid = spot_mask.astype(F32)
    kind2 = cell_type.reshape(blocks, 128)
    filt2 = filter_logits.reshape(blocks, 128)
    keep2 = keep.reshape(blocks, 128)

    expr4 = expr.reshape(8, 16, 16, cells)
    keep_row = keep.reshape(1, cells)

    ids = jnp.stack([first, second, y, core]).astype(jnp.int32)

    def pred_part(one, two, more, cuts, *others):
        return pred_call(after(ids, *others), (one, two), expr4, keep_row, masses, totals, more, cuts)

    masses, types, totals, *far = expo_call(
        ids, ((2, 0), (2, 1)), map_logits, kind2, filt2, expr4
    )
    far_right, far_left = along(far[0], 1), along(far[1], -1)
    near = pred_part((1, 1), (-1, 0), (), 2, *far)
    near_right, near_left = along(near[0], 1), along(near[1], -1)
    late = pred_part((1, 0), (-1, 1), (far_right, far_left), 1, *near)
    late_right, late_left = along(late[0], 1), along(late[1], -1)
    own = pred_part((0, 0), (0, 1), (near_left, near_right), 2, *late)
    mine, *pieces = merge_call(own, (late_right, late_left))
    pieces = [across(piece, step + 1) for step, piece in enumerate(pieces)]
    spatial_squares = jnp.sum(after(spatial, mine) ** 2, axis=0)
    types = types + swap_along(after(types, spatial_squares), 1)
    types = types + swap_along(types, 3)
    spot_rows = stacked([spot_valid, slide_id.astype(F32), spatial_squares])
    mine = after(mine, spot_rows, types)
    piece = mine + pieces[0] + pieces[1] + pieces[2]
    totals = piece[-1]
    piece = piece[:-1].reshape(8, 16, spots)
    share = 1.0 / totals[0]
    mass = totals[1] * share

    got = [across(piece, step) for step in (1, 2, 3)]
    sums, slides = stats_call(
        ids,
        piece,
        spatial.reshape(8, 16, 16, spots),
        spot_rows,
        totals,
    )
    sums = sums + swap_along(sums, 1)
    sums = sums + swap_along(sums, 3)
    mine = after((jnp.stack([piece, got[2]]), jnp.stack([got[1], got[0]])), sums)
    right0, left1 = along(mine[0], 1), along(mine[1], -1)
    right1, left0 = along(mine[1], 1), along(mine[0], -1)
    sums = sums + swap_across(after(sums, *mine), 1)
    sums = sums + swap_across(sums, 3)
    right0, left1, sums = lax.optimization_barrier((right0, left1, sums))
    far0, far1 = along(right0, 1), along(left1, -1)
    genes_slides = jnp.concatenate([sums[:48], slides])
    genes_slides = genes_slides + swap(genes_slides, 0, 0, 0, 1)
    genes_slides = genes_slides + swap(genes_slides, 0, 0, 1, 0)
    genes_slides = after(genes_slides, right1, left0)
    genes_slides = genes_slides + swap(genes_slides, 0, 0, 3, 0)
    pred = [*mine, right0, right1, left0, left1, far0, far1]
    gene_coef, spot_coef, scalars = coef_call(ids, genes_slides, sums, spot_rows, totals)
    spatial4 = spatial.reshape(8, RING, genes // 32, spots)
    grad, column_a = grad_call(ids, pred[:6], spatial4, gene_coef, spot_coef, 0, (0, 1, 2, 3))

    def last_grad(chips, grad, *others):
        return grad_call(
            after(ids, *others), pred[6:], spatial4, gene_coef, spot_coef, 12, chips, (grad,)
        )

    def back_part(steps, grad, *others, **rows):
        return back_call(after(ids, *others), steps, grad, masses, expr, **rows)

    rows = genes // 16
    grad, column_b = last_grad((2,), grad)
    sums_a, far_a = back_part([(2, 1)], grad, first=[spot_coef])
    far_got = swap(far_a, 0, 0, 0, 1)
    sums_b, far_b = back_part([(2, 0)], grad, far_a)
    far = far_b + far_got
    far_up, far_down = up(far[:rows], 1), up(far[rows:], -1)
    grad, column_c = last_grad((1, -1, 0), grad, far)
    sums_c, up_a, down_a, own_a = back_part([(1, 1), (-1, 1), (0, 1)], grad)
    up_got, down_got, own_got = (swap(one, 0, 0, 0, 1) for one in (up_a, down_a, own_a))
    sums_d, up_b, down_b = back_part([(1, 0), (-1, 0)], grad, up_a)
    types = types + swap_across(after(types, up_a), 1)
    above, below = lift_call(up_b, down_b, *after((far_up, far_down), types))
    above, below = join_call(above, below, up_got, down_got)
    near_up, near_down = up(above, 1), up(below, -1)
    types_got = swap_across(after(types, above), 3)
    last, own_b = back_part(
        [(0, 0)], grad, above, below, last=[sums_a, sums_b, sums_c, sums_d, scalars]
    )
    last_got = swap(last, 0, 0, 0, 1)
    own = own_b + own_got

    column = jnp.sum(column_a + column_b + column_c, axis=0) * share + spot_coef[32] * mass
    map_rows = stacked([spot_coef[32], column])
    map_args = (expr, grad.reshape(2, genes, spots), masses, keep2, map_rows, all_cells * genes)
    grad_map = map_call(*map_args)
    types_got, last_got = after((types_got, last_got), grad_map)
    types = types + types_got
    last = after(last + last_got, own)
    got = [up(last, step) for step in (1, 2, 3)]
    grad_weighted = after(own, grad_map) + near_up + near_down
    grad_expr = grad_weighted * (keep * (genes * all_spots))[None, :]

    type_fraction = types * share

    grad_filter, loss_terms = finish_call(
        last, got, totals, scalars, cell_type.reshape(1, cells), filter_logits.reshape(1, cells), all_cells
    )
    return (loss_terms[0, :5], type_fraction, grad_map, grad_filter.reshape(cells), grad_expr)


def solution(mesh):
    in_specs = (
        P("cells", "spots"),
        P("cells"),
        P(None, "cells"),
        P(None, "spots"),
        P("cells"),
        P("spots"),
        P("spots"),
    )
    out_specs = (P(), P(None, "spots"), P("cells", "spots"), P("cells"), P("spots", "cells"))
    return jax.shard_map(
        on_device, mesh=mesh, in_specs=in_specs, out_specs=out_specs, check_vma=False
    )
```

```python
import functools

import jax
import jax.numpy as jnp
from jax import lax
from jax.experimental import pallas as pl
from jax.experimental.pallas import tpu as pltpu
from jax.sharding import PartitionSpec as P

TYPES = 32
SLIDES = 3
RING = 4
F32 = jnp.float32
BF16 = jnp.bfloat16


def vmem(mib):
    return pltpu.CompilerParams(vmem_limit_bytes=mib << 20)


def fixed(shape):
    return pl.BlockSpec(shape, lambda *_: (0,) * len(shape), pipeline_mode=pl.Buffered(1))


def streamed(array):
    return pltpu.with_memory_space_constraint(array, pltpu.HBM)


RESIDENT = pl.BlockSpec(memory_space=pltpu.VMEM)


def cost(flops, moved):
    return pl.CostEstimate(flops=int(flops) // 8, bytes_accessed=int(moved) // 8, transcendentals=0)


NO_COST = pl.CostEstimate(flops=0, bytes_accessed=0, transcendentals=0)


def route(target):
    def flat(z, x, y, core):
        return ((z % RING * RING + x % RING) * RING + y % RING) * 2 + core

    return [
        (flat(z, x, y, core), flat(*target(z, x, y, core)))
        for z in range(RING)
        for x in range(RING)
        for y in range(RING)
        for core in range(2)
    ]


def send(array, target):
    return lax.ppermute(array, ("cells", "spots"), route(target))


def along(array, step):
    return send(array, lambda z, x, y, c: (z, x + step, y, c) if c == 0 else (z + step, x, y, c))


def across(array, step):
    return send(array, lambda z, x, y, c: (z + step, x, y, c) if c == 0 else (z, x + step, y, c))


def up(array, step):
    return send(array, lambda z, x, y, c: (z, x, y + step, c))


def swap(array, mz, mx, my, mc):
    return send(array, lambda z, x, y, c: (z ^ mz, x ^ mx, y ^ my, c ^ mc))


def swap_along(array, mask):
    return send(array, lambda z, x, y, c: (z, x ^ mask, y, c) if c == 0 else (z ^ mask, x, y, c))


def swap_across(array, mask):
    return send(array, lambda z, x, y, c: (z ^ mask, x, y, c) if c == 0 else (z, x ^ mask, y, c))


def after(value, *others):
    return lax.optimization_barrier((value, *others))[0]


def split(value):
    high = value.astype(BF16)
    return high, (value - high.astype(F32)).astype(BF16)


def product(left, right, dims):
    def one(a, b):
        return lax.dot_general(a, b, (dims, ((), ())), preferred_element_type=F32)

    return one(left[0], right[0]) + one(left[0], right[1]) + one(left[1], right[0])


def gene_group(ids, step, half, sub):
    return ((ids[0] + step) & 3) * RING + ((ids[1] + 2 * half + sub) & 3)


PIECES = [
    (step, half, sub)
    for step, half in ((0, 0), (0, 1), (-1, 0), (-1, 1), (1, 0), (1, 1), (2, 0), (2, 1))
    for sub in range(2)
]


def pick(index, values):
    out = values[0]
    for k, value in enumerate(values[1:]):
        out = jnp.where(index == k + 1, value, out)
    return out


def stacked(rows):
    row = lax.broadcasted_iota(jnp.int32, (8, rows[0].shape[0]), 0)
    out = jnp.zeros(row.shape, F32)
    for k, value in enumerate(rows):
        out = jnp.where(row == k, value[None, :], out)
    return out


def as_column(row):
    return jnp.broadcast_to(row, (128, 128)).T[:, :1]


def expo_kernel(ids, logits, kind, filt, *refs):
    expr, (masses, types, totals, out0, out1) = refs[:4], refs[4:]
    step = pl.program_id(0)
    count = logits.shape[0] // 128

    @pl.when(step == 0)
    def _():
        for out in (types, totals, out0, out1):
            out[...] = jnp.zeros_like(out)

    keeps = []
    lane = lax.broadcasted_iota(jnp.int32, (1, totals.shape[1]), 1)
    cell_sums = jnp.zeros(lane.shape, F32)
    for part in range(count):
        rows = slice(part * 128, part * 128 + 128)
        label = kind[pl.ds(step * count + part, 1), :]
        valid = (label >= 0).astype(F32)
        keep = valid * jax.nn.sigmoid(filt[pl.ds(step * count + part, 1), :])
        keeps.append(keep)
        for k, one in enumerate((valid, keep, keep - keep * keep)):
            cell_sums += jnp.where(lane == k, jnp.sum(one, axis=1, keepdims=True), 0.0)
        expo = jnp.exp(logits[rows]) * as_column(valid)
        masses[0, rows], masses[1, rows] = split(expo)
        whole = jnp.sum(expo, axis=0, keepdims=True)
        kept = jnp.sum(expo * as_column(keep), axis=0, keepdims=True)
        row = lax.broadcasted_iota(jnp.int32, types.shape, 0)
        types[...] += jnp.where(row == jnp.max(label, axis=1, keepdims=True), whole, 0.0)
        row = lax.broadcasted_iota(jnp.int32, totals.shape, 0)
        totals[...] += jnp.where(row == 0, whole, jnp.where(row == 1, kept, 0.0))
    totals[2:3, :] += cell_sums
    weighted = jnp.concatenate([part[...].reshape(-1, logits.shape[0]) for part in expr])
    weighted = weighted * jnp.concatenate(keeps, axis=1)
    part = product(split(weighted), masses, ((1,), (0,)))
    half = part.shape[0] // 2
    for index, out in enumerate((out0, out1)):
        new = part[index * half : index * half + half].reshape(-1, 8, part.shape[1])
        out[: half // 8] += new
        out[half // 8] = totals[...]


def expo_call(ids, parts, logits, kind, filt, expr):
    cells, spots = logits.shape
    blocks, groups, rows, _ = expr.shape
    block = 256

    def genes(part, sub):
        return pl.BlockSpec(
            (blocks, 1, rows, block), lambda i, ids: (0, gene_group(ids, *part, sub), 0, i)
        )

    return pl.pallas_call(
        expo_kernel,
        grid_spec=pltpu.PrefetchScalarGridSpec(
            num_scalar_prefetch=1,
            grid=(cells // block,),
            in_specs=[
                pl.BlockSpec((block, spots), lambda i, w: (i, 0)),
                fixed(kind.shape),
                fixed(filt.shape),
            ]
            + [genes(part, sub) for part in parts for sub in range(2)],
            out_specs=[
                pl.BlockSpec((2, block, spots), lambda i, w: (0, i, 0)),
                fixed((TYPES, spots)),
                fixed((8, spots)),
                fixed((blocks * rows // 4 + 1, 8, spots)),
                fixed((blocks * rows // 4 + 1, 8, spots)),
            ],
        ),
        out_shape=[
            jax.ShapeDtypeStruct((2, cells, spots), BF16),
            jax.ShapeDtypeStruct((TYPES, spots), F32),
            jax.ShapeDtypeStruct((8, spots), F32),
            jax.ShapeDtypeStruct((blocks * rows // 4 + 1, 8, spots), F32),
            jax.ShapeDtypeStruct((blocks * rows // 4 + 1, 8, spots), F32),
        ],
        compiler_params=vmem(16),
        cost_estimate=cost(0, cells * spots * 8),
        name="expo",
    )(ids, streamed(logits), streamed(kind), streamed(filt), *[streamed(expr)] * 4)


def pred_kernel(ids, expr_a, expr_b, keep, masses, totals, *refs, cuts):
    more, outs = refs[:-2], refs[-2:]
    rows = 2 * expr_a.shape[0] * expr_a.shape[2]
    weighted = jnp.concatenate(
        [part[...].reshape(rows // 2, keep.shape[1]) for part in (expr_a, expr_b)]
    )
    weighted = split(weighted * keep[...])
    width = masses.shape[2] // cuts

    def half(index, _):
        columns = pl.ds(pl.multiple_of(index * width, width), width)
        part = product(weighted, (masses[0, :, columns], masses[1, :, columns]), ((1,), (0,)))
        part = part.reshape(rows // 8, 8, width)
        for step, out in enumerate(outs):

            @pl.when(pl.program_id(0) == step)
            def _(step=step, out=out):
                if more:
                    out[: rows // 8, :, columns] = part + more[step][: rows // 8, :, columns]
                    out[rows // 8, :, columns] = totals[:, columns] + more[step][rows // 8, :, columns]
                else:
                    out[: rows // 8, :, columns] = part
                    out[rows // 8, :, columns] = totals[:, columns]

        return 0

    lax.fori_loop(0, cuts, half, 0)


def pred_call(ids, parts, expr, keep, masses, totals, more, cuts):
    blocks, groups, rows, cells = expr.shape
    spots = masses.shape[2]
    tiles = blocks * rows // 4 + 1

    def genes(sub):
        def place(i, ids):
            step, half = (pick(i, [part[k] for part in parts]) for k in range(2))
            return (0, gene_group(ids, step, half, sub), 0, 0)

        return pl.BlockSpec((blocks, 1, rows, cells), place)

    return pl.pallas_call(
        functools.partial(pred_kernel, cuts=cuts),
        grid_spec=pltpu.PrefetchScalarGridSpec(
            num_scalar_prefetch=1,
            grid=(2,),
            in_specs=[
                genes(0),
                genes(1),
                fixed((1, cells)),
                RESIDENT,
                fixed((8, spots)),
            ]
            + [RESIDENT] * len(more),
            out_specs=[RESIDENT] * 2,
        ),
        out_shape=[jax.ShapeDtypeStruct((tiles, 8, spots), F32)] * 2,
        compiler_params=vmem(16),
        cost_estimate=cost(24 * blocks * rows * cells * spots, 4 * cells * spots + 16 * blocks * rows * (cells + spots)),
        name="pred",
    )(ids, *[streamed(expr)] * 2, keep, masses, totals, *more)


def merge_kernel(own0, own1, got0, got1, *outs):
    tiles = outs[0].shape[0] - 1
    for half, (own, got) in enumerate(((own0, got0), (own1, got1))):
        for sub in range(2):
            out = outs[2 * half + sub]
            out[:tiles] = own[sub * tiles : sub * tiles + tiles] + got[sub * tiles : sub * tiles + tiles]
            out[tiles] = own[2 * tiles] + got[2 * tiles]


def merge_call(own, got):
    tiles, _, spots = own[0].shape
    block = 256
    whole = pl.BlockSpec((tiles, 8, block), lambda i: (0, 0, i))
    piece = (tiles // 2 + 1, 8, spots)
    return pl.pallas_call(
        merge_kernel,
        grid=(spots // block,),
        in_specs=[whole] * 4,
        out_specs=[pl.BlockSpec((tiles // 2 + 1, 8, block), lambda i: (0, 0, i))] * 4,
        out_shape=[jax.ShapeDtypeStruct(piece, F32)] * 4,
        compiler_params=vmem(12),
        cost_estimate=NO_COST,
        name="merge",
    )(*own, *got)


def stats_kernel(ids, piece, spatial, spot, totals, gene, slide_sums):
    rows = piece.shape[0] * piece.shape[1]
    valid, slide = spot[0:1, :], spot[1:2, :]
    share = 1.0 / totals[0:1, :]
    mass = totals[1:2, :] * share
    value = piece[...].reshape(rows, piece.shape[2]) * share
    data = spatial[...].reshape(value.shape)
    cross, square = value * data, value * value
    lane = lax.broadcasted_iota(jnp.int32, (rows, 128), 1)
    sums = jnp.zeros((rows, 128), F32)
    for index, one in enumerate((cross, square, data * data)):
        sums = jnp.where(lane == index, jnp.sum(one * valid, axis=1, keepdims=True), sums)
    sums = sums.T
    gene[...] = jnp.zeros_like(gene)
    slide_sums[...] = jnp.zeros_like(slide_sums)
    for index in range(3):
        gene[pl.ds(16 * index + gene_group(ids, 0, 0, 0), 1), :] = sums[index : index + 1, :]
    lane = lax.broadcasted_iota(jnp.int32, (1, 128), 1)
    slides = jnp.zeros((1, 128), F32)
    logs = jnp.log(jnp.where(valid > 0, mass, 1.0))
    for k in range(SLIDES):
        inside = jnp.where(slide == k, valid, 0.0)
        for index, one in enumerate((inside, inside * mass, inside * logs)):
            total = jnp.sum(one, axis=1, keepdims=True)
            slides = jnp.where(lane == 3 * index + k, total, slides)
    slide_sums[0:1, :] = slides
    for index, one in enumerate((cross, square)):
        total = jnp.sum(one, axis=0, keepdims=True)
        for k in range(total.shape[1] // 128):
            at = 48 + 8 * index + k
            gene[at : at + 1, :] = total[:, 128 * k : 128 * k + 128]


def stats_call(ids, piece, spatial, spot, totals):
    blocks, rows, spots = piece.shape
    return pl.pallas_call(
        stats_kernel,
        grid_spec=pltpu.PrefetchScalarGridSpec(
            num_scalar_prefetch=1,
            grid=(1,),
            in_specs=[
                fixed((blocks, rows, spots)),
                pl.BlockSpec((blocks, 1, rows, spots), lambda i, ids: (0, gene_group(ids, 0, 0, 0), 0, 0)),
                fixed((8, spots)),
                fixed((8, spots)),
            ],
            out_specs=[fixed((64, 128)), fixed((8, 128))],
        ),
        out_shape=[jax.ShapeDtypeStruct((64, 128), F32), jax.ShapeDtypeStruct((8, 128), F32)],
        compiler_params=vmem(8),
        cost_estimate=NO_COST,
        name="stats",
    )(ids, piece, spatial, spot, totals)


def coef_kernel(ids, genes_slides, sums, spot, totals, gene, rows, scalars, pairs):
    valid, slide, squares = (spot[k : k + 1, :] for k in range(3))
    share = 1.0 / totals[0:1, :]
    mass = totals[1:2, :] * share
    genes = float(16 * sums.shape[1])

    def wide(index):
        return jnp.concatenate([sums[index + k : index + k + 1, :] for k in range(8)], axis=1)

    dots, own = wide(48), wide(56)
    dot, aa, bb = genes_slides[0:16, :], genes_slides[16:32, :], genes_slides[32:48, :]
    scale = lax.rsqrt(aa * bb + 1e-06)
    pairs[0:16, :] = dot * scale**3 * bb / genes
    pairs[16:32, :] = scale / genes
    pair = [pairs[pl.ds(k + gene_group(ids, *one), 1), :] for k in (0, 16) for one in PIECES]
    gene[...] = jnp.concatenate([*pair, jnp.zeros((96, 128), F32)]).T
    total = jnp.sum(jnp.sum(dot * scale, axis=1, keepdims=True), axis=0, keepdims=True)
    nvs = jnp.zeros((1, 1), F32)
    density = jnp.zeros((1, 1), F32)
    nk, tk = jnp.ones_like(valid), jnp.ones_like(valid)
    for k in range(SLIDES):
        count, held, logs = (genes_slides[48:49, 3 * j + k : 3 * j + k + 1] for j in range(3))
        some = count > 0
        safe = jnp.where(some, count, 1.0)
        nvs += count
        density += jnp.where(some, jnp.log(jnp.where(some, held, 1.0) / safe) - logs / safe, 0.0)
        here = (slide == k) & (valid > 0)
        nk = jnp.where(here, count, nk)
        tk = jnp.where(here, held, tk)
    scale = lax.rsqrt(own * squares + 1e-06)
    grad_mass = valid / SLIDES * (1.0 / tk - 1.0 / (nk * jnp.where(valid > 0, mass, 1.0)))
    mask = valid * share
    by_pred, by_data = dots * scale**3 * squares / nvs, scale / nvs
    for index, one in enumerate((by_pred * share * mask, by_data * mask, mask, share * mask)):
        rows[8 * index : 8 * index + 8, :] = jnp.broadcast_to(one, (8, one.shape[1]))
    rows[32:40, :] = jnp.concatenate([grad_mass * share, jnp.zeros((7, valid.shape[1]), F32)])
    cosines = jnp.sum(valid * dots * scale, axis=1, keepdims=True)
    lane = lax.broadcasted_iota(jnp.int32, (1, 128), 1)
    out = jnp.zeros((1, 128), F32)
    for index, one in enumerate((total / genes, cosines / nvs, density / SLIDES)):
        out = jnp.where(lane == index, one, out)
    scalars[...] = out


def coef_call(ids, genes_slides, sums, spot, totals):
    spots = spot.shape[1]
    return pl.pallas_call(
        coef_kernel,
        grid_spec=pltpu.PrefetchScalarGridSpec(
            num_scalar_prefetch=1,
            grid=(1,),
            in_specs=[fixed(genes_slides.shape), fixed(sums.shape), fixed((8, spots)), fixed((8, spots))],
            out_specs=[fixed((128, 128)), fixed((40, spots)), fixed((1, 128))],
            scratch_shapes=[pltpu.VMEM((32, 128), F32)],
        ),
        out_shape=[
            jax.ShapeDtypeStruct((128, 128), F32),
            jax.ShapeDtypeStruct((40, spots), F32),
            jax.ShapeDtypeStruct((1, 128), F32),
        ],
        compiler_params=vmem(6),
        cost_estimate=NO_COST,
        name="coef",
    )(ids, genes_slides, sums, spot, totals)


def grad_rows(pred, data, gene, spot, lane):
    by_pred = gene[:, lane : lane + 1].reshape(2, 8, 1)
    by_data = gene[:, 16 + lane : 17 + lane].reshape(2, 8, 1)
    pred, data = pred.reshape(2, 8, pred.shape[1]), data.reshape(2, 8, data.shape[1])
    grad = pred * (by_pred * spot[24:32, :] + spot[0:8, :])
    grad = grad - data * (by_data * spot[16:24, :] + spot[8:16, :])
    return grad.reshape(16, grad.shape[2]), jnp.sum(grad * pred, axis=0)


def grad_kernel(ids, *refs, count, lane, chips):
    pred, data, refs = refs[: 2 * count], refs[2 * count : 3 * count], refs[3 * count :]
    gene, spot, grad, column = refs[0], refs[1], refs[-2], refs[-1]
    step = pl.program_id(0)
    chip = (ids[2] + pick(step, chips)) & 3

    @pl.when(step == 0)
    def _():
        column[...] = jnp.zeros_like(column)

    def half_of(half, _):
        block = chip * 2 + half
        factors = gene[pl.ds(pl.multiple_of(16 * half, 16), 16), :]
        total = jnp.zeros(column.shape, F32)
        for index, part in enumerate(pred):
            for sub in range(2):
                at = gene_group(ids, *PIECES[lane + 2 * index + sub])
                row = pl.multiple_of((at & 3) * 16, 16)
                to = pl.ds(pl.multiple_of(at * 16, 16), 16)
                rows, inner = grad_rows(
                    part[sub, block],
                    data[index // 2][half, 0, pl.ds(row, 16), :],
                    factors,
                    spot,
                    lane + 2 * index + sub,
                )
                grad[0, block, to, :], grad[1, block, to, :] = split(rows)
                total += inner
        column[...] += total
        return 0

    lax.fori_loop(0, 2, half_of, 0)


def grad_call(ids, pred, spatial, gene, spot, lane, chips, done=()):
    blocks, groups, rows, spots = spatial.shape
    count = len(pred) // 2

    def chip(i, ids):
        return (ids[2] + pick(i, chips)) & 3

    def group(k):
        step = PIECES[lane + 4 * k][0]
        return pl.BlockSpec(
            (2, 1, rows, spots), lambda i, ids: (chip(i, ids), (ids[0] + step) & 3, 0, 0)
        )

    return pl.pallas_call(
        functools.partial(grad_kernel, count=count, lane=lane, chips=chips),
        grid_spec=pltpu.PrefetchScalarGridSpec(
            num_scalar_prefetch=1,
            grid=(len(chips),),
            in_specs=[RESIDENT] * (2 * count)
            + [group(k) for k in range(count)]
            + [pl.BlockSpec((32, 128), lambda i, ids: (chip(i, ids), 0)), fixed(spot.shape)]
            + [RESIDENT] * len(done),
            out_specs=[RESIDENT, fixed((8, spots))],
        ),
        out_shape=[
            jax.ShapeDtypeStruct((2, blocks, groups * rows, spots), BF16),
            jax.ShapeDtypeStruct((8, spots), F32),
        ],
        input_output_aliases={3 * count + 3: 0} if done else {},
        compiler_params=vmem(12),
        cost_estimate=NO_COST,
        name="grad",
    )(ids, *pred, *[spatial] * count, gene, spot, *done)


def back_kernel(ids, grad, masses, expr, *refs, parts, first, last):
    more, (sums, *outs), (held, ready) = refs[: first + 5 * last], refs[first + 5 * last : -2], refs[-2:]
    step = pl.program_id(0)
    rows = grad.shape[2]

    def block(part):
        return ((ids[2] + part[0]) & 3) * 2 + (ids[3] ^ part[1])

    def fetch(k):
        start = pl.multiple_of(block(parts[k]) * rows, rows)
        return pltpu.make_async_copy(expr.at[pl.ds(start, rows), :], held.at[k], ready.at[k])

    @pl.when(step == 0)
    def _():
        for k in range(len(parts)):
            fetch(k).start()

    @pl.when(step == 0)
    def _():
        if last:
            sums[...] = more[0][...] + more[1][...] + more[2][...] + more[3][...]
        else:
            sums[...] = jnp.zeros_like(sums)

    here = block([pick(step, [part[k] for part in parts]) for k in range(2)])
    left = grad[0, here], grad[1, here]
    if first:
        pair = split(jnp.concatenate([more[0][...], jnp.zeros_like(more[0])]))
        left = [jnp.concatenate(both) for both in zip(left, pair)]
    part = product(left, masses, ((1,), (1,)))
    if first:
        sums[...] = part[rows : rows + 8]
        part = part[:rows]
    for k, out in enumerate(outs):

        @pl.when(step == k)
        def _(k=k, out=out):
            out[...] = part
            fetch(k).wait()

    sums[...] += jnp.sum((part * held[step]).reshape(-1, 8, part.shape[1]), axis=0)
    if last:

        @pl.when(step == len(parts) - 1)
        def _():
            total = jnp.sum(sums[...], axis=0, keepdims=True)
            sums[...] = jnp.zeros_like(sums)
            sums[0:1, :] = total
            sums[1:2, 0:128] = more[4][...]


def back_call(ids, parts, grad, masses, expr, first=(), last=()):
    _, blocks, rows, spots = grad.shape
    cells = masses.shape[1]
    return pl.pallas_call(
        functools.partial(back_kernel, parts=parts, first=len(first), last=len(last) // 5),
        grid_spec=pltpu.PrefetchScalarGridSpec(
            num_scalar_prefetch=1,
            grid=(len(parts),),
            in_specs=[RESIDENT, RESIDENT, pl.BlockSpec(memory_space=pl.ANY)]
            + [pl.BlockSpec((8, spots), lambda i, ids: (4, 0))] * len(first)
            + [fixed(one.shape) for one in last],
            out_specs=[fixed((8, cells))] + [RESIDENT] * len(parts),
            scratch_shapes=[
                pltpu.VMEM((len(parts), rows, cells), F32),
                pltpu.SemaphoreType.DMA((len(parts),)),
            ],
        ),
        out_shape=[jax.ShapeDtypeStruct((8, cells), F32)]
        + [jax.ShapeDtypeStruct((rows, cells), F32)] * len(parts),
        compiler_params=vmem(22),
        cost_estimate=NO_COST,
        name="back",
    )(ids, grad, masses, streamed(expr), *first, *last)


def lift_kernel(above, below, far_up, far_down, out_above, out_below):
    rows = far_up.shape[0]
    out_above[:rows, :] = above[:rows, :] + far_up[...]
    out_above[rows:, :] = above[rows:, :]
    out_below[:rows, :] = below[:rows, :]
    out_below[rows:, :] = below[rows:, :] + far_down[...]


def lift_call(above, below, far_up, far_down):
    rows, cells = far_up.shape
    block = 256
    far = pl.BlockSpec((rows, block), lambda i: (0, i))
    whole = pl.BlockSpec((2 * rows, block), lambda i: (0, i))
    return pl.pallas_call(
        lift_kernel,
        grid=(cells // block,),
        in_specs=[whole, whole, far, far],
        out_specs=[whole, whole],
        out_shape=[jax.ShapeDtypeStruct(above.shape, F32)] * 2,
        compiler_params=vmem(8),
        cost_estimate=pl.CostEstimate(flops=10**10, bytes_accessed=0, transcendentals=0),
        name="lift",
    )(above, below, far_up, far_down)


def join_kernel(above, below, got_above, got_below, out_above, out_below):
    out_above[...] = above[...] + got_above[...]
    out_below[...] = below[...] + got_below[...]


def join_call(above, below, got_above, got_below):
    rows, cells = above.shape
    whole = pl.BlockSpec((rows, 256), lambda i: (0, i))
    return pl.pallas_call(
        join_kernel,
        grid=(cells // 256,),
        in_specs=[whole] * 4,
        out_specs=[whole] * 2,
        out_shape=[jax.ShapeDtypeStruct(above.shape, F32)] * 2,
        compiler_params=vmem(8),
        cost_estimate=NO_COST,
        name="join",
    )(above, below, got_above, got_below)


def map_kernel(expr, grad, masses, keep, spot, out, held, ready, *, scale):
    index = pl.program_id(0)
    quarter, block = held.shape[2:]
    count = held.shape[1]

    def fetch(at, k):
        columns = pl.ds(pl.multiple_of(at * block, block), block)
        return pltpu.make_async_copy(
            expr.at[pl.ds(k * quarter, quarter), columns], held.at[at & 1, k], ready.at[at & 1, k]
        )

    @pl.when(index == 0)
    def _():
        for k in range(count):
            fetch(index, k).start()

    @pl.when(index + 1 < pl.num_programs(0))
    def _():
        for k in range(count):
            fetch(index + 1, k).start()

    inner = spot[0:1, :]
    for k in range(count):
        fetch(index, k).wait()
        rows = slice(k * quarter, k * quarter + quarter)
        pair = grad[0, rows, :], grad[1, rows, :]
        inner = inner + product(split(held[index & 1, k]), pair, ((0,), (0,)))
    at = pl.multiple_of(index * block, block)
    expo = masses[0, pl.ds(at, block), :].astype(F32) + masses[1, pl.ds(at, block), :].astype(F32)
    for part in range(block // 128):
        rows = slice(part * 128, part * 128 + 128)
        weight = as_column(keep[pl.ds(index * (block // 128) + part, 1), :])
        out[rows, :] = (scale * expo[rows]) * (weight * inner[rows] - spot[1:2, :])


def map_call(expr, grad, masses, keep, spot, scale):
    genes, cells = expr.shape
    spots = masses.shape[2]
    block, count = 256, 4
    return pl.pallas_call(
        functools.partial(map_kernel, scale=scale),
        grid=(cells // block,),
        in_specs=[
            pl.BlockSpec(memory_space=pl.ANY),
            RESIDENT,
            RESIDENT,
            fixed(keep.shape),
            fixed((8, spots)),
        ],
        out_specs=pl.BlockSpec((block, spots), lambda i: (i, 0)),
        out_shape=jax.ShapeDtypeStruct((cells, spots), F32),
        scratch_shapes=[
            pltpu.VMEM((2, count, genes // count, block), F32),
            pltpu.SemaphoreType.DMA((2, count)),
        ],
        compiler_params=vmem(24),
        cost_estimate=NO_COST,
        name="grad_map",
    )(streamed(expr), grad, masses, keep, spot)


def finish_kernel(last, got1, got2, got3, totals, scalars, kind, filt, grad_filter, terms, *, all_cells):
    total = (last[...] + got2[...]) + (got1[...] + got3[...])
    nvalid, retained, reg_sum = (totals[2:3, k : k + 1] for k in range(3))
    valid = (kind[...] >= 0).astype(F32)
    sigma = jax.nn.sigmoid(filt[...])
    keep = sigma * valid
    shifted = (retained - 0.35 * nvalid) / (0.1 * all_cells)
    count_term = jnp.sqrt(shifted * shifted + 1.0)
    grad_keep = total[0:1, :] + shifted / count_term / (0.1 * all_cells) + (1.0 - 2.0 * keep) / nvalid
    row = valid * sigma * (1.0 - sigma) * grad_keep * all_cells
    for k in range(grad_filter.shape[0]):
        grad_filter[k : k + 1, :] = row[:, 128 * k : 128 * k + 128]
    lane = lax.broadcasted_iota(jnp.int32, (1, 128), 1)
    out = jnp.zeros((1, 128), F32)
    parts = (scalars[:, 0:1], total[1:2, 1:2], scalars[:, 2:3], count_term, reg_sum / nvalid)
    for index, one in enumerate(parts):
        out = jnp.where(lane == index, one, out)
    terms[...] = out[0, :5]


def finish_call(last, got, totals, scalars, kind, filt, all_cells):
    return pl.pallas_call(
        functools.partial(finish_kernel, all_cells=float(all_cells)),
        grid=(1,),
        in_specs=[fixed(one.shape) for one in (last, *got, totals, scalars, kind, filt)],
        out_specs=[fixed((kind.shape[1] // 128, 128)), fixed((5,))],
        out_shape=[
            jax.ShapeDtypeStruct((kind.shape[1] // 128, 128), F32),
            jax.ShapeDtypeStruct((5,), F32),
        ],
        compiler_params=vmem(4),
        cost_estimate=NO_COST,
        name="finish",
    )(last, *got, totals, scalars, kind, filt)


def on_device(map_logits, filter_logits, expr, spatial, cell_type, slide_id, spot_mask):
    genes, cells = expr.shape
    spots = map_logits.shape[1]
    all_cells = cells * lax.axis_size("cells")
    all_spots = spots * lax.axis_size("spots")
    cell_place = lax.axis_index("cells")
    z, x = cell_place >> 2, cell_place & 3
    spot_place = lax.axis_index("spots")
    y, core = spot_place >> 1, spot_place & 1
    first = jnp.where(core == 0, x, z)
    second = jnp.where(core == 0, z, x)
    blocks = cells // 128

    valid = (cell_type >= 0).astype(F32)
    sigma = jax.nn.sigmoid(filter_logits)
    keep = sigma * valid
    spot_valid = spot_mask.astype(F32)
    kind2 = cell_type.reshape(blocks, 128)
    filt2 = filter_logits.reshape(blocks, 128)
    keep2 = keep.reshape(blocks, 128)

    expr4 = expr.reshape(8, 16, 16, cells)
    keep_row = keep.reshape(1, cells)

    ids = jnp.stack([first, second, y, core]).astype(jnp.int32)

    def pred_part(one, two, more, cuts, *others):
        return pred_call(after(ids, *others), (one, two), expr4, keep_row, masses, totals, more, cuts)

    masses, types, totals, *far = expo_call(
        ids, ((2, 0), (2, 1)), map_logits, kind2, filt2, expr4
    )
    far_right, far_left = along(far[0], 1), along(far[1], -1)
    near = pred_part((1, 1), (-1, 0), (), 2, *far)
    near_right, near_left = along(near[0], 1), along(near[1], -1)
    late = pred_part((1, 0), (-1, 1), (far_right, far_left), 1, *near)
    late_right, late_left = along(late[0], 1), along(late[1], -1)
    own = pred_part((0, 0), (0, 1), (near_left, near_right), 2, *late)
    mine, *pieces = merge_call(own, (late_right, late_left))
    pieces = [across(piece, step + 1) for step, piece in enumerate(pieces)]
    spatial_squares = jnp.sum(after(spatial, mine) ** 2, axis=0)
    types = types + swap_along(after(types, spatial_squares), 1)
    spot_rows = stacked([spot_valid, slide_id.astype(F32), spatial_squares])
    mine = after(mine, spot_rows, types)
    piece = mine + pieces[0] + pieces[1] + pieces[2]
    totals = piece[-1]
    piece = piece[:-1].reshape(8, 16, spots)
    share = 1.0 / totals[0]
    mass = totals[1] * share

    got = [across(piece, step) for step in (1, 2, 3)]
    sums, slides = stats_call(
        ids,
        piece,
        spatial.reshape(8, 16, 16, spots),
        spot_rows,
        totals,
    )
    sums = sums + swap_along(sums, 1)
    sums = sums + swap_along(sums, 3)
    types = types + swap_along(after(types, slides), 3)
    mine = after((jnp.stack([piece, got[2]]), jnp.stack([got[1], got[0]])), sums, types)
    right0, left1 = along(mine[0], 1), along(mine[1], -1)
    right1, left0 = along(mine[1], 1), along(mine[0], -1)
    sums = sums + swap_across(after(sums, *mine), 1)
    sums = sums + swap_across(sums, 3)
    right0, left1, sums = lax.optimization_barrier((right0, left1, sums))
    far0, far1 = along(right0, 1), along(left1, -1)
    genes_slides = jnp.concatenate([sums[:48], slides])
    genes_slides = genes_slides + swap(genes_slides, 0, 0, 0, 1)
    genes_slides = genes_slides + swap(genes_slides, 0, 0, 1, 0)
    genes_slides = after(genes_slides, right1, left0)
    genes_slides = genes_slides + swap(genes_slides, 0, 0, 3, 0)
    pred = [*mine, right0, right1, left0, left1, far0, far1]
    gene_coef, spot_coef, scalars = coef_call(ids, genes_slides, sums, spot_rows, totals)
    spatial4 = spatial.reshape(8, RING, genes // 32, spots)
    grad, column_a = grad_call(ids, pred[:6], spatial4, gene_coef, spot_coef, 0, (0, 1, 2, 3))

    def last_grad(chips, grad, *others):
        return grad_call(
            after(ids, *others), pred[6:], spatial4, gene_coef, spot_coef, 12, chips, (grad,)
        )

    def back_part(steps, grad, *others, **rows):
        return back_call(after(ids, *others), steps, grad, masses, expr, **rows)

    rows = genes // 16
    grad, column_b = last_grad((2,), grad)
    sums_a, far_a = back_part([(2, 1)], grad, first=[spot_coef])
    far_got = swap(far_a, 0, 0, 0, 1)
    sums_b, far_b = back_part([(2, 0)], grad, far_a)
    far = far_b + far_got
    far_up, far_down = up(far[:rows], 1), up(far[rows:], -1)
    grad, column_c = last_grad((1, -1, 0), grad, far)
    sums_c, up_a, down_a, own_a = back_part([(1, 1), (-1, 1), (0, 1)], grad)
    up_got, down_got, own_got = (swap(one, 0, 0, 0, 1) for one in (up_a, down_a, own_a))
    sums_d, up_b, down_b = back_part([(1, 0), (-1, 0)], grad, up_a)
    types = types + swap_across(after(types, up_a), 1)
    above, below = lift_call(up_b, down_b, *after((far_up, far_down), types))
    above, below = join_call(above, below, up_got, down_got)
    near_up, near_down = up(above, 1), up(below, -1)
    types_got = swap_across(after(types, above), 3)
    last, own_b = back_part(
        [(0, 0)], grad, above, below, last=[sums_a, sums_b, sums_c, sums_d, scalars]
    )
    last_got = swap(last, 0, 0, 0, 1)
    own = own_b + own_got

    column = jnp.sum(column_a + column_b + column_c, axis=0) * share + spot_coef[32] * mass
    map_rows = stacked([spot_coef[32], column])
    map_args = (expr, grad.reshape(2, genes, spots), masses, keep2, map_rows, all_cells * genes)
    grad_map = map_call(*map_args)
    types_got, last_got = after((types_got, last_got), grad_map)
    types = types + types_got
    last = after(last + last_got, own)
    got = [up(last, step) for step in (1, 2, 3)]
    grad_weighted = after(own, grad_map) + near_up + near_down
    grad_expr = grad_weighted * (keep * (genes * all_spots))[None, :]

    type_fraction = types * share

    grad_filter, loss_terms = finish_call(
        last, got, totals, scalars, cell_type.reshape(1, cells), filter_logits.reshape(1, cells), all_cells
    )
    return (loss_terms, type_fraction, grad_map, grad_filter.reshape(cells), grad_expr)


def solution(mesh):
    in_specs = (
        P("cells", "spots"),
        P("cells"),
        P(None, "cells"),
        P(None, "spots"),
        P("cells"),
        P("spots"),
        P("spots"),
    )
    out_specs = (P(), P(None, "spots"), P("cells", "spots"), P("cells"), P("spots", "cells"))
    return jax.shard_map(
        on_device, mesh=mesh, in_specs=in_specs, out_specs=out_specs, check_vma=False
    )
```

```python
import functools

import jax
import jax.numpy as jnp
from jax import lax
from jax.experimental import pallas as pl
from jax.experimental.pallas import tpu as pltpu
from jax.sharding import PartitionSpec as P

TYPES = 32
SLIDES = 3
RING = 4
F32 = jnp.float32
BF16 = jnp.bfloat16


def vmem(mib):
    return pltpu.CompilerParams(vmem_limit_bytes=mib << 20)


def fixed(shape):
    return pl.BlockSpec(shape, lambda *_: (0,) * len(shape), pipeline_mode=pl.Buffered(1))


def streamed(array):
    return pltpu.with_memory_space_constraint(array, pltpu.HBM)


RESIDENT = pl.BlockSpec(memory_space=pltpu.VMEM)


def cost(flops, moved):
    return pl.CostEstimate(flops=int(flops) // 8, bytes_accessed=int(moved) // 8, transcendentals=0)


NO_COST = pl.CostEstimate(flops=0, bytes_accessed=0, transcendentals=0)


def route(target):
    def flat(z, x, y, core):
        return ((z % RING * RING + x % RING) * RING + y % RING) * 2 + core

    return [
        (flat(z, x, y, core), flat(*target(z, x, y, core)))
        for z in range(RING)
        for x in range(RING)
        for y in range(RING)
        for core in range(2)
    ]


def send(array, target):
    return lax.ppermute(array, ("cells", "spots"), route(target))


def along(array, step):
    return send(array, lambda z, x, y, c: (z, x + step, y, c) if c == 0 else (z + step, x, y, c))


def across(array, step):
    return send(array, lambda z, x, y, c: (z + step, x, y, c) if c == 0 else (z, x + step, y, c))


def up(array, step):
    return send(array, lambda z, x, y, c: (z, x, y + step, c))


def swap(array, mz, mx, my, mc):
    return send(array, lambda z, x, y, c: (z ^ mz, x ^ mx, y ^ my, c ^ mc))


def swap_along(array, mask):
    return send(array, lambda z, x, y, c: (z, x ^ mask, y, c) if c == 0 else (z ^ mask, x, y, c))


def swap_across(array, mask):
    return send(array, lambda z, x, y, c: (z ^ mask, x, y, c) if c == 0 else (z, x ^ mask, y, c))


def after(value, *others):
    return lax.optimization_barrier((value, *others))[0]


def split(value):
    high = value.astype(BF16)
    return high, (value - high.astype(F32)).astype(BF16)


def product(left, right, dims):
    def one(a, b):
        return lax.dot_general(a, b, (dims, ((), ())), preferred_element_type=F32)

    return one(left[0], right[0]) + one(left[0], right[1]) + one(left[1], right[0])


def gene_group(ids, step, half, sub):
    return ((ids[0] + step) & 3) * RING + ((ids[1] + 2 * half + sub) & 3)


PIECES = [
    (step, half, sub)
    for step, half in ((0, 0), (0, 1), (-1, 0), (-1, 1), (1, 0), (1, 1), (2, 0), (2, 1))
    for sub in range(2)
]


def pick(index, values):
    out = values[0]
    for k, value in enumerate(values[1:]):
        out = jnp.where(index == k + 1, value, out)
    return out


def stacked(rows):
    row = lax.broadcasted_iota(jnp.int32, (8, rows[0].shape[0]), 0)
    out = jnp.zeros(row.shape, F32)
    for k, value in enumerate(rows):
        out = jnp.where(row == k, value[None, :], out)
    return out


def as_column(row):
    return jnp.broadcast_to(row, (128, 128)).T[:, :1]


def expo_kernel(ids, logits, kind, filt, *refs):
    expr, (masses, types, totals, out0, out1) = refs[:4], refs[4:]
    step = pl.program_id(0)
    block = logits.shape[0]
    count = block // 128

    @pl.when(step == 0)
    def _():
        for out in (types, totals, out0, out1):
            out[...] = jnp.zeros_like(out)

    masses[0], masses[1] = split(jnp.exp(logits[...]))
    labels = [kind[pl.ds(step * count + part, 1), :] for part in range(count)]
    valids = [(label >= 0).astype(F32) for label in labels]
    keeps = [
        valid * jax.nn.sigmoid(filt[pl.ds(step * count + part, 1), :])
        for part, valid in enumerate(valids)
    ]
    keep = jnp.concatenate(keeps, axis=1)
    lane = lax.broadcasted_iota(jnp.int32, (1, block), 1) // 128
    valid = jnp.concatenate(valids, axis=1)
    row = lax.broadcasted_iota(jnp.int32, (16, block), 0)
    extra = jnp.where(row == count, keep, jnp.where(row == lane, valid, 0.0))
    weighted = jnp.concatenate([part[...].reshape(-1, block) for part in expr]) * keep
    part = product(split(jnp.concatenate([weighted, extra])), masses, ((1,), (0,)))
    half = weighted.shape[0] // 2
    whole = [part[2 * half + k : 2 * half + k + 1] for k in range(count + 1)]
    row = lax.broadcasted_iota(jnp.int32, types.shape, 0)
    for label, one in zip(labels, whole):
        types[...] += jnp.where(row == jnp.max(label, axis=1, keepdims=True), one, 0.0)
    lane = lax.broadcasted_iota(jnp.int32, (1, totals.shape[1]), 1)
    cell_sums = jnp.zeros(lane.shape, F32)
    for k, one in enumerate((valid, keep, keep - keep * keep)):
        cell_sums += jnp.where(lane == k, jnp.sum(one, axis=1, keepdims=True), 0.0)
    totals[0:1, :] += sum(whole[1:count], whole[0])
    totals[1:2, :] += whole[count]
    totals[2:3, :] += cell_sums
    for index, out in enumerate((out0, out1)):
        new = part[index * half : index * half + half].reshape(-1, 8, part.shape[1])
        out[: half // 8] += new
        out[half // 8] = totals[...]


def expo_call(ids, parts, logits, kind, filt, expr):
    cells, spots = logits.shape
    blocks, groups, rows, _ = expr.shape
    block = 256

    def genes(part, sub):
        return pl.BlockSpec(
            (blocks, 1, rows, block), lambda i, ids: (0, gene_group(ids, *part, sub), 0, i)
        )

    return pl.pallas_call(
        expo_kernel,
        grid_spec=pltpu.PrefetchScalarGridSpec(
            num_scalar_prefetch=1,
            grid=(cells // block,),
            in_specs=[
                pl.BlockSpec((block, spots), lambda i, w: (i, 0)),
                fixed(kind.shape),
                fixed(filt.shape),
            ]
            + [genes(part, sub) for part in parts for sub in range(2)],
            out_specs=[
                pl.BlockSpec((2, block, spots), lambda i, w: (0, i, 0)),
                fixed((TYPES, spots)),
                fixed((8, spots)),
                fixed((blocks * rows // 4 + 1, 8, spots)),
                fixed((blocks * rows // 4 + 1, 8, spots)),
            ],
        ),
        out_shape=[
            jax.ShapeDtypeStruct((2, cells, spots), BF16),
            jax.ShapeDtypeStruct((TYPES, spots), F32),
            jax.ShapeDtypeStruct((8, spots), F32),
            jax.ShapeDtypeStruct((blocks * rows // 4 + 1, 8, spots), F32),
            jax.ShapeDtypeStruct((blocks * rows // 4 + 1, 8, spots), F32),
        ],
        compiler_params=vmem(16),
        cost_estimate=cost(0, cells * spots * 8),
        name="expo",
    )(ids, streamed(logits), streamed(kind), streamed(filt), *[streamed(expr)] * 4)


def pred_kernel(ids, expr_a, expr_b, keep, masses, totals, *refs, cuts):
    more, outs = refs[:-2], refs[-2:]
    rows = 2 * expr_a.shape[0] * expr_a.shape[2]
    weighted = jnp.concatenate(
        [part[...].reshape(rows // 2, keep.shape[1]) for part in (expr_a, expr_b)]
    )
    weighted = split(weighted * keep[...])
    width = masses.shape[2] // cuts

    def half(index, _):
        columns = pl.ds(pl.multiple_of(index * width, width), width)
        part = product(weighted, (masses[0, :, columns], masses[1, :, columns]), ((1,), (0,)))
        part = part.reshape(rows // 8, 8, width)
        for step, out in enumerate(outs):

            @pl.when(pl.program_id(0) == step)
            def _(step=step, out=out):
                if more:
                    out[: rows // 8, :, columns] = part + more[step][: rows // 8, :, columns]
                    out[rows // 8, :, columns] = totals[:, columns] + more[step][rows // 8, :, columns]
                else:
                    out[: rows // 8, :, columns] = part
                    out[rows // 8, :, columns] = totals[:, columns]

        return 0

    lax.fori_loop(0, cuts, half, 0)


def pred_call(ids, parts, expr, keep, masses, totals, more, cuts):
    blocks, groups, rows, cells = expr.shape
    spots = masses.shape[2]
    tiles = blocks * rows // 4 + 1

    def genes(sub):
        def place(i, ids):
            step, half = (pick(i, [part[k] for part in parts]) for k in range(2))
            return (0, gene_group(ids, step, half, sub), 0, 0)

        return pl.BlockSpec((blocks, 1, rows, cells), place)

    return pl.pallas_call(
        functools.partial(pred_kernel, cuts=cuts),
        grid_spec=pltpu.PrefetchScalarGridSpec(
            num_scalar_prefetch=1,
            grid=(2,),
            in_specs=[
                genes(0),
                genes(1),
                fixed((1, cells)),
                RESIDENT,
                fixed((8, spots)),
            ]
            + [RESIDENT] * len(more),
            out_specs=[RESIDENT] * 2,
        ),
        out_shape=[jax.ShapeDtypeStruct((tiles, 8, spots), F32)] * 2,
        compiler_params=vmem(16),
        cost_estimate=cost(24 * blocks * rows * cells * spots, 4 * cells * spots + 16 * blocks * rows * (cells + spots)),
        name="pred",
    )(ids, *[streamed(expr)] * 2, keep, masses, totals, *more)


def merge_kernel(own0, own1, got0, got1, *outs):
    tiles = outs[0].shape[0] - 1
    for half, (own, got) in enumerate(((own0, got0), (own1, got1))):
        for sub in range(2):
            out = outs[2 * half + sub]
            out[:tiles] = own[sub * tiles : sub * tiles + tiles] + got[sub * tiles : sub * tiles + tiles]
            out[tiles] = own[2 * tiles] + got[2 * tiles]


def merge_call(own, got):
    tiles, _, spots = own[0].shape
    block = 256
    whole = pl.BlockSpec((tiles, 8, block), lambda i: (0, 0, i))
    piece = (tiles // 2 + 1, 8, spots)
    return pl.pallas_call(
        merge_kernel,
        grid=(spots // block,),
        in_specs=[whole] * 4,
        out_specs=[pl.BlockSpec((tiles // 2 + 1, 8, block), lambda i: (0, 0, i))] * 4,
        out_shape=[jax.ShapeDtypeStruct(piece, F32)] * 4,
        compiler_params=vmem(12),
        cost_estimate=NO_COST,
        name="merge",
    )(*own, *got)


def stats_kernel(ids, piece, spatial, spot, totals, gene, slide_sums):
    rows = piece.shape[0] * piece.shape[1]
    valid, slide = spot[0:1, :], spot[1:2, :]
    share = 1.0 / totals[0:1, :]
    mass = totals[1:2, :] * share
    value = piece[...].reshape(rows, piece.shape[2]) * share
    data = spatial[...].reshape(value.shape)
    cross, square = value * data, value * value
    lane = lax.broadcasted_iota(jnp.int32, (rows, 128), 1)
    sums = jnp.zeros((rows, 128), F32)
    for index, one in enumerate((cross, square, data * data)):
        sums = jnp.where(lane == index, jnp.sum(one * valid, axis=1, keepdims=True), sums)
    sums = sums.T
    gene[...] = jnp.zeros_like(gene)
    slide_sums[...] = jnp.zeros_like(slide_sums)
    for index in range(3):
        gene[pl.ds(16 * index + gene_group(ids, 0, 0, 0), 1), :] = sums[index : index + 1, :]
    lane = lax.broadcasted_iota(jnp.int32, (1, 128), 1)
    slides = jnp.zeros((1, 128), F32)
    logs = jnp.log(jnp.where(valid > 0, mass, 1.0))
    for k in range(SLIDES):
        inside = jnp.where(slide == k, valid, 0.0)
        for index, one in enumerate((inside, inside * mass, inside * logs)):
            total = jnp.sum(one, axis=1, keepdims=True)
            slides = jnp.where(lane == 3 * index + k, total, slides)
    slide_sums[0:1, :] = slides
    for index, one in enumerate((cross, square)):
        total = jnp.sum(one, axis=0, keepdims=True)
        for k in range(total.shape[1] // 128):
            at = 48 + 8 * index + k
            gene[at : at + 1, :] = total[:, 128 * k : 128 * k + 128]


def stats_call(ids, piece, spatial, spot, totals):
    blocks, rows, spots = piece.shape
    return pl.pallas_call(
        stats_kernel,
        grid_spec=pltpu.PrefetchScalarGridSpec(
            num_scalar_prefetch=1,
            grid=(1,),
            in_specs=[
                fixed((blocks, rows, spots)),
                pl.BlockSpec((blocks, 1, rows, spots), lambda i, ids: (0, gene_group(ids, 0, 0, 0), 0, 0)),
                fixed((8, spots)),
                fixed((8, spots)),
            ],
            out_specs=[fixed((64, 128)), fixed((8, 128))],
        ),
        out_shape=[jax.ShapeDtypeStruct((64, 128), F32), jax.ShapeDtypeStruct((8, 128), F32)],
        compiler_params=vmem(8),
        cost_estimate=NO_COST,
        name="stats",
    )(ids, piece, spatial, spot, totals)


def coef_kernel(ids, genes_slides, sums, spot, totals, gene, rows, scalars, pairs):
    valid, slide, squares = (spot[k : k + 1, :] for k in range(3))
    share = 1.0 / totals[0:1, :]
    mass = totals[1:2, :] * share
    genes = float(16 * sums.shape[1])

    def wide(index):
        return jnp.concatenate([sums[index + k : index + k + 1, :] for k in range(8)], axis=1)

    dots, own = wide(48), wide(56)
    dot, aa, bb = genes_slides[0:16, :], genes_slides[16:32, :], genes_slides[32:48, :]
    scale = lax.rsqrt(aa * bb + 1e-06)
    pairs[0:16, :] = dot * scale**3 * bb / genes
    pairs[16:32, :] = scale / genes
    pair = [pairs[pl.ds(k + gene_group(ids, *one), 1), :] for k in (0, 16) for one in PIECES]
    gene[...] = jnp.concatenate([*pair, jnp.zeros((96, 128), F32)]).T
    total = jnp.sum(jnp.sum(dot * scale, axis=1, keepdims=True), axis=0, keepdims=True)
    nvs = jnp.zeros((1, 1), F32)
    density = jnp.zeros((1, 1), F32)
    nk, tk = jnp.ones_like(valid), jnp.ones_like(valid)
    for k in range(SLIDES):
        count, held, logs = (genes_slides[48:49, 3 * j + k : 3 * j + k + 1] for j in range(3))
        some = count > 0
        safe = jnp.where(some, count, 1.0)
        nvs += count
        density += jnp.where(some, jnp.log(jnp.where(some, held, 1.0) / safe) - logs / safe, 0.0)
        here = (slide == k) & (valid > 0)
        nk = jnp.where(here, count, nk)
        tk = jnp.where(here, held, tk)
    scale = lax.rsqrt(own * squares + 1e-06)
    grad_mass = valid / SLIDES * (1.0 / tk - 1.0 / (nk * jnp.where(valid > 0, mass, 1.0)))
    mask = valid * share
    by_pred, by_data = dots * scale**3 * squares / nvs, scale / nvs
    for index, one in enumerate((by_pred * share * mask, by_data * mask, mask, share * mask)):
        rows[8 * index : 8 * index + 8, :] = jnp.broadcast_to(one, (8, one.shape[1]))
    rows[32:40, :] = jnp.concatenate([grad_mass * share, jnp.zeros((7, valid.shape[1]), F32)])
    cosines = jnp.sum(valid * dots * scale, axis=1, keepdims=True)
    lane = lax.broadcasted_iota(jnp.int32, (1, 128), 1)
    out = jnp.zeros((1, 128), F32)
    for index, one in enumerate((total / genes, cosines / nvs, density / SLIDES)):
        out = jnp.where(lane == index, one, out)
    scalars[...] = out


def coef_call(ids, genes_slides, sums, spot, totals):
    spots = spot.shape[1]
    return pl.pallas_call(
        coef_kernel,
        grid_spec=pltpu.PrefetchScalarGridSpec(
            num_scalar_prefetch=1,
            grid=(1,),
            in_specs=[fixed(genes_slides.shape), fixed(sums.shape), fixed((8, spots)), fixed((8, spots))],
            out_specs=[fixed((128, 128)), fixed((40, spots)), fixed((1, 128))],
            scratch_shapes=[pltpu.VMEM((32, 128), F32)],
        ),
        out_shape=[
            jax.ShapeDtypeStruct((128, 128), F32),
            jax.ShapeDtypeStruct((40, spots), F32),
            jax.ShapeDtypeStruct((1, 128), F32),
        ],
        compiler_params=vmem(6),
        cost_estimate=NO_COST,
        name="coef",
    )(ids, genes_slides, sums, spot, totals)


def grad_rows(pred, data, gene, spot, lane):
    by_pred = gene[:, lane : lane + 1].reshape(2, 8, 1)
    by_data = gene[:, 16 + lane : 17 + lane].reshape(2, 8, 1)
    pred, data = pred.reshape(2, 8, pred.shape[1]), data.reshape(2, 8, data.shape[1])
    grad = pred * (by_pred * spot[24:32, :] + spot[0:8, :])
    grad = grad - data * (by_data * spot[16:24, :] + spot[8:16, :])
    return grad.reshape(16, grad.shape[2]), jnp.sum(grad * pred, axis=0)


def grad_kernel(ids, *refs, count, lane, chips):
    pred, data, refs = refs[: 2 * count], refs[2 * count : 3 * count], refs[3 * count :]
    gene, spot, grad, column = refs[0], refs[1], refs[-2], refs[-1]
    step = pl.program_id(0)
    chip = (ids[2] + pick(step, chips)) & 3

    @pl.when(step == 0)
    def _():
        column[...] = jnp.zeros_like(column)

    def half_of(half, _):
        block = chip * 2 + half
        factors = gene[pl.ds(pl.multiple_of(16 * half, 16), 16), :]
        total = jnp.zeros(column.shape, F32)
        for index, part in enumerate(pred):
            for sub in range(2):
                at = gene_group(ids, *PIECES[lane + 2 * index + sub])
                row = pl.multiple_of((at & 3) * 16, 16)
                to = pl.ds(pl.multiple_of(at * 16, 16), 16)
                rows, inner = grad_rows(
                    part[sub, block],
                    data[index // 2][half, 0, pl.ds(row, 16), :],
                    factors,
                    spot,
                    lane + 2 * index + sub,
                )
                grad[0, block, to, :], grad[1, block, to, :] = split(rows)
                total += inner
        column[...] += total
        return 0

    lax.fori_loop(0, 2, half_of, 0)


def grad_call(ids, pred, spatial, gene, spot, lane, chips, done=()):
    blocks, groups, rows, spots = spatial.shape
    count = len(pred) // 2

    def chip(i, ids):
        return (ids[2] + pick(i, chips)) & 3

    def group(k):
        step = PIECES[lane + 4 * k][0]
        return pl.BlockSpec(
            (2, 1, rows, spots), lambda i, ids: (chip(i, ids), (ids[0] + step) & 3, 0, 0)
        )

    return pl.pallas_call(
        functools.partial(grad_kernel, count=count, lane=lane, chips=chips),
        grid_spec=pltpu.PrefetchScalarGridSpec(
            num_scalar_prefetch=1,
            grid=(len(chips),),
            in_specs=[RESIDENT] * (2 * count)
            + [group(k) for k in range(count)]
            + [pl.BlockSpec((32, 128), lambda i, ids: (chip(i, ids), 0)), fixed(spot.shape)]
            + [RESIDENT] * len(done),
            out_specs=[RESIDENT, fixed((8, spots))],
        ),
        out_shape=[
            jax.ShapeDtypeStruct((2, blocks, groups * rows, spots), BF16),
            jax.ShapeDtypeStruct((8, spots), F32),
        ],
        input_output_aliases={3 * count + 3: 0} if done else {},
        compiler_params=vmem(12),
        cost_estimate=NO_COST,
        name="grad",
    )(ids, *pred, *[spatial] * count, gene, spot, *done)


def back_kernel(ids, grad, masses, expr, *refs, parts, first, last):
    more, (sums, *outs), (held, ready) = refs[: first + 5 * last], refs[first + 5 * last : -2], refs[-2:]
    step = pl.program_id(0)
    rows = grad.shape[2]

    def block(part):
        return ((ids[2] + part[0]) & 3) * 2 + (ids[3] ^ part[1])

    def fetch(k):
        start = pl.multiple_of(block(parts[k]) * rows, rows)
        return pltpu.make_async_copy(expr.at[pl.ds(start, rows), :], held.at[k], ready.at[k])

    @pl.when(step == 0)
    def _():
        for k in range(len(parts)):
            fetch(k).start()

    @pl.when(step == 0)
    def _():
        if last:
            sums[...] = more[0][...] + more[1][...] + more[2][...] + more[3][...]
        else:
            sums[...] = jnp.zeros_like(sums)

    here = block([pick(step, [part[k] for part in parts]) for k in range(2)])
    left = grad[0, here], grad[1, here]
    if first:
        pair = split(jnp.concatenate([more[0][...], jnp.zeros_like(more[0])]))
        left = [jnp.concatenate(both) for both in zip(left, pair)]
    part = product(left, masses, ((1,), (1,)))
    if first:
        sums[...] = part[rows : rows + 8]
        part = part[:rows]
    for k, out in enumerate(outs):

        @pl.when(step == k)
        def _(k=k, out=out):
            out[...] = part
            fetch(k).wait()

    sums[...] += jnp.sum((part * held[step]).reshape(-1, 8, part.shape[1]), axis=0)
    if last:

        @pl.when(step == len(parts) - 1)
        def _():
            total = jnp.sum(sums[...], axis=0, keepdims=True)
            sums[...] = jnp.zeros_like(sums)
            sums[0:1, :] = total
            sums[1:2, 0:128] = more[4][...]


def back_call(ids, parts, grad, masses, expr, first=(), last=()):
    _, blocks, rows, spots = grad.shape
    cells = masses.shape[1]
    return pl.pallas_call(
        functools.partial(back_kernel, parts=parts, first=len(first), last=len(last) // 5),
        grid_spec=pltpu.PrefetchScalarGridSpec(
            num_scalar_prefetch=1,
            grid=(len(parts),),
            in_specs=[RESIDENT, RESIDENT, pl.BlockSpec(memory_space=pl.ANY)]
            + [pl.BlockSpec((8, spots), lambda i, ids: (4, 0))] * len(first)
            + [fixed(one.shape) for one in last],
            out_specs=[fixed((8, cells))] + [RESIDENT] * len(parts),
            scratch_shapes=[
                pltpu.VMEM((len(parts), rows, cells), F32),
                pltpu.SemaphoreType.DMA((len(parts),)),
            ],
        ),
        out_shape=[jax.ShapeDtypeStruct((8, cells), F32)]
        + [jax.ShapeDtypeStruct((rows, cells), F32)] * len(parts),
        compiler_params=vmem(22),
        cost_estimate=NO_COST,
        name="back",
    )(ids, grad, masses, streamed(expr), *first, *last)


def lift_kernel(above, below, far_up, far_down, out_above, out_below):
    rows = far_up.shape[0]
    out_above[:rows, :] = above[:rows, :] + far_up[...]
    out_above[rows:, :] = above[rows:, :]
    out_below[:rows, :] = below[:rows, :]
    out_below[rows:, :] = below[rows:, :] + far_down[...]


def lift_call(above, below, far_up, far_down):
    rows, cells = far_up.shape
    block = 256
    far = pl.BlockSpec((rows, block), lambda i: (0, i))
    whole = pl.BlockSpec((2 * rows, block), lambda i: (0, i))
    return pl.pallas_call(
        lift_kernel,
        grid=(cells // block,),
        in_specs=[whole, whole, far, far],
        out_specs=[whole, whole],
        out_shape=[jax.ShapeDtypeStruct(above.shape, F32)] * 2,
        compiler_params=vmem(8),
        cost_estimate=pl.CostEstimate(flops=10**10, bytes_accessed=0, transcendentals=0),
        name="lift",
    )(above, below, far_up, far_down)


def join_kernel(above, below, got_above, got_below, out_above, out_below):
    out_above[...] = above[...] + got_above[...]
    out_below[...] = below[...] + got_below[...]


def join_call(above, below, got_above, got_below):
    rows, cells = above.shape
    whole = pl.BlockSpec((rows, 256), lambda i: (0, i))
    return pl.pallas_call(
        join_kernel,
        grid=(cells // 256,),
        in_specs=[whole] * 4,
        out_specs=[whole] * 2,
        out_shape=[jax.ShapeDtypeStruct(above.shape, F32)] * 2,
        compiler_params=vmem(8),
        cost_estimate=NO_COST,
        name="join",
    )(above, below, got_above, got_below)


def map_kernel(expr, grad, masses, keep, valid, spot, out, held, ready, *, scale):
    index = pl.program_id(0)
    quarter, block = held.shape[2:]
    count = held.shape[1]

    def fetch(at, k):
        columns = pl.ds(pl.multiple_of(at * block, block), block)
        return pltpu.make_async_copy(
            expr.at[pl.ds(k * quarter, quarter), columns], held.at[at & 1, k], ready.at[at & 1, k]
        )

    @pl.when(index == 0)
    def _():
        for k in range(count):
            fetch(index, k).start()

    @pl.when(index + 1 < pl.num_programs(0))
    def _():
        for k in range(count):
            fetch(index + 1, k).start()

    inner = spot[0:1, :]
    for k in range(count):
        fetch(index, k).wait()
        rows = slice(k * quarter, k * quarter + quarter)
        pair = grad[0, rows, :], grad[1, rows, :]
        inner = inner + product(split(held[index & 1, k]), pair, ((0,), (0,)))
    at = pl.multiple_of(index * block, block)
    expo = masses[0, pl.ds(at, block), :].astype(F32) + masses[1, pl.ds(at, block), :].astype(F32)
    for part in range(block // 128):
        rows = slice(part * 128, part * 128 + 128)
        place = pl.ds(index * (block // 128) + part, 1)
        weight, mask = as_column(keep[place, :]), as_column(valid[place, :])
        out[rows, :] = (scale * expo[rows]) * (weight * inner[rows] - mask * spot[1:2, :])


def map_call(expr, grad, masses, keep, valid, spot, scale):
    genes, cells = expr.shape
    spots = masses.shape[2]
    block, count = 256, 4
    return pl.pallas_call(
        functools.partial(map_kernel, scale=scale),
        grid=(cells // block,),
        in_specs=[
            pl.BlockSpec(memory_space=pl.ANY),
            RESIDENT,
            RESIDENT,
            fixed(keep.shape),
            fixed(valid.shape),
            fixed((8, spots)),
        ],
        out_specs=pl.BlockSpec((block, spots), lambda i: (i, 0)),
        out_shape=jax.ShapeDtypeStruct((cells, spots), F32),
        scratch_shapes=[
            pltpu.VMEM((2, count, genes // count, block), F32),
            pltpu.SemaphoreType.DMA((2, count)),
        ],
        compiler_params=vmem(24),
        cost_estimate=NO_COST,
        name="grad_map",
    )(streamed(expr), grad, masses, keep, valid, spot)


def finish_kernel(last, got1, got2, got3, totals, scalars, kind, filt, grad_filter, terms, *, all_cells):
    total = (last[...] + got2[...]) + (got1[...] + got3[...])
    nvalid, retained, reg_sum = (totals[2:3, k : k + 1] for k in range(3))
    valid = (kind[...] >= 0).astype(F32)
    sigma = jax.nn.sigmoid(filt[...])
    keep = sigma * valid
    shifted = (retained - 0.35 * nvalid) / (0.1 * all_cells)
    count_term = jnp.sqrt(shifted * shifted + 1.0)
    grad_keep = total[0:1, :] + shifted / count_term / (0.1 * all_cells) + (1.0 - 2.0 * keep) / nvalid
    row = valid * sigma * (1.0 - sigma) * grad_keep * all_cells
    for k in range(grad_filter.shape[0]):
        grad_filter[k : k + 1, :] = row[:, 128 * k : 128 * k + 128]
    lane = lax.broadcasted_iota(jnp.int32, (1, 128), 1)
    out = jnp.zeros((1, 128), F32)
    parts = (scalars[:, 0:1], total[1:2, 1:2], scalars[:, 2:3], count_term, reg_sum / nvalid)
    for index, one in enumerate(parts):
        out = jnp.where(lane == index, one, out)
    terms[...] = out[0, :5]


def finish_call(last, got, totals, scalars, kind, filt, all_cells):
    return pl.pallas_call(
        functools.partial(finish_kernel, all_cells=float(all_cells)),
        grid=(1,),
        in_specs=[fixed(one.shape) for one in (last, *got, totals, scalars, kind, filt)],
        out_specs=[fixed((kind.shape[1] // 128, 128)), fixed((5,))],
        out_shape=[
            jax.ShapeDtypeStruct((kind.shape[1] // 128, 128), F32),
            jax.ShapeDtypeStruct((5,), F32),
        ],
        compiler_params=vmem(4),
        cost_estimate=NO_COST,
        name="finish",
    )(last, *got, totals, scalars, kind, filt)


def on_device(map_logits, filter_logits, expr, spatial, cell_type, slide_id, spot_mask):
    genes, cells = expr.shape
    spots = map_logits.shape[1]
    all_cells = cells * lax.axis_size("cells")
    all_spots = spots * lax.axis_size("spots")
    cell_place = lax.axis_index("cells")
    z, x = cell_place >> 2, cell_place & 3
    spot_place = lax.axis_index("spots")
    y, core = spot_place >> 1, spot_place & 1
    first = jnp.where(core == 0, x, z)
    second = jnp.where(core == 0, z, x)
    blocks = cells // 128

    valid = (cell_type >= 0).astype(F32)
    sigma = jax.nn.sigmoid(filter_logits)
    keep = sigma * valid
    spot_valid = spot_mask.astype(F32)
    kind2 = cell_type.reshape(blocks, 128)
    filt2 = filter_logits.reshape(blocks, 128)
    keep2 = keep.reshape(blocks, 128)

    expr4 = expr.reshape(8, 16, 16, cells)
    keep_row = keep.reshape(1, cells)

    ids = jnp.stack([first, second, y, core]).astype(jnp.int32)

    def pred_part(one, two, more, cuts, *others):
        return pred_call(after(ids, *others), (one, two), expr4, keep_row, masses, totals, more, cuts)

    masses, types, totals, *far = expo_call(
        ids, ((2, 0), (2, 1)), map_logits, kind2, filt2, expr4
    )
    far_right, far_left = along(far[0], 1), along(far[1], -1)
    near = pred_part((1, 1), (-1, 0), (), 2, *far)
    near_right, near_left = along(near[0], 1), along(near[1], -1)
    late = pred_part((1, 0), (-1, 1), (far_right, far_left), 1, *near)
    late_right, late_left = along(late[0], 1), along(late[1], -1)
    own = pred_part((0, 0), (0, 1), (near_left, near_right), 2, *late)
    mine, *pieces = merge_call(own, (late_right, late_left))
    pieces = [across(piece, step + 1) for step, piece in enumerate(pieces)]
    spatial_squares = jnp.sum(after(spatial, mine) ** 2, axis=0)
    types = types + swap_along(after(types, spatial_squares), 1)
    spot_rows = stacked([spot_valid, slide_id.astype(F32), spatial_squares])
    mine = after(mine, spot_rows, types)
    piece = mine + pieces[0] + pieces[1] + pieces[2]
    totals = piece[-1]
    piece = piece[:-1].reshape(8, 16, spots)
    share = 1.0 / totals[0]
    mass = totals[1] * share

    got = [across(piece, step) for step in (1, 2, 3)]
    sums, slides = stats_call(
        ids,
        piece,
        spatial.reshape(8, 16, 16, spots),
        spot_rows,
        totals,
    )
    sums = sums + swap_along(sums, 1)
    sums = sums + swap_along(sums, 3)
    types = types + swap_along(after(types, slides), 3)
    mine = after((jnp.stack([piece, got[2]]), jnp.stack([got[1], got[0]])), sums, types)
    right0, left1 = along(mine[0], 1), along(mine[1], -1)
    right1, left0 = along(mine[1], 1), along(mine[0], -1)
    sums = sums + swap_across(after(sums, *mine), 1)
    sums = sums + swap_across(sums, 3)
    right0, left1, sums = lax.optimization_barrier((right0, left1, sums))
    far0, far1 = along(right0, 1), along(left1, -1)
    genes_slides = jnp.concatenate([sums[:48], slides])
    genes_slides = genes_slides + swap(genes_slides, 0, 0, 0, 1)
    genes_slides = genes_slides + swap(genes_slides, 0, 0, 1, 0)
    genes_slides = after(genes_slides, right1, left0)
    genes_slides = genes_slides + swap(genes_slides, 0, 0, 3, 0)
    pred = [*mine, right0, right1, left0, left1, far0, far1]
    gene_coef, spot_coef, scalars = coef_call(ids, genes_slides, sums, spot_rows, totals)
    spatial4 = spatial.reshape(8, RING, genes // 32, spots)
    grad, column_a = grad_call(ids, pred[:6], spatial4, gene_coef, spot_coef, 0, (0, 1, 2, 3))

    def last_grad(chips, grad, *others):
        return grad_call(
            after(ids, *others), pred[6:], spatial4, gene_coef, spot_coef, 12, chips, (grad,)
        )

    def back_part(steps, grad, *others, **rows):
        return back_call(after(ids, *others), steps, grad, masses, expr, **rows)

    rows = genes // 16
    grad, column_b = last_grad((2,), grad)
    sums_a, far_a = back_part([(2, 1)], grad, first=[spot_coef])
    far_got = swap(far_a, 0, 0, 0, 1)
    sums_b, far_b = back_part([(2, 0)], grad, far_a)
    far = far_b + far_got
    far_up, far_down = up(far[:rows], 1), up(far[rows:], -1)
    grad, column_c = last_grad((1, -1, 0), grad, far)
    sums_c, up_a, down_a, own_a = back_part([(1, 1), (-1, 1), (0, 1)], grad)
    up_got, down_got, own_got = (swap(one, 0, 0, 0, 1) for one in (up_a, down_a, own_a))
    sums_d, up_b, down_b = back_part([(1, 0), (-1, 0)], grad, up_a)
    types = types + swap_across(after(types, up_a), 1)
    above, below = lift_call(up_b, down_b, *after((far_up, far_down), types))
    above, below = join_call(above, below, up_got, down_got)
    near_up, near_down = up(above, 1), up(below, -1)
    types_got = swap_across(after(types, above), 3)
    last, own_b = back_part(
        [(0, 0)], grad, above, below, last=[sums_a, sums_b, sums_c, sums_d, scalars]
    )
    last_got = swap(last, 0, 0, 0, 1)
    own = own_b + own_got

    column = jnp.sum(column_a + column_b + column_c, axis=0) * share + spot_coef[32] * mass
    map_rows = stacked([spot_coef[32], column])
    valid2 = valid.reshape(blocks, 128)
    map_args = (expr, grad.reshape(2, genes, spots), masses, keep2, valid2, map_rows, all_cells * genes)
    grad_map = map_call(*map_args)
    types_got, last_got = after((types_got, last_got), grad_map)
    types = types + types_got
    last = after(last + last_got, own)
    got = [up(last, step) for step in (1, 2, 3)]
    grad_weighted = after(own, grad_map) + near_up + near_down
    grad_expr = grad_weighted * (keep * (genes * all_spots))[None, :]

    type_fraction = types * share

    grad_filter, loss_terms = finish_call(
        last, got, totals, scalars, cell_type.reshape(1, cells), filter_logits.reshape(1, cells), all_cells
    )
    return (loss_terms, type_fraction, grad_map, grad_filter.reshape(cells), grad_expr)


def solution(mesh):
    in_specs = (
        P("cells", "spots"),
        P("cells"),
        P(None, "cells"),
        P(None, "spots"),
        P("cells"),
        P("spots"),
        P("spots"),
    )
    out_specs = (P(), P(None, "spots"), P("cells", "spots"), P("cells"), P("spots", "cells"))
    return jax.shard_map(
        on_device, mesh=mesh, in_specs=in_specs, out_specs=out_specs, check_vma=False
    )
```

```python
import functools

import jax
import jax.numpy as jnp
from jax import lax
from jax.experimental import pallas as pl
from jax.experimental.pallas import tpu as pltpu
from jax.sharding import PartitionSpec as P

TYPES = 32
SLIDES = 3
RING = 4
F32 = jnp.float32
BF16 = jnp.bfloat16


def vmem(mib):
    return pltpu.CompilerParams(vmem_limit_bytes=mib << 20)


def fixed(shape):
    return pl.BlockSpec(shape, lambda *_: (0,) * len(shape), pipeline_mode=pl.Buffered(1))


def streamed(array):
    return pltpu.with_memory_space_constraint(array, pltpu.HBM)


RESIDENT = pl.BlockSpec(memory_space=pltpu.VMEM)


def cost(flops, moved):
    return pl.CostEstimate(flops=int(flops) // 8, bytes_accessed=int(moved) // 8, transcendentals=0)


NO_COST = pl.CostEstimate(flops=0, bytes_accessed=0, transcendentals=0)


def route(target):
    def flat(z, x, y, core):
        return ((z % RING * RING + x % RING) * RING + y % RING) * 2 + core

    return [
        (flat(z, x, y, core), flat(*target(z, x, y, core)))
        for z in range(RING)
        for x in range(RING)
        for y in range(RING)
        for core in range(2)
    ]


def send(array, target):
    return lax.ppermute(array, ("cells", "spots"), route(target))


def along(array, step):
    return send(array, lambda z, x, y, c: (z, x + step, y, c) if c == 0 else (z + step, x, y, c))


def across(array, step):
    return send(array, lambda z, x, y, c: (z + step, x, y, c) if c == 0 else (z, x + step, y, c))


def up(array, step):
    return send(array, lambda z, x, y, c: (z, x, y + step, c))


def swap(array, mz, mx, my, mc):
    return send(array, lambda z, x, y, c: (z ^ mz, x ^ mx, y ^ my, c ^ mc))


def swap_along(array, mask):
    return send(array, lambda z, x, y, c: (z, x ^ mask, y, c) if c == 0 else (z ^ mask, x, y, c))


def swap_across(array, mask):
    return send(array, lambda z, x, y, c: (z ^ mask, x, y, c) if c == 0 else (z, x ^ mask, y, c))


def after(value, *others):
    return lax.optimization_barrier((value, *others))[0]


def split(value):
    high = value.astype(BF16)
    return high, (value - high.astype(F32)).astype(BF16)


def product(left, right, dims):
    def one(a, b):
        return lax.dot_general(a, b, (dims, ((), ())), preferred_element_type=F32)

    return one(left[0], right[0]) + one(left[0], right[1]) + one(left[1], right[0])


def gene_group(ids, step, half, sub):
    return ((ids[0] + step) & 3) * RING + ((ids[1] + 2 * half + sub) & 3)


PIECES = [
    (step, half, sub)
    for step, half in ((0, 0), (0, 1), (-1, 0), (-1, 1), (1, 0), (1, 1), (2, 0), (2, 1))
    for sub in range(2)
]


def pick(index, values):
    out = values[0]
    for k, value in enumerate(values[1:]):
        out = jnp.where(index == k + 1, value, out)
    return out


def stacked(rows):
    row = lax.broadcasted_iota(jnp.int32, (8, rows[0].shape[0]), 0)
    out = jnp.zeros(row.shape, F32)
    for k, value in enumerate(rows):
        out = jnp.where(row == k, value[None, :], out)
    return out


def as_column(row):
    return jnp.broadcast_to(row, (128, 128)).T[:, :1]


def expo_kernel(ids, logits, kind, filt, *refs):
    expr, (masses, types, totals, out0, out1) = refs[:4], refs[4:]
    step = pl.program_id(0)
    block = logits.shape[0]
    count = block // 128

    @pl.when(step == 0)
    def _():
        for out in (types, totals, out0, out1):
            out[...] = jnp.zeros_like(out)

    masses[0], masses[1] = split(jnp.exp(logits[...]))
    labels = [kind[pl.ds(step * count + part, 1), :] for part in range(count)]
    valids = [(label >= 0).astype(F32) for label in labels]
    keeps = [
        valid * jax.nn.sigmoid(filt[pl.ds(step * count + part, 1), :])
        for part, valid in enumerate(valids)
    ]
    keep = jnp.concatenate(keeps, axis=1)
    lane = lax.broadcasted_iota(jnp.int32, (1, block), 1) // 128
    valid = jnp.concatenate(valids, axis=1)
    row = lax.broadcasted_iota(jnp.int32, (16, block), 0)
    extra = jnp.where(row == count, keep, jnp.where(row == lane, valid, 0.0))
    weighted = jnp.concatenate([part[...].reshape(-1, block) for part in expr]) * keep
    part = product(split(jnp.concatenate([weighted, extra])), masses, ((1,), (0,)))
    half = weighted.shape[0] // 2
    whole = [part[2 * half + k : 2 * half + k + 1] for k in range(count + 1)]
    row = lax.broadcasted_iota(jnp.int32, types.shape, 0)
    for label, one in zip(labels, whole):
        types[...] += jnp.where(row == jnp.max(label, axis=1, keepdims=True), one, 0.0)
    lane = lax.broadcasted_iota(jnp.int32, (1, totals.shape[1]), 1)
    cell_sums = jnp.zeros(lane.shape, F32)
    for k, one in enumerate((valid, keep, keep - keep * keep)):
        cell_sums += jnp.where(lane == k, jnp.sum(one, axis=1, keepdims=True), 0.0)
    totals[0:1, :] += sum(whole[1:count], whole[0])
    totals[1:2, :] += whole[count]
    totals[2:3, :] += cell_sums
    for index, out in enumerate((out0, out1)):
        new = part[index * half : index * half + half].reshape(-1, 8, part.shape[1])
        out[: half // 8] += new
        out[half // 8] = totals[...]


def expo_call(ids, parts, logits, kind, filt, expr):
    cells, spots = logits.shape
    blocks, groups, rows, _ = expr.shape
    block = 256

    def genes(part, sub):
        return pl.BlockSpec(
            (blocks, 1, rows, block), lambda i, ids: (0, gene_group(ids, *part, sub), 0, i)
        )

    return pl.pallas_call(
        expo_kernel,
        grid_spec=pltpu.PrefetchScalarGridSpec(
            num_scalar_prefetch=1,
            grid=(cells // block,),
            in_specs=[
                pl.BlockSpec((block, spots), lambda i, w: (i, 0)),
                fixed(kind.shape),
                fixed(filt.shape),
            ]
            + [genes(part, sub) for part in parts for sub in range(2)],
            out_specs=[
                pl.BlockSpec((2, block, spots), lambda i, w: (0, i, 0)),
                fixed((TYPES, spots)),
                fixed((8, spots)),
                fixed((blocks * rows // 4 + 1, 8, spots)),
                fixed((blocks * rows // 4 + 1, 8, spots)),
            ],
        ),
        out_shape=[
            jax.ShapeDtypeStruct((2, cells, spots), BF16),
            jax.ShapeDtypeStruct((TYPES, spots), F32),
            jax.ShapeDtypeStruct((8, spots), F32),
            jax.ShapeDtypeStruct((blocks * rows // 4 + 1, 8, spots), F32),
            jax.ShapeDtypeStruct((blocks * rows // 4 + 1, 8, spots), F32),
        ],
        compiler_params=vmem(16),
        cost_estimate=cost(0, cells * spots * 8),
        name="expo",
    )(ids, streamed(logits), streamed(kind), streamed(filt), *[streamed(expr)] * 4)


def pred_kernel(ids, expr_a, expr_b, keep, masses, totals, *refs, cuts):
    more, outs = refs[:-2], refs[-2:]
    rows = 2 * expr_a.shape[0] * expr_a.shape[2]
    weighted = jnp.concatenate(
        [part[...].reshape(rows // 2, keep.shape[1]) for part in (expr_a, expr_b)]
    )
    weighted = split(weighted * keep[...])
    width = masses.shape[2] // cuts

    def half(index, _):
        columns = pl.ds(pl.multiple_of(index * width, width), width)
        part = product(weighted, (masses[0, :, columns], masses[1, :, columns]), ((1,), (0,)))
        part = part.reshape(rows // 8, 8, width)
        for step, out in enumerate(outs):

            @pl.when(pl.program_id(0) == step)
            def _(step=step, out=out):
                if more:
                    out[: rows // 8, :, columns] = part + more[step][: rows // 8, :, columns]
                    out[rows // 8, :, columns] = totals[:, columns] + more[step][rows // 8, :, columns]
                else:
                    out[: rows // 8, :, columns] = part
                    out[rows // 8, :, columns] = totals[:, columns]

        return 0

    lax.fori_loop(0, cuts, half, 0)


def pred_call(ids, parts, expr, keep, masses, totals, more, cuts):
    blocks, groups, rows, cells = expr.shape
    spots = masses.shape[2]
    tiles = blocks * rows // 4 + 1

    def genes(sub):
        def place(i, ids):
            step, half = (pick(i, [part[k] for part in parts]) for k in range(2))
            return (0, gene_group(ids, step, half, sub), 0, 0)

        return pl.BlockSpec((blocks, 1, rows, cells), place)

    return pl.pallas_call(
        functools.partial(pred_kernel, cuts=cuts),
        grid_spec=pltpu.PrefetchScalarGridSpec(
            num_scalar_prefetch=1,
            grid=(2,),
            in_specs=[
                genes(0),
                genes(1),
                fixed((1, cells)),
                RESIDENT,
                fixed((8, spots)),
            ]
            + [RESIDENT] * len(more),
            out_specs=[RESIDENT] * 2,
        ),
        out_shape=[jax.ShapeDtypeStruct((tiles, 8, spots), F32)] * 2,
        compiler_params=vmem(16),
        cost_estimate=cost(24 * blocks * rows * cells * spots, 4 * cells * spots + 16 * blocks * rows * (cells + spots)),
        name="pred",
    )(ids, *[streamed(expr)] * 2, keep, masses, totals, *more)


def merge_kernel(own0, own1, got0, got1, *outs):
    tiles = outs[0].shape[0] - 1
    for half, (own, got) in enumerate(((own0, got0), (own1, got1))):
        for sub in range(2):
            out = outs[2 * half + sub]
            out[:tiles] = own[sub * tiles : sub * tiles + tiles] + got[sub * tiles : sub * tiles + tiles]
            out[tiles] = own[2 * tiles] + got[2 * tiles]


def merge_call(own, got):
    tiles, _, spots = own[0].shape
    block = 256
    whole = pl.BlockSpec((tiles, 8, block), lambda i: (0, 0, i))
    piece = (tiles // 2 + 1, 8, spots)
    return pl.pallas_call(
        merge_kernel,
        grid=(spots // block,),
        in_specs=[whole] * 4,
        out_specs=[pl.BlockSpec((tiles // 2 + 1, 8, block), lambda i: (0, 0, i))] * 4,
        out_shape=[jax.ShapeDtypeStruct(piece, F32)] * 4,
        compiler_params=vmem(12),
        cost_estimate=NO_COST,
        name="merge",
    )(*own, *got)


def stats_kernel(ids, piece, spatial, spot, totals, gene, slide_sums):
    rows = piece.shape[0] * piece.shape[1]
    valid, slide = spot[0:1, :], spot[1:2, :]
    share = 1.0 / totals[0:1, :]
    mass = totals[1:2, :] * share
    value = piece[...].reshape(rows, piece.shape[2]) * share
    data = spatial[...].reshape(value.shape)
    cross, square = value * data, value * value
    lane = lax.broadcasted_iota(jnp.int32, (rows, 128), 1)
    sums = jnp.zeros((rows, 128), F32)
    for index, one in enumerate((cross, square, data * data)):
        sums = jnp.where(lane == index, jnp.sum(one * valid, axis=1, keepdims=True), sums)
    sums = sums.T
    gene[...] = jnp.zeros_like(gene)
    slide_sums[...] = jnp.zeros_like(slide_sums)
    for index in range(3):
        gene[pl.ds(16 * index + gene_group(ids, 0, 0, 0), 1), :] = sums[index : index + 1, :]
    lane = lax.broadcasted_iota(jnp.int32, (1, 128), 1)
    slides = jnp.zeros((1, 128), F32)
    logs = jnp.log(jnp.where(valid > 0, mass, 1.0))
    for k in range(SLIDES):
        inside = jnp.where(slide == k, valid, 0.0)
        for index, one in enumerate((inside, inside * mass, inside * logs)):
            total = jnp.sum(one, axis=1, keepdims=True)
            slides = jnp.where(lane == 3 * index + k, total, slides)
    slide_sums[0:1, :] = slides
    for index, one in enumerate((cross, square)):
        total = jnp.sum(one, axis=0, keepdims=True)
        for k in range(total.shape[1] // 128):
            at = 48 + 8 * index + k
            gene[at : at + 1, :] = total[:, 128 * k : 128 * k + 128]


def stats_call(ids, piece, spatial, spot, totals):
    blocks, rows, spots = piece.shape
    return pl.pallas_call(
        stats_kernel,
        grid_spec=pltpu.PrefetchScalarGridSpec(
            num_scalar_prefetch=1,
            grid=(1,),
            in_specs=[
                fixed((blocks, rows, spots)),
                pl.BlockSpec((blocks, 1, rows, spots), lambda i, ids: (0, gene_group(ids, 0, 0, 0), 0, 0)),
                fixed((8, spots)),
                fixed((8, spots)),
            ],
            out_specs=[fixed((64, 128)), fixed((8, 128))],
        ),
        out_shape=[jax.ShapeDtypeStruct((64, 128), F32), jax.ShapeDtypeStruct((8, 128), F32)],
        compiler_params=vmem(8),
        cost_estimate=NO_COST,
        name="stats",
    )(ids, piece, spatial, spot, totals)


def coef_kernel(ids, genes_slides, sums, spot, totals, gene, rows, scalars, pairs):
    valid, slide, squares = (spot[k : k + 1, :] for k in range(3))
    share = 1.0 / totals[0:1, :]
    mass = totals[1:2, :] * share
    genes = float(16 * sums.shape[1])

    def wide(index):
        return jnp.concatenate([sums[index + k : index + k + 1, :] for k in range(8)], axis=1)

    dots, own = wide(48), wide(56)
    dot, aa, bb = genes_slides[0:16, :], genes_slides[16:32, :], genes_slides[32:48, :]
    scale = lax.rsqrt(aa * bb + 1e-06)
    pairs[0:16, :] = dot * scale**3 * bb / genes
    pairs[16:32, :] = scale / genes
    pair = [pairs[pl.ds(k + gene_group(ids, *one), 1), :] for k in (0, 16) for one in PIECES]
    gene[...] = jnp.concatenate([*pair, jnp.zeros((96, 128), F32)]).T
    total = jnp.sum(jnp.sum(dot * scale, axis=1, keepdims=True), axis=0, keepdims=True)
    nvs = jnp.zeros((1, 1), F32)
    density = jnp.zeros((1, 1), F32)
    nk, tk = jnp.ones_like(valid), jnp.ones_like(valid)
    for k in range(SLIDES):
        count, held, logs = (genes_slides[48:49, 3 * j + k : 3 * j + k + 1] for j in range(3))
        some = count > 0
        safe = jnp.where(some, count, 1.0)
        nvs += count
        density += jnp.where(some, jnp.log(jnp.where(some, held, 1.0) / safe) - logs / safe, 0.0)
        here = (slide == k) & (valid > 0)
        nk = jnp.where(here, count, nk)
        tk = jnp.where(here, held, tk)
    scale = lax.rsqrt(own * squares + 1e-06)
    grad_mass = valid / SLIDES * (1.0 / tk - 1.0 / (nk * jnp.where(valid > 0, mass, 1.0)))
    mask = valid * share
    by_pred, by_data = dots * scale**3 * squares / nvs, scale / nvs
    for index, one in enumerate((by_pred * share * mask, by_data * mask, mask, share * mask)):
        rows[8 * index : 8 * index + 8, :] = jnp.broadcast_to(one, (8, one.shape[1]))
    rows[32:40, :] = jnp.concatenate([grad_mass * share, jnp.zeros((7, valid.shape[1]), F32)])
    cosines = jnp.sum(valid * dots * scale, axis=1, keepdims=True)
    lane = lax.broadcasted_iota(jnp.int32, (1, 128), 1)
    out = jnp.zeros((1, 128), F32)
    for index, one in enumerate((total / genes, cosines / nvs, density / SLIDES)):
        out = jnp.where(lane == index, one, out)
    scalars[...] = out


def coef_call(ids, genes_slides, sums, spot, totals):
    spots = spot.shape[1]
    return pl.pallas_call(
        coef_kernel,
        grid_spec=pltpu.PrefetchScalarGridSpec(
            num_scalar_prefetch=1,
            grid=(1,),
            in_specs=[fixed(genes_slides.shape), fixed(sums.shape), fixed((8, spots)), fixed((8, spots))],
            out_specs=[fixed((128, 128)), fixed((40, spots)), fixed((1, 128))],
            scratch_shapes=[pltpu.VMEM((32, 128), F32)],
        ),
        out_shape=[
            jax.ShapeDtypeStruct((128, 128), F32),
            jax.ShapeDtypeStruct((40, spots), F32),
            jax.ShapeDtypeStruct((1, 128), F32),
        ],
        compiler_params=vmem(6),
        cost_estimate=NO_COST,
        name="coef",
    )(ids, genes_slides, sums, spot, totals)


def grad_rows(pred, data, gene, spot, lane):
    by_pred = gene[:, lane : lane + 1].reshape(2, 8, 1)
    by_data = gene[:, 16 + lane : 17 + lane].reshape(2, 8, 1)
    pred, data = pred.reshape(2, 8, pred.shape[1]), data.reshape(2, 8, data.shape[1])
    grad = pred * (by_pred * spot[24:32, :] + spot[0:8, :])
    grad = grad - data * (by_data * spot[16:24, :] + spot[8:16, :])
    return grad.reshape(16, grad.shape[2]), jnp.sum(grad * pred, axis=0)


def grad_kernel(ids, *refs, count, lane, chips):
    pred, data, refs = refs[: 2 * count], refs[2 * count : 3 * count], refs[3 * count :]
    gene, spot, grad, column = refs[0], refs[1], refs[-2], refs[-1]
    step = pl.program_id(0)
    chip = (ids[2] + pick(step, chips)) & 3

    @pl.when(step == 0)
    def _():
        column[...] = jnp.zeros_like(column)

    def half_of(half, _):
        block = chip * 2 + half
        factors = gene[pl.ds(pl.multiple_of(16 * half, 16), 16), :]
        total = jnp.zeros(column.shape, F32)
        for index, part in enumerate(pred):
            for sub in range(2):
                at = gene_group(ids, *PIECES[lane + 2 * index + sub])
                row = pl.multiple_of((at & 3) * 16, 16)
                to = pl.ds(pl.multiple_of(at * 16, 16), 16)
                rows, inner = grad_rows(
                    part[sub, block],
                    data[index // 2][half, 0, pl.ds(row, 16), :],
                    factors,
                    spot,
                    lane + 2 * index + sub,
                )
                grad[0, block, to, :], grad[1, block, to, :] = split(rows)
                total += inner
        column[...] += total
        return 0

    lax.fori_loop(0, 2, half_of, 0)


def grad_call(ids, pred, spatial, gene, spot, lane, chips, done=()):
    blocks, groups, rows, spots = spatial.shape
    count = len(pred) // 2

    def chip(i, ids):
        return (ids[2] + pick(i, chips)) & 3

    def group(k):
        step = PIECES[lane + 4 * k][0]
        return pl.BlockSpec(
            (2, 1, rows, spots), lambda i, ids: (chip(i, ids), (ids[0] + step) & 3, 0, 0)
        )

    return pl.pallas_call(
        functools.partial(grad_kernel, count=count, lane=lane, chips=chips),
        grid_spec=pltpu.PrefetchScalarGridSpec(
            num_scalar_prefetch=1,
            grid=(len(chips),),
            in_specs=[RESIDENT] * (2 * count)
            + [group(k) for k in range(count)]
            + [pl.BlockSpec((32, 128), lambda i, ids: (chip(i, ids), 0)), fixed(spot.shape)]
            + [RESIDENT] * len(done),
            out_specs=[RESIDENT, fixed((8, spots))],
        ),
        out_shape=[
            jax.ShapeDtypeStruct((2, blocks, groups * rows, spots), BF16),
            jax.ShapeDtypeStruct((8, spots), F32),
        ],
        input_output_aliases={3 * count + 3: 0} if done else {},
        compiler_params=vmem(12),
        cost_estimate=NO_COST,
        name="grad",
    )(ids, *pred, *[spatial] * count, gene, spot, *done)


def back_kernel(ids, grad, masses, expr, *refs, parts, first, last):
    more, (sums, *outs), (held, ready) = refs[: first + 5 * last], refs[first + 5 * last : -2], refs[-2:]
    step = pl.program_id(0)
    rows = grad.shape[2]

    def block(part):
        return ((ids[2] + part[0]) & 3) * 2 + (ids[3] ^ part[1])

    def fetch(k):
        start = pl.multiple_of(block(parts[k]) * rows, rows)
        return pltpu.make_async_copy(expr.at[pl.ds(start, rows), :], held.at[k], ready.at[k])

    @pl.when(step == 0)
    def _():
        for k in range(len(parts)):
            fetch(k).start()

    @pl.when(step == 0)
    def _():
        if last:
            sums[...] = more[0][...] + more[1][...] + more[2][...] + more[3][...]
        else:
            sums[...] = jnp.zeros_like(sums)

    here = block([pick(step, [part[k] for part in parts]) for k in range(2)])
    left = grad[0, here], grad[1, here]
    if first:
        pair = split(jnp.concatenate([more[0][...], jnp.zeros_like(more[0])]))
        left = [jnp.concatenate(both) for both in zip(left, pair)]
    part = product(left, masses, ((1,), (1,)))
    if first:
        sums[...] = part[rows : rows + 8]
        part = part[:rows]
    for k, out in enumerate(outs):

        @pl.when(step == k)
        def _(k=k, out=out):
            out[...] = part
            fetch(k).wait()

    sums[...] += jnp.sum((part * held[step]).reshape(-1, 8, part.shape[1]), axis=0)
    if last:

        @pl.when(step == len(parts) - 1)
        def _():
            total = jnp.sum(sums[...], axis=0, keepdims=True)
            sums[...] = jnp.zeros_like(sums)
            sums[0:1, :] = total
            sums[1:2, 0:128] = more[4][...]


def back_call(ids, parts, grad, masses, expr, first=(), last=()):
    _, blocks, rows, spots = grad.shape
    cells = masses.shape[1]
    return pl.pallas_call(
        functools.partial(back_kernel, parts=parts, first=len(first), last=len(last) // 5),
        grid_spec=pltpu.PrefetchScalarGridSpec(
            num_scalar_prefetch=1,
            grid=(len(parts),),
            in_specs=[RESIDENT, RESIDENT, pl.BlockSpec(memory_space=pl.ANY)]
            + [pl.BlockSpec((8, spots), lambda i, ids: (4, 0))] * len(first)
            + [fixed(one.shape) for one in last],
            out_specs=[fixed((8, cells))] + [RESIDENT] * len(parts),
            scratch_shapes=[
                pltpu.VMEM((len(parts), rows, cells), F32),
                pltpu.SemaphoreType.DMA((len(parts),)),
            ],
        ),
        out_shape=[jax.ShapeDtypeStruct((8, cells), F32)]
        + [jax.ShapeDtypeStruct((rows, cells), F32)] * len(parts),
        compiler_params=vmem(22),
        cost_estimate=NO_COST,
        name="back",
    )(ids, grad, masses, streamed(expr), *first, *last)


def lift_kernel(above, below, far_up, far_down, out_above, out_below):
    rows = far_up.shape[0]
    out_above[:rows, :] = above[:rows, :] + far_up[...]
    out_above[rows:, :] = above[rows:, :]
    out_below[:rows, :] = below[:rows, :]
    out_below[rows:, :] = below[rows:, :] + far_down[...]


def lift_call(above, below, far_up, far_down):
    rows, cells = far_up.shape
    block = 256
    far = pl.BlockSpec((rows, block), lambda i: (0, i))
    whole = pl.BlockSpec((2 * rows, block), lambda i: (0, i))
    return pl.pallas_call(
        lift_kernel,
        grid=(cells // block,),
        in_specs=[whole, whole, far, far],
        out_specs=[whole, whole],
        out_shape=[jax.ShapeDtypeStruct(above.shape, F32)] * 2,
        compiler_params=vmem(8),
        cost_estimate=pl.CostEstimate(flops=10**10, bytes_accessed=0, transcendentals=0),
        name="lift",
    )(above, below, far_up, far_down)


def join_kernel(above, below, got_above, got_below, out_above, out_below):
    out_above[...] = above[...] + got_above[...]
    out_below[...] = below[...] + got_below[...]


def join_call(above, below, got_above, got_below):
    rows, cells = above.shape
    whole = pl.BlockSpec((rows, 256), lambda i: (0, i))
    return pl.pallas_call(
        join_kernel,
        grid=(cells // 256,),
        in_specs=[whole] * 4,
        out_specs=[whole] * 2,
        out_shape=[jax.ShapeDtypeStruct(above.shape, F32)] * 2,
        compiler_params=vmem(8),
        cost_estimate=NO_COST,
        name="join",
    )(above, below, got_above, got_below)


def map_kernel(expr, grad, masses, keep, valid, spot, out, held, ready, *, scale):
    index = pl.program_id(0)
    quarter, block = held.shape[2:]
    count = held.shape[1]

    def fetch(at, k):
        columns = pl.ds(pl.multiple_of(at * block, block), block)
        return pltpu.make_async_copy(
            expr.at[pl.ds(k * quarter, quarter), columns], held.at[at & 1, k], ready.at[at & 1, k]
        )

    @pl.when(index == 0)
    def _():
        for k in range(count):
            fetch(index, k).start()

    @pl.when(index + 1 < pl.num_programs(0))
    def _():
        for k in range(count):
            fetch(index + 1, k).start()

    inner = spot[0:1, :]
    for k in range(count):
        fetch(index, k).wait()
        rows = slice(k * quarter, k * quarter + quarter)
        pair = grad[0, rows, :], grad[1, rows, :]
        inner = inner + product(split(held[index & 1, k]), pair, ((0,), (0,)))
    at = pl.multiple_of(index * block, block)
    expo = masses[0, pl.ds(at, block), :].astype(F32) + masses[1, pl.ds(at, block), :].astype(F32)
    for part in range(block // 128):
        rows = slice(part * 128, part * 128 + 128)
        place = pl.ds(index * (block // 128) + part, 1)
        weight, mask = as_column(keep[place, :]), as_column(valid[place, :])
        out[rows, :] = (scale * expo[rows]) * (weight * inner[rows] - mask * spot[1:2, :])


def map_call(expr, grad, masses, keep, valid, spot, scale):
    genes, cells = expr.shape
    spots = masses.shape[2]
    block, count = 256, 4
    return pl.pallas_call(
        functools.partial(map_kernel, scale=scale),
        grid=(cells // block,),
        in_specs=[
            pl.BlockSpec(memory_space=pl.ANY),
            RESIDENT,
            RESIDENT,
            fixed(keep.shape),
            fixed(valid.shape),
            fixed((8, spots)),
        ],
        out_specs=pl.BlockSpec((block, spots), lambda i: (i, 0)),
        out_shape=jax.ShapeDtypeStruct((cells, spots), F32),
        scratch_shapes=[
            pltpu.VMEM((2, count, genes // count, block), F32),
            pltpu.SemaphoreType.DMA((2, count)),
        ],
        compiler_params=vmem(24),
        cost_estimate=NO_COST,
        name="grad_map",
    )(streamed(expr), grad, masses, keep, valid, spot)


def finish_kernel(last, got1, got2, got3, totals, scalars, kind, filt, grad_filter, terms, *, all_cells):
    total = (last[...] + got2[...]) + (got1[...] + got3[...])
    nvalid, retained, reg_sum = (totals[2:3, k : k + 1] for k in range(3))
    valid = (kind[...] >= 0).astype(F32)
    sigma = jax.nn.sigmoid(filt[...])
    keep = sigma * valid
    shifted = (retained - 0.35 * nvalid) / (0.1 * all_cells)
    count_term = jnp.sqrt(shifted * shifted + 1.0)
    grad_keep = total[0:1, :] + shifted / count_term / (0.1 * all_cells) + (1.0 - 2.0 * keep) / nvalid
    row = valid * sigma * (1.0 - sigma) * grad_keep * all_cells
    for k in range(grad_filter.shape[0]):
        grad_filter[k : k + 1, :] = row[:, 128 * k : 128 * k + 128]
    lane = lax.broadcasted_iota(jnp.int32, (1, 128), 1)
    out = jnp.zeros((1, 128), F32)
    parts = (scalars[:, 0:1], total[1:2, 1:2], scalars[:, 2:3], count_term, reg_sum / nvalid)
    for index, one in enumerate(parts):
        out = jnp.where(lane == index, one, out)
    terms[...] = out[0, :5]


def finish_call(last, got, totals, scalars, kind, filt, all_cells):
    return pl.pallas_call(
        functools.partial(finish_kernel, all_cells=float(all_cells)),
        grid=(1,),
        in_specs=[fixed(one.shape) for one in (last, *got, totals, scalars, kind, filt)],
        out_specs=[fixed((kind.shape[1] // 128, 128)), fixed((5,))],
        out_shape=[
            jax.ShapeDtypeStruct((kind.shape[1] // 128, 128), F32),
            jax.ShapeDtypeStruct((5,), F32),
        ],
        compiler_params=vmem(4),
        cost_estimate=NO_COST,
        name="finish",
    )(last, *got, totals, scalars, kind, filt)


def on_device(map_logits, filter_logits, expr, spatial, cell_type, slide_id, spot_mask):
    genes, cells = expr.shape
    spots = map_logits.shape[1]
    all_cells = cells * lax.axis_size("cells")
    all_spots = spots * lax.axis_size("spots")
    cell_place = lax.axis_index("cells")
    z, x = cell_place >> 2, cell_place & 3
    spot_place = lax.axis_index("spots")
    y, core = spot_place >> 1, spot_place & 1
    first = jnp.where(core == 0, x, z)
    second = jnp.where(core == 0, z, x)
    blocks = cells // 128

    valid = (cell_type >= 0).astype(F32)
    sigma = jax.nn.sigmoid(filter_logits)
    keep = sigma * valid
    spot_valid = spot_mask.astype(F32)
    kind2 = cell_type.reshape(blocks, 128)
    filt2 = filter_logits.reshape(blocks, 128)
    keep2 = keep.reshape(blocks, 128)

    expr4 = expr.reshape(8, 16, 16, cells)
    keep_row = keep.reshape(1, cells)

    ids = jnp.stack([first, second, y, core]).astype(jnp.int32)

    def pred_part(one, two, more, cuts, *others):
        return pred_call(after(ids, *others), (one, two), expr4, keep_row, masses, totals, more, cuts)

    masses, types, totals, *far = expo_call(
        ids, ((2, 0), (2, 1)), map_logits, kind2, filt2, expr4
    )
    far_right, far_left = along(far[0], 1), along(far[1], -1)
    near = pred_part((1, 1), (-1, 0), (), 2, *far)
    near_right, near_left = along(near[0], 1), along(near[1], -1)
    late = pred_part((1, 0), (-1, 1), (far_right, far_left), 1, *near)
    late_right, late_left = along(late[0], 1), along(late[1], -1)
    own = pred_part((0, 0), (0, 1), (near_left, near_right), 2, *late)
    mine, *pieces = merge_call(own, (late_right, late_left))
    pieces = [across(piece, step + 1) for step, piece in enumerate(pieces)]
    spatial_squares = jnp.sum(after(spatial, mine) ** 2, axis=0)
    types = types + swap_along(after(types, spatial_squares), 1)
    spot_rows = stacked([spot_valid, slide_id.astype(F32), spatial_squares])
    mine = after(mine, spot_rows, types)
    piece = mine + pieces[0] + pieces[1] + pieces[2]
    totals = piece[-1]
    piece = piece[:-1].reshape(8, 16, spots)
    share = 1.0 / totals[0]
    mass = totals[1] * share

    got = [across(piece, step) for step in (1, 2, 3)]
    sums, slides = stats_call(
        ids,
        piece,
        spatial.reshape(8, 16, 16, spots),
        spot_rows,
        totals,
    )
    sums = sums + swap_along(sums, 1)
    sums = sums + swap_along(sums, 3)
    types = types + swap_along(after(types, slides), 3)
    mine = after((jnp.stack([piece, got[2]]), jnp.stack([got[1], got[0]])), sums, types)
    right0, left1 = along(mine[0], 1), along(mine[1], -1)
    right1, left0 = along(mine[1], 1), along(mine[0], -1)
    sums = sums + swap_across(after(sums, *mine), 1)
    sums = sums + swap_across(sums, 3)
    right0, left1, sums = lax.optimization_barrier((right0, left1, sums))
    far0, far1 = along(right0, 1), along(left1, -1)
    genes_slides = jnp.concatenate([sums[:48], slides])
    genes_slides = genes_slides + swap(genes_slides, 0, 0, 0, 1)
    genes_slides = genes_slides + swap(genes_slides, 0, 0, 1, 0)
    genes_slides = after(genes_slides, right1, left0)
    genes_slides = genes_slides + swap(genes_slides, 0, 0, 3, 0)
    pred = [*mine, right0, right1, left0, left1, far0, far1]
    gene_coef, spot_coef, scalars = coef_call(ids, genes_slides, sums, spot_rows, totals)
    spatial4 = spatial.reshape(8, RING, genes // 32, spots)
    grad, column_a = grad_call(ids, pred[:6], spatial4, gene_coef, spot_coef, 0, (0, 1, 2, 3))

    def last_grad(chips, grad, *others):
        return grad_call(
            after(ids, *others), pred[6:], spatial4, gene_coef, spot_coef, 12, chips, (grad,)
        )

    def back_part(steps, grad, *others, **rows):
        return back_call(after(ids, *others), steps, grad, masses, expr, **rows)

    rows = genes // 16
    grad, column_b = last_grad((2,), grad)
    sums_a, far_a = back_part([(2, 1)], grad, first=[spot_coef])
    far_got = swap(far_a, 0, 0, 0, 1)
    sums_b, far_b = back_part([(2, 0)], grad, far_a)
    far = far_b + far_got
    far_up, far_down = up(far[:rows], 1), up(far[rows:], -1)
    grad, column_c = last_grad((1, -1, 0), grad, far)
    sums_c, up_a, down_a, own_a = back_part([(1, 1), (-1, 1), (0, 1)], grad)
    up_got, down_got, own_got = (swap(one, 0, 0, 0, 1) for one in (up_a, down_a, own_a))
    sums_d, up_b, down_b = back_part([(1, 0), (-1, 0)], grad, up_a)
    types = types + swap_across(after(types, up_a), 1)
    above, below = lift_call(up_b, down_b, *after((far_up, far_down), types))
    above, below = join_call(above, below, up_got, down_got)
    near_up, near_down = up(above, 1), up(below, -1)
    types_got = swap_across(after(types, above), 3)
    last, own_b = back_part(
        [(0, 0)], grad, above, below, last=[sums_a, sums_b, sums_c, sums_d, scalars]
    )
    last_got = swap(last, 0, 0, 0, 1)
    own = own_b + own_got

    column = jnp.sum(column_a + column_b + column_c, axis=0) * share + spot_coef[32] * mass
    map_rows = stacked([spot_coef[32], column])
    valid2 = valid.reshape(blocks, 128)
    map_args = (expr, grad.reshape(2, genes, spots), masses, keep2, valid2, map_rows, all_cells * genes)
    grad_map = map_call(*map_args)
    types_got, last_got = after((types_got, last_got), grad_map)
    types = types + types_got
    last = after(last + last_got, own)
    got = [up(last, step) for step in (1, 2, 3)]
    grad_weighted = after(own, grad_map) + near_up + near_down
    grad_expr = grad_weighted * (keep * (genes * all_spots))[None, :]
    got = after(tuple(got), grad_expr)

    type_fraction = types * share

    grad_filter, loss_terms = finish_call(
        last, got, totals, scalars, cell_type.reshape(1, cells), filter_logits.reshape(1, cells), all_cells
    )
    return (loss_terms, type_fraction, grad_map, grad_filter.reshape(cells), grad_expr)


def solution(mesh):
    in_specs = (
        P("cells", "spots"),
        P("cells"),
        P(None, "cells"),
        P(None, "spots"),
        P("cells"),
        P("spots"),
        P("spots"),
    )
    out_specs = (P(), P(None, "spots"), P("cells", "spots"), P("cells"), P("spots", "cells"))
    return jax.shard_map(
        on_device, mesh=mesh, in_specs=in_specs, out_specs=out_specs, check_vma=False
    )
```

```python
import functools

import jax
import jax.numpy as jnp
from jax import lax
from jax.experimental import pallas as pl
from jax.experimental.pallas import tpu as pltpu
from jax.sharding import PartitionSpec as P

TYPES = 32
SLIDES = 3
RING = 4
F32 = jnp.float32
BF16 = jnp.bfloat16


def vmem(mib):
    return pltpu.CompilerParams(vmem_limit_bytes=mib << 20)


def fixed(shape):
    return pl.BlockSpec(shape, lambda *_: (0,) * len(shape), pipeline_mode=pl.Buffered(1))


def streamed(array):
    return pltpu.with_memory_space_constraint(array, pltpu.HBM)


RESIDENT = pl.BlockSpec(memory_space=pltpu.VMEM)


def cost(flops, moved):
    return pl.CostEstimate(flops=int(flops) // 8, bytes_accessed=int(moved) // 8, transcendentals=0)


NO_COST = pl.CostEstimate(flops=0, bytes_accessed=0, transcendentals=0)


def route(target):
    def flat(z, x, y, core):
        return ((z % RING * RING + x % RING) * RING + y % RING) * 2 + core

    return [
        (flat(z, x, y, core), flat(*target(z, x, y, core)))
        for z in range(RING)
        for x in range(RING)
        for y in range(RING)
        for core in range(2)
    ]


def send(array, target):
    return lax.ppermute(array, ("cells", "spots"), route(target))


def along(array, step):
    return send(array, lambda z, x, y, c: (z, x + step, y, c) if c == 0 else (z + step, x, y, c))


def across(array, step):
    return send(array, lambda z, x, y, c: (z + step, x, y, c) if c == 0 else (z, x + step, y, c))


def up(array, step):
    return send(array, lambda z, x, y, c: (z, x, y + step, c))


def swap(array, mz, mx, my, mc):
    return send(array, lambda z, x, y, c: (z ^ mz, x ^ mx, y ^ my, c ^ mc))


def swap_along(array, mask):
    return send(array, lambda z, x, y, c: (z, x ^ mask, y, c) if c == 0 else (z ^ mask, x, y, c))


def swap_across(array, mask):
    return send(array, lambda z, x, y, c: (z ^ mask, x, y, c) if c == 0 else (z, x ^ mask, y, c))


def after(value, *others):
    return lax.optimization_barrier((value, *others))[0]


def split(value):
    high = value.astype(BF16)
    return high, (value - high.astype(F32)).astype(BF16)


def product(left, right, dims):
    def one(a, b):
        return lax.dot_general(a, b, (dims, ((), ())), preferred_element_type=F32)

    return one(left[0], right[0]) + one(left[0], right[1]) + one(left[1], right[0])


def gene_group(ids, step, half, sub):
    return ((ids[0] + step) & 3) * RING + ((ids[1] + 2 * half + sub) & 3)


PIECES = [
    (step, half, sub)
    for step, half in ((0, 0), (0, 1), (-1, 0), (-1, 1), (1, 0), (1, 1), (2, 0), (2, 1))
    for sub in range(2)
]


def pick(index, values):
    out = values[0]
    for k, value in enumerate(values[1:]):
        out = jnp.where(index == k + 1, value, out)
    return out


def stacked(rows):
    row = lax.broadcasted_iota(jnp.int32, (8, rows[0].shape[0]), 0)
    out = jnp.zeros(row.shape, F32)
    for k, value in enumerate(rows):
        out = jnp.where(row == k, value[None, :], out)
    return out


def as_column(row):
    return jnp.broadcast_to(row, (128, 128)).T[:, :1]


def expo_kernel(ids, logits, kind, filt, *refs):
    expr, (masses, types, totals, out0, out1) = refs[:4], refs[4:]
    step = pl.program_id(0)
    block = logits.shape[0]
    count = block // 128

    @pl.when(step == 0)
    def _():
        for out in (types, totals, out0, out1):
            out[...] = jnp.zeros_like(out)

    masses[0], masses[1] = split(jnp.exp(logits[...]))
    labels = [kind[pl.ds(step * count + part, 1), :] for part in range(count)]
    valids = [(label >= 0).astype(F32) for label in labels]
    keeps = [
        valid * jax.nn.sigmoid(filt[pl.ds(step * count + part, 1), :])
        for part, valid in enumerate(valids)
    ]
    keep = jnp.concatenate(keeps, axis=1)
    lane = lax.broadcasted_iota(jnp.int32, (1, block), 1) // 128
    valid = jnp.concatenate(valids, axis=1)
    row = lax.broadcasted_iota(jnp.int32, (16, block), 0)
    extra = jnp.where(row == count, keep, jnp.where(row == lane, valid, 0.0))
    weighted = jnp.concatenate([part[...].reshape(-1, block) for part in expr]) * keep
    part = product(split(jnp.concatenate([weighted, extra])), masses, ((1,), (0,)))
    half = weighted.shape[0] // 2
    whole = [part[2 * half + k : 2 * half + k + 1] for k in range(count + 1)]
    row = lax.broadcasted_iota(jnp.int32, types.shape, 0)
    for label, one in zip(labels, whole):
        types[...] += jnp.where(row == jnp.max(label, axis=1, keepdims=True), one, 0.0)
    lane = lax.broadcasted_iota(jnp.int32, (1, totals.shape[1]), 1)
    cell_sums = jnp.zeros(lane.shape, F32)
    for k, one in enumerate((valid, keep, keep - keep * keep)):
        cell_sums += jnp.where(lane == k, jnp.sum(one, axis=1, keepdims=True), 0.0)
    totals[0:1, :] += sum(whole[1:count], whole[0])
    totals[1:2, :] += whole[count]
    totals[2:3, :] += cell_sums
    for index, out in enumerate((out0, out1)):
        new = part[index * half : index * half + half].reshape(-1, 8, part.shape[1])
        out[: half // 8] += new
        out[half // 8] = totals[...]


def expo_call(ids, parts, logits, kind, filt, expr):
    cells, spots = logits.shape
    blocks, groups, rows, _ = expr.shape
    block = 256

    def genes(part, sub):
        return pl.BlockSpec(
            (blocks, 1, rows, block), lambda i, ids: (0, gene_group(ids, *part, sub), 0, i)
        )

    return pl.pallas_call(
        expo_kernel,
        grid_spec=pltpu.PrefetchScalarGridSpec(
            num_scalar_prefetch=1,
            grid=(cells // block,),
            in_specs=[
                pl.BlockSpec((block, spots), lambda i, w: (i, 0)),
                fixed(kind.shape),
                fixed(filt.shape),
            ]
            + [genes(part, sub) for part in parts for sub in range(2)],
            out_specs=[
                pl.BlockSpec((2, block, spots), lambda i, w: (0, i, 0)),
                fixed((TYPES, spots)),
                fixed((8, spots)),
                fixed((blocks * rows // 4 + 1, 8, spots)),
                fixed((blocks * rows // 4 + 1, 8, spots)),
            ],
        ),
        out_shape=[
            jax.ShapeDtypeStruct((2, cells, spots), BF16),
            jax.ShapeDtypeStruct((TYPES, spots), F32),
            jax.ShapeDtypeStruct((8, spots), F32),
            jax.ShapeDtypeStruct((blocks * rows // 4 + 1, 8, spots), F32),
            jax.ShapeDtypeStruct((blocks * rows // 4 + 1, 8, spots), F32),
        ],
        compiler_params=vmem(16),
        cost_estimate=cost(0, cells * spots * 8),
        name="expo",
    )(ids, streamed(logits), streamed(kind), streamed(filt), *[streamed(expr)] * 4)


def pred_kernel(ids, expr_a, expr_b, keep, masses, totals, *refs, cuts):
    more, outs = refs[:-2], refs[-2:]
    rows = 2 * expr_a.shape[0] * expr_a.shape[2]
    weighted = jnp.concatenate(
        [part[...].reshape(rows // 2, keep.shape[1]) for part in (expr_a, expr_b)]
    )
    weighted = split(weighted * keep[...])
    width = masses.shape[2] // cuts

    def half(index, _):
        columns = pl.ds(pl.multiple_of(index * width, width), width)
        part = product(weighted, (masses[0, :, columns], masses[1, :, columns]), ((1,), (0,)))
        part = part.reshape(rows // 8, 8, width)
        for step, out in enumerate(outs):

            @pl.when(pl.program_id(0) == step)
            def _(step=step, out=out):
                if more:
                    out[: rows // 8, :, columns] = part + more[step][: rows // 8, :, columns]
                    out[rows // 8, :, columns] = totals[:, columns] + more[step][rows // 8, :, columns]
                else:
                    out[: rows // 8, :, columns] = part
                    out[rows // 8, :, columns] = totals[:, columns]

        return 0

    lax.fori_loop(0, cuts, half, 0)


def pred_call(ids, parts, expr, keep, masses, totals, more, cuts):
    blocks, groups, rows, cells = expr.shape
    spots = masses.shape[2]
    tiles = blocks * rows // 4 + 1

    def genes(sub):
        def place(i, ids):
            step, half = (pick(i, [part[k] for part in parts]) for k in range(2))
            return (0, gene_group(ids, step, half, sub), 0, 0)

        return pl.BlockSpec((blocks, 1, rows, cells), place)

    return pl.pallas_call(
        functools.partial(pred_kernel, cuts=cuts),
        grid_spec=pltpu.PrefetchScalarGridSpec(
            num_scalar_prefetch=1,
            grid=(2,),
            in_specs=[
                genes(0),
                genes(1),
                fixed((1, cells)),
                RESIDENT,
                fixed((8, spots)),
            ]
            + [RESIDENT] * len(more),
            out_specs=[RESIDENT] * 2,
        ),
        out_shape=[jax.ShapeDtypeStruct((tiles, 8, spots), F32)] * 2,
        compiler_params=vmem(16),
        cost_estimate=cost(24 * blocks * rows * cells * spots, 4 * cells * spots + 16 * blocks * rows * (cells + spots)),
        name="pred",
    )(ids, *[streamed(expr)] * 2, keep, masses, totals, *more)


def merge_kernel(own0, own1, got0, got1, *outs):
    tiles = outs[0].shape[0] - 1
    for half, (own, got) in enumerate(((own0, got0), (own1, got1))):
        for sub in range(2):
            out = outs[2 * half + sub]
            out[:tiles] = own[sub * tiles : sub * tiles + tiles] + got[sub * tiles : sub * tiles + tiles]
            out[tiles] = own[2 * tiles] + got[2 * tiles]


def merge_call(own, got):
    tiles, _, spots = own[0].shape
    block = 256
    whole = pl.BlockSpec((tiles, 8, block), lambda i: (0, 0, i))
    piece = (tiles // 2 + 1, 8, spots)
    return pl.pallas_call(
        merge_kernel,
        grid=(spots // block,),
        in_specs=[whole] * 4,
        out_specs=[pl.BlockSpec((tiles // 2 + 1, 8, block), lambda i: (0, 0, i))] * 4,
        out_shape=[jax.ShapeDtypeStruct(piece, F32)] * 4,
        compiler_params=vmem(12),
        cost_estimate=NO_COST,
        name="merge",
    )(*own, *got)


def stats_kernel(ids, piece, spatial, spot, totals, gene, slide_sums):
    rows = piece.shape[0] * piece.shape[1]
    valid, slide = spot[0:1, :], spot[1:2, :]
    share = 1.0 / totals[0:1, :]
    mass = totals[1:2, :] * share
    value = piece[...].reshape(rows, piece.shape[2]) * share
    data = spatial[...].reshape(value.shape)
    cross, square = value * data, value * value
    lane = lax.broadcasted_iota(jnp.int32, (rows, 128), 1)
    sums = jnp.zeros((rows, 128), F32)
    for index, one in enumerate((cross, square, data * data)):
        sums = jnp.where(lane == index, jnp.sum(one * valid, axis=1, keepdims=True), sums)
    sums = sums.T
    gene[...] = jnp.zeros_like(gene)
    slide_sums[...] = jnp.zeros_like(slide_sums)
    for index in range(3):
        gene[pl.ds(16 * index + gene_group(ids, 0, 0, 0), 1), :] = sums[index : index + 1, :]
    lane = lax.broadcasted_iota(jnp.int32, (1, 128), 1)
    slides = jnp.zeros((1, 128), F32)
    logs = jnp.log(jnp.where(valid > 0, mass, 1.0))
    for k in range(SLIDES):
        inside = jnp.where(slide == k, valid, 0.0)
        for index, one in enumerate((inside, inside * mass, inside * logs)):
            total = jnp.sum(one, axis=1, keepdims=True)
            slides = jnp.where(lane == 3 * index + k, total, slides)
    slide_sums[0:1, :] = slides
    for index, one in enumerate((cross, square)):
        total = jnp.sum(one, axis=0, keepdims=True)
        for k in range(total.shape[1] // 128):
            at = 48 + 8 * index + k
            gene[at : at + 1, :] = total[:, 128 * k : 128 * k + 128]


def stats_call(ids, piece, spatial, spot, totals):
    blocks, rows, spots = piece.shape
    return pl.pallas_call(
        stats_kernel,
        grid_spec=pltpu.PrefetchScalarGridSpec(
            num_scalar_prefetch=1,
            grid=(1,),
            in_specs=[
                fixed((blocks, rows, spots)),
                pl.BlockSpec((blocks, 1, rows, spots), lambda i, ids: (0, gene_group(ids, 0, 0, 0), 0, 0)),
                fixed((8, spots)),
                fixed((8, spots)),
            ],
            out_specs=[fixed((64, 128)), fixed((8, 128))],
        ),
        out_shape=[jax.ShapeDtypeStruct((64, 128), F32), jax.ShapeDtypeStruct((8, 128), F32)],
        compiler_params=vmem(8),
        cost_estimate=NO_COST,
        name="stats",
    )(ids, piece, spatial, spot, totals)


def coef_kernel(ids, genes_slides, sums, spot, totals, gene, rows, scalars, pairs):
    valid, slide, squares = (spot[k : k + 1, :] for k in range(3))
    share = 1.0 / totals[0:1, :]
    mass = totals[1:2, :] * share
    genes = float(16 * sums.shape[1])

    def wide(index):
        return jnp.concatenate([sums[index + k : index + k + 1, :] for k in range(8)], axis=1)

    dots, own = wide(48), wide(56)
    dot, aa, bb = genes_slides[0:16, :], genes_slides[16:32, :], genes_slides[32:48, :]
    scale = lax.rsqrt(aa * bb + 1e-06)
    pairs[0:16, :] = dot * scale**3 * bb / genes
    pairs[16:32, :] = scale / genes
    pair = [pairs[pl.ds(k + gene_group(ids, *one), 1), :] for k in (0, 16) for one in PIECES]
    gene[...] = jnp.concatenate([*pair, jnp.zeros((96, 128), F32)]).T
    total = jnp.sum(jnp.sum(dot * scale, axis=1, keepdims=True), axis=0, keepdims=True)
    nvs = jnp.zeros((1, 1), F32)
    density = jnp.zeros((1, 1), F32)
    nk, tk = jnp.ones_like(valid), jnp.ones_like(valid)
    for k in range(SLIDES):
        count, held, logs = (genes_slides[48:49, 3 * j + k : 3 * j + k + 1] for j in range(3))
        some = count > 0
        safe = jnp.where(some, count, 1.0)
        nvs += count
        density += jnp.where(some, jnp.log(jnp.where(some, held, 1.0) / safe) - logs / safe, 0.0)
        here = (slide == k) & (valid > 0)
        nk = jnp.where(here, count, nk)
        tk = jnp.where(here, held, tk)
    scale = lax.rsqrt(own * squares + 1e-06)
    grad_mass = valid / SLIDES * (1.0 / tk - 1.0 / (nk * jnp.where(valid > 0, mass, 1.0)))
    mask = valid * share
    by_pred, by_data = dots * scale**3 * squares / nvs, scale / nvs
    for index, one in enumerate((by_pred * share * mask, by_data * mask, mask, share * mask)):
        rows[8 * index : 8 * index + 8, :] = jnp.broadcast_to(one, (8, one.shape[1]))
    rows[32:40, :] = jnp.concatenate([grad_mass * share, jnp.zeros((7, valid.shape[1]), F32)])
    cosines = jnp.sum(valid * dots * scale, axis=1, keepdims=True)
    lane = lax.broadcasted_iota(jnp.int32, (1, 128), 1)
    out = jnp.zeros((1, 128), F32)
    for index, one in enumerate((total / genes, cosines / nvs, density / SLIDES)):
        out = jnp.where(lane == index, one, out)
    scalars[...] = out


def coef_call(ids, genes_slides, sums, spot, totals):
    spots = spot.shape[1]
    return pl.pallas_call(
        coef_kernel,
        grid_spec=pltpu.PrefetchScalarGridSpec(
            num_scalar_prefetch=1,
            grid=(1,),
            in_specs=[fixed(genes_slides.shape), fixed(sums.shape), fixed((8, spots)), fixed((8, spots))],
            out_specs=[fixed((128, 128)), fixed((40, spots)), fixed((1, 128))],
            scratch_shapes=[pltpu.VMEM((32, 128), F32)],
        ),
        out_shape=[
            jax.ShapeDtypeStruct((128, 128), F32),
            jax.ShapeDtypeStruct((40, spots), F32),
            jax.ShapeDtypeStruct((1, 128), F32),
        ],
        compiler_params=vmem(6),
        cost_estimate=NO_COST,
        name="coef",
    )(ids, genes_slides, sums, spot, totals)


def grad_rows(pred, data, gene, spot, lane):
    by_pred = gene[:, lane : lane + 1].reshape(2, 8, 1)
    by_data = gene[:, 16 + lane : 17 + lane].reshape(2, 8, 1)
    pred, data = pred.reshape(2, 8, pred.shape[1]), data.reshape(2, 8, data.shape[1])
    grad = pred * (by_pred * spot[24:32, :] + spot[0:8, :])
    grad = grad - data * (by_data * spot[16:24, :] + spot[8:16, :])
    return grad.reshape(16, grad.shape[2]), jnp.sum(grad * pred, axis=0)


def grad_kernel(ids, *refs, count, lane, chips):
    pred, data, refs = refs[: 2 * count], refs[2 * count : 3 * count], refs[3 * count :]
    gene, spot, grad, column = refs[0], refs[1], refs[-2], refs[-1]
    step = pl.program_id(0)
    chip = (ids[2] + pick(step, chips)) & 3

    @pl.when(step == 0)
    def _():
        column[...] = jnp.zeros_like(column)

    def half_of(half, _):
        block = chip * 2 + half
        factors = gene[pl.ds(pl.multiple_of(16 * half, 16), 16), :]
        total = jnp.zeros(column.shape, F32)
        for index, part in enumerate(pred):
            for sub in range(2):
                at = gene_group(ids, *PIECES[lane + 2 * index + sub])
                row = pl.multiple_of((at & 3) * 16, 16)
                to = pl.ds(pl.multiple_of(at * 16, 16), 16)
                rows, inner = grad_rows(
                    part[sub, block],
                    data[index // 2][half, 0, pl.ds(row, 16), :],
                    factors,
                    spot,
                    lane + 2 * index + sub,
                )
                grad[0, block, to, :], grad[1, block, to, :] = split(rows)
                total += inner
        column[...] += total
        return 0

    lax.fori_loop(0, 2, half_of, 0)


def grad_call(ids, pred, spatial, gene, spot, lane, chips, done=()):
    blocks, groups, rows, spots = spatial.shape
    count = len(pred) // 2

    def chip(i, ids):
        return (ids[2] + pick(i, chips)) & 3

    def group(k):
        step = PIECES[lane + 4 * k][0]
        return pl.BlockSpec(
            (2, 1, rows, spots), lambda i, ids: (chip(i, ids), (ids[0] + step) & 3, 0, 0)
        )

    return pl.pallas_call(
        functools.partial(grad_kernel, count=count, lane=lane, chips=chips),
        grid_spec=pltpu.PrefetchScalarGridSpec(
            num_scalar_prefetch=1,
            grid=(len(chips),),
            in_specs=[RESIDENT] * (2 * count)
            + [group(k) for k in range(count)]
            + [pl.BlockSpec((32, 128), lambda i, ids: (chip(i, ids), 0)), fixed(spot.shape)]
            + [RESIDENT] * len(done),
            out_specs=[RESIDENT, fixed((8, spots))],
        ),
        out_shape=[
            jax.ShapeDtypeStruct((2, blocks, groups * rows, spots), BF16),
            jax.ShapeDtypeStruct((8, spots), F32),
        ],
        input_output_aliases={3 * count + 3: 0} if done else {},
        compiler_params=vmem(12),
        cost_estimate=NO_COST,
        name="grad",
    )(ids, *pred, *[spatial] * count, gene, spot, *done)


def back_kernel(ids, grad, masses, expr, *refs, parts, first, last):
    more, (sums, *outs), (held, ready) = refs[: first + 5 * last], refs[first + 5 * last : -2], refs[-2:]
    step = pl.program_id(0)
    rows = grad.shape[2]

    def block(part):
        return ((ids[2] + part[0]) & 3) * 2 + (ids[3] ^ part[1])

    def fetch(k):
        start = pl.multiple_of(block(parts[k]) * rows, rows)
        return pltpu.make_async_copy(expr.at[pl.ds(start, rows), :], held.at[k], ready.at[k])

    @pl.when(step == 0)
    def _():
        for k in range(len(parts)):
            fetch(k).start()

    @pl.when(step == 0)
    def _():
        if last:
            sums[...] = more[0][...] + more[1][...] + more[2][...] + more[3][...]
        else:
            sums[...] = jnp.zeros_like(sums)

    here = block([pick(step, [part[k] for part in parts]) for k in range(2)])
    left = grad[0, here], grad[1, here]
    if first:
        pair = split(jnp.concatenate([more[0][...], jnp.zeros_like(more[0])]))
        left = [jnp.concatenate(both) for both in zip(left, pair)]
    part = product(left, masses, ((1,), (1,)))
    if first:
        sums[...] = part[rows : rows + 8]
        part = part[:rows]
    for k, out in enumerate(outs):

        @pl.when(step == k)
        def _(k=k, out=out):
            out[...] = part
            fetch(k).wait()

    sums[...] += jnp.sum((part * held[step]).reshape(-1, 8, part.shape[1]), axis=0)
    if last:

        @pl.when(step == len(parts) - 1)
        def _():
            total = jnp.sum(sums[...], axis=0, keepdims=True)
            sums[...] = jnp.zeros_like(sums)
            sums[0:1, :] = total
            sums[1:2, 0:128] = more[4][...]


def back_call(ids, parts, grad, masses, expr, first=(), last=()):
    _, blocks, rows, spots = grad.shape
    cells = masses.shape[1]
    return pl.pallas_call(
        functools.partial(back_kernel, parts=parts, first=len(first), last=len(last) // 5),
        grid_spec=pltpu.PrefetchScalarGridSpec(
            num_scalar_prefetch=1,
            grid=(len(parts),),
            in_specs=[RESIDENT, RESIDENT, pl.BlockSpec(memory_space=pl.ANY)]
            + [pl.BlockSpec((8, spots), lambda i, ids: (4, 0))] * len(first)
            + [fixed(one.shape) for one in last],
            out_specs=[fixed((8, cells))] + [RESIDENT] * len(parts),
            scratch_shapes=[
                pltpu.VMEM((len(parts), rows, cells), F32),
                pltpu.SemaphoreType.DMA((len(parts),)),
            ],
        ),
        out_shape=[jax.ShapeDtypeStruct((8, cells), F32)]
        + [jax.ShapeDtypeStruct((rows, cells), F32)] * len(parts),
        compiler_params=vmem(22),
        cost_estimate=NO_COST,
        name="back",
    )(ids, grad, masses, streamed(expr), *first, *last)


def lift_kernel(above, below, far_up, far_down, out_above, out_below):
    rows = far_up.shape[0]
    out_above[:rows, :] = above[:rows, :] + far_up[...]
    out_above[rows:, :] = above[rows:, :]
    out_below[:rows, :] = below[:rows, :]
    out_below[rows:, :] = below[rows:, :] + far_down[...]


def lift_call(above, below, far_up, far_down):
    rows, cells = far_up.shape
    block = 256
    far = pl.BlockSpec((rows, block), lambda i: (0, i))
    whole = pl.BlockSpec((2 * rows, block), lambda i: (0, i))
    return pl.pallas_call(
        lift_kernel,
        grid=(cells // block,),
        in_specs=[whole, whole, far, far],
        out_specs=[whole, whole],
        out_shape=[jax.ShapeDtypeStruct(above.shape, F32)] * 2,
        compiler_params=vmem(8),
        cost_estimate=pl.CostEstimate(flops=10**10, bytes_accessed=0, transcendentals=0),
        name="lift",
    )(above, below, far_up, far_down)


def join_kernel(above, below, got_above, got_below, out_above, out_below):
    out_above[...] = above[...] + got_above[...]
    out_below[...] = below[...] + got_below[...]


def join_call(above, below, got_above, got_below):
    rows, cells = above.shape
    whole = pl.BlockSpec((rows, 256), lambda i: (0, i))
    return pl.pallas_call(
        join_kernel,
        grid=(cells // 256,),
        in_specs=[whole] * 4,
        out_specs=[whole] * 2,
        out_shape=[jax.ShapeDtypeStruct(above.shape, F32)] * 2,
        compiler_params=vmem(8),
        cost_estimate=NO_COST,
        name="join",
    )(above, below, got_above, got_below)


def map_kernel(expr, grad, masses, keep, valid, spot, *rest, scale, start):
    out, held, ready, inner = rest[-4:]
    index = pl.program_id(0)
    quarter, block = held.shape[2:]
    count = held.shape[1]

    def fetch(at, k):
        columns = pl.ds(pl.multiple_of((at + start) * block, block), block)
        return pltpu.make_async_copy(
            expr.at[pl.ds(pl.multiple_of(k * quarter, quarter), quarter), columns], held.at[at & 1, k], ready.at[at & 1, k]
        )

    @pl.when(index == 0)
    def _():
        for k in range(count):
            fetch(index, k).start()

    @pl.when(index + 1 < pl.num_programs(0))
    def _():
        for k in range(count):
            fetch(index + 1, k).start()

    inner[...] = jnp.broadcast_to(spot[0:1, :], inner.shape)

    def add(k, _):
        fetch(index, k).wait()
        rows = pl.ds(pl.multiple_of(k * quarter, quarter), quarter)
        pair = grad[0, rows, :], grad[1, rows, :]
        inner[...] += product(split(held[index & 1, k]), pair, ((0,), (0,)))
        return 0

    lax.fori_loop(0, count, add, 0)
    at = pl.multiple_of((index + start) * block, block)
    expo = masses[0, pl.ds(at, block), :].astype(F32) + masses[1, pl.ds(at, block), :].astype(F32)
    for part in range(block // 128):
        rows = slice(part * 128, part * 128 + 128)
        place = pl.ds((index + start) * (block // 128) + part, 1)
        weight, mask = as_column(keep[place, :]), as_column(valid[place, :])
        out[rows, :] = (scale * expo[rows]) * (weight * inner[rows, :] - mask * spot[1:2, :])


def map_call(start, stop, expr, grad, masses, keep, valid, spot, scale, done=()):
    genes, cells = expr.shape
    spots = masses.shape[2]
    block, count = 256, 4
    return pl.pallas_call(
        functools.partial(map_kernel, scale=scale, start=start),
        grid=(stop - start,),
        in_specs=[
            pl.BlockSpec(memory_space=pl.ANY),
            RESIDENT,
            RESIDENT,
            fixed(keep.shape),
            fixed(valid.shape),
            fixed((8, spots)),
        ]
        + [pl.BlockSpec(memory_space=pl.ANY)] * len(done),
        out_specs=pl.BlockSpec((block, spots), lambda i: (i + start, 0)),
        out_shape=jax.ShapeDtypeStruct((cells, spots), F32),
        scratch_shapes=[
            pltpu.VMEM((2, count, genes // count, block), F32),
            pltpu.SemaphoreType.DMA((2, count)),
            pltpu.VMEM((block, spots), F32),
        ],
        input_output_aliases={6: 0} if done else {},
        compiler_params=vmem(24),
        cost_estimate=NO_COST,
        name="grad_map",
    )(streamed(expr), grad, masses, keep, valid, spot, *done)


def finish_kernel(last, got1, got2, got3, totals, scalars, kind, filt, grad_filter, terms, *, all_cells):
    total = (last[...] + got2[...]) + (got1[...] + got3[...])
    nvalid, retained, reg_sum = (totals[2:3, k : k + 1] for k in range(3))
    valid = (kind[...] >= 0).astype(F32)
    sigma = jax.nn.sigmoid(filt[...])
    keep = sigma * valid
    shifted = (retained - 0.35 * nvalid) / (0.1 * all_cells)
    count_term = jnp.sqrt(shifted * shifted + 1.0)
    grad_keep = total[0:1, :] + shifted / count_term / (0.1 * all_cells) + (1.0 - 2.0 * keep) / nvalid
    row = valid * sigma * (1.0 - sigma) * grad_keep * all_cells
    for k in range(grad_filter.shape[0]):
        grad_filter[k : k + 1, :] = row[:, 128 * k : 128 * k + 128]
    lane = lax.broadcasted_iota(jnp.int32, (1, 128), 1)
    out = jnp.zeros((1, 128), F32)
    parts = (scalars[:, 0:1], total[1:2, 1:2], scalars[:, 2:3], count_term, reg_sum / nvalid)
    for index, one in enumerate(parts):
        out = jnp.where(lane == index, one, out)
    terms[...] = out[0, :5]


def finish_call(last, got, totals, scalars, kind, filt, all_cells):
    return pl.pallas_call(
        functools.partial(finish_kernel, all_cells=float(all_cells)),
        grid=(1,),
        in_specs=[fixed(one.shape) for one in (last, *got, totals, scalars, kind, filt)],
        out_specs=[fixed((kind.shape[1] // 128, 128)), fixed((5,))],
        out_shape=[
            jax.ShapeDtypeStruct((kind.shape[1] // 128, 128), F32),
            jax.ShapeDtypeStruct((5,), F32),
        ],
        compiler_params=vmem(4),
        cost_estimate=NO_COST,
        name="finish",
    )(last, *got, totals, scalars, kind, filt)


def on_device(map_logits, filter_logits, expr, spatial, cell_type, slide_id, spot_mask):
    genes, cells = expr.shape
    spots = map_logits.shape[1]
    all_cells = cells * lax.axis_size("cells")
    all_spots = spots * lax.axis_size("spots")
    cell_place = lax.axis_index("cells")
    z, x = cell_place >> 2, cell_place & 3
    spot_place = lax.axis_index("spots")
    y, core = spot_place >> 1, spot_place & 1
    first = jnp.where(core == 0, x, z)
    second = jnp.where(core == 0, z, x)
    blocks = cells // 128

    valid = (cell_type >= 0).astype(F32)
    sigma = jax.nn.sigmoid(filter_logits)
    keep = sigma * valid
    spot_valid = spot_mask.astype(F32)
    kind2 = cell_type.reshape(blocks, 128)
    filt2 = filter_logits.reshape(blocks, 128)
    keep2 = keep.reshape(blocks, 128)

    expr4 = expr.reshape(8, 16, 16, cells)
    keep_row = keep.reshape(1, cells)

    ids = jnp.stack([first, second, y, core]).astype(jnp.int32)

    def pred_part(one, two, more, cuts, *others):
        return pred_call(after(ids, *others), (one, two), expr4, keep_row, masses, totals, more, cuts)

    masses, types, totals, *far = expo_call(
        ids, ((2, 0), (2, 1)), map_logits, kind2, filt2, expr4
    )
    far_right, far_left = along(far[0], 1), along(far[1], -1)
    near = pred_part((1, 1), (-1, 0), (), 2, *far)
    near_right, near_left = along(near[0], 1), along(near[1], -1)
    late = pred_part((1, 0), (-1, 1), (far_right, far_left), 1, *near)
    late_right, late_left = along(late[0], 1), along(late[1], -1)
    own = pred_part((0, 0), (0, 1), (near_left, near_right), 2, *late)
    mine, *pieces = merge_call(own, (late_right, late_left))
    pieces = [across(piece, step + 1) for step, piece in enumerate(pieces)]
    spatial_squares = jnp.sum(after(spatial, mine) ** 2, axis=0)
    types = types + swap_along(after(types, spatial_squares), 1)
    spot_rows = stacked([spot_valid, slide_id.astype(F32), spatial_squares])
    mine = after(mine, spot_rows, types)
    piece = mine + pieces[0] + pieces[1] + pieces[2]
    totals = piece[-1]
    piece = piece[:-1].reshape(8, 16, spots)
    share = 1.0 / totals[0]
    mass = totals[1] * share

    got = [across(piece, step) for step in (1, 2, 3)]
    sums, slides = stats_call(
        ids,
        piece,
        spatial.reshape(8, 16, 16, spots),
        spot_rows,
        totals,
    )
    sums = sums + swap_along(sums, 1)
    sums = sums + swap_along(sums, 3)
    types = types + swap_along(after(types, slides), 3)
    mine = after((jnp.stack([piece, got[2]]), jnp.stack([got[1], got[0]])), sums, types)
    right0, left1 = along(mine[0], 1), along(mine[1], -1)
    right1, left0 = along(mine[1], 1), along(mine[0], -1)
    sums = sums + swap_across(after(sums, *mine), 1)
    sums = sums + swap_across(sums, 3)
    right0, left1, sums = lax.optimization_barrier((right0, left1, sums))
    far0, far1 = along(right0, 1), along(left1, -1)
    genes_slides = jnp.concatenate([sums[:48], slides])
    genes_slides = genes_slides + swap(genes_slides, 0, 0, 0, 1)
    genes_slides = genes_slides + swap(genes_slides, 0, 0, 1, 0)
    genes_slides = after(genes_slides, right1, left0)
    genes_slides = genes_slides + swap(genes_slides, 0, 0, 3, 0)
    pred = [*mine, right0, right1, left0, left1, far0, far1]
    gene_coef, spot_coef, scalars = coef_call(ids, genes_slides, sums, spot_rows, totals)
    spatial4 = spatial.reshape(8, RING, genes // 32, spots)
    grad, column_a = grad_call(ids, pred[:6], spatial4, gene_coef, spot_coef, 0, (0, 1, 2, 3))

    def last_grad(chips, grad, *others):
        return grad_call(
            after(ids, *others), pred[6:], spatial4, gene_coef, spot_coef, 12, chips, (grad,)
        )

    def back_part(steps, grad, *others, **rows):
        return back_call(after(ids, *others), steps, grad, masses, expr, **rows)

    rows = genes // 16
    grad, column_b = last_grad((2,), grad)
    sums_a, far_a = back_part([(2, 1)], grad, first=[spot_coef])
    far_got = swap(far_a, 0, 0, 0, 1)
    sums_b, far_b = back_part([(2, 0)], grad, far_a)
    far = far_b + far_got
    far_up, far_down = up(far[:rows], 1), up(far[rows:], -1)
    grad, column_c = last_grad((1, -1, 0), grad, far)
    sums_c, up_a, down_a, own_a = back_part([(1, 1), (-1, 1), (0, 1)], grad)
    up_got, down_got, own_got = (swap(one, 0, 0, 0, 1) for one in (up_a, down_a, own_a))
    sums_d, up_b, down_b = back_part([(1, 0), (-1, 0)], grad, up_a)
    types = types + swap_across(after(types, up_a), 1)
    above, below = lift_call(up_b, down_b, *after((far_up, far_down), types))
    above, below = join_call(above, below, up_got, down_got)
    near_up, near_down = up(above, 1), up(below, -1)
    types_got = swap_across(after(types, above), 3)
    last, own_b = back_part(
        [(0, 0)], grad, above, below, last=[sums_a, sums_b, sums_c, sums_d, scalars]
    )
    last_got = swap(last, 0, 0, 0, 1)
    own = own_b + own_got

    column = jnp.sum(column_a + column_b + column_c, axis=0) * share + spot_coef[32] * mass
    map_rows = stacked([spot_coef[32], column])
    valid2 = valid.reshape(blocks, 128)
    map_args = (expr, grad.reshape(2, genes, spots), masses, keep2, valid2, map_rows, all_cells * genes)
    steps = cells // 256
    grad_map = map_call(0, steps - 2, *map_args)
    types_got, last_got = after((types_got, last_got), grad_map)
    types = types + types_got
    last = after(last + last_got, own)
    got = [up(last, step) for step in (1, 2, 3)]
    grad_map = map_call(steps - 2, steps, *map_args, done=(after(grad_map, last),))
    got = after(tuple(got), grad_map)
    grad_weighted = after(own, grad_map) + near_up + near_down
    grad_expr = grad_weighted * (keep * (genes * all_spots))[None, :]
    got = after(got, grad_expr)

    type_fraction = types * share

    grad_filter, loss_terms = finish_call(
        last, got, totals, scalars, cell_type.reshape(1, cells), filter_logits.reshape(1, cells), all_cells
    )
    return (loss_terms, type_fraction, grad_map, grad_filter.reshape(cells), grad_expr)


def solution(mesh):
    in_specs = (
        P("cells", "spots"),
        P("cells"),
        P(None, "cells"),
        P(None, "spots"),
        P("cells"),
        P("spots"),
        P("spots"),
    )
    out_specs = (P(), P(None, "spots"), P("cells", "spots"), P("cells"), P("spots", "cells"))
    return jax.shard_map(
        on_device, mesh=mesh, in_specs=in_specs, out_specs=out_specs, check_vma=False
    )
```

```python
import functools

import jax
import jax.numpy as jnp
from jax import lax
from jax.experimental import pallas as pl
from jax.experimental.pallas import tpu as pltpu
from jax.sharding import PartitionSpec as P

TYPES = 32
SLIDES = 3
RING = 4
F32 = jnp.float32
BF16 = jnp.bfloat16


def vmem(mib):
    return pltpu.CompilerParams(vmem_limit_bytes=mib << 20)


def fixed(shape):
    return pl.BlockSpec(shape, lambda *_: (0,) * len(shape), pipeline_mode=pl.Buffered(1))


def streamed(array):
    return pltpu.with_memory_space_constraint(array, pltpu.HBM)


RESIDENT = pl.BlockSpec(memory_space=pltpu.VMEM)


def cost(flops, moved):
    return pl.CostEstimate(flops=int(flops) // 8, bytes_accessed=int(moved) // 8, transcendentals=0)


NO_COST = pl.CostEstimate(flops=0, bytes_accessed=0, transcendentals=0)


def route(target):
    def flat(z, x, y, core):
        return ((z % RING * RING + x % RING) * RING + y % RING) * 2 + core

    return [
        (flat(z, x, y, core), flat(*target(z, x, y, core)))
        for z in range(RING)
        for x in range(RING)
        for y in range(RING)
        for core in range(2)
    ]


def send(array, target):
    return lax.ppermute(array, ("cells", "spots"), route(target))


def along(array, step):
    return send(array, lambda z, x, y, c: (z, x + step, y, c) if c == 0 else (z + step, x, y, c))


def across(array, step):
    return send(array, lambda z, x, y, c: (z + step, x, y, c) if c == 0 else (z, x + step, y, c))


def up(array, step):
    return send(array, lambda z, x, y, c: (z, x, y + step, c))


def swap(array, mz, mx, my, mc):
    return send(array, lambda z, x, y, c: (z ^ mz, x ^ mx, y ^ my, c ^ mc))


def swap_along(array, mask):
    return send(array, lambda z, x, y, c: (z, x ^ mask, y, c) if c == 0 else (z ^ mask, x, y, c))


def swap_across(array, mask):
    return send(array, lambda z, x, y, c: (z ^ mask, x, y, c) if c == 0 else (z, x ^ mask, y, c))


def after(value, *others):
    return lax.optimization_barrier((value, *others))[0]


def split(value):
    high = value.astype(BF16)
    return high, (value - high.astype(F32)).astype(BF16)


def product(left, right, dims):
    def one(a, b):
        return lax.dot_general(a, b, (dims, ((), ())), preferred_element_type=F32)

    return one(left[0], right[0]) + one(left[0], right[1]) + one(left[1], right[0])


def gene_group(ids, step, half, sub):
    return ((ids[0] + step) & 3) * RING + ((ids[1] + 2 * half + sub) & 3)


PIECES = [
    (step, half, sub)
    for step, half in ((0, 0), (0, 1), (-1, 0), (-1, 1), (1, 0), (1, 1), (2, 0), (2, 1))
    for sub in range(2)
]


def pick(index, values):
    out = values[0]
    for k, value in enumerate(values[1:]):
        out = jnp.where(index == k + 1, value, out)
    return out


def stacked(rows):
    row = lax.broadcasted_iota(jnp.int32, (8, rows[0].shape[0]), 0)
    out = jnp.zeros(row.shape, F32)
    for k, value in enumerate(rows):
        out = jnp.where(row == k, value[None, :], out)
    return out


def as_column(row):
    return jnp.broadcast_to(row, (128, 128)).T[:, :1]


def expo_kernel(ids, logits, kind, filt, *refs):
    expr, (masses, types, totals, out0, out1) = refs[:4], refs[4:]
    step = pl.program_id(0)
    block = logits.shape[0]
    count = block // 128

    @pl.when(step == 0)
    def _():
        for out in (types, totals, out0, out1):
            out[...] = jnp.zeros_like(out)

    masses[0], masses[1] = split(jnp.exp(logits[...]))
    labels = [kind[pl.ds(step * count + part, 1), :] for part in range(count)]
    valids = [(label >= 0).astype(F32) for label in labels]
    keeps = [
        valid * jax.nn.sigmoid(filt[pl.ds(step * count + part, 1), :])
        for part, valid in enumerate(valids)
    ]
    keep = jnp.concatenate(keeps, axis=1)
    lane = lax.broadcasted_iota(jnp.int32, (1, block), 1) // 128
    valid = jnp.concatenate(valids, axis=1)
    row = lax.broadcasted_iota(jnp.int32, (16, block), 0)
    extra = jnp.where(row == count, keep, jnp.where(row == lane, valid, 0.0))
    weighted = jnp.concatenate([part[...].reshape(-1, block) for part in expr]) * keep
    part = product(split(jnp.concatenate([weighted, extra])), masses, ((1,), (0,)))
    half = weighted.shape[0] // 2
    whole = [part[2 * half + k : 2 * half + k + 1] for k in range(count + 1)]
    row = lax.broadcasted_iota(jnp.int32, types.shape, 0)
    for label, one in zip(labels, whole):
        types[...] += jnp.where(row == jnp.max(label, axis=1, keepdims=True), one, 0.0)
    lane = lax.broadcasted_iota(jnp.int32, (1, totals.shape[1]), 1)
    cell_sums = jnp.zeros(lane.shape, F32)
    for k, one in enumerate((valid, keep, keep - keep * keep)):
        cell_sums += jnp.where(lane == k, jnp.sum(one, axis=1, keepdims=True), 0.0)
    totals[0:1, :] += sum(whole[1:count], whole[0])
    totals[1:2, :] += whole[count]
    totals[2:3, :] += cell_sums
    for index, out in enumerate((out0, out1)):
        new = part[index * half : index * half + half].reshape(-1, 8, part.shape[1])
        out[: half // 8] += new
        out[half // 8] = totals[...]


def expo_call(ids, parts, logits, kind, filt, expr):
    cells, spots = logits.shape
    blocks, groups, rows, _ = expr.shape
    block = 256

    def genes(part, sub):
        return pl.BlockSpec(
            (blocks, 1, rows, block), lambda i, ids: (0, gene_group(ids, *part, sub), 0, i)
        )

    return pl.pallas_call(
        expo_kernel,
        grid_spec=pltpu.PrefetchScalarGridSpec(
            num_scalar_prefetch=1,
            grid=(cells // block,),
            in_specs=[
                pl.BlockSpec((block, spots), lambda i, w: (i, 0)),
                fixed(kind.shape),
                fixed(filt.shape),
            ]
            + [genes(part, sub) for part in parts for sub in range(2)],
            out_specs=[
                pl.BlockSpec((2, block, spots), lambda i, w: (0, i, 0)),
                fixed((TYPES, spots)),
                fixed((8, spots)),
                fixed((blocks * rows // 4 + 1, 8, spots)),
                fixed((blocks * rows // 4 + 1, 8, spots)),
            ],
        ),
        out_shape=[
            jax.ShapeDtypeStruct((2, cells, spots), BF16),
            jax.ShapeDtypeStruct((TYPES, spots), F32),
            jax.ShapeDtypeStruct((8, spots), F32),
            jax.ShapeDtypeStruct((blocks * rows // 4 + 1, 8, spots), F32),
            jax.ShapeDtypeStruct((blocks * rows // 4 + 1, 8, spots), F32),
        ],
        compiler_params=vmem(16),
        cost_estimate=cost(0, cells * spots * 8),
        name="expo",
    )(ids, streamed(logits), streamed(kind), streamed(filt), *[streamed(expr)] * 4)


def pred_kernel(ids, expr_a, expr_b, keep, masses, totals, *refs, cuts):
    more, outs = refs[:-2], refs[-2:]
    rows = 2 * expr_a.shape[0] * expr_a.shape[2]
    weighted = jnp.concatenate(
        [part[...].reshape(rows // 2, keep.shape[1]) for part in (expr_a, expr_b)]
    )
    weighted = split(weighted * keep[...])
    width = masses.shape[2] // cuts

    def half(index, _):
        columns = pl.ds(pl.multiple_of(index * width, width), width)
        part = product(weighted, (masses[0, :, columns], masses[1, :, columns]), ((1,), (0,)))
        part = part.reshape(rows // 8, 8, width)
        for step, out in enumerate(outs):

            @pl.when(pl.program_id(0) == step)
            def _(step=step, out=out):
                if more:
                    out[: rows // 8, :, columns] = part + more[step][: rows // 8, :, columns]
                    out[rows // 8, :, columns] = totals[:, columns] + more[step][rows // 8, :, columns]
                else:
                    out[: rows // 8, :, columns] = part
                    out[rows // 8, :, columns] = totals[:, columns]

        return 0

    lax.fori_loop(0, cuts, half, 0)


def pred_call(ids, parts, expr, keep, masses, totals, more, cuts):
    blocks, groups, rows, cells = expr.shape
    spots = masses.shape[2]
    tiles = blocks * rows // 4 + 1

    def genes(sub):
        def place(i, ids):
            step, half = (pick(i, [part[k] for part in parts]) for k in range(2))
            return (0, gene_group(ids, step, half, sub), 0, 0)

        return pl.BlockSpec((blocks, 1, rows, cells), place)

    return pl.pallas_call(
        functools.partial(pred_kernel, cuts=cuts),
        grid_spec=pltpu.PrefetchScalarGridSpec(
            num_scalar_prefetch=1,
            grid=(2,),
            in_specs=[
                genes(0),
                genes(1),
                fixed((1, cells)),
                RESIDENT,
                fixed((8, spots)),
            ]
            + [RESIDENT] * len(more),
            out_specs=[RESIDENT] * 2,
        ),
        out_shape=[jax.ShapeDtypeStruct((tiles, 8, spots), F32)] * 2,
        compiler_params=vmem(16),
        cost_estimate=cost(24 * blocks * rows * cells * spots, 4 * cells * spots + 16 * blocks * rows * (cells + spots)),
        name="pred",
    )(ids, *[streamed(expr)] * 2, keep, masses, totals, *more)


def merge_kernel(own0, own1, got0, got1, *outs):
    tiles = outs[0].shape[0] - 1
    for half, (own, got) in enumerate(((own0, got0), (own1, got1))):
        for sub in range(2):
            out = outs[2 * half + sub]
            out[:tiles] = own[sub * tiles : sub * tiles + tiles] + got[sub * tiles : sub * tiles + tiles]
            out[tiles] = own[2 * tiles] + got[2 * tiles]


def merge_call(own, got):
    tiles, _, spots = own[0].shape
    block = 256
    whole = pl.BlockSpec((tiles, 8, block), lambda i: (0, 0, i))
    piece = (tiles // 2 + 1, 8, spots)
    return pl.pallas_call(
        merge_kernel,
        grid=(spots // block,),
        in_specs=[whole] * 4,
        out_specs=[pl.BlockSpec((tiles // 2 + 1, 8, block), lambda i: (0, 0, i))] * 4,
        out_shape=[jax.ShapeDtypeStruct(piece, F32)] * 4,
        compiler_params=vmem(12),
        cost_estimate=NO_COST,
        name="merge",
    )(*own, *got)


def stats_kernel(ids, piece, spatial, spot, totals, gene, slide_sums):
    rows = piece.shape[0] * piece.shape[1]
    valid, slide = spot[0:1, :], spot[1:2, :]
    share = 1.0 / totals[0:1, :]
    mass = totals[1:2, :] * share
    value = piece[...].reshape(rows, piece.shape[2]) * share
    data = spatial[...].reshape(value.shape)
    cross, square = value * data, value * value
    lane = lax.broadcasted_iota(jnp.int32, (rows, 128), 1)
    sums = jnp.zeros((rows, 128), F32)
    for index, one in enumerate((cross, square, data * data)):
        sums = jnp.where(lane == index, jnp.sum(one * valid, axis=1, keepdims=True), sums)
    sums = sums.T
    gene[...] = jnp.zeros_like(gene)
    slide_sums[...] = jnp.zeros_like(slide_sums)
    for index in range(3):
        gene[pl.ds(16 * index + gene_group(ids, 0, 0, 0), 1), :] = sums[index : index + 1, :]
    lane = lax.broadcasted_iota(jnp.int32, (1, 128), 1)
    slides = jnp.zeros((1, 128), F32)
    logs = jnp.log(jnp.where(valid > 0, mass, 1.0))
    for k in range(SLIDES):
        inside = jnp.where(slide == k, valid, 0.0)
        for index, one in enumerate((inside, inside * mass, inside * logs)):
            total = jnp.sum(one, axis=1, keepdims=True)
            slides = jnp.where(lane == 3 * index + k, total, slides)
    slide_sums[0:1, :] = slides
    for index, one in enumerate((cross, square)):
        total = jnp.sum(one, axis=0, keepdims=True)
        for k in range(total.shape[1] // 128):
            at = 48 + 8 * index + k
            gene[at : at + 1, :] = total[:, 128 * k : 128 * k + 128]


def stats_call(ids, piece, spatial, spot, totals):
    blocks, rows, spots = piece.shape
    return pl.pallas_call(
        stats_kernel,
        grid_spec=pltpu.PrefetchScalarGridSpec(
            num_scalar_prefetch=1,
            grid=(1,),
            in_specs=[
                fixed((blocks, rows, spots)),
                pl.BlockSpec((blocks, 1, rows, spots), lambda i, ids: (0, gene_group(ids, 0, 0, 0), 0, 0)),
                fixed((8, spots)),
                fixed((8, spots)),
            ],
            out_specs=[fixed((64, 128)), fixed((8, 128))],
        ),
        out_shape=[jax.ShapeDtypeStruct((64, 128), F32), jax.ShapeDtypeStruct((8, 128), F32)],
        compiler_params=vmem(8),
        cost_estimate=NO_COST,
        name="stats",
    )(ids, piece, spatial, spot, totals)


def coef_kernel(ids, genes_slides, sums, spot, totals, gene, rows, scalars, pairs):
    valid, slide, squares = (spot[k : k + 1, :] for k in range(3))
    share = 1.0 / totals[0:1, :]
    mass = totals[1:2, :] * share
    genes = float(16 * sums.shape[1])

    def wide(index):
        return jnp.concatenate([sums[index + k : index + k + 1, :] for k in range(8)], axis=1)

    dots, own = wide(48), wide(56)
    dot, aa, bb = genes_slides[0:16, :], genes_slides[16:32, :], genes_slides[32:48, :]
    scale = lax.rsqrt(aa * bb + 1e-06)
    pairs[0:16, :] = dot * scale**3 * bb / genes
    pairs[16:32, :] = scale / genes
    pair = [pairs[pl.ds(k + gene_group(ids, *one), 1), :] for k in (0, 16) for one in PIECES]
    gene[...] = jnp.concatenate([*pair, jnp.zeros((96, 128), F32)]).T
    total = jnp.sum(jnp.sum(dot * scale, axis=1, keepdims=True), axis=0, keepdims=True)
    nvs = jnp.zeros((1, 1), F32)
    density = jnp.zeros((1, 1), F32)
    nk, tk = jnp.ones_like(valid), jnp.ones_like(valid)
    for k in range(SLIDES):
        count, held, logs = (genes_slides[48:49, 3 * j + k : 3 * j + k + 1] for j in range(3))
        some = count > 0
        safe = jnp.where(some, count, 1.0)
        nvs += count
        density += jnp.where(some, jnp.log(jnp.where(some, held, 1.0) / safe) - logs / safe, 0.0)
        here = (slide == k) & (valid > 0)
        nk = jnp.where(here, count, nk)
        tk = jnp.where(here, held, tk)
    scale = lax.rsqrt(own * squares + 1e-06)
    grad_mass = valid / SLIDES * (1.0 / tk - 1.0 / (nk * jnp.where(valid > 0, mass, 1.0)))
    mask = valid * share
    by_pred, by_data = dots * scale**3 * squares / nvs, scale / nvs
    for index, one in enumerate((by_pred * share * mask, by_data * mask, mask, share * mask)):
        rows[8 * index : 8 * index + 8, :] = jnp.broadcast_to(one, (8, one.shape[1]))
    rows[32:40, :] = jnp.concatenate([grad_mass * share, jnp.zeros((7, valid.shape[1]), F32)])
    cosines = jnp.sum(valid * dots * scale, axis=1, keepdims=True)
    lane = lax.broadcasted_iota(jnp.int32, (1, 128), 1)
    out = jnp.zeros((1, 128), F32)
    for index, one in enumerate((total / genes, cosines / nvs, density / SLIDES)):
        out = jnp.where(lane == index, one, out)
    scalars[...] = out


def coef_call(ids, genes_slides, sums, spot, totals):
    spots = spot.shape[1]
    return pl.pallas_call(
        coef_kernel,
        grid_spec=pltpu.PrefetchScalarGridSpec(
            num_scalar_prefetch=1,
            grid=(1,),
            in_specs=[fixed(genes_slides.shape), fixed(sums.shape), fixed((8, spots)), fixed((8, spots))],
            out_specs=[fixed((128, 128)), fixed((40, spots)), fixed((1, 128))],
            scratch_shapes=[pltpu.VMEM((32, 128), F32)],
        ),
        out_shape=[
            jax.ShapeDtypeStruct((128, 128), F32),
            jax.ShapeDtypeStruct((40, spots), F32),
            jax.ShapeDtypeStruct((1, 128), F32),
        ],
        compiler_params=vmem(6),
        cost_estimate=NO_COST,
        name="coef",
    )(ids, genes_slides, sums, spot, totals)


def grad_rows(pred, data, gene, spot, lane):
    by_pred = gene[:, lane : lane + 1].reshape(2, 8, 1)
    by_data = gene[:, 16 + lane : 17 + lane].reshape(2, 8, 1)
    pred, data = pred.reshape(2, 8, pred.shape[1]), data.reshape(2, 8, data.shape[1])
    grad = pred * (by_pred * spot[24:32, :] + spot[0:8, :])
    grad = grad - data * (by_data * spot[16:24, :] + spot[8:16, :])
    return grad.reshape(16, grad.shape[2]), jnp.sum(grad * pred, axis=0)


def grad_kernel(ids, *refs, count, lane, chips):
    pred, data, refs = refs[: 2 * count], refs[2 * count : 3 * count], refs[3 * count :]
    gene, spot, grad, column = refs[0], refs[1], refs[-2], refs[-1]
    step = pl.program_id(0)
    chip = (ids[2] + pick(step, chips)) & 3

    @pl.when(step == 0)
    def _():
        column[...] = jnp.zeros_like(column)

    def half_of(half, _):
        block = chip * 2 + half
        factors = gene[pl.ds(pl.multiple_of(16 * half, 16), 16), :]
        total = jnp.zeros(column.shape, F32)
        for index, part in enumerate(pred):
            for sub in range(2):
                at = gene_group(ids, *PIECES[lane + 2 * index + sub])
                row = pl.multiple_of((at & 3) * 16, 16)
                to = pl.ds(pl.multiple_of(at * 16, 16), 16)
                rows, inner = grad_rows(
                    part[sub, block],
                    data[index // 2][half, 0, pl.ds(row, 16), :],
                    factors,
                    spot,
                    lane + 2 * index + sub,
                )
                grad[0, block, to, :], grad[1, block, to, :] = split(rows)
                total += inner
        column[...] += total
        return 0

    lax.fori_loop(0, 2, half_of, 0)


def grad_call(ids, pred, spatial, gene, spot, lane, chips, done=()):
    blocks, groups, rows, spots = spatial.shape
    count = len(pred) // 2

    def chip(i, ids):
        return (ids[2] + pick(i, chips)) & 3

    def group(k):
        step = PIECES[lane + 4 * k][0]
        return pl.BlockSpec(
            (2, 1, rows, spots), lambda i, ids: (chip(i, ids), (ids[0] + step) & 3, 0, 0)
        )

    return pl.pallas_call(
        functools.partial(grad_kernel, count=count, lane=lane, chips=chips),
        grid_spec=pltpu.PrefetchScalarGridSpec(
            num_scalar_prefetch=1,
            grid=(len(chips),),
            in_specs=[RESIDENT] * (2 * count)
            + [group(k) for k in range(count)]
            + [pl.BlockSpec((32, 128), lambda i, ids: (chip(i, ids), 0)), fixed(spot.shape)]
            + [RESIDENT] * len(done),
            out_specs=[RESIDENT, fixed((8, spots))],
        ),
        out_shape=[
            jax.ShapeDtypeStruct((2, blocks, groups * rows, spots), BF16),
            jax.ShapeDtypeStruct((8, spots), F32),
        ],
        input_output_aliases={3 * count + 3: 0} if done else {},
        compiler_params=vmem(12),
        cost_estimate=NO_COST,
        name="grad",
    )(ids, *pred, *[spatial] * count, gene, spot, *done)


def back_kernel(ids, grad, masses, expr, *refs, parts, first, last):
    more, (sums, *outs), (held, ready) = refs[: first + 5 * last], refs[first + 5 * last : -2], refs[-2:]
    step = pl.program_id(0)
    rows = grad.shape[2]

    def block(part):
        return ((ids[2] + part[0]) & 3) * 2 + (ids[3] ^ part[1])

    def fetch(k):
        start = pl.multiple_of(block(parts[k]) * rows, rows)
        return pltpu.make_async_copy(expr.at[pl.ds(start, rows), :], held.at[k], ready.at[k])

    @pl.when(step == 0)
    def _():
        for k in range(len(parts)):
            fetch(k).start()

    @pl.when(step == 0)
    def _():
        if last:
            sums[...] = more[0][...] + more[1][...] + more[2][...] + more[3][...]
        else:
            sums[...] = jnp.zeros_like(sums)

    here = block([pick(step, [part[k] for part in parts]) for k in range(2)])
    left = grad[0, here], grad[1, here]
    if first:
        pair = split(jnp.concatenate([more[0][...], jnp.zeros_like(more[0])]))
        left = [jnp.concatenate(both) for both in zip(left, pair)]
    part = product(left, masses, ((1,), (1,)))
    if first:
        sums[...] = part[rows : rows + 8]
        part = part[:rows]
    for k, out in enumerate(outs):

        @pl.when(step == k)
        def _(k=k, out=out):
            out[...] = part
            fetch(k).wait()

    sums[...] += jnp.sum((part * held[step]).reshape(-1, 8, part.shape[1]), axis=0)
    if last:

        @pl.when(step == len(parts) - 1)
        def _():
            total = jnp.sum(sums[...], axis=0, keepdims=True)
            sums[...] = jnp.zeros_like(sums)
            sums[0:1, :] = total
            sums[1:2, 0:128] = more[4][...]


def back_call(ids, parts, grad, masses, expr, first=(), last=()):
    _, blocks, rows, spots = grad.shape
    cells = masses.shape[1]
    return pl.pallas_call(
        functools.partial(back_kernel, parts=parts, first=len(first), last=len(last) // 5),
        grid_spec=pltpu.PrefetchScalarGridSpec(
            num_scalar_prefetch=1,
            grid=(len(parts),),
            in_specs=[RESIDENT, RESIDENT, pl.BlockSpec(memory_space=pl.ANY)]
            + [pl.BlockSpec((8, spots), lambda i, ids: (4, 0))] * len(first)
            + [fixed(one.shape) for one in last],
            out_specs=[fixed((8, cells))] + [RESIDENT] * len(parts),
            scratch_shapes=[
                pltpu.VMEM((len(parts), rows, cells), F32),
                pltpu.SemaphoreType.DMA((len(parts),)),
            ],
        ),
        out_shape=[jax.ShapeDtypeStruct((8, cells), F32)]
        + [jax.ShapeDtypeStruct((rows, cells), F32)] * len(parts),
        compiler_params=vmem(22),
        cost_estimate=NO_COST,
        name="back",
    )(ids, grad, masses, streamed(expr), *first, *last)


def lift_kernel(above, below, far_up, far_down, out_above, out_below):
    rows = far_up.shape[0]
    out_above[:rows, :] = above[:rows, :] + far_up[...]
    out_above[rows:, :] = above[rows:, :]
    out_below[:rows, :] = below[:rows, :]
    out_below[rows:, :] = below[rows:, :] + far_down[...]


def lift_call(above, below, far_up, far_down):
    rows, cells = far_up.shape
    block = 256
    far = pl.BlockSpec((rows, block), lambda i: (0, i))
    whole = pl.BlockSpec((2 * rows, block), lambda i: (0, i))
    return pl.pallas_call(
        lift_kernel,
        grid=(cells // block,),
        in_specs=[whole, whole, far, far],
        out_specs=[whole, whole],
        out_shape=[jax.ShapeDtypeStruct(above.shape, F32)] * 2,
        compiler_params=vmem(8),
        cost_estimate=pl.CostEstimate(flops=10**10, bytes_accessed=0, transcendentals=0),
        name="lift",
    )(above, below, far_up, far_down)


def join_kernel(above, below, got_above, got_below, out_above, out_below):
    out_above[...] = above[...] + got_above[...]
    out_below[...] = below[...] + got_below[...]


def join_call(above, below, got_above, got_below):
    rows, cells = above.shape
    whole = pl.BlockSpec((rows, 256), lambda i: (0, i))
    return pl.pallas_call(
        join_kernel,
        grid=(cells // 256,),
        in_specs=[whole] * 4,
        out_specs=[whole] * 2,
        out_shape=[jax.ShapeDtypeStruct(above.shape, F32)] * 2,
        compiler_params=vmem(8),
        cost_estimate=NO_COST,
        name="join",
    )(above, below, got_above, got_below)


def map_kernel(expr, grad, masses, keep, valid, spot, out, held, ready, *, scale):
    index = pl.program_id(0)
    quarter, block = held.shape[2:]
    count = held.shape[1]

    def fetch(at, k):
        columns = pl.ds(pl.multiple_of(at * block, block), block)
        return pltpu.make_async_copy(
            expr.at[pl.ds(k * quarter, quarter), columns], held.at[at & 1, k], ready.at[at & 1, k]
        )

    @pl.when(index == 0)
    def _():
        for k in range(count):
            fetch(index, k).start()

    @pl.when(index + 1 < pl.num_programs(0))
    def _():
        for k in range(count):
            fetch(index + 1, k).start()

    inner = spot[0:1, :]
    for k in range(count):
        fetch(index, k).wait()
        rows = slice(k * quarter, k * quarter + quarter)
        pair = grad[0, rows, :], grad[1, rows, :]
        inner = inner + product(split(held[index & 1, k]), pair, ((0,), (0,)))
    at = pl.multiple_of(index * block, block)
    expo = masses[0, pl.ds(at, block), :].astype(F32) + masses[1, pl.ds(at, block), :].astype(F32)
    for part in range(block // 128):
        rows = slice(part * 128, part * 128 + 128)
        place = pl.ds(index * (block // 128) + part, 1)
        weight, mask = as_column(keep[place, :]), as_column(valid[place, :])
        out[rows, :] = (scale * expo[rows]) * (weight * inner[rows] - mask * spot[1:2, :])


def map_call(expr, grad, masses, keep, valid, spot, scale):
    genes, cells = expr.shape
    spots = masses.shape[2]
    block, count = 256, 4
    return pl.pallas_call(
        functools.partial(map_kernel, scale=scale),
        grid=(cells // block,),
        in_specs=[
            pl.BlockSpec(memory_space=pl.ANY),
            RESIDENT,
            RESIDENT,
            fixed(keep.shape),
            fixed(valid.shape),
            fixed((8, spots)),
        ],
        out_specs=pl.BlockSpec((block, spots), lambda i: (i, 0)),
        out_shape=jax.ShapeDtypeStruct((cells, spots), F32),
        scratch_shapes=[
            pltpu.VMEM((2, count, genes // count, block), F32),
            pltpu.SemaphoreType.DMA((2, count)),
        ],
        compiler_params=vmem(24),
        cost_estimate=NO_COST,
        name="grad_map",
    )(streamed(expr), grad, masses, keep, valid, spot)


def finish_kernel(last, got1, got2, got3, totals, scalars, kind, filt, grad_filter, terms, *, all_cells):
    total = (last[...] + got2[...]) + (got1[...] + got3[...])
    nvalid, retained, reg_sum = (totals[2:3, k : k + 1] for k in range(3))
    valid = (kind[...] >= 0).astype(F32)
    sigma = jax.nn.sigmoid(filt[...])
    keep = sigma * valid
    shifted = (retained - 0.35 * nvalid) / (0.1 * all_cells)
    count_term = jnp.sqrt(shifted * shifted + 1.0)
    grad_keep = total[0:1, :] + shifted / count_term / (0.1 * all_cells) + (1.0 - 2.0 * keep) / nvalid
    row = valid * sigma * (1.0 - sigma) * grad_keep * all_cells
    for k in range(grad_filter.shape[0]):
        grad_filter[k : k + 1, :] = row[:, 128 * k : 128 * k + 128]
    lane = lax.broadcasted_iota(jnp.int32, (1, 128), 1)
    out = jnp.zeros((1, 128), F32)
    parts = (scalars[:, 0:1], total[1:2, 1:2], scalars[:, 2:3], count_term, reg_sum / nvalid)
    for index, one in enumerate(parts):
        out = jnp.where(lane == index, one, out)
    terms[...] = out[0, :5]


def finish_call(last, got, totals, scalars, kind, filt, all_cells):
    return pl.pallas_call(
        functools.partial(finish_kernel, all_cells=float(all_cells)),
        grid=(1,),
        in_specs=[fixed(one.shape) for one in (last, *got, totals, scalars, kind, filt)],
        out_specs=[fixed((kind.shape[1] // 128, 128)), fixed((5,))],
        out_shape=[
            jax.ShapeDtypeStruct((kind.shape[1] // 128, 128), F32),
            jax.ShapeDtypeStruct((5,), F32),
        ],
        compiler_params=vmem(4),
        cost_estimate=NO_COST,
        name="finish",
    )(last, *got, totals, scalars, kind, filt)


def on_device(map_logits, filter_logits, expr, spatial, cell_type, slide_id, spot_mask):
    genes, cells = expr.shape
    spots = map_logits.shape[1]
    all_cells = cells * lax.axis_size("cells")
    all_spots = spots * lax.axis_size("spots")
    cell_place = lax.axis_index("cells")
    z, x = cell_place >> 2, cell_place & 3
    spot_place = lax.axis_index("spots")
    y, core = spot_place >> 1, spot_place & 1
    first = jnp.where(core == 0, x, z)
    second = jnp.where(core == 0, z, x)
    blocks = cells // 128

    valid = (cell_type >= 0).astype(F32)
    sigma = jax.nn.sigmoid(filter_logits)
    keep = sigma * valid
    spot_valid = spot_mask.astype(F32)
    kind2 = cell_type.reshape(blocks, 128)
    filt2 = filter_logits.reshape(blocks, 128)
    keep2 = keep.reshape(blocks, 128)

    expr4 = expr.reshape(8, 16, 16, cells)
    keep_row = keep.reshape(1, cells)

    ids = jnp.stack([first, second, y, core]).astype(jnp.int32)

    def pred_part(one, two, more, cuts, *others):
        return pred_call(after(ids, *others), (one, two), expr4, keep_row, masses, totals, more, cuts)

    masses, types, totals, *far = expo_call(
        ids, ((2, 0), (2, 1)), map_logits, kind2, filt2, expr4
    )
    far_right, far_left = along(far[0], 1), along(far[1], -1)
    near = pred_part((1, 1), (-1, 0), (), 2, *far)
    near_right, near_left = along(near[0], 1), along(near[1], -1)
    late = pred_part((1, 0), (-1, 1), (far_right, far_left), 1, *near)
    late_right, late_left = along(late[0], 1), along(late[1], -1)
    own = pred_part((0, 0), (0, 1), (near_left, near_right), 2, *late)
    mine, *pieces = merge_call(own, (late_right, late_left))
    pieces = [across(piece, step + 1) for step, piece in enumerate(pieces)]
    spatial_squares = jnp.sum(after(spatial, mine) ** 2, axis=0)
    types = types + swap_along(after(types, spatial_squares), 1)
    spot_rows = stacked([spot_valid, slide_id.astype(F32), spatial_squares])
    mine = after(mine, spot_rows, types)
    piece = mine + pieces[0] + pieces[1] + pieces[2]
    totals = piece[-1]
    piece = piece[:-1].reshape(8, 16, spots)
    share = 1.0 / totals[0]
    mass = totals[1] * share

    got = [across(piece, step) for step in (1, 2, 3)]
    sums, slides = stats_call(
        ids,
        piece,
        spatial.reshape(8, 16, 16, spots),
        spot_rows,
        totals,
    )
    sums = sums + swap_along(sums, 1)
    sums = sums + swap_along(sums, 3)
    types = types + swap_along(after(types, slides), 3)
    mine = after((jnp.stack([piece, got[2]]), jnp.stack([got[1], got[0]])), sums, types)
    right0, left1 = along(mine[0], 1), along(mine[1], -1)
    right1, left0 = along(mine[1], 1), along(mine[0], -1)
    sums = sums + swap_across(after(sums, *mine), 1)
    sums = sums + swap_across(sums, 3)
    right0, left1, sums = lax.optimization_barrier((right0, left1, sums))
    far0, far1 = along(right0, 1), along(left1, -1)
    genes_slides = jnp.concatenate([sums[:48], slides])
    genes_slides = genes_slides + swap(genes_slides, 0, 0, 0, 1)
    genes_slides = genes_slides + swap(genes_slides, 0, 0, 1, 0)
    genes_slides = after(genes_slides, right1, left0)
    genes_slides = genes_slides + swap(genes_slides, 0, 0, 3, 0)
    pred = [*mine, right0, right1, left0, left1, far0, far1]
    gene_coef, spot_coef, scalars = coef_call(ids, genes_slides, sums, spot_rows, totals)
    spatial4 = spatial.reshape(8, RING, genes // 32, spots)
    grad, column_a = grad_call(ids, pred[:6], spatial4, gene_coef, spot_coef, 0, (0, 1, 2, 3))

    def last_grad(chips, grad, *others):
        return grad_call(
            after(ids, *others), pred[6:], spatial4, gene_coef, spot_coef, 12, chips, (grad,)
        )

    def back_part(steps, grad, *others, **rows):
        return back_call(after(ids, *others), steps, grad, masses, expr, **rows)

    rows = genes // 16
    grad, column_b = last_grad((2,), grad)
    sums_a, far_a = back_part([(2, 1)], grad, first=[spot_coef])
    far_got = swap(far_a, 0, 0, 0, 1)
    sums_b, far_b = back_part([(2, 0)], grad, far_a)
    far = far_b + far_got
    far_up, far_down = up(far[:rows], 1), up(far[rows:], -1)
    grad, column_c = last_grad((1, -1, 0), grad, far)
    sums_c, up_a, down_a, own_a = back_part([(1, 1), (-1, 1), (0, 1)], grad)
    up_got, down_got, own_got = (swap(one, 0, 0, 0, 1) for one in (up_a, down_a, own_a))
    sums_d, up_b, down_b = back_part([(1, 0), (-1, 0)], grad, up_a)
    types = types + swap_across(after(types, up_a), 1)
    above, below = lift_call(up_b, down_b, *after((far_up, far_down), types))
    above, below = join_call(above, below, up_got, down_got)
    near_up, near_down = up(above, 1), up(below, -1)
    types_got = swap_across(after(types, above), 3)
    last, own_b = back_part(
        [(0, 0)], grad, above, below, last=[sums_a, sums_b, sums_c, sums_d, scalars]
    )
    last_got = swap(last, 0, 0, 0, 1)
    own = own_b + own_got

    column = jnp.sum(column_a + column_b + column_c, axis=0) * share + spot_coef[32] * mass
    types = types + types_got
    last = after(last + last_got, (own, types))
    got = [up(last, step) for step in (1, 2, 3)]
    map_rows = after(stacked([spot_coef[32], column]), last)
    valid2 = valid.reshape(blocks, 128)
    map_args = (expr, grad.reshape(2, genes, spots), masses, keep2, valid2, map_rows, all_cells * genes)
    grad_map = map_call(*map_args)
    got = after(tuple(got), grad_map)
    grad_weighted = after(own, grad_map) + near_up + near_down
    grad_expr = grad_weighted * (keep * (genes * all_spots))[None, :]
    got = after(tuple(got), grad_expr)

    type_fraction = types * share

    grad_filter, loss_terms = finish_call(
        last, got, totals, scalars, cell_type.reshape(1, cells), filter_logits.reshape(1, cells), all_cells
    )
    return (loss_terms, type_fraction, grad_map, grad_filter.reshape(cells), grad_expr)


def solution(mesh):
    in_specs = (
        P("cells", "spots"),
        P("cells"),
        P(None, "cells"),
        P(None, "spots"),
        P("cells"),
        P("spots"),
        P("spots"),
    )
    out_specs = (P(), P(None, "spots"), P("cells", "spots"), P("cells"), P("spots", "cells"))
    return jax.shard_map(
        on_device, mesh=mesh, in_specs=in_specs, out_specs=out_specs, check_vma=False
    )
```
